32 devices in a mesh: dp: 8 (over z, x), ctx: 4 (over y, core).
Axes of the slice: x: 2, y: 2, z: 4, core: 2. Of those that a mesh axis runs over, the one named last changes fastest.
Arguments:
- tokens_in: bfloat16 [16, 1024, 768], P('dp', 'ctx'), may hold values from -6 to 6
- out_grad: bfloat16 [16, 1024, 768], P('dp', 'ctx'), may hold values from -6 to 6
- w_query: bfloat16 [768, 768], P(('dp', 'ctx')), may hold values from -0.3125 to 0.3125
- w_key: bfloat16 [768, 768], P(('dp', 'ctx')), may hold values from -0.21875 to 0.21875
- w_value: bfloat16 [768, 768], P(('dp', 'ctx')), may hold values from -0.21875 to 0.21875
- w_out: bfloat16 [768, 768], P(('dp', 'ctx')), may hold values from -0.875 to 0.875
- w_up: bfloat16 [768, 3072], P(('dp', 'ctx')), may hold values from -0.21875 to 0.21875
- w_down: bfloat16 [3072, 768], P(('dp', 'ctx')), may hold values from -0.109375 to 0.109375
- b_query: bfloat16 [768], P(('dp', 'ctx')), may hold values from -4 to 4
- b_value: bfloat16 [768], P(('dp', 'ctx')), may hold values from -4 to 4
- b_out: bfloat16 [768], P(('dp', 'ctx')), may hold values from -4 to 4
- b_up: bfloat16 [3072], P(('dp', 'ctx')), may hold values from -4 to 4
- b_down: bfloat16 [768], P(('dp', 'ctx')), may hold values from -4 to 4
- norm1_gain: bfloat16 [768], P(('dp', 'ctx')), may hold values from 0.25 to 1.75
- norm1_shift: bfloat16 [768], P(('dp', 'ctx')), may hold values from -4 to 4
- norm2_gain: bfloat16 [768], P(('dp', 'ctx')), may hold values from 0.25 to 1.75
- norm2_shift: bfloat16 [768], P(('dp', 'ctx')), may hold values from -4 to 4
Outputs:
- layer_out: bfloat16 [16, 1024, 768], P('dp', 'ctx')
- grad_tokens: float32 [16, 1024, 768], P('dp', 'ctx')
- grad_w_query: float32 [768, 768], P(('dp', 'ctx'))
- grad_w_key: float32 [768, 768], P(('dp', 'ctx'))
- grad_w_value: float32 [768, 768], P(('dp', 'ctx'))
- grad_w_out: float32 [768, 768], P(('dp', 'ctx'))
- grad_w_up: float32 [768, 3072], P(('dp', 'ctx'))
- grad_w_down: float32 [3072, 768], P(('dp', 'ctx'))
- grad_b_query: float32 [768], P(('dp', 'ctx'))
- grad_b_value: float32 [768], P(('dp', 'ctx'))
- grad_b_out: float32 [768], P(('dp', 'ctx'))
- grad_b_up: float32 [3072], P(('dp', 'ctx'))
- grad_b_down: float32 [768], P(('dp', 'ctx'))
- grad_norm1_gain: float32 [768], P(('dp', 'ctx'))
- grad_norm1_shift: float32 [768], P(('dp', 'ctx'))
- grad_norm2_gain: float32 [768], P(('dp', 'ctx'))
- grad_norm2_shift: float32 [768], P(('dp', 'ctx'))
The draws below stay inside these ranges and needn't reach their ends.
All inputs are finite; a program needn't handle non-finite values.
Results may differ from the reference program's by a relative error of at most 0.017.
Values may be sent and summed in bfloat16 or wider, within the bound.
No kernel may reach another device: no remote copies, remote signals or barrier semaphores. Data moves between devices by JAX's collectives and lax.ppermute only.
A program may use at most 192 MiB of HBM per device.

```python
import jax
import jax.numpy as jnp
from jax import lax

D = 768
HEADS = 12
DH = 64
FF = 3072
LEN = 1024
SEQS = 16


def level_of(key, extent, pieces, smallest, largest):
    loudness = 1.0
    for position, parts in pieces:
        heights = jax.random.uniform(jax.random.fold_in(jax.random.fold_in(key, 6), position), (parts,), jnp.float32, smallest / len(pieces), largest / len(pieces))
        loudness = loudness * jnp.repeat(jnp.exp(heights), extent[position] // parts).reshape((-1,) + (1,) * (len(extent) - 1 - position))
    return loudness


def centred(key, extent, deviation, most, pieces=(), held_as=jnp.bfloat16):
    result = jax.random.normal(key, extent, jnp.float32) * deviation
    if len(pieces) > 0:
        result = level_of(key, extent, pieces, -0.22, 0.18) * result
    return jnp.clip(result, min=-most, max=most).astype(held_as)


def setup_inputs(seed: int = 0) -> dict:
    seeds = jax.random.split(jax.random.key(seed), 18)
    return {
        "tokens_in": centred(seeds[0], (SEQS, LEN, D), 1.0, 6.0, ((0, 8), (1, 4))),
        "out_grad": centred(seeds[1], (SEQS, LEN, D), 1.0, 6.0, ((0, 8), (1, 4))),
        "w_query": centred(seeds[2], (D, D), (D // 2) ** -0.5, 0.3125, ((0, 32),)),
        "w_key": centred(seeds[3], (D, D), D ** -0.5, 0.21875, ((0, 32),)),
        "w_value": centred(seeds[4], (D, D), D ** -0.5, 0.21875, ((0, 32),)),
        "w_out": centred(seeds[5], (D, D), (D // 16) ** -0.5, 0.875, ((0, 32),)),
        "w_up": centred(seeds[6], (D, FF), D ** -0.5, 0.21875, ((0, 32),)),
        "w_down": centred(seeds[7], (FF, D), FF ** -0.5, 0.109375, ((0, 32),)),
        "b_query": centred(seeds[8], (D,), 0.3, 4.0, ((0, 32),)),
        "b_value": centred(seeds[9], (D,), 0.3, 4.0, ((0, 32),)),
        "b_out": centred(seeds[10], (D,), 0.3, 4.0, ((0, 32),)),
        "b_up": centred(seeds[11], (FF,), 0.3, 4.0, ((0, 32),)),
        "b_down": centred(seeds[12], (D,), 0.3, 4.0, ((0, 32),)),
        "norm1_gain": jnp.clip(1.0 + 0.15 * jax.random.normal(seeds[13], (D,), jnp.float32), 0.25, 1.75).astype(jnp.bfloat16),
        "norm1_shift": centred(seeds[14], (D,), 0.3, 4.0, ((0, 32),)),
        "norm2_gain": jnp.clip(1.0 + 0.15 * jax.random.normal(seeds[15], (D,), jnp.float32), 0.25, 1.75).astype(jnp.bfloat16),
        "norm2_shift": centred(seeds[16], (D,), 0.3, 4.0, ((0, 32),)),
    }


@jax.custom_vjp
def low(v):
    return lax.optimization_barrier(v.astype(jnp.bfloat16)).astype(jnp.float32)

@jax.custom_vjp
def low_back(v):
    return v

def low_keep(v):
    return (low(v), None)

def low_pass(kept, grad):
    return (grad,)

def back_keep(v):
    return (v, None)

def back_low(kept, grad):
    return (low(grad),)
low.defvjp(low_keep, low_pass)
low_back.defvjp(back_keep, back_low)

def both_round(values):
    return low(low_back(values))

def matmul(left, right):
    return jnp.dot(left, right, precision=lax.Precision.HIGHEST, preferred_element_type=jnp.float32)

def layer_norm(values, norm_gain, norm_shift):
    centre = values - lax.optimization_barrier(jnp.mean(values, axis=-1, keepdims=True))
    spread = lax.optimization_barrier(jnp.mean(centre * centre, axis=-1, keepdims=True))
    return centre * lax.rsqrt(spread + 1e-05) * norm_gain + norm_shift

def gelu_tanh(values):
    return 0.5 * values * (1.0 + jnp.tanh(0.7978845608028654 * (values + 0.044715 * values * values * values)))

def forward(tokens, params):
    w_query, w_key, w_value, w_out, w_up, w_down, b_query, b_value, b_out, b_up, b_down, gain_one, shift_one, gain_two, shift_two = params
    length = tokens.shape[0]
    query_scale = DH ** (-0.5)
    normed = low(layer_norm(tokens, gain_one, shift_one))
    queries = both_round((matmul(normed, w_query) + b_query) * query_scale).reshape(length, HEADS, DH)
    key_rows = both_round(matmul(normed, w_key)).reshape(length, HEADS, DH)
    value_rows = both_round(matmul(normed, w_value) + b_value).reshape(length, HEADS, DH)
    scores = low_back(jnp.einsum('qhd,khd->hqk', queries, key_rows, precision=lax.Precision.HIGHEST))
    places = jnp.arange(length)
    allowed = places[:, None] >= places[None, :]
    scores = jnp.where(allowed[None], scores, -1e+30)
    row_max = lax.optimization_barrier(jnp.max(scores, axis=-1, keepdims=True))
    exp_scores = jnp.exp(scores - row_max)
    softmax_rows = low(exp_scores / lax.optimization_barrier(jnp.sum(exp_scores, axis=-1, keepdims=True)))
    mixed_heads = both_round(jnp.einsum('hqk,khd->qhd', softmax_rows, value_rows, precision=lax.Precision.HIGHEST).reshape(length, D))
    branch = low_back(matmul(mixed_heads, w_out) + b_out)
    residual = tokens + branch
    normed_two = low(layer_norm(residual, gain_two, shift_two))
    hidden_pre = low_back(matmul(normed_two, w_up) + b_up)
    active = low(gelu_tanh(hidden_pre))
    return residual + matmul(active, w_down) + b_down

def reference(tokens_in, out_grad, w_query, w_key, w_value, w_out, w_up, w_down, b_query, b_value, b_out, b_up, b_down, norm1_gain, norm1_shift, norm2_gain, norm2_shift):
    params = tuple((weight_arg.astype(jnp.float32) for weight_arg in (w_query, w_key, w_value, w_out, w_up, w_down, b_query, b_value, b_out, b_up, b_down, norm1_gain, norm1_shift, norm2_gain, norm2_shift)))
    zero_grads = tuple((jnp.zeros(weight_arg.shape, jnp.float32) for weight_arg in params))

    def one_sequence(totals, inputs_pair):
        tokens, cotangent = inputs_pair
        output, pullback = jax.vjp(forward, tokens.astype(jnp.float32), params)
        grad_in, grad_params = pullback(cotangent.astype(jnp.float32))
        totals = tuple((running + update for running, update in zip(totals, grad_params)))
        return (totals, (output.astype(jnp.bfloat16), grad_in))
    totals, (outputs, grads_in) = lax.scan(one_sequence, zero_grads, (tokens_in, out_grad))
    return (outputs, grads_in, totals[0], totals[1], totals[2], totals[3], totals[4], totals[5], totals[6], totals[7], totals[8], totals[9], totals[10], totals[11], totals[12], totals[13], totals[14])
```

```python
import jax
import jax.numpy as jnp
from jax import lax
from jax.sharding import Mesh
from jax.sharding import PartitionSpec as P

HEADS = 12
DH = 64
MICRO = 2


def shifted(value, axis, by):
    peers = lax.axis_size(axis)
    return lax.ppermute(value, axis, [(i, (i + by) % peers) for i in range(peers)])


def as_sent(value):
    return jax.tree.map(lambda a: a.astype(jnp.bfloat16) if a.dtype == jnp.float32 else a, value)


def layer_norm(values, norm_gain, norm_shift):
    centre = values - jnp.mean(values, axis=-1, keepdims=True)
    spread = jnp.mean(centre * centre, axis=-1, keepdims=True)
    return centre * lax.rsqrt(spread + 1e-05) * norm_gain + norm_shift


def gelu_tanh(values):
    return (
        0.5
        * values
        * (1.0 + jnp.tanh(0.7978845608028654 * (values + 0.044715 * values * values * values)))
    )


def project(left, right):
    return jnp.einsum("scd,de->sce", left, right, preferred_element_type=jnp.float32)


def project_back(left, right):
    return jnp.einsum("sce,de->scd", left, right, preferred_element_type=jnp.float32)


def weight_grad(left, right):
    return jnp.einsum("scd,sce->de", left, right, preferred_element_type=jnp.float32)


def column_sum(values):
    return jnp.sum(values.astype(jnp.float32), axis=(0, 1))


def masked_scores(query_heads, key_full, first_pos):
    seq_count, key_len = (key_full.shape[0], key_full.shape[1])
    key_heads = key_full.reshape(seq_count, key_len, HEADS, DH)
    scores = jnp.einsum(
        "sqhd,skhd->shqk", query_heads, key_heads, preferred_element_type=jnp.float32
    )
    row_pos = first_pos + jnp.arange(query_heads.shape[1], dtype=jnp.int32)
    col_pos = jnp.arange(key_len, dtype=jnp.int32)
    allowed = row_pos[:, None] >= col_pos[None, :]
    return (jnp.where(allowed, scores, -1e30), key_heads)


def micro_step(tokens, cotangent, shards, forward_weights):
    (
        w_query,
        w_key,
        w_value,
        w_out,
        w_up,
        w_down,
        b_query,
        b_value,
        b_out,
        b_up,
        b_down,
        gain_one,
        shift_one,
        gain_two,
        shift_two,
    ) = forward_weights
    seq_count, block_rows, width = tokens.shape
    query_scale = DH ** (-0.5)
    first_pos = lax.axis_index("ctx") * block_rows
    gain_one32, shift_one32 = (gain_one.astype(jnp.float32), shift_one.astype(jnp.float32))
    gain_two32, shift_two32 = (gain_two.astype(jnp.float32), shift_two.astype(jnp.float32))
    tokens32 = tokens.astype(jnp.float32)
    normed = layer_norm(tokens32, gain_one32, shift_one32).astype(jnp.bfloat16)
    queries = ((project(normed, w_query) + b_query.astype(jnp.float32)) * query_scale).astype(
        jnp.bfloat16
    )
    keys_local = project(normed, w_key).astype(jnp.bfloat16)
    values_local = (project(normed, w_value) + b_value.astype(jnp.float32)).astype(jnp.bfloat16)
    key_full, value_full = (
        lax.all_gather(keys_local, "ctx", axis=1, tiled=True),
        lax.all_gather(values_local, "ctx", axis=1, tiled=True),
    )
    query_heads = queries.reshape(seq_count, block_rows, HEADS, DH)
    scores, key_heads = masked_scores(query_heads, key_full, first_pos)
    row_max = jnp.max(scores, axis=-1, keepdims=True)
    exp_scores = jnp.exp(scores - row_max)
    row_total = jnp.sum(exp_scores, axis=-1, keepdims=True)
    probs_low = (exp_scores / row_total).astype(jnp.bfloat16)
    value_heads = value_full.reshape(seq_count, value_full.shape[1], HEADS, DH)
    mixed_heads = jnp.einsum(
        "shqk,skhd->sqhd", probs_low, value_heads, preferred_element_type=jnp.float32
    ).reshape(seq_count, block_rows, width)
    mixed_heads = mixed_heads.astype(jnp.bfloat16)
    residual = tokens32 + project(mixed_heads, w_out) + b_out.astype(jnp.float32)
    normed_two = layer_norm(residual, gain_two32, shift_two32).astype(jnp.bfloat16)
    hidden_pre = project(normed_two, w_up) + b_up.astype(jnp.float32)
    active = gelu_tanh(hidden_pre).astype(jnp.bfloat16)
    output = (residual + project(active, w_down) + b_down.astype(jnp.float32)).astype(jnp.bfloat16)
    back_weights = (
        lax.all_gather(shards[0], ("dp", "ctx"), axis=0, tiled=True),
        lax.all_gather(shards[1], ("dp", "ctx"), axis=0, tiled=True),
        lax.all_gather(shards[2], ("dp", "ctx"), axis=0, tiled=True),
        lax.all_gather(shards[3], ("dp", "ctx"), axis=0, tiled=True),
        lax.all_gather(shards[4], ("dp", "ctx"), axis=0, tiled=True),
        lax.all_gather(shards[5], ("dp", "ctx"), axis=0, tiled=True),
        lax.all_gather(shards[6], ("dp", "ctx"), axis=0, tiled=True),
        lax.all_gather(shards[7], ("dp", "ctx"), axis=0, tiled=True),
        lax.all_gather(shards[8], ("dp", "ctx"), axis=0, tiled=True),
        lax.all_gather(shards[9], ("dp", "ctx"), axis=0, tiled=True),
        lax.all_gather(shards[10], ("dp", "ctx"), axis=0, tiled=True),
        lax.all_gather(shards[11], ("dp", "ctx"), axis=0, tiled=True),
        lax.all_gather(shards[12], ("dp", "ctx"), axis=0, tiled=True),
        lax.all_gather(shards[13], ("dp", "ctx"), axis=0, tiled=True),
        lax.all_gather(shards[14], ("dp", "ctx"), axis=0, tiled=True),
    )
    w_query, w_key, w_value, w_out, w_up, w_down = back_weights[:6]
    grad_active = project_back(cotangent, w_down)
    _, gelu_pull = jax.vjp(gelu_tanh, hidden_pre)
    grad_pre = gelu_pull(grad_active)[0].astype(jnp.bfloat16)
    grad_normed_two = project_back(grad_pre, w_up)
    _, norm_pull_two = jax.vjp(layer_norm, residual, gain_two32, shift_two32)
    grad_res_part, grad_gain_two, grad_shift_two = norm_pull_two(grad_normed_two)
    grad_residual = cotangent.astype(jnp.float32) + grad_res_part
    grad_branch = grad_residual.astype(jnp.bfloat16)
    grad_mixed = project_back(grad_branch, w_out).astype(jnp.bfloat16)
    key_full, value_full = (
        lax.all_gather(keys_local, "ctx", axis=1, tiled=True),
        lax.all_gather(values_local, "ctx", axis=1, tiled=True),
    )
    value_heads = value_full.reshape(seq_count, value_full.shape[1], HEADS, DH)
    scores, key_heads = masked_scores(query_heads, key_full, first_pos)
    probs = jnp.exp(scores - row_max) / row_total
    probs_low = probs.astype(jnp.bfloat16)
    grad_heads = grad_mixed.reshape(seq_count, block_rows, HEADS, DH)
    grad_probs = jnp.einsum(
        "sqhd,skhd->shqk", grad_heads, value_heads, preferred_element_type=jnp.float32
    )
    inner_rows = jnp.sum(probs * grad_probs, axis=-1, keepdims=True)
    grad_scores = (probs * (grad_probs - inner_rows)).astype(jnp.bfloat16)
    grad_queries = jnp.einsum(
        "shqk,skhd->sqhd", grad_scores, key_heads, preferred_element_type=jnp.float32
    )
    grad_queries = grad_queries.reshape(seq_count, block_rows, width).astype(jnp.bfloat16)
    query_grad = grad_queries * query_scale

    def key_terms(first_row, row_count):
        score_part = lax.dynamic_slice_in_dim(grad_scores, first_row, row_count, 3)
        prob_part = lax.dynamic_slice_in_dim(probs_low, first_row, row_count, 3)
        key_part = jnp.einsum(
            "shqk,sqhd->kshd", score_part, query_heads, preferred_element_type=jnp.float32
        )
        value_part = jnp.einsum(
            "shqk,sqhd->kshd", prob_part, grad_heads, preferred_element_type=jnp.float32
        )
        return jnp.concatenate(
            (
                key_part.reshape(row_count, seq_count, width),
                value_part.reshape(row_count, seq_count, width),
            ),
            axis=2,
        )

    cycle_size = lax.axis_size("ctx")
    own_index = lax.axis_index("ctx")

    def carry_step(step, carried):
        holder = (own_index - step) % cycle_size
        carried = carried + key_terms(holder * block_rows, block_rows)
        return shifted(carried.astype(jnp.bfloat16), "ctx", 1).astype(carried.dtype)

    start_sums = jnp.zeros((block_rows, seq_count, 2 * width), jnp.float32)
    key_sums = lax.fori_loop(0, cycle_size, carry_step, start_sums)
    key_sums = jnp.transpose(key_sums, (1, 0, 2))
    grad_keys = key_sums[:, :, :width].astype(jnp.bfloat16)
    grad_values = key_sums[:, :, width:].astype(jnp.bfloat16)
    grad_normed = (
        project_back(query_grad, w_query)
        + project_back(grad_keys, w_key)
        + project_back(grad_values, w_value)
    )
    _, norm_pull_one = jax.vjp(layer_norm, tokens32, gain_one32, shift_one32)
    grad_tok_part, grad_gain_one, grad_shift_one = norm_pull_one(grad_normed)
    grad_tokens = grad_residual + grad_tok_part
    small_grads = (grad_gain_one, grad_shift_one, grad_gain_two, grad_shift_two)
    operands = (
        normed,
        query_grad,
        grad_keys,
        grad_values,
        mixed_heads,
        grad_branch,
        normed_two,
        grad_pre,
        active,
        cotangent,
    )
    return (output, grad_tokens, small_grads, operands)


def owner_sum(grads):
    dp_count = lax.axis_size("dp")
    ctx_count = lax.axis_size("ctx")
    blocks = tuple((grad_part.reshape(dp_count, ctx_count, -1) for grad_part in grads))
    first_section = jax.tree.map(
        lambda part, own: part.astype(own.dtype),
        lax.all_to_all(as_sent(blocks), "ctx", split_axis=1, concat_axis=1, tiled=True),
        blocks,
    )
    partial_sums = tuple((jnp.sum(piece, axis=1, keepdims=True) for piece in first_section))
    second_section = jax.tree.map(
        lambda part, own: part.astype(own.dtype),
        lax.all_to_all(as_sent(partial_sums), "dp", split_axis=0, concat_axis=0, tiled=True),
        partial_sums,
    )
    owned = []
    for grad_part, piece in zip(grads, second_section):
        summed = jnp.sum(piece, axis=(0, 1))
        row_count = grad_part.shape[0] // (dp_count * ctx_count)
        owned.append(summed.reshape((row_count,) + grad_part.shape[1:]))
    return owned


def on_device(
    tokens_in,
    out_grad,
    w_query,
    w_key,
    w_value,
    w_out,
    w_up,
    w_down,
    b_query,
    b_value,
    b_out,
    b_up,
    b_down,
    norm1_gain,
    norm1_shift,
    norm2_gain,
    norm2_shift,
):
    shards = (
        w_query,
        w_key,
        w_value,
        w_out,
        w_up,
        w_down,
        b_query,
        b_value,
        b_out,
        b_up,
        b_down,
        norm1_gain,
        norm1_shift,
        norm2_gain,
        norm2_shift,
    )
    per_micro = tokens_in.shape[0] // MICRO
    outputs = []
    grads_in = []
    operand_lists = []
    small_total = None
    for micro_index in range(MICRO):
        lower = micro_index * per_micro
        tokens = tokens_in[lower : lower + per_micro]
        cotangent = out_grad[lower : lower + per_micro]
        forward_weights = (
            lax.all_gather(shards[0], ("dp", "ctx"), axis=0, tiled=True),
            lax.all_gather(shards[1], ("dp", "ctx"), axis=0, tiled=True),
            lax.all_gather(shards[2], ("dp", "ctx"), axis=0, tiled=True),
            lax.all_gather(shards[3], ("dp", "ctx"), axis=0, tiled=True),
            lax.all_gather(shards[4], ("dp", "ctx"), axis=0, tiled=True),
            lax.all_gather(shards[5], ("dp", "ctx"), axis=0, tiled=True),
            lax.all_gather(shards[6], ("dp", "ctx"), axis=0, tiled=True),
            lax.all_gather(shards[7], ("dp", "ctx"), axis=0, tiled=True),
            lax.all_gather(shards[8], ("dp", "ctx"), axis=0, tiled=True),
            lax.all_gather(shards[9], ("dp", "ctx"), axis=0, tiled=True),
            lax.all_gather(shards[10], ("dp", "ctx"), axis=0, tiled=True),
            lax.all_gather(shards[11], ("dp", "ctx"), axis=0, tiled=True),
            lax.all_gather(shards[12], ("dp", "ctx"), axis=0, tiled=True),
            lax.all_gather(shards[13], ("dp", "ctx"), axis=0, tiled=True),
            lax.all_gather(shards[14], ("dp", "ctx"), axis=0, tiled=True),
        )
        output, grad_tokens, small_grads, operands = micro_step(
            tokens, cotangent, shards, forward_weights
        )
        outputs.append(output)
        grads_in.append(grad_tokens)
        operand_lists.append(operands)
        if small_total is None:
            small_total = small_grads
        else:
            small_total = tuple(
                (total_grad + update for total_grad, update in zip(small_total, small_grads))
            )
    joined = tuple(
        (jnp.concatenate([entry[index] for entry in operand_lists], axis=0) for index in range(10))
    )
    (
        normed,
        query_grad,
        grad_keys,
        grad_values,
        mixed_heads,
        grad_branch,
        normed_two,
        grad_pre,
        active,
        cotangent,
    ) = joined
    grads = (
        weight_grad(normed, query_grad),
        weight_grad(normed, grad_keys),
        weight_grad(normed, grad_values),
        weight_grad(mixed_heads, grad_branch),
        weight_grad(normed_two, grad_pre),
        weight_grad(active, cotangent),
        column_sum(query_grad),
        column_sum(grad_values),
        column_sum(grad_branch),
        column_sum(grad_pre),
        column_sum(cotangent),
        small_total[0],
        small_total[1],
        small_total[2],
        small_total[3],
    )
    owned = owner_sum(grads)
    layer_out = jnp.concatenate(outputs, axis=0)
    grad_tokens_all = jnp.concatenate(grads_in, axis=0)
    return (
        layer_out,
        grad_tokens_all,
        owned[0],
        owned[1],
        owned[2],
        owned[3],
        owned[4],
        owned[5],
        owned[6],
        owned[7],
        owned[8],
        owned[9],
        owned[10],
        owned[11],
        owned[12],
        owned[13],
        owned[14],
    )


BF = jnp.bfloat16
F32 = jnp.float32
SMALL = 8


def other_core(value):
    return lax.ppermute(value, "core", [(0, 1), (1, 0)])


def other_x(value):
    return lax.ppermute(value, "x", [(0, 1), (1, 0)])


def other_y(value):
    return lax.ppermute(value, "y", [(0, 1), (1, 0)])


def other_z(value, by):
    return lax.ppermute(value, "z", [(i, i ^ by) for i in range(lax.axis_size("z"))])


def pair(bit, own, received):
    return jnp.stack((jnp.where(bit == 0, own, received), jnp.where(bit == 0, received, own)))


def pick(value, index, axis):
    return lax.dynamic_index_in_dim(value, index, axis, keepdims=False)


def in_order(index, pieces):
    level = list(pieces)
    bit = 0
    ordered = [p[None] for p in level]
    while len(ordered) > 1:
        flag = (index >> bit) & 1
        ordered = [
            jnp.concatenate(
                (jnp.where(flag == 0, a, b), jnp.where(flag == 0, b, a)), axis=0
            )
            for a, b in zip(ordered[::2], ordered[1::2])
        ]
        bit += 1
    return ordered[0]


def gather_chips(unit, z, x, y):
    z_count = lax.axis_size("z")
    along_z = in_order(z, [unit] + [other_z(unit, k) for k in range(1, z_count)])
    half = z_count // 2
    first, second = along_z[:half], along_z[half:]
    first = pair(x, first, other_x(first))
    second = pair(y, second, other_y(second))
    first = pair(y, first, other_y(first))
    second = pair(x, second, other_x(second))
    return jnp.concatenate((jnp.moveaxis(first, 2, 0).swapaxes(1, 2), jnp.moveaxis(second, 2, 0)))


def reduce_chips(parts, z, x, y, y_first):
    if y_first:
        kept = pick(parts, y, 2).astype(F32) + other_y(pick(parts, 1 - y, 2).astype(BF)).astype(F32)
        kept = pick(kept, x, 1) + other_x(pick(kept, 1 - x, 1).astype(BF)).astype(F32)
    else:
        kept = pick(parts, x, 1).astype(F32) + other_x(pick(parts, 1 - x, 1).astype(BF)).astype(F32)
        kept = pick(kept, y, 1) + other_y(pick(kept, 1 - y, 1).astype(BF)).astype(F32)
    total = pick(kept, z, 0)
    for k in range(1, lax.axis_size("z")):
        total = total + other_z(pick(kept, z ^ k, 0).astype(BF), k).astype(F32)
    return total


def mm(left, right, dims):
    return lax.dot_general(left, right, (dims, ((), ())), preferred_element_type=F32)


def norm_stats(values):
    centre = values - jnp.mean(values, axis=-1, keepdims=True)
    spread = jnp.mean(centre * centre, axis=-1, keepdims=True)
    rate = lax.rsqrt(spread + 1e-05)
    return centre * rate, rate


def norm_back(unit, rate, gain, grad):
    scaled = grad * gain
    return rate * (
        scaled
        - jnp.mean(scaled, axis=-1, keepdims=True)
        - unit * jnp.mean(scaled * unit, axis=-1, keepdims=True)
    )


def attend(queries, keys, values):
    length, width = queries.shape
    heads = width // DH
    q, k, v = (a.reshape(length, heads, DH) for a in (queries, keys, values))
    scores = jnp.einsum("qhd,khd->hqk", q, k, preferred_element_type=F32)
    allowed = jnp.arange(length)[:, None] >= jnp.arange(length)[None, :]
    scores = jnp.where(allowed, scores, -1e30)
    row_max = jnp.max(scores, axis=-1, keepdims=True)
    exp_scores = jnp.exp(scores - row_max)
    row_total = jnp.sum(exp_scores, axis=-1, keepdims=True)
    probs_low = (exp_scores / row_total).astype(BF)
    mixed = jnp.einsum("hqk,khd->qhd", probs_low, v, preferred_element_type=F32)
    return mixed.reshape(length, width).astype(BF), (row_max, row_total)


def attend_back(queries, keys, values, kept, grad_mixed):
    length, width = queries.shape
    heads = width // DH
    row_max, row_total = kept
    q, k, v, g = (a.reshape(length, heads, DH) for a in (queries, keys, values, grad_mixed))
    scores = jnp.einsum("qhd,khd->hqk", q, k, preferred_element_type=F32)
    allowed = jnp.arange(length)[:, None] >= jnp.arange(length)[None, :]
    scores = jnp.where(allowed, scores, -1e30)
    probs = jnp.exp(scores - row_max) / row_total
    probs_low = probs.astype(BF)
    grad_probs = jnp.einsum("qhd,khd->hqk", g, v, preferred_element_type=F32)
    inner = jnp.sum(probs * grad_probs, axis=-1, keepdims=True)
    grad_scores = (probs * (grad_probs - inner)).astype(BF)
    grad_q = jnp.einsum("hqk,khd->qhd", grad_scores, k, preferred_element_type=F32)
    grad_k = jnp.einsum("hqk,qhd->khd", grad_scores, q, preferred_element_type=F32)
    grad_v = jnp.einsum("hqk,qhd->khd", probs_low, g, preferred_element_type=F32)
    return tuple(a.reshape(length, width).astype(BF) for a in (grad_q, grad_k, grad_v))


def chip_step(
    tokens_in,
    out_grad,
    w_query,
    w_key,
    w_value,
    w_out,
    w_up,
    w_down,
    b_query,
    b_value,
    b_out,
    b_up,
    b_down,
    norm1_gain,
    norm1_shift,
    norm2_gain,
    norm2_shift,
):
    z, x, y, core = (lax.axis_index(name) for name in ("z", "x", "y", "core"))
    z_count = lax.axis_size("z")
    chips = z_count * 4
    half_chips = chips // 2
    _, block, width = tokens_in.shape
    half = width // 2
    rows = w_query.shape[0]
    hidden_rows = w_down.shape[0]
    hidden = hidden_rows * chips
    query_scale = DH ** (-0.5)

    def own_positions(value):
        return pair(y, pick(value, y, 0), other_y(pick(value, 1 - y, 0)))

    def whole(mine):
        return pair(core, mine, other_core(mine)).swapaxes(0, 1).reshape(4 * block, -1)

    def own_rows(value, which):
        return pick(value.reshape(2, 2, block, -1), which, 1)

    def chip_sum(partial):
        return own_rows(partial, core) + other_core(own_rows(partial, 1 - core).astype(BF)).astype(F32)

    three = jnp.stack((w_query, w_key, w_value)).reshape(3, rows, 2, half)
    vectors = (
        b_query, b_value, b_out, b_down, norm1_gain, norm1_shift, norm2_gain, norm2_shift, b_up
    )
    small = jnp.concatenate(vectors)
    small_rows = jnp.zeros((SMALL, half), BF).at[0, : small.shape[0]].set(small)
    unit = pair(
        core,
        jnp.concatenate((pick(three, core, 2).reshape(3 * rows, half), small_rows)),
        other_core(
            jnp.concatenate((pick(three, 1 - core, 2).reshape(3 * rows, half), small_rows))
        ),
    )
    up_parts = w_up.reshape(rows, chips, 2, hidden_rows)
    up_unit = pair(
        core,
        pick(up_parts, core, 2).reshape(rows, hidden),
        other_core(pick(up_parts, 1 - core, 2).reshape(rows, hidden)),
    )
    late = jnp.concatenate(
        (up_unit.reshape(-1, width), w_down.reshape(-1, width), w_out.reshape(-1, width))
    )
    late = lax.all_gather(late, ("z", "x", "y"), axis=0, tiled=False)
    mine = own_positions(tokens_in)
    tokens = whole(mine).astype(F32)
    mine32 = mine.astype(F32)
    first = gather_chips(unit, z, x, y)
    up_size = 2 * rows * hidden // width
    up_c = late[:, :up_size].reshape(width, hidden)
    down_c = late[:, up_size : up_size + hidden_rows].reshape(hidden, width)
    out_parts = late[:, up_size + hidden_rows :].reshape(2, half_chips, rows, width)
    out_c = (
        pair(core, pick(out_parts, core, 0), other_core(pick(out_parts, 1 - core, 0)))
        .swapaxes(0, 1)
        .reshape(half, width)
    )
    three_c = first[..., : 3 * rows, :].reshape(chips * 2, 3, rows, half)
    query_c, key_c, value_c = (three_c[:, i].reshape(width, half) for i in range(3))
    small_all = first[..., 3 * rows, : small.shape[0]].reshape(chips * 2, -1)

    def vector(i):
        return small_all[:, i * rows : (i + 1) * rows].reshape(width).astype(F32)

    def core_half(value):
        return pick(value.reshape(2, half), core, 0)

    bias_q, bias_v, bias_o, bias_d, gain1, shift1, gain2, shift2 = (vector(i) for i in range(8))
    bias_u = pick(small_all[:, 8 * rows :].reshape(chips, 2, hidden_rows), core, 1)
    bias_u = bias_u.reshape(hidden).astype(F32)

    unit1, _ = norm_stats(tokens)
    normed = (unit1 * gain1 + shift1).astype(BF)
    rightwards = ((1,), (0,))
    queries = ((mm(normed, query_c, rightwards) + core_half(bias_q)) * query_scale).astype(BF)
    keys = mm(normed, key_c, rightwards).astype(BF)
    values = (mm(normed, value_c, rightwards) + core_half(bias_v)).astype(BF)
    mixed, kept = attend(queries, keys, values)
    grad_mine = own_positions(out_grad)
    grad_whole = whole(grad_mine)
    residual = mine32 + chip_sum(mm(mixed, out_c, rightwards)) + bias_o
    unit2, rate2 = norm_stats(residual)
    normed2 = whole((unit2 * gain2 + shift2).astype(BF))
    hidden_pre = mm(normed2, up_c, rightwards) + bias_u
    active, gelu_pull = jax.vjp(gelu_tanh, hidden_pre)
    active = active.astype(BF)
    output = residual + chip_sum(mm(active, down_c, rightwards)) + bias_d
    output = output.astype(BF)
    layer_out = pair(y, pick(output, y, 0), other_y(pick(output, 1 - y, 0)))

    across = ((1,), (1,))
    over_rows = ((0,), (0,))
    grad_pre32 = gelu_pull(mm(grad_whole, down_c, across))[0]
    grad_pre = grad_pre32.astype(BF)
    grad_normed2 = chip_sum(mm(grad_pre, up_c, across))
    grad_residual = grad_mine.astype(F32) + norm_back(unit2, rate2, gain2, grad_normed2)
    branch_mine = grad_residual.astype(BF)
    branch = whole(branch_mine)
    grad_up = mm(normed2, grad_pre, over_rows)
    grad_down = mm(active, grad_whole, over_rows)
    grad_out = mm(mixed, branch, over_rows).reshape(half_chips, 2, rows, width)
    grad_out = pair(core, pick(grad_out, core, 1), other_core(pick(grad_out, 1 - core, 1).astype(BF)).astype(F32))
    by_chip = (z_count, 2, 2)
    sum_up = reduce_chips(grad_up.reshape(by_chip + (2 * rows, hidden)), z, x, y, True)
    down_out = jnp.concatenate(
        (grad_down.reshape(chips, hidden_rows, width), grad_out.reshape(chips, rows, width)), axis=1
    )
    sum_down_out = reduce_chips(down_out.reshape(by_chip + (-1, width)), z, x, y, False)
    grad_mixed = mm(branch, out_c, across).astype(BF)
    grad_q, grad_k, grad_v = attend_back(queries, keys, values, kept, grad_mixed)
    grad_qkv = jnp.concatenate((grad_q * query_scale, grad_k, grad_v), axis=1)
    weights_c = jnp.concatenate((query_c, key_c, value_c), axis=1)
    grad_three = mm(normed, grad_qkv, over_rows)
    grad_normed1 = chip_sum(mm(grad_qkv, weights_c, across))
    unit1_mine, rate1_mine = norm_stats(mine32)
    grad_tokens = grad_residual + norm_back(unit1_mine, rate1_mine, gain1, grad_normed1)
    from_y = other_y(pick(grad_tokens, 1 - y, 0).astype(BF)).astype(F32)
    grad_tokens = pair(y, pick(grad_tokens, y, 0), from_y)

    def sums(value):
        return jnp.sum(value.astype(F32), axis=tuple(range(value.ndim - 1)))

    def placed(value):
        return jnp.where(
            (jnp.arange(2) == core)[:, None], value[None], jnp.zeros((), F32)
        ).reshape(width)

    bias_sums = sums(grad_qkv)
    small_grads = [
        placed(bias_sums[:half]),
        placed(bias_sums[2 * half :]),
        sums(branch_mine),
        sums(grad_mine),
        sums(grad_normed1 * unit1_mine),
        sums(grad_normed1),
        sums(grad_normed2 * unit2),
        sums(grad_normed2),
    ]
    small_grads = [g.reshape(chips, 2, rows) for g in small_grads]
    up_sums = sums(grad_pre).reshape(chips, 1, hidden_rows)
    small_grads.append(
        jnp.where((jnp.arange(2) == core)[None, :, None], up_sums, jnp.zeros((), F32))
    )
    small_grads = jnp.concatenate(small_grads, axis=2).reshape(chips, 1, -1)
    last = grad_three.reshape(chips, 2 * rows, 3 * half)
    last = jnp.concatenate(
        (last, jnp.pad(small_grads, ((0, 0), (0, SMALL - 1), (0, 3 * half - small_grads.shape[2])))), axis=1
    )
    last_a = reduce_chips(last[:, :, : 3 * half // 2].reshape(by_chip + (-1, 3 * half // 2)), z, x, y, True)
    last_b = reduce_chips(last[:, :, 3 * half // 2 :].reshape(by_chip + (-1, 3 * half // 2)), z, x, y, False)
    last = jnp.concatenate((last_a, last_b), axis=1)
    small_mine = last[2 * rows, : 2 * small.shape[0]].reshape(2, -1)
    small_sum = pick(small_mine, core, 0) + other_core(pick(small_mine, 1 - core, 0))
    three_mine = last[: 2 * rows].reshape(2, rows, 3 * half)
    up_mine = sum_up.reshape(2, rows, hidden)
    to_core = jnp.concatenate((pick(three_mine, 1 - core, 0), pick(up_mine, 1 - core, 0)), axis=1)
    to_core = other_core(to_core)
    three_out = pair(core, pick(three_mine, core, 0), to_core[:, : 3 * half])
    three_out = three_out.reshape(2, rows, 3, half)
    up_out = pair(core, pick(up_mine, core, 0), to_core[:, 3 * half :])
    up_out = up_out.reshape(2, rows, chips, hidden_rows)
    up_out = jnp.moveaxis(up_out, 0, 2).reshape(rows, 2 * hidden)
    three_out = jnp.moveaxis(three_out, 0, 2)
    g_q, g_k, g_v = (three_out[:, i].reshape(rows, width) for i in range(3))
    g_small = [small_sum[i * rows : (i + 1) * rows] for i in range(8)]
    return (
        layer_out,
        grad_tokens,
        g_q,
        g_k,
        g_v,
        sum_down_out[hidden_rows:],
        up_out,
        sum_down_out[:hidden_rows],
        g_small[0],
        g_small[1],
        g_small[2],
        small_sum[8 * rows :],
        g_small[3],
        g_small[4],
        g_small[5],
        g_small[6],
        g_small[7],
    )


def solution(mesh):
    dp_count, ctx_count = mesh.shape["dp"], mesh.shape["ctx"]

    def run(*args):
        per_dp = args[0].shape[0] // dp_count
        if ctx_count == 4 and per_dp == 2 and dp_count == 8:
            devices = mesh.devices.reshape(dp_count // 2, 2, ctx_count // 2, 2)
            used = Mesh(devices, ("z", "x", "y", "core"))
            body, dp, ctx = chip_step, ("z", "x"), ("y", "core")
        else:
            used, body, dp, ctx = mesh, on_device, ("dp",), ("ctx",)
        tokens, matrix, bias = P(dp, ctx, None), P(dp + ctx, None), P(dp + ctx)
        return jax.shard_map(
            body,
            mesh=used,
            in_specs=(tokens,) * 2 + (matrix,) * 6 + (bias,) * 9,
            out_specs=(tokens,) * 2 + (matrix,) * 6 + (bias,) * 9,
            check_vma=False,
        )(*args)

    return run
```

```python
import jax
import jax.numpy as jnp
from jax import lax
from jax.experimental import pallas as pl
from jax.experimental.pallas import tpu as pltpu
from jax.sharding import Mesh
from jax.sharding import PartitionSpec as P

HEADS = 12
DH = 64
MICRO = 2


def shifted(value, axis, by):
    peers = lax.axis_size(axis)
    return lax.ppermute(value, axis, [(i, (i + by) % peers) for i in range(peers)])


def as_sent(value):
    return jax.tree.map(lambda a: a.astype(jnp.bfloat16) if a.dtype == jnp.float32 else a, value)


def layer_norm(values, norm_gain, norm_shift):
    centre = values - jnp.mean(values, axis=-1, keepdims=True)
    spread = jnp.mean(centre * centre, axis=-1, keepdims=True)
    return centre * lax.rsqrt(spread + 1e-05) * norm_gain + norm_shift


def gelu_tanh(values):
    return (
        0.5
        * values
        * (1.0 + jnp.tanh(0.7978845608028654 * (values + 0.044715 * values * values * values)))
    )


def project(left, right):
    return jnp.einsum("scd,de->sce", left, right, preferred_element_type=jnp.float32)


def project_back(left, right):
    return jnp.einsum("sce,de->scd", left, right, preferred_element_type=jnp.float32)


def weight_grad(left, right):
    return jnp.einsum("scd,sce->de", left, right, preferred_element_type=jnp.float32)


def column_sum(values):
    return jnp.sum(values.astype(jnp.float32), axis=(0, 1))


def masked_scores(query_heads, key_full, first_pos):
    seq_count, key_len = (key_full.shape[0], key_full.shape[1])
    key_heads = key_full.reshape(seq_count, key_len, HEADS, DH)
    scores = jnp.einsum(
        "sqhd,skhd->shqk", query_heads, key_heads, preferred_element_type=jnp.float32
    )
    row_pos = first_pos + jnp.arange(query_heads.shape[1], dtype=jnp.int32)
    col_pos = jnp.arange(key_len, dtype=jnp.int32)
    allowed = row_pos[:, None] >= col_pos[None, :]
    return (jnp.where(allowed, scores, -1e30), key_heads)


def micro_step(tokens, cotangent, shards, forward_weights):
    (
        w_query,
        w_key,
        w_value,
        w_out,
        w_up,
        w_down,
        b_query,
        b_value,
        b_out,
        b_up,
        b_down,
        gain_one,
        shift_one,
        gain_two,
        shift_two,
    ) = forward_weights
    seq_count, block_rows, width = tokens.shape
    query_scale = DH ** (-0.5)
    first_pos = lax.axis_index("ctx") * block_rows
    gain_one32, shift_one32 = (gain_one.astype(jnp.float32), shift_one.astype(jnp.float32))
    gain_two32, shift_two32 = (gain_two.astype(jnp.float32), shift_two.astype(jnp.float32))
    tokens32 = tokens.astype(jnp.float32)
    normed = layer_norm(tokens32, gain_one32, shift_one32).astype(jnp.bfloat16)
    queries = ((project(normed, w_query) + b_query.astype(jnp.float32)) * query_scale).astype(
        jnp.bfloat16
    )
    keys_local = project(normed, w_key).astype(jnp.bfloat16)
    values_local = (project(normed, w_value) + b_value.astype(jnp.float32)).astype(jnp.bfloat16)
    key_full, value_full = (
        lax.all_gather(keys_local, "ctx", axis=1, tiled=True),
        lax.all_gather(values_local, "ctx", axis=1, tiled=True),
    )
    query_heads = queries.reshape(seq_count, block_rows, HEADS, DH)
    scores, key_heads = masked_scores(query_heads, key_full, first_pos)
    row_max = jnp.max(scores, axis=-1, keepdims=True)
    exp_scores = jnp.exp(scores - row_max)
    row_total = jnp.sum(exp_scores, axis=-1, keepdims=True)
    probs_low = (exp_scores / row_total).astype(jnp.bfloat16)
    value_heads = value_full.reshape(seq_count, value_full.shape[1], HEADS, DH)
    mixed_heads = jnp.einsum(
        "shqk,skhd->sqhd", probs_low, value_heads, preferred_element_type=jnp.float32
    ).reshape(seq_count, block_rows, width)
    mixed_heads = mixed_heads.astype(jnp.bfloat16)
    residual = tokens32 + project(mixed_heads, w_out) + b_out.astype(jnp.float32)
    normed_two = layer_norm(residual, gain_two32, shift_two32).astype(jnp.bfloat16)
    hidden_pre = project(normed_two, w_up) + b_up.astype(jnp.float32)
    active = gelu_tanh(hidden_pre).astype(jnp.bfloat16)
    output = (residual + project(active, w_down) + b_down.astype(jnp.float32)).astype(jnp.bfloat16)
    back_weights = (
        lax.all_gather(shards[0], ("dp", "ctx"), axis=0, tiled=True),
        lax.all_gather(shards[1], ("dp", "ctx"), axis=0, tiled=True),
        lax.all_gather(shards[2], ("dp", "ctx"), axis=0, tiled=True),
        lax.all_gather(shards[3], ("dp", "ctx"), axis=0, tiled=True),
        lax.all_gather(shards[4], ("dp", "ctx"), axis=0, tiled=True),
        lax.all_gather(shards[5], ("dp", "ctx"), axis=0, tiled=True),
        lax.all_gather(shards[6], ("dp", "ctx"), axis=0, tiled=True),
        lax.all_gather(shards[7], ("dp", "ctx"), axis=0, tiled=True),
        lax.all_gather(shards[8], ("dp", "ctx"), axis=0, tiled=True),
        lax.all_gather(shards[9], ("dp", "ctx"), axis=0, tiled=True),
        lax.all_gather(shards[10], ("dp", "ctx"), axis=0, tiled=True),
        lax.all_gather(shards[11], ("dp", "ctx"), axis=0, tiled=True),
        lax.all_gather(shards[12], ("dp", "ctx"), axis=0, tiled=True),
        lax.all_gather(shards[13], ("dp", "ctx"), axis=0, tiled=True),
        lax.all_gather(shards[14], ("dp", "ctx"), axis=0, tiled=True),
    )
    w_query, w_key, w_value, w_out, w_up, w_down = back_weights[:6]
    grad_active = project_back(cotangent, w_down)
    _, gelu_pull = jax.vjp(gelu_tanh, hidden_pre)
    grad_pre = gelu_pull(grad_active)[0].astype(jnp.bfloat16)
    grad_normed_two = project_back(grad_pre, w_up)
    _, norm_pull_two = jax.vjp(layer_norm, residual, gain_two32, shift_two32)
    grad_res_part, grad_gain_two, grad_shift_two = norm_pull_two(grad_normed_two)
    grad_residual = cotangent.astype(jnp.float32) + grad_res_part
    grad_branch = grad_residual.astype(jnp.bfloat16)
    grad_mixed = project_back(grad_branch, w_out).astype(jnp.bfloat16)
    key_full, value_full = (
        lax.all_gather(keys_local, "ctx", axis=1, tiled=True),
        lax.all_gather(values_local, "ctx", axis=1, tiled=True),
    )
    value_heads = value_full.reshape(seq_count, value_full.shape[1], HEADS, DH)
    scores, key_heads = masked_scores(query_heads, key_full, first_pos)
    probs = jnp.exp(scores - row_max) / row_total
    probs_low = probs.astype(jnp.bfloat16)
    grad_heads = grad_mixed.reshape(seq_count, block_rows, HEADS, DH)
    grad_probs = jnp.einsum(
        "sqhd,skhd->shqk", grad_heads, value_heads, preferred_element_type=jnp.float32
    )
    inner_rows = jnp.sum(probs * grad_probs, axis=-1, keepdims=True)
    grad_scores = (probs * (grad_probs - inner_rows)).astype(jnp.bfloat16)
    grad_queries = jnp.einsum(
        "shqk,skhd->sqhd", grad_scores, key_heads, preferred_element_type=jnp.float32
    )
    grad_queries = grad_queries.reshape(seq_count, block_rows, width).astype(jnp.bfloat16)
    query_grad = grad_queries * query_scale

    def key_terms(first_row, row_count):
        score_part = lax.dynamic_slice_in_dim(grad_scores, first_row, row_count, 3)
        prob_part = lax.dynamic_slice_in_dim(probs_low, first_row, row_count, 3)
        key_part = jnp.einsum(
            "shqk,sqhd->kshd", score_part, query_heads, preferred_element_type=jnp.float32
        )
        value_part = jnp.einsum(
            "shqk,sqhd->kshd", prob_part, grad_heads, preferred_element_type=jnp.float32
        )
        return jnp.concatenate(
            (
                key_part.reshape(row_count, seq_count, width),
                value_part.reshape(row_count, seq_count, width),
            ),
            axis=2,
        )

    cycle_size = lax.axis_size("ctx")
    own_index = lax.axis_index("ctx")

    def carry_step(step, carried):
        holder = (own_index - step) % cycle_size
        carried = carried + key_terms(holder * block_rows, block_rows)
        return shifted(carried.astype(jnp.bfloat16), "ctx", 1).astype(carried.dtype)

    start_sums = jnp.zeros((block_rows, seq_count, 2 * width), jnp.float32)
    key_sums = lax.fori_loop(0, cycle_size, carry_step, start_sums)
    key_sums = jnp.transpose(key_sums, (1, 0, 2))
    grad_keys = key_sums[:, :, :width].astype(jnp.bfloat16)
    grad_values = key_sums[:, :, width:].astype(jnp.bfloat16)
    grad_normed = (
        project_back(query_grad, w_query)
        + project_back(grad_keys, w_key)
        + project_back(grad_values, w_value)
    )
    _, norm_pull_one = jax.vjp(layer_norm, tokens32, gain_one32, shift_one32)
    grad_tok_part, grad_gain_one, grad_shift_one = norm_pull_one(grad_normed)
    grad_tokens = grad_residual + grad_tok_part
    small_grads = (grad_gain_one, grad_shift_one, grad_gain_two, grad_shift_two)
    operands = (
        normed,
        query_grad,
        grad_keys,
        grad_values,
        mixed_heads,
        grad_branch,
        normed_two,
        grad_pre,
        active,
        cotangent,
    )
    return (output, grad_tokens, small_grads, operands)


def owner_sum(grads):
    dp_count = lax.axis_size("dp")
    ctx_count = lax.axis_size("ctx")
    blocks = tuple((grad_part.reshape(dp_count, ctx_count, -1) for grad_part in grads))
    first_section = jax.tree.map(
        lambda part, own: part.astype(own.dtype),
        lax.all_to_all(as_sent(blocks), "ctx", split_axis=1, concat_axis=1, tiled=True),
        blocks,
    )
    partial_sums = tuple((jnp.sum(piece, axis=1, keepdims=True) for piece in first_section))
    second_section = jax.tree.map(
        lambda part, own: part.astype(own.dtype),
        lax.all_to_all(as_sent(partial_sums), "dp", split_axis=0, concat_axis=0, tiled=True),
        partial_sums,
    )
    owned = []
    for grad_part, piece in zip(grads, second_section):
        summed = jnp.sum(piece, axis=(0, 1))
        row_count = grad_part.shape[0] // (dp_count * ctx_count)
        owned.append(summed.reshape((row_count,) + grad_part.shape[1:]))
    return owned


def on_device(
    tokens_in,
    out_grad,
    w_query,
    w_key,
    w_value,
    w_out,
    w_up,
    w_down,
    b_query,
    b_value,
    b_out,
    b_up,
    b_down,
    norm1_gain,
    norm1_shift,
    norm2_gain,
    norm2_shift,
):
    shards = (
        w_query,
        w_key,
        w_value,
        w_out,
        w_up,
        w_down,
        b_query,
        b_value,
        b_out,
        b_up,
        b_down,
        norm1_gain,
        norm1_shift,
        norm2_gain,
        norm2_shift,
    )
    per_micro = tokens_in.shape[0] // MICRO
    outputs = []
    grads_in = []
    operand_lists = []
    small_total = None
    for micro_index in range(MICRO):
        lower = micro_index * per_micro
        tokens = tokens_in[lower : lower + per_micro]
        cotangent = out_grad[lower : lower + per_micro]
        forward_weights = (
            lax.all_gather(shards[0], ("dp", "ctx"), axis=0, tiled=True),
            lax.all_gather(shards[1], ("dp", "ctx"), axis=0, tiled=True),
            lax.all_gather(shards[2], ("dp", "ctx"), axis=0, tiled=True),
            lax.all_gather(shards[3], ("dp", "ctx"), axis=0, tiled=True),
            lax.all_gather(shards[4], ("dp", "ctx"), axis=0, tiled=True),
            lax.all_gather(shards[5], ("dp", "ctx"), axis=0, tiled=True),
            lax.all_gather(shards[6], ("dp", "ctx"), axis=0, tiled=True),
            lax.all_gather(shards[7], ("dp", "ctx"), axis=0, tiled=True),
            lax.all_gather(shards[8], ("dp", "ctx"), axis=0, tiled=True),
            lax.all_gather(shards[9], ("dp", "ctx"), axis=0, tiled=True),
            lax.all_gather(shards[10], ("dp", "ctx"), axis=0, tiled=True),
            lax.all_gather(shards[11], ("dp", "ctx"), axis=0, tiled=True),
            lax.all_gather(shards[12], ("dp", "ctx"), axis=0, tiled=True),
            lax.all_gather(shards[13], ("dp", "ctx"), axis=0, tiled=True),
            lax.all_gather(shards[14], ("dp", "ctx"), axis=0, tiled=True),
        )
        output, grad_tokens, small_grads, operands = micro_step(
            tokens, cotangent, shards, forward_weights
        )
        outputs.append(output)
        grads_in.append(grad_tokens)
        operand_lists.append(operands)
        if small_total is None:
            small_total = small_grads
        else:
            small_total = tuple(
                (total_grad + update for total_grad, update in zip(small_total, small_grads))
            )
    joined = tuple(
        (jnp.concatenate([entry[index] for entry in operand_lists], axis=0) for index in range(10))
    )
    (
        normed,
        query_grad,
        grad_keys,
        grad_values,
        mixed_heads,
        grad_branch,
        normed_two,
        grad_pre,
        active,
        cotangent,
    ) = joined
    grads = (
        weight_grad(normed, query_grad),
        weight_grad(normed, grad_keys),
        weight_grad(normed, grad_values),
        weight_grad(mixed_heads, grad_branch),
        weight_grad(normed_two, grad_pre),
        weight_grad(active, cotangent),
        column_sum(query_grad),
        column_sum(grad_values),
        column_sum(grad_branch),
        column_sum(grad_pre),
        column_sum(cotangent),
        small_total[0],
        small_total[1],
        small_total[2],
        small_total[3],
    )
    owned = owner_sum(grads)
    layer_out = jnp.concatenate(outputs, axis=0)
    grad_tokens_all = jnp.concatenate(grads_in, axis=0)
    return (
        layer_out,
        grad_tokens_all,
        owned[0],
        owned[1],
        owned[2],
        owned[3],
        owned[4],
        owned[5],
        owned[6],
        owned[7],
        owned[8],
        owned[9],
        owned[10],
        owned[11],
        owned[12],
        owned[13],
        owned[14],
    )


BF = jnp.bfloat16
F32 = jnp.float32
SMALL = 8


def other_core(value):
    return lax.ppermute(value, "core", [(0, 1), (1, 0)])


def other_x(value):
    return lax.ppermute(value, "x", [(0, 1), (1, 0)])


def other_y(value):
    return lax.ppermute(value, "y", [(0, 1), (1, 0)])


def other_z(value, by):
    return lax.ppermute(value, "z", [(i, i ^ by) for i in range(lax.axis_size("z"))])


def pair(bit, own, received):
    return jnp.stack((jnp.where(bit == 0, own, received), jnp.where(bit == 0, received, own)))


def pick(value, index, axis):
    return lax.dynamic_index_in_dim(value, index, axis, keepdims=False)


def in_order(index, pieces):
    level = list(pieces)
    bit = 0
    ordered = [p[None] for p in level]
    while len(ordered) > 1:
        flag = (index >> bit) & 1
        ordered = [
            jnp.concatenate(
                (jnp.where(flag == 0, a, b), jnp.where(flag == 0, b, a)), axis=0
            )
            for a, b in zip(ordered[::2], ordered[1::2])
        ]
        bit += 1
    return ordered[0]


def gather_chips(unit, z, x, y):
    z_count = lax.axis_size("z")
    along_z = in_order(z, [unit] + [other_z(unit, k) for k in range(1, z_count)])
    half = z_count // 2
    first, second = along_z[:half], along_z[half:]
    first = pair(x, first, other_x(first))
    second = pair(y, second, other_y(second))
    first = pair(y, first, other_y(first))
    second = pair(x, second, other_x(second))
    return jnp.concatenate((jnp.moveaxis(first, 2, 0).swapaxes(1, 2), jnp.moveaxis(second, 2, 0)))


def reduce_chips(parts, z, x, y, y_first):
    def block(bit, axis):
        return jnp.concatenate([pick(part, bit, axis) for part in parts], axis=2)

    first, other, second, other_second = (
        (y, other_y, x, other_x) if y_first else (x, other_x, y, other_y)
    )
    axis = 2 if y_first else 1
    kept = block(first, axis).astype(F32) + other(block(1 - first, axis).astype(BF)).astype(F32)
    kept = pick(kept, second, 1) + other_second(pick(kept, 1 - second, 1).astype(BF)).astype(F32)
    total = pick(kept, z, 0)
    for k in range(1, lax.axis_size("z")):
        total = total + other_z(pick(kept, z ^ k, 0).astype(BF), k).astype(F32)
    return total


def mm(left, right, dims):
    return lax.dot_general(left, right, (dims, ((), ())), preferred_element_type=F32)


def norm_stats(values):
    centre = values - jnp.mean(values, axis=-1, keepdims=True)
    spread = jnp.mean(centre * centre, axis=-1, keepdims=True)
    rate = lax.rsqrt(spread + 1e-05)
    return centre * rate, rate


def norm_back(unit, rate, gain, grad):
    scaled = grad * gain
    return rate * (
        scaled
        - jnp.mean(scaled, axis=-1, keepdims=True)
        - unit * jnp.mean(scaled * unit, axis=-1, keepdims=True)
    )


VMEM_LIMIT = 56 * 1024 * 1024
QUERY_BLOCK = 256
ROW_BLOCK = 512


def lane_masks(dtype):
    lane = lax.broadcasted_iota(jnp.int32, (1, 2 * DH), 1)
    return [(lane < DH).astype(dtype), (lane >= DH).astype(dtype)]


def visible(key_count, query_block):
    key_pos = lax.broadcasted_iota(jnp.int32, (query_block, query_block), 0)
    query_pos = lax.broadcasted_iota(jnp.int32, (query_block, query_block), 1)
    return key_pos <= query_pos


def masked_tail(scores, allowed):
    key_count, query_block = scores.shape
    tail = jnp.where(allowed, scores[key_count - query_block :], -1e30)
    if key_count == query_block:
        return tail
    return jnp.concatenate((scores[: key_count - query_block], tail), axis=0)


def nt(left, right):
    return lax.dot_general(left, right, (((1,), (1,)), ((), ())), preferred_element_type=F32)


def nn(left, right):
    return lax.dot_general(left, right, (((1,), (0,)), ((), ())), preferred_element_type=F32)


def attend_kernel(q_ref, k_ref, v_ref, mixed_ref, lse_ref):
    length = q_ref.shape[0]
    masks = lane_masks(BF)
    allowed = visible(QUERY_BLOCK, QUERY_BLOCK)
    keys = k_ref[...]
    masked_keys = [keys * m for m in masks]
    v_t = v_ref[...].T
    row = lax.broadcasted_iota(jnp.int32, (2 * DH, 1), 0)
    values_t = [jnp.where(row < DH, v_t, jnp.zeros((), BF)), jnp.where(row >= DH, v_t, jnp.zeros((), BF))]
    for start in range(0, length, QUERY_BLOCK):
        stop = start + QUERY_BLOCK
        q = q_ref[start:stop, :]
        mixed_t = None
        for head in range(2):
            scores = masked_tail(nt(masked_keys[head][:stop], q), allowed)
            top = jnp.max(scores, axis=0, keepdims=True)
            powers = jnp.exp(scores - top)
            total = jnp.sum(powers, axis=0, keepdims=True)
            low = (powers * (1.0 / total)).astype(BF)
            part = nn(values_t[head][:, :stop], low)
            mixed_t = part if mixed_t is None else mixed_t + part
            lse_ref[0, head : head + 1, start:stop] = top + jnp.log(total)
        mixed_ref[start:stop, :] = mixed_t.T.astype(BF)


def attend_back_kernel(q_ref, k_ref, v_ref, g_ref, mixed_ref, lse_ref, gq_ref, gk_ref, gv_ref, ka, va):
    length = q_ref.shape[0]
    masks = lane_masks(BF)
    allowed = visible(QUERY_BLOCK, QUERY_BLOCK)
    keys, values = k_ref[...], v_ref[...]
    masked_keys = [keys * m for m in masks]
    masked_values = [values * m for m in masks]
    keys_t = [m.T for m in masked_keys]
    for start in range(length - QUERY_BLOCK, -1, -QUERY_BLOCK):
        stop = start + QUERY_BLOCK
        q, g = q_ref[start:stop, :], g_ref[start:stop, :]
        products = (g.astype(F32) * mixed_ref[start:stop, :].astype(F32)).T
        grad_q_t = None
        grad_k = grad_v = None
        for head in range(2):
            inner = jnp.sum(products[head * DH : (head + 1) * DH], axis=0, keepdims=True)
            scores = masked_tail(nt(masked_keys[head][:stop], q), allowed)
            probs = jnp.exp(scores - lse_ref[0, head : head + 1, start:stop])
            grad_probs = nt(masked_values[head][:stop], g)
            grad_scores = (probs * (grad_probs - inner)).astype(BF)
            part_v = nn(probs.astype(BF), g * masks[head])
            part_k = nn(grad_scores, q * masks[head])
            part_q = nn(keys_t[head][:, :stop], grad_scores)
            grad_v = part_v if head == 0 else grad_v + part_v
            grad_k = part_k if head == 0 else grad_k + part_k
            grad_q_t = part_q if head == 0 else grad_q_t + part_q
        gq_ref[start:stop, :] = grad_q_t.T.astype(BF)
        if stop == length:
            ka[...] = grad_k
            va[...] = grad_v
        else:
            ka[:stop, :] += grad_k
            va[:stop, :] += grad_v
    gk_ref[...] = ka[...].astype(BF)
    gv_ref[...] = va[...].astype(BF)


def attend(queries, keys, values):
    length, width = queries.shape
    pairs = width // (2 * DH)
    block = pl.BlockSpec((length, 2 * DH), lambda i: (0, i))
    return pl.pallas_call(
        attend_kernel,
        grid=(pairs,),
        in_specs=[block] * 3,
        out_specs=[block, pl.BlockSpec((1, 2, length), lambda i: (i, 0, 0))],
        out_shape=[
            jax.ShapeDtypeStruct((length, width), BF),
            jax.ShapeDtypeStruct((pairs, 2, length), F32),
        ],
        compiler_params=pltpu.CompilerParams(vmem_limit_bytes=VMEM_LIMIT),
        cost_estimate=pl.CostEstimate(
            flops=4 * length * length * width, bytes_accessed=8 * length * width,
            transcendentals=length * length * width // DH,
        ),
        name="attend",
    )(queries, keys, values)


def attend_back(queries, keys, values, mixed, lse, grad_mixed, pair_index, pairs):
    length = queries.shape[0]
    block = pl.BlockSpec((length, 2 * DH), lambda i: (0, i + pair_index))
    out_block = pl.BlockSpec((length, 2 * DH), lambda i: (0, i))
    width = pairs * 2 * DH
    return pl.pallas_call(
        attend_back_kernel,
        grid=(pairs,),
        in_specs=[block] * 5 + [pl.BlockSpec((1, 2, length), lambda i: (i + pair_index, 0, 0))],
        out_specs=[out_block] * 3,
        out_shape=[jax.ShapeDtypeStruct((length, width), BF)] * 3,
        scratch_shapes=[pltpu.VMEM((length, 2 * DH), F32)] * 2,
        compiler_params=pltpu.CompilerParams(vmem_limit_bytes=VMEM_LIMIT),
        cost_estimate=pl.CostEstimate(
            flops=10 * length * length * width, bytes_accessed=16 * length * width,
            transcendentals=length * length * width // DH,
        ),
        name="attend_back",
    )(queries, keys, values, grad_mixed, mixed, lse)


def hidden_kernel(n_ref, g_ref, up_ref, down_ref, bias_ref, y_ref, gn_ref, gu_ref, gd_ref, gb_ref, n_t):
    step = pl.program_id(0)

    @pl.when(step == 0)
    def _():
        n_t[...] = n_ref[...].T
        y_ref[...] = jnp.zeros(y_ref.shape, F32)
        gn_ref[...] = jnp.zeros(gn_ref.shape, F32)

    up = up_ref[...].reshape(-1, up_ref.shape[2])
    down = down_ref[...].reshape(-1, down_ref.shape[2])
    length = n_ref.shape[0]
    grad_up = grad_down = bias_sum = None
    for start in range(0, length, ROW_BLOCK):
        rows = slice(start, start + ROW_BLOCK)
        n, g = n_ref[rows, :], g_ref[rows, :]
        pre = nn(n, up) + bias_ref[0]
        square = pre * pre
        bent = jnp.tanh(0.7978845608028654 * (pre + 0.044715 * square * pre))
        half = 0.5 * (1.0 + bent)
        active = (pre * half).astype(BF)
        slope = half + 0.5 * pre * (1.0 - bent * bent) * (
            0.7978845608028654 * (1.0 + 3 * 0.044715 * square)
        )
        grad_pre32 = nt(g, down) * slope
        grad_pre = grad_pre32.astype(BF)
        y_ref[rows, :] += nn(active, down)
        gn_ref[rows, :] += nt(grad_pre, up)
        part_up = nn(n_t[:, rows], grad_pre)
        part_down = lax.dot_general(active, g, (((0,), (0,)), ((), ())), preferred_element_type=F32)
        part_bias = jnp.sum(grad_pre.astype(F32), axis=0, keepdims=True)
        grad_up = part_up if start == 0 else grad_up + part_up
        grad_down = part_down if start == 0 else grad_down + part_down
        bias_sum = part_bias if start == 0 else bias_sum + part_bias
    gu_ref[...] = grad_up.astype(BF).reshape(gu_ref.shape)
    gd_ref[...] = grad_down.astype(BF).reshape(gd_ref.shape)
    gb_ref[0] = bias_sum


def feed_forward(normed, grad_out, late, bias, hidden_rows):
    length, width = normed.shape
    chips = late.shape[0]
    steps = 4
    tile = chips * hidden_rows // steps
    up_rows = width // chips
    per_half = steps // 2
    down_chips = chips // steps
    full = pl.BlockSpec((length, width), lambda i: (0, 0))
    hidden = tile * steps
    return pl.pallas_call(
        hidden_kernel,
        grid=(steps,),
        in_specs=[
            full,
            full,
            pl.BlockSpec((chips, up_rows, tile), lambda i: (0, i // per_half, i % per_half)),
            pl.BlockSpec((down_chips, hidden_rows, width), lambda i: (i, 1, 0)),
            pl.BlockSpec((1, 1, tile), lambda i: (i, 0, 0)),
        ],
        out_specs=[
            full,
            full,
            pl.BlockSpec((chips, up_rows, tile), lambda i: (0, 0, i)),
            pl.BlockSpec((down_chips, hidden_rows, width), lambda i: (i, 0, 0)),
            pl.BlockSpec((1, 1, tile), lambda i: (i, 0, 0)),
        ],
        out_shape=[
            jax.ShapeDtypeStruct((length, width), F32),
            jax.ShapeDtypeStruct((length, width), F32),
            jax.ShapeDtypeStruct((chips, up_rows, hidden), BF),
            jax.ShapeDtypeStruct((chips, hidden_rows, width), BF),
            jax.ShapeDtypeStruct((steps, 1, tile), F32),
        ],
        scratch_shapes=[pltpu.VMEM((width, length), BF)],
        compiler_params=pltpu.CompilerParams(vmem_limit_bytes=VMEM_LIMIT),
        cost_estimate=pl.CostEstimate(
            flops=12 * length * width * hidden, bytes_accessed=24 * length * width,
            transcendentals=length * hidden,
        ),
        name="feed_forward",
    )(normed, grad_out, late, late, bias.reshape(steps, 1, tile))


def chip_step(
    tokens_in,
    out_grad,
    w_query,
    w_key,
    w_value,
    w_out,
    w_up,
    w_down,
    b_query,
    b_value,
    b_out,
    b_up,
    b_down,
    norm1_gain,
    norm1_shift,
    norm2_gain,
    norm2_shift,
):
    z, x, y, core = (lax.axis_index(name) for name in ("z", "x", "y", "core"))
    z_count = lax.axis_size("z")
    chips = z_count * 4
    half_chips = chips // 2
    _, block, width = tokens_in.shape
    half = width // 2
    rows = w_query.shape[0]
    hidden_rows = w_down.shape[0]
    hidden = hidden_rows * chips
    query_scale = DH ** (-0.5)

    def own_positions(value):
        return pair(y, pick(value, y, 0), other_y(pick(value, 1 - y, 0)))

    def whole(mine):
        return pair(core, mine, other_core(mine)).swapaxes(0, 1).reshape(4 * block, -1)

    def own_rows(value, which):
        return pick(value.reshape(2, 2, block, -1), which, 1)

    def chip_sum(partial):
        return own_rows(partial, core) + other_core(own_rows(partial, 1 - core).astype(BF)).astype(F32)

    three = jnp.stack((w_query, w_key, w_value)).reshape(3, rows, 2, half)
    vectors = (
        b_query, b_value, b_out, b_down, norm1_gain, norm1_shift, norm2_gain, norm2_shift, b_up
    )
    small = jnp.concatenate(vectors)
    small_rows = jnp.zeros((SMALL, half), BF).at[0, : small.shape[0]].set(small)
    unit = pair(
        core,
        jnp.concatenate((pick(three, core, 2).reshape(3 * rows, half), small_rows)),
        other_core(
            jnp.concatenate((pick(three, 1 - core, 2).reshape(3 * rows, half), small_rows))
        ),
    )
    up_parts = w_up.reshape(rows, chips, 2, hidden_rows)
    up_unit = pair(
        core,
        pick(up_parts, core, 2).reshape(rows, hidden),
        other_core(pick(up_parts, 1 - core, 2).reshape(rows, hidden)),
    )
    up_unit = up_unit.reshape(2 * rows, 2, width)
    late = jnp.concatenate((up_unit[:, 0], up_unit[:, 1], w_down, w_out))
    late = lax.all_gather(late, ("z", "x", "y"), axis=0, tiled=False)
    mine = own_positions(tokens_in)
    tokens = whole(mine).astype(F32)
    mine32 = mine.astype(F32)
    first = gather_chips(unit, z, x, y)
    out_parts = late[:, 2 * hidden_rows :].reshape(2, half_chips, rows, width)
    out_c = (
        pair(core, pick(out_parts, core, 0), other_core(pick(out_parts, 1 - core, 0)))
        .swapaxes(0, 1)
        .reshape(half, width)
    )
    three_c = first[..., : 3 * rows, :].reshape(chips * 2, 3, rows, half)
    query_c, key_c, value_c = (three_c[:, i].reshape(width, half) for i in range(3))
    small_all = first[..., 3 * rows, : small.shape[0]].reshape(chips * 2, -1)

    def vector(i):
        return small_all[:, i * rows : (i + 1) * rows].reshape(width).astype(F32)

    def core_half(value):
        return pick(value.reshape(2, half), core, 0)

    bias_q, bias_v, bias_o, bias_d, gain1, shift1, gain2, shift2 = (vector(i) for i in range(8))
    bias_u = pick(small_all[:, 8 * rows :].reshape(chips, 2, hidden_rows), core, 1)
    bias_u = bias_u.reshape(hidden).astype(F32)

    unit1, _ = norm_stats(tokens)
    normed = (unit1 * gain1 + shift1).astype(BF)
    rightwards = ((1,), (0,))
    queries = ((mm(normed, query_c, rightwards) + core_half(bias_q)) * query_scale).astype(BF)
    keys = mm(normed, key_c, rightwards).astype(BF)
    values = (mm(normed, value_c, rightwards) + core_half(bias_v)).astype(BF)
    mixed, lse = attend(queries, keys, values)
    grad_mine = own_positions(out_grad)
    grad_whole = whole(grad_mine)
    residual = mine32 + chip_sum(mm(mixed, out_c, rightwards)) + bias_o
    unit2, rate2 = norm_stats(residual)
    normed2 = whole((unit2 * gain2 + shift2).astype(BF))
    down_part, normed2_part, grad_up, grad_down, up_sums = feed_forward(
        normed2, grad_whole, late, bias_u, hidden_rows
    )
    output = residual + chip_sum(down_part) + bias_d
    output = output.astype(BF)
    layer_out = pair(y, pick(output, y, 0), other_y(pick(output, 1 - y, 0)))

    across = ((1,), (1,))
    over_rows = ((0,), (0,))
    grad_normed2 = chip_sum(normed2_part)
    grad_residual = grad_mine.astype(F32) + norm_back(unit2, rate2, gain2, grad_normed2)
    branch_mine = grad_residual.astype(BF)
    branch = whole(branch_mine)
    grad_out = mm(mixed, branch, over_rows).reshape(half_chips, 2, rows, width)
    grad_out = pair(core, pick(grad_out, core, 1), other_core(pick(grad_out, 1 - core, 1).astype(BF)).astype(F32))
    by_chip = (z_count, 2, 2)
    sum_up = reduce_chips((grad_up.reshape(by_chip + (2 * rows, hidden)),), z, x, y, True)
    down_out = (
        grad_down.reshape(by_chip + (hidden_rows, width)),
        grad_out.reshape(by_chip + (rows, width)),
    )
    sum_down_out = reduce_chips(down_out, z, x, y, False)
    grad_mixed = mm(branch, out_c, across).astype(BF)
    grad_q, grad_k, grad_v = attend_back(
        queries, keys, values, mixed, lse, grad_mixed, 0, half // (2 * DH)
    )
    grad_qkv = jnp.concatenate((grad_q * query_scale, grad_k, grad_v), axis=1)
    weights_c = jnp.concatenate((query_c, key_c, value_c), axis=1)
    grad_three = mm(normed, grad_qkv, over_rows)
    grad_normed1 = chip_sum(mm(grad_qkv, weights_c, across))
    unit1_mine, rate1_mine = norm_stats(mine32)
    grad_tokens = grad_residual + norm_back(unit1_mine, rate1_mine, gain1, grad_normed1)
    from_y = other_y(pick(grad_tokens, 1 - y, 0).astype(BF)).astype(F32)
    grad_tokens = pair(y, pick(grad_tokens, y, 0), from_y)

    def sums(value):
        return jnp.sum(value.astype(F32), axis=tuple(range(value.ndim - 1)))

    def placed(value):
        return jnp.where(
            (jnp.arange(2) == core)[:, None], value[None], jnp.zeros((), F32)
        ).reshape(width)

    bias_sums = sums(grad_qkv)
    small_grads = [
        placed(bias_sums[:half]),
        placed(bias_sums[2 * half :]),
        sums(branch_mine),
        sums(grad_mine),
        sums(grad_normed1 * unit1_mine),
        sums(grad_normed1),
        sums(grad_normed2 * unit2),
        sums(grad_normed2),
    ]
    small_grads = [g.reshape(chips, 2, rows) for g in small_grads]
    up_sums = up_sums.reshape(chips, 1, hidden_rows)
    small_grads.append(
        jnp.where((jnp.arange(2) == core)[None, :, None], up_sums, jnp.zeros((), F32))
    )
    small_grads = jnp.concatenate(small_grads, axis=2).reshape(chips, 1, -1)
    last = grad_three.reshape(chips, 2 * rows, 3 * half)
    last = jnp.concatenate(
        (last, jnp.pad(small_grads, ((0, 0), (0, SMALL - 1), (0, 3 * half - small_grads.shape[2])))), axis=1
    )
    last_a = reduce_chips((last[:, :, : 3 * half // 2].reshape(by_chip + (-1, 3 * half // 2)),), z, x, y, True)
    last_b = reduce_chips((last[:, :, 3 * half // 2 :].reshape(by_chip + (-1, 3 * half // 2)),), z, x, y, False)
    last = jnp.concatenate((last_a, last_b), axis=1)
    small_mine = last[2 * rows, : 2 * small.shape[0]].reshape(2, -1)
    small_sum = pick(small_mine, core, 0) + other_core(pick(small_mine, 1 - core, 0))
    three_mine = last[: 2 * rows].reshape(2, rows, 3 * half)
    up_mine = sum_up.reshape(2, rows, hidden)
    to_core = jnp.concatenate((pick(three_mine, 1 - core, 0), pick(up_mine, 1 - core, 0)), axis=1)
    to_core = other_core(to_core)
    three_out = pair(core, pick(three_mine, core, 0), to_core[:, : 3 * half])
    three_out = three_out.reshape(2, rows, 3, half)
    up_out = pair(core, pick(up_mine, core, 0), to_core[:, 3 * half :])
    up_out = up_out.reshape(2, rows, chips, hidden_rows)
    up_out = jnp.moveaxis(up_out, 0, 2).reshape(rows, 2 * hidden)
    three_out = jnp.moveaxis(three_out, 0, 2)
    g_q, g_k, g_v = (three_out[:, i].reshape(rows, width) for i in range(3))
    g_small = [small_sum[i * rows : (i + 1) * rows] for i in range(8)]
    return (
        layer_out,
        grad_tokens,
        g_q,
        g_k,
        g_v,
        sum_down_out[hidden_rows:],
        up_out,
        sum_down_out[:hidden_rows],
        g_small[0],
        g_small[1],
        g_small[2],
        small_sum[8 * rows :],
        g_small[3],
        g_small[4],
        g_small[5],
        g_small[6],
        g_small[7],
    )


def solution(mesh):
    dp_count, ctx_count = mesh.shape["dp"], mesh.shape["ctx"]

    def run(*args):
        per_dp = args[0].shape[0] // dp_count
        if ctx_count == 4 and per_dp == 2 and dp_count == 8:
            devices = mesh.devices.reshape(dp_count // 2, 2, ctx_count // 2, 2)
            used = Mesh(devices, ("z", "x", "y", "core"))
            body, dp, ctx = chip_step, ("z", "x"), ("y", "core")
        else:
            used, body, dp, ctx = mesh, on_device, ("dp",), ("ctx",)
        tokens, matrix, bias = P(dp, ctx, None), P(dp + ctx, None), P(dp + ctx)
        return jax.shard_map(
            body,
            mesh=used,
            in_specs=(tokens,) * 2 + (matrix,) * 6 + (bias,) * 9,
            out_specs=(tokens,) * 2 + (matrix,) * 6 + (bias,) * 9,
            check_vma=False,
        )(*args)

    return run
```

```python
import jax
import jax.numpy as jnp
from jax import lax
from jax.experimental import pallas as pl
from jax.experimental.pallas import tpu as pltpu
from jax.sharding import Mesh
from jax.sharding import PartitionSpec as P

HEADS = 12
DH = 64
MICRO = 2


def shifted(value, axis, by):
    peers = lax.axis_size(axis)
    return lax.ppermute(value, axis, [(i, (i + by) % peers) for i in range(peers)])


def as_sent(value):
    return jax.tree.map(lambda a: a.astype(jnp.bfloat16) if a.dtype == jnp.float32 else a, value)


def layer_norm(values, norm_gain, norm_shift):
    centre = values - jnp.mean(values, axis=-1, keepdims=True)
    spread = jnp.mean(centre * centre, axis=-1, keepdims=True)
    return centre * lax.rsqrt(spread + 1e-05) * norm_gain + norm_shift


def gelu_tanh(values):
    return (
        0.5
        * values
        * (1.0 + jnp.tanh(0.7978845608028654 * (values + 0.044715 * values * values * values)))
    )


def project(left, right):
    return jnp.einsum("scd,de->sce", left, right, preferred_element_type=jnp.float32)


def project_back(left, right):
    return jnp.einsum("sce,de->scd", left, right, preferred_element_type=jnp.float32)


def weight_grad(left, right):
    return jnp.einsum("scd,sce->de", left, right, preferred_element_type=jnp.float32)


def column_sum(values):
    return jnp.sum(values.astype(jnp.float32), axis=(0, 1))


def masked_scores(query_heads, key_full, first_pos):
    seq_count, key_len = (key_full.shape[0], key_full.shape[1])
    key_heads = key_full.reshape(seq_count, key_len, HEADS, DH)
    scores = jnp.einsum(
        "sqhd,skhd->shqk", query_heads, key_heads, preferred_element_type=jnp.float32
    )
    row_pos = first_pos + jnp.arange(query_heads.shape[1], dtype=jnp.int32)
    col_pos = jnp.arange(key_len, dtype=jnp.int32)
    allowed = row_pos[:, None] >= col_pos[None, :]
    return (jnp.where(allowed, scores, -1e30), key_heads)


def micro_step(tokens, cotangent, shards, forward_weights):
    (
        w_query,
        w_key,
        w_value,
        w_out,
        w_up,
        w_down,
        b_query,
        b_value,
        b_out,
        b_up,
        b_down,
        gain_one,
        shift_one,
        gain_two,
        shift_two,
    ) = forward_weights
    seq_count, block_rows, width = tokens.shape
    query_scale = DH ** (-0.5)
    first_pos = lax.axis_index("ctx") * block_rows
    gain_one32, shift_one32 = (gain_one.astype(jnp.float32), shift_one.astype(jnp.float32))
    gain_two32, shift_two32 = (gain_two.astype(jnp.float32), shift_two.astype(jnp.float32))
    tokens32 = tokens.astype(jnp.float32)
    normed = layer_norm(tokens32, gain_one32, shift_one32).astype(jnp.bfloat16)
    queries = ((project(normed, w_query) + b_query.astype(jnp.float32)) * query_scale).astype(
        jnp.bfloat16
    )
    keys_local = project(normed, w_key).astype(jnp.bfloat16)
    values_local = (project(normed, w_value) + b_value.astype(jnp.float32)).astype(jnp.bfloat16)
    key_full, value_full = (
        lax.all_gather(keys_local, "ctx", axis=1, tiled=True),
        lax.all_gather(values_local, "ctx", axis=1, tiled=True),
    )
    query_heads = queries.reshape(seq_count, block_rows, HEADS, DH)
    scores, key_heads = masked_scores(query_heads, key_full, first_pos)
    row_max = jnp.max(scores, axis=-1, keepdims=True)
    exp_scores = jnp.exp(scores - row_max)
    row_total = jnp.sum(exp_scores, axis=-1, keepdims=True)
    probs_low = (exp_scores / row_total).astype(jnp.bfloat16)
    value_heads = value_full.reshape(seq_count, value_full.shape[1], HEADS, DH)
    mixed_heads = jnp.einsum(
        "shqk,skhd->sqhd", probs_low, value_heads, preferred_element_type=jnp.float32
    ).reshape(seq_count, block_rows, width)
    mixed_heads = mixed_heads.astype(jnp.bfloat16)
    residual = tokens32 + project(mixed_heads, w_out) + b_out.astype(jnp.float32)
    normed_two = layer_norm(residual, gain_two32, shift_two32).astype(jnp.bfloat16)
    hidden_pre = project(normed_two, w_up) + b_up.astype(jnp.float32)
    active = gelu_tanh(hidden_pre).astype(jnp.bfloat16)
    output = (residual + project(active, w_down) + b_down.astype(jnp.float32)).astype(jnp.bfloat16)
    back_weights = (
        lax.all_gather(shards[0], ("dp", "ctx"), axis=0, tiled=True),
        lax.all_gather(shards[1], ("dp", "ctx"), axis=0, tiled=True),
        lax.all_gather(shards[2], ("dp", "ctx"), axis=0, tiled=True),
        lax.all_gather(shards[3], ("dp", "ctx"), axis=0, tiled=True),
        lax.all_gather(shards[4], ("dp", "ctx"), axis=0, tiled=True),
        lax.all_gather(shards[5], ("dp", "ctx"), axis=0, tiled=True),
        lax.all_gather(shards[6], ("dp", "ctx"), axis=0, tiled=True),
        lax.all_gather(shards[7], ("dp", "ctx"), axis=0, tiled=True),
        lax.all_gather(shards[8], ("dp", "ctx"), axis=0, tiled=True),
        lax.all_gather(shards[9], ("dp", "ctx"), axis=0, tiled=True),
        lax.all_gather(shards[10], ("dp", "ctx"), axis=0, tiled=True),
        lax.all_gather(shards[11], ("dp", "ctx"), axis=0, tiled=True),
        lax.all_gather(shards[12], ("dp", "ctx"), axis=0, tiled=True),
        lax.all_gather(shards[13], ("dp", "ctx"), axis=0, tiled=True),
        lax.all_gather(shards[14], ("dp", "ctx"), axis=0, tiled=True),
    )
    w_query, w_key, w_value, w_out, w_up, w_down = back_weights[:6]
    grad_active = project_back(cotangent, w_down)
    _, gelu_pull = jax.vjp(gelu_tanh, hidden_pre)
    grad_pre = gelu_pull(grad_active)[0].astype(jnp.bfloat16)
    grad_normed_two = project_back(grad_pre, w_up)
    _, norm_pull_two = jax.vjp(layer_norm, residual, gain_two32, shift_two32)
    grad_res_part, grad_gain_two, grad_shift_two = norm_pull_two(grad_normed_two)
    grad_residual = cotangent.astype(jnp.float32) + grad_res_part
    grad_branch = grad_residual.astype(jnp.bfloat16)
    grad_mixed = project_back(grad_branch, w_out).astype(jnp.bfloat16)
    key_full, value_full = (
        lax.all_gather(keys_local, "ctx", axis=1, tiled=True),
        lax.all_gather(values_local, "ctx", axis=1, tiled=True),
    )
    value_heads = value_full.reshape(seq_count, value_full.shape[1], HEADS, DH)
    scores, key_heads = masked_scores(query_heads, key_full, first_pos)
    probs = jnp.exp(scores - row_max) / row_total
    probs_low = probs.astype(jnp.bfloat16)
    grad_heads = grad_mixed.reshape(seq_count, block_rows, HEADS, DH)
    grad_probs = jnp.einsum(
        "sqhd,skhd->shqk", grad_heads, value_heads, preferred_element_type=jnp.float32
    )
    inner_rows = jnp.sum(probs * grad_probs, axis=-1, keepdims=True)
    grad_scores = (probs * (grad_probs - inner_rows)).astype(jnp.bfloat16)
    grad_queries = jnp.einsum(
        "shqk,skhd->sqhd", grad_scores, key_heads, preferred_element_type=jnp.float32
    )
    grad_queries = grad_queries.reshape(seq_count, block_rows, width).astype(jnp.bfloat16)
    query_grad = grad_queries * query_scale

    def key_terms(first_row, row_count):
        score_part = lax.dynamic_slice_in_dim(grad_scores, first_row, row_count, 3)
        prob_part = lax.dynamic_slice_in_dim(probs_low, first_row, row_count, 3)
        key_part = jnp.einsum(
            "shqk,sqhd->kshd", score_part, query_heads, preferred_element_type=jnp.float32
        )
        value_part = jnp.einsum(
            "shqk,sqhd->kshd", prob_part, grad_heads, preferred_element_type=jnp.float32
        )
        return jnp.concatenate(
            (
                key_part.reshape(row_count, seq_count, width),
                value_part.reshape(row_count, seq_count, width),
            ),
            axis=2,
        )

    cycle_size = lax.axis_size("ctx")
    own_index = lax.axis_index("ctx")

    def carry_step(step, carried):
        holder = (own_index - step) % cycle_size
        carried = carried + key_terms(holder * block_rows, block_rows)
        return shifted(carried.astype(jnp.bfloat16), "ctx", 1).astype(carried.dtype)

    start_sums = jnp.zeros((block_rows, seq_count, 2 * width), jnp.float32)
    key_sums = lax.fori_loop(0, cycle_size, carry_step, start_sums)
    key_sums = jnp.transpose(key_sums, (1, 0, 2))
    grad_keys = key_sums[:, :, :width].astype(jnp.bfloat16)
    grad_values = key_sums[:, :, width:].astype(jnp.bfloat16)
    grad_normed = (
        project_back(query_grad, w_query)
        + project_back(grad_keys, w_key)
        + project_back(grad_values, w_value)
    )
    _, norm_pull_one = jax.vjp(layer_norm, tokens32, gain_one32, shift_one32)
    grad_tok_part, grad_gain_one, grad_shift_one = norm_pull_one(grad_normed)
    grad_tokens = grad_residual + grad_tok_part
    small_grads = (grad_gain_one, grad_shift_one, grad_gain_two, grad_shift_two)
    operands = (
        normed,
        query_grad,
        grad_keys,
        grad_values,
        mixed_heads,
        grad_branch,
        normed_two,
        grad_pre,
        active,
        cotangent,
    )
    return (output, grad_tokens, small_grads, operands)


def owner_sum(grads):
    dp_count = lax.axis_size("dp")
    ctx_count = lax.axis_size("ctx")
    blocks = tuple((grad_part.reshape(dp_count, ctx_count, -1) for grad_part in grads))
    first_section = jax.tree.map(
        lambda part, own: part.astype(own.dtype),
        lax.all_to_all(as_sent(blocks), "ctx", split_axis=1, concat_axis=1, tiled=True),
        blocks,
    )
    partial_sums = tuple((jnp.sum(piece, axis=1, keepdims=True) for piece in first_section))
    second_section = jax.tree.map(
        lambda part, own: part.astype(own.dtype),
        lax.all_to_all(as_sent(partial_sums), "dp", split_axis=0, concat_axis=0, tiled=True),
        partial_sums,
    )
    owned = []
    for grad_part, piece in zip(grads, second_section):
        summed = jnp.sum(piece, axis=(0, 1))
        row_count = grad_part.shape[0] // (dp_count * ctx_count)
        owned.append(summed.reshape((row_count,) + grad_part.shape[1:]))
    return owned


def on_device(
    tokens_in,
    out_grad,
    w_query,
    w_key,
    w_value,
    w_out,
    w_up,
    w_down,
    b_query,
    b_value,
    b_out,
    b_up,
    b_down,
    norm1_gain,
    norm1_shift,
    norm2_gain,
    norm2_shift,
):
    shards = (
        w_query,
        w_key,
        w_value,
        w_out,
        w_up,
        w_down,
        b_query,
        b_value,
        b_out,
        b_up,
        b_down,
        norm1_gain,
        norm1_shift,
        norm2_gain,
        norm2_shift,
    )
    per_micro = tokens_in.shape[0] // MICRO
    outputs = []
    grads_in = []
    operand_lists = []
    small_total = None
    for micro_index in range(MICRO):
        lower = micro_index * per_micro
        tokens = tokens_in[lower : lower + per_micro]
        cotangent = out_grad[lower : lower + per_micro]
        forward_weights = (
            lax.all_gather(shards[0], ("dp", "ctx"), axis=0, tiled=True),
            lax.all_gather(shards[1], ("dp", "ctx"), axis=0, tiled=True),
            lax.all_gather(shards[2], ("dp", "ctx"), axis=0, tiled=True),
            lax.all_gather(shards[3], ("dp", "ctx"), axis=0, tiled=True),
            lax.all_gather(shards[4], ("dp", "ctx"), axis=0, tiled=True),
            lax.all_gather(shards[5], ("dp", "ctx"), axis=0, tiled=True),
            lax.all_gather(shards[6], ("dp", "ctx"), axis=0, tiled=True),
            lax.all_gather(shards[7], ("dp", "ctx"), axis=0, tiled=True),
            lax.all_gather(shards[8], ("dp", "ctx"), axis=0, tiled=True),
            lax.all_gather(shards[9], ("dp", "ctx"), axis=0, tiled=True),
            lax.all_gather(shards[10], ("dp", "ctx"), axis=0, tiled=True),
            lax.all_gather(shards[11], ("dp", "ctx"), axis=0, tiled=True),
            lax.all_gather(shards[12], ("dp", "ctx"), axis=0, tiled=True),
            lax.all_gather(shards[13], ("dp", "ctx"), axis=0, tiled=True),
            lax.all_gather(shards[14], ("dp", "ctx"), axis=0, tiled=True),
        )
        output, grad_tokens, small_grads, operands = micro_step(
            tokens, cotangent, shards, forward_weights
        )
        outputs.append(output)
        grads_in.append(grad_tokens)
        operand_lists.append(operands)
        if small_total is None:
            small_total = small_grads
        else:
            small_total = tuple(
                (total_grad + update for total_grad, update in zip(small_total, small_grads))
            )
    joined = tuple(
        (jnp.concatenate([entry[index] for entry in operand_lists], axis=0) for index in range(10))
    )
    (
        normed,
        query_grad,
        grad_keys,
        grad_values,
        mixed_heads,
        grad_branch,
        normed_two,
        grad_pre,
        active,
        cotangent,
    ) = joined
    grads = (
        weight_grad(normed, query_grad),
        weight_grad(normed, grad_keys),
        weight_grad(normed, grad_values),
        weight_grad(mixed_heads, grad_branch),
        weight_grad(normed_two, grad_pre),
        weight_grad(active, cotangent),
        column_sum(query_grad),
        column_sum(grad_values),
        column_sum(grad_branch),
        column_sum(grad_pre),
        column_sum(cotangent),
        small_total[0],
        small_total[1],
        small_total[2],
        small_total[3],
    )
    owned = owner_sum(grads)
    layer_out = jnp.concatenate(outputs, axis=0)
    grad_tokens_all = jnp.concatenate(grads_in, axis=0)
    return (
        layer_out,
        grad_tokens_all,
        owned[0],
        owned[1],
        owned[2],
        owned[3],
        owned[4],
        owned[5],
        owned[6],
        owned[7],
        owned[8],
        owned[9],
        owned[10],
        owned[11],
        owned[12],
        owned[13],
        owned[14],
    )


BF = jnp.bfloat16
F32 = jnp.float32
SMALL = 8


def other_core(value):
    return lax.ppermute(value, "core", [(0, 1), (1, 0)])


def other_x(value):
    return lax.ppermute(value, "x", [(0, 1), (1, 0)])


def other_y(value):
    return lax.ppermute(value, "y", [(0, 1), (1, 0)])


def other_z(value, by):
    return lax.ppermute(value, "z", [(i, i ^ by) for i in range(lax.axis_size("z"))])


def pair(bit, own, received):
    return jnp.stack((jnp.where(bit == 0, own, received), jnp.where(bit == 0, received, own)))


def pick(value, index, axis):
    return lax.dynamic_index_in_dim(value, index, axis, keepdims=False)


def in_order(index, pieces):
    level = list(pieces)
    bit = 0
    ordered = [p[None] for p in level]
    while len(ordered) > 1:
        flag = (index >> bit) & 1
        ordered = [
            jnp.concatenate(
                (jnp.where(flag == 0, a, b), jnp.where(flag == 0, b, a)), axis=0
            )
            for a, b in zip(ordered[::2], ordered[1::2])
        ]
        bit += 1
    return ordered[0]


def gather_chips(unit, z, x, y):
    z_count = lax.axis_size("z")
    along_z = in_order(z, [unit] + [other_z(unit, k) for k in range(1, z_count)])
    half = z_count // 2
    first, second = along_z[:half], along_z[half:]
    first = pair(x, first, other_x(first))
    second = pair(y, second, other_y(second))
    first = pair(y, first, other_y(first))
    second = pair(x, second, other_x(second))
    return jnp.concatenate((jnp.moveaxis(first, 2, 0).swapaxes(1, 2), jnp.moveaxis(second, 2, 0)))


def joined(parts, bit, axis):
    return jnp.concatenate([pick(part, bit, axis).astype(BF) for part in parts], axis=2)


def summed(parts, bit, axis, received):
    kept = jnp.concatenate([pick(part, bit, axis).astype(F32) for part in parts], axis=2)
    return kept + received.astype(F32)


VMEM_LIMIT = 56 * 1024 * 1024
QUERY_BLOCK = 256


def lane_masks(dtype):
    lane = lax.broadcasted_iota(jnp.int32, (1, 2 * DH), 1)
    return [(lane < DH).astype(dtype), (lane >= DH).astype(dtype)]


def visible(key_count, query_block):
    key_pos = lax.broadcasted_iota(jnp.int32, (query_block, query_block), 0)
    query_pos = lax.broadcasted_iota(jnp.int32, (query_block, query_block), 1)
    return key_pos <= query_pos


def masked_tail(scores, allowed):
    key_count, query_block = scores.shape
    tail = jnp.where(allowed, scores[key_count - query_block :], -1e30)
    if key_count == query_block:
        return tail
    return jnp.concatenate((scores[: key_count - query_block], tail), axis=0)


def nt(left, right):
    return lax.dot_general(left, right, (((1,), (1,)), ((), ())), preferred_element_type=F32)


def nn(left, right):
    return lax.dot_general(left, right, (((1,), (0,)), ((), ())), preferred_element_type=F32)


def attend_kernel(q_ref, k_ref, v_ref, mixed_ref, lse_ref):
    length = q_ref.shape[0]
    masks = lane_masks(BF)
    allowed = visible(QUERY_BLOCK, QUERY_BLOCK)
    keys = k_ref[...]
    masked_keys = [keys * m for m in masks]
    v_t = v_ref[...].T
    row = lax.broadcasted_iota(jnp.int32, (2 * DH, 1), 0)
    values_t = [jnp.where(row < DH, v_t, jnp.zeros((), BF)), jnp.where(row >= DH, v_t, jnp.zeros((), BF))]
    for start in range(0, length, QUERY_BLOCK):
        stop = start + QUERY_BLOCK
        q = q_ref[start:stop, :]
        mixed_t = None
        for head in range(2):
            scores = masked_tail(nt(masked_keys[head][:stop], q), allowed)
            top = jnp.max(scores, axis=0, keepdims=True)
            powers = jnp.exp(scores - top)
            total = jnp.sum(powers, axis=0, keepdims=True)
            low = (powers * (1.0 / total)).astype(BF)
            part = nn(values_t[head][:, :stop], low)
            mixed_t = part if mixed_t is None else mixed_t + part
            lse_ref[0, head : head + 1, start:stop] = top + jnp.log(total)
        mixed_ref[start:stop, :] = mixed_t.T.astype(BF)


def attend_back_kernel(q_ref, k_ref, v_ref, g_ref, mixed_ref, lse_ref, gq_ref, gk_ref, gv_ref, ka, va):
    length = q_ref.shape[0]
    masks = lane_masks(BF)
    allowed = visible(QUERY_BLOCK, QUERY_BLOCK)
    keys, values = k_ref[...], v_ref[...]
    masked_keys = [keys * m for m in masks]
    masked_values = [values * m for m in masks]
    keys_t = [m.T for m in masked_keys]
    for start in range(length - QUERY_BLOCK, -1, -QUERY_BLOCK):
        stop = start + QUERY_BLOCK
        q, g = q_ref[start:stop, :], g_ref[start:stop, :]
        products = (g.astype(F32) * mixed_ref[start:stop, :].astype(F32)).T
        grad_q_t = None
        grad_k = grad_v = None
        for head in range(2):
            inner = jnp.sum(products[head * DH : (head + 1) * DH], axis=0, keepdims=True)
            scores = masked_tail(nt(masked_keys[head][:stop], q), allowed)
            probs = jnp.exp(scores - lse_ref[0, head : head + 1, start:stop])
            grad_probs = nt(masked_values[head][:stop], g)
            grad_scores = (probs * (grad_probs - inner)).astype(BF)
            part_v = nn(probs.astype(BF), g * masks[head])
            part_k = nn(grad_scores, q * masks[head])
            part_q = nn(keys_t[head][:, :stop], grad_scores)
            grad_v = part_v if head == 0 else grad_v + part_v
            grad_k = part_k if head == 0 else grad_k + part_k
            grad_q_t = part_q if head == 0 else grad_q_t + part_q
        gq_ref[start:stop, :] = grad_q_t.T.astype(BF)
        if stop == length:
            ka[...] = grad_k
            va[...] = grad_v
        else:
            ka[:stop, :] += grad_k
            va[:stop, :] += grad_v
    gk_ref[...] = ka[...].astype(BF)
    gv_ref[...] = va[...].astype(BF)


def attend(queries, keys, values):
    length, width = queries.shape
    pairs = width // (2 * DH)
    block = pl.BlockSpec((length, 2 * DH), lambda i: (0, i))
    return pl.pallas_call(
        attend_kernel,
        grid=(pairs,),
        in_specs=[block] * 3,
        out_specs=[block, pl.BlockSpec((1, 2, length), lambda i: (i, 0, 0))],
        out_shape=[
            jax.ShapeDtypeStruct((length, width), BF),
            jax.ShapeDtypeStruct((pairs, 2, length), F32),
        ],
        compiler_params=pltpu.CompilerParams(vmem_limit_bytes=VMEM_LIMIT),
        cost_estimate=pl.CostEstimate(
            flops=4 * length * length * width, bytes_accessed=8 * length * width,
            transcendentals=length * length * width // DH,
        ),
        name="attend",
    )(queries, keys, values)


def attend_back(queries, keys, values, mixed, lse, grad_mixed, pair_index, pairs):
    length = queries.shape[0]
    block = pl.BlockSpec((length, 2 * DH), lambda i: (0, i + pair_index))
    out_block = pl.BlockSpec((length, 2 * DH), lambda i: (0, i))
    width = pairs * 2 * DH
    return pl.pallas_call(
        attend_back_kernel,
        grid=(pairs,),
        in_specs=[block] * 5 + [pl.BlockSpec((1, 2, length), lambda i: (i + pair_index, 0, 0))],
        out_specs=[out_block] * 3,
        out_shape=[jax.ShapeDtypeStruct((length, width), BF)] * 3,
        scratch_shapes=[pltpu.VMEM((length, 2 * DH), F32)] * 2,
        compiler_params=pltpu.CompilerParams(vmem_limit_bytes=VMEM_LIMIT),
        cost_estimate=pl.CostEstimate(
            flops=10 * length * length * width, bytes_accessed=16 * length * width,
            transcendentals=length * length * width // DH,
        ),
        name="attend_back",
    )(queries, keys, values, grad_mixed, mixed, lse)


def position_blocks(core, block):
    return [
        (b, own, pl.multiple_of(b * 2 * block + (core if own else 1 - core) * block, block))
        for b in range(2)
        for own in (True, False)
    ]


def normalise(values):
    centre = values - jnp.mean(values, axis=-1, keepdims=True)
    spread = jnp.mean(centre * centre, axis=-1, keepdims=True)
    rate = lax.rsqrt(spread + 1e-05)
    return centre * rate, rate


def normalise_back(unit, rate, gain, grad):
    scaled = grad * gain
    return rate * (
        scaled
        - jnp.mean(scaled, axis=-1, keepdims=True)
        - unit * jnp.mean(scaled * unit, axis=-1, keepdims=True)
    )


B_QUERY, B_VALUE, B_OUT, B_DOWN, GAIN1, SHIFT1, GAIN2, SHIFT2 = range(8)


def enter_kernel(core_ref, mine_ref, other_ref, vec_ref, half_ref, w_ref, n_ref, q_ref, k_ref, v_ref):
    core = core_ref[0]
    block = mine_ref.shape[0] // 2
    for b, own, row in position_blocks(core, block):
        tokens = (mine_ref if own else other_ref)[b * block : (b + 1) * block, :].astype(F32)
        unit, _ = normalise(tokens)
        normed = (unit * vec_ref[GAIN1 : GAIN1 + 1, :] + vec_ref[SHIFT1 : SHIFT1 + 1, :]).astype(BF)
        rows = pl.ds(row, block)
        n_ref[rows, :] = normed
        q = (nn(normed, w_ref[0]) + half_ref[B_QUERY : B_QUERY + 1, :]) * DH ** (-0.5)
        q_ref[rows, :] = q.astype(BF)
        k_ref[rows, :] = nn(normed, w_ref[1]).astype(BF)
        v_ref[rows, :] = (nn(normed, w_ref[2]) + half_ref[B_VALUE : B_VALUE + 1, :]).astype(BF)


def out_kernel(core_ref, mixed_ref, w_ref, mine_ref, other_ref):
    block = mine_ref.shape[0] // 2
    for b, own, row in position_blocks(core_ref[0], block):
        part = nn(mixed_ref[pl.ds(row, block), :], w_ref[...])
        ref = mine_ref if own else other_ref
        ref[b * block : (b + 1) * block, :] = part.astype(ref.dtype)


def middle_kernel(tokens_ref, part_ref, received_ref, vec_ref, residual_ref, n_ref):
    residual = (
        tokens_ref[...].astype(F32)
        + part_ref[...]
        + received_ref[...].astype(F32)
        + vec_ref[B_OUT : B_OUT + 1, :]
    )
    unit, _ = normalise(residual)
    residual_ref[...] = residual
    n_ref[...] = (unit * vec_ref[GAIN2 : GAIN2 + 1, :] + vec_ref[SHIFT2 : SHIFT2 + 1, :]).astype(BF)


def middle_back_kernel(residual_ref, gn_ref, gn_received_ref, g_ref, vec_ref, gr_ref, branch_ref, sums_ref):
    unit, rate = normalise(residual_ref[...])
    grad_normed = gn_ref[...] + gn_received_ref[...].astype(F32)
    cotangent = g_ref[...].astype(F32)
    grad = cotangent + normalise_back(unit, rate, vec_ref[GAIN2 : GAIN2 + 1, :], grad_normed)
    gr_ref[...] = grad
    branch = grad.astype(BF)
    branch_ref[...] = branch
    for i, value in enumerate((branch.astype(F32), cotangent, grad_normed * unit, grad_normed)):
        sums_ref[0, i : i + 1, :] = jnp.sum(value, axis=0, keepdims=True)


def mixed_back_kernel(core_ref, mixed_ref, mine_ref, other_ref, w_ref, gm_ref, gw_ref):
    block = mine_ref.shape[0] // 2
    total = None
    for b, own, row in position_blocks(core_ref[0], block):
        branch = (mine_ref if own else other_ref)[b * block : (b + 1) * block, :]
        rows = pl.ds(row, block)
        gm_ref[rows, :] = nt(branch, w_ref[...]).astype(BF)
        part = nn(mixed_ref[rows, :].T, branch)
        total = part if total is None else total + part
    gw_ref[...] = total.astype(BF)


def enter_back_kernel(
    core_ref, n_ref, q_ref, k_ref, v_ref, w_ref, gw_ref, mine_ref, other_ref, sums_ref
):
    block = mine_ref.shape[0] // 2
    n_t = n_ref[...].T
    scale = jnp.asarray(DH ** (-0.5), BF)
    grads = [q_ref[...] * scale, k_ref[...], v_ref[...]]
    for i, grad in enumerate(grads):
        gw_ref[i] = nn(n_t, grad).astype(BF)
    sums_ref[0:1, :] = jnp.sum(grads[0].astype(F32), axis=0, keepdims=True)
    sums_ref[1:2, :] = jnp.sum(grads[2].astype(F32), axis=0, keepdims=True)
    for b, own, row in position_blocks(core_ref[0], block):
        rows = pl.ds(row, block)
        part = (
            nt(q_ref[rows, :] * scale, w_ref[0])
            + nt(k_ref[rows, :], w_ref[1])
            + nt(v_ref[rows, :], w_ref[2])
        )
        ref = mine_ref if own else other_ref
        ref[b * block : (b + 1) * block, :] = part.astype(ref.dtype)


def leave_kernel(tokens_ref, gn_ref, gn_received_ref, gr_ref, vec_ref, gt_ref, sums_ref):
    unit, rate = normalise(tokens_ref[...].astype(F32))
    grad_normed = gn_ref[...] + gn_received_ref[...].astype(F32)
    gt_ref[...] = gr_ref[...] + normalise_back(unit, rate, vec_ref[GAIN1 : GAIN1 + 1, :], grad_normed)
    for i, value in enumerate((grad_normed * unit, grad_normed)):
        sums_ref[0, i : i + 1, :] = jnp.sum(value, axis=0, keepdims=True)


def shape(dims, dtype):
    return jax.ShapeDtypeStruct(dims, dtype)


def whole_call(kernel, outs, *args, flops=0, scalars=0):
    in_specs = [
        pl.BlockSpec(memory_space=pltpu.SMEM if i < scalars else pltpu.VMEM)
        for i in range(len(args))
    ]
    moved = sum(a.size * a.dtype.itemsize for a in list(args) + outs)
    return pl.pallas_call(
        kernel,
        in_specs=in_specs,
        out_specs=[pl.BlockSpec(memory_space=pltpu.VMEM)] * len(outs),
        out_shape=outs,
        compiler_params=pltpu.CompilerParams(vmem_limit_bytes=VMEM_LIMIT),
        cost_estimate=pl.CostEstimate(flops=flops, bytes_accessed=moved, transcendentals=0),
        name=kernel.__name__,
    )(*args)


def row_call(kernel, outs, sums, *args):
    length, width = args[0].shape
    block = length // 2
    rows = pl.BlockSpec((block, width), lambda i: (i, 0))
    out_shape = [shape((length, width), dtype) for dtype in outs]
    out_specs = [rows] * len(outs)
    if sums:
        out_shape.append(shape((2, sums, width), F32))
        out_specs.append(pl.BlockSpec((1, sums, width), lambda i: (i, 0, 0)))
    moved = sum(a.size * a.dtype.itemsize for a in list(args) + out_shape)
    return pl.pallas_call(
        kernel,
        grid=(2,),
        in_specs=[rows] * (len(args) - 1) + [pl.BlockSpec(args[-1].shape, lambda i: (0, 0))],
        out_specs=out_specs,
        out_shape=out_shape,
        compiler_params=pltpu.CompilerParams(vmem_limit_bytes=VMEM_LIMIT),
        cost_estimate=pl.CostEstimate(flops=0, bytes_accessed=moved, transcendentals=0),
        name=kernel.__name__,
    )(*args)


def hidden_kernel(
    n_mine, n_other, g_mine, g_other, up_ref, down_ref, bias_ref,
    y_mine, y_other, gn_mine, gn_other, gu_ref, gd_ref, gb_ref, n_t, y_sum, gn_sum,
):
    step = pl.program_id(0)
    length = n_mine.shape[0]

    @pl.when(step == 0)
    def _():
        n_t[:, :length] = n_mine[...].T
        n_t[:, length:] = n_other[...].T
        for ref in (y_mine, gn_mine, y_sum, gn_sum):
            ref[...] = jnp.zeros(ref.shape, F32)

    up = up_ref[...].reshape(-1, up_ref.shape[2])
    down = down_ref[...].reshape(-1, down_ref.shape[2])
    grad_up = grad_down = bias_sum = None
    for part, (n_ref, g_ref, y_ref, gn_ref) in enumerate(
        ((n_mine, g_mine, y_mine, gn_mine), (n_other, g_other, y_sum, gn_sum))
    ):
        n, g = n_ref[...], g_ref[...]
        pre = nn(n, up) + bias_ref[0]
        square = pre * pre
        bent = jnp.tanh(0.7978845608028654 * (pre + 0.044715 * square * pre))
        half = 0.5 * (1.0 + bent)
        active = (pre * half).astype(BF)
        slope = half + 0.5 * pre * (1.0 - bent * bent) * (
            0.7978845608028654 * (1.0 + 3 * 0.044715 * square)
        )
        grad_pre = (nt(g, down) * slope).astype(BF)
        y_ref[...] += nn(active, down)
        gn_ref[...] += nt(grad_pre, up)
        part_up = nn(n_t[:, part * length : (part + 1) * length], grad_pre)
        part_down = lax.dot_general(active, g, (((0,), (0,)), ((), ())), preferred_element_type=F32)
        part_bias = jnp.sum(grad_pre.astype(F32), axis=0, keepdims=True)
        grad_up = part_up if part == 0 else grad_up + part_up
        grad_down = part_down if part == 0 else grad_down + part_down
        bias_sum = part_bias if part == 0 else bias_sum + part_bias
    gu_ref[...] = grad_up.astype(BF).reshape(gu_ref.shape)
    gd_ref[...] = grad_down.astype(BF).reshape(gd_ref.shape)
    gb_ref[0] = bias_sum

    @pl.when(step == pl.num_programs(0) - 1)
    def _():
        y_other[...] = y_sum[...].astype(BF)
        gn_other[...] = gn_sum[...].astype(BF)


def feed_forward(n_mine, n_other, g_mine, g_other, late, bias, hidden_rows):
    length, width = n_mine.shape
    chips = late.shape[0]
    steps = 4
    tile = chips * hidden_rows // steps
    up_rows = width // chips
    per_half = steps // 2
    down_chips = chips // steps
    full = pl.BlockSpec((length, width), lambda i: (0, 0))
    hidden = tile * steps
    return pl.pallas_call(
        hidden_kernel,
        grid=(steps,),
        in_specs=[full] * 4
        + [
            pl.BlockSpec((chips, up_rows, tile), lambda i: (0, i // per_half, i % per_half)),
            pl.BlockSpec((down_chips, hidden_rows, width), lambda i: (i, 1, 0)),
            pl.BlockSpec((1, 1, tile), lambda i: (i, 0, 0)),
        ],
        out_specs=[full] * 4
        + [
            pl.BlockSpec((chips, up_rows, tile), lambda i: (0, 0, i)),
            pl.BlockSpec((down_chips, hidden_rows, width), lambda i: (i, 0, 0)),
            pl.BlockSpec((1, 1, tile), lambda i: (i, 0, 0)),
        ],
        out_shape=[
            shape((length, width), F32),
            shape((length, width), BF),
            shape((length, width), F32),
            shape((length, width), BF),
            shape((chips, up_rows, hidden), BF),
            shape((chips, hidden_rows, width), BF),
            shape((steps, 1, tile), F32),
        ],
        scratch_shapes=[pltpu.VMEM((width, 2 * length), BF)] + [pltpu.VMEM((length, width), F32)] * 2,
        compiler_params=pltpu.CompilerParams(vmem_limit_bytes=VMEM_LIMIT),
        cost_estimate=pl.CostEstimate(
            flops=24 * length * width * hidden, bytes_accessed=48 * length * width,
            transcendentals=2 * length * hidden,
        ),
        name="feed_forward",
    )(n_mine, n_other, g_mine, g_other, late, late, bias.reshape(steps, 1, tile))


def chip_step(
    tokens_in,
    out_grad,
    w_query,
    w_key,
    w_value,
    w_out,
    w_up,
    w_down,
    b_query,
    b_value,
    b_out,
    b_up,
    b_down,
    norm1_gain,
    norm1_shift,
    norm2_gain,
    norm2_shift,
):
    z, x, y, core = (lax.axis_index(name) for name in ("z", "x", "y", "core"))
    z_count = lax.axis_size("z")
    chips = z_count * 4
    half_chips = chips // 2
    _, block, width = tokens_in.shape
    half = width // 2
    rows = w_query.shape[0]
    hidden_rows = w_down.shape[0]
    hidden = hidden_rows * chips

    def own_positions(value):
        return pair(y, pick(value, y, 0), other_y(pick(value, 1 - y, 0))).reshape(2 * block, width)

    three = jnp.stack((w_query, w_key, w_value)).reshape(3, rows, 2, half)
    vectors = (
        b_query, b_value, b_out, b_down, norm1_gain, norm1_shift, norm2_gain, norm2_shift, b_up
    )
    small = jnp.concatenate(vectors)
    small_rows = jnp.zeros((SMALL, half), BF).at[0, : small.shape[0]].set(small)
    unit = pair(
        core,
        jnp.concatenate((pick(three, core, 2).reshape(3 * rows, half), small_rows)),
        other_core(
            jnp.concatenate((pick(three, 1 - core, 2).reshape(3 * rows, half), small_rows))
        ),
    )
    up_parts = w_up.reshape(rows, chips, 2, hidden_rows)
    up_unit = pair(
        core,
        pick(up_parts, core, 2).reshape(rows, hidden),
        other_core(pick(up_parts, 1 - core, 2).reshape(rows, hidden)),
    )
    up_unit = up_unit.reshape(2 * rows, 2, width)
    late = jnp.concatenate((up_unit[:, 0], up_unit[:, 1], w_down, w_out))
    late = lax.all_gather(late, ("z", "x", "y"), axis=0, tiled=False)
    mine = own_positions(tokens_in)
    other = other_core(mine)
    core_index = core.reshape(1).astype(jnp.int32)
    first = gather_chips(unit, z, x, y)
    three_c = first[..., : 3 * rows, :].reshape(chips * 2, 3, rows, half)
    three_c = three_c.swapaxes(0, 1).reshape(3, width, half)
    small_all = first[..., 3 * rows, : small.shape[0]].reshape(chips * 2, -1)
    vectors = small_all[:, : 8 * rows].reshape(chips * 2, 8, rows).swapaxes(0, 1)
    vectors = vectors.reshape(8, width).astype(F32)
    halves = pick(vectors.reshape(8, 2, half), core, 1)
    bias_u = pick(small_all[:, 8 * rows :].reshape(chips, 2, hidden_rows), core, 1)
    bias_u = bias_u.reshape(hidden).astype(F32)

    length = 4 * block
    heads_shape = shape((length, half), BF)
    normed, queries, keys, values = whole_call(
        enter_kernel,
        [shape((length, width), BF)] + [heads_shape] * 3,
        core_index, mine, other, vectors, halves, three_c,
        flops=6 * length * width * half, scalars=1,
    )
    mixed, lse = attend(queries, keys, values)
    late, mixed = lax.optimization_barrier((late, mixed))
    out_parts = late[:, 2 * hidden_rows :].reshape(2, half_chips, rows, width)
    out_c = (
        pair(core, pick(out_parts, core, 0), other_core(pick(out_parts, 1 - core, 0)))
        .swapaxes(0, 1)
        .reshape(half, width)
    )
    grad_mine = own_positions(out_grad)
    grad_other = other_core(grad_mine)
    mine_shape = shape((2 * block, width), F32)
    sent_shape = shape((2 * block, width), BF)
    part, to_other = whole_call(
        out_kernel, [mine_shape, sent_shape], core_index, mixed, out_c,
        flops=2 * length * width * half, scalars=1,
    )
    residual, normed2 = row_call(middle_kernel, (F32, BF), 0, mine, part, other_core(to_other), vectors)
    y_mine, y_other, gn_mine, gn_other, grad_up, grad_down, up_sums = feed_forward(
        normed2, other_core(normed2), grad_mine, grad_other, late, bias_u, hidden_rows
    )

    by_chip = (z_count, 2, 2)
    ups = (grad_up.reshape(by_chip + (2 * rows, hidden)),)
    downs = (grad_down.reshape(by_chip + (hidden_rows, width)),)
    up_from = other_y(joined(ups, 1 - y, 2))
    down_from = other_x(joined(downs, 1 - x, 1))
    grad_residual, branch, sums2 = row_call(
        middle_back_kernel, (F32, BF), 4, residual, gn_mine, other_core(gn_other), grad_mine, vectors
    )
    grad_mixed, grad_out = whole_call(
        mixed_back_kernel, [heads_shape, shape((half, width), BF)],
        core_index, mixed, branch, other_core(branch), out_c,
        flops=4 * length * width * half, scalars=1,
    )
    grads = attend_back(
        queries, keys, values, mixed, lse, grad_mixed, 0, half // (2 * DH)
    )
    up_from, down_from, grads = lax.optimization_barrier((up_from, down_from, grads))
    ups = (summed(ups, y, 2, up_from),)
    downs = (summed(downs, x, 1, down_from),)
    up_from = other_x(joined(ups, 1 - x, 1))
    down_from = other_y(joined(downs, 1 - y, 1))
    grad_three, gn_mine, gn_other, sums_heads = whole_call(
        enter_back_kernel,
        [shape((3, width, half), BF), mine_shape, sent_shape, shape((2, half), F32)],
        core_index, normed, *grads, three_c,
        flops=12 * length * width * half, scalars=1,
    )
    grad_tokens, sums1 = row_call(
        leave_kernel, (F32,), 2, mine, gn_mine, other_core(gn_other), grad_residual, vectors
    )
    output = residual + y_mine + other_core(y_other).astype(F32) + vectors[B_DOWN]
    output = output.astype(BF).reshape(2, block, width)
    layer_out = pair(y, pick(output, y, 0), other_y(pick(output, 1 - y, 0)))

    placed = jnp.where((jnp.arange(2) == core)[None, :, None], sums_heads[:, None], 0.0)
    small_grads = jnp.concatenate(
        (placed.reshape(2, width), sums2[0, :2] + sums2[1, :2], sums1[0] + sums1[1], sums2[0, 2:] + sums2[1, 2:])
    )
    small_grads = small_grads.reshape(8, chips * 2, rows).swapaxes(0, 1).reshape(chips, 2, 8 * rows)
    up_sums = jnp.where(
        (jnp.arange(2) == core)[None, :, None], up_sums.reshape(chips, 1, hidden_rows), 0.0
    )
    small_grads = jnp.concatenate((small_grads, up_sums), axis=2)
    small_grads = jnp.pad(small_grads, ((0, 0), (0, SMALL - 2), (0, half - small_grads.shape[2])))
    small_grads = small_grads.reshape(by_chip + (SMALL, half)).astype(BF)

    grad_out = grad_out.reshape(half_chips, 2, rows, width)
    grad_out = pair(
        core,
        pick(grad_out, core, 1),
        other_core(pick(grad_out, 1 - core, 1)),
    ).reshape(by_chip + (rows, width))
    three = grad_three.reshape((3,) + by_chip + (2 * rows, half))
    lefts = (three[0], three[1])
    rights = (three[2], grad_out[..., :half], grad_out[..., half:], small_grads)
    up_from, down_from, lefts, rights = lax.optimization_barrier((up_from, down_from, lefts, rights))
    left_from = other_y(joined(lefts, 1 - y, 2))
    right_from = other_x(joined(rights, 1 - x, 1))
    ups = summed(ups, x, 1, up_from)
    downs = summed(downs, y, 1, down_from)

    def along_z(value):
        kept = pick(value, z, 0)
        for k in range(1, z_count):
            kept = kept + other_z(pick(value, z ^ k, 0).astype(BF), k).astype(F32)
        return kept

    forward_sum = along_z(jnp.concatenate((ups[..., :width], ups[..., width:], downs), axis=1))
    from_y = other_y(pick(grad_tokens.reshape(2, block, width), 1 - y, 0).astype(BF)).astype(F32)
    grad_tokens = pair(y, pick(grad_tokens.reshape(2, block, width), y, 0), from_y)
    lefts = (summed(lefts, y, 2, left_from),)
    rights = (summed(rights, x, 1, right_from),)
    lefts = summed(lefts, x, 1, other_x(joined(lefts, 1 - x, 1)))
    rights = summed(rights, y, 1, other_y(joined(rights, 1 - y, 1)))
    last = along_z(jnp.concatenate((lefts, rights), axis=1))

    up_mine = forward_sum[: 4 * rows].reshape(2, 2, rows, width)
    down_mine = forward_sum[4 * rows :]
    three_mine = last[: 6 * rows].reshape(3, 2, rows, half)
    out_mine = jnp.concatenate((last[6 * rows : 7 * rows], last[7 * rows : 8 * rows]), axis=1)
    small_mine = last[8 * rows : 8 * rows + 2, : small.shape[0]]
    up_from = other_core(pick(up_mine, 1 - core, 1))
    small_from = jnp.pad(pick(small_mine, 1 - core, 0)[None], ((0, 7), (0, half - small.shape[0])))
    three_from = other_core(
        jnp.concatenate((pick(three_mine, 1 - core, 1).reshape(3 * rows, half), small_from))
    )
    small_sum = pick(small_mine, core, 0) + three_from[3 * rows, : small.shape[0]]
    three_out = pair(core, pick(three_mine, core, 1), three_from[: 3 * rows].reshape(3, rows, half))
    up_out = pair(core, pick(up_mine, core, 1), up_from)
    up_out = up_out.reshape(2, 2, rows, half_chips, hidden_rows)
    up_out = jnp.transpose(up_out, (2, 1, 3, 0, 4)).reshape(rows, 2 * hidden)
    g_q, g_k, g_v = (jnp.concatenate((three_out[0, i], three_out[1, i]), axis=1) for i in range(3))
    g_small = [small_sum[i * rows : (i + 1) * rows] for i in range(8)]
    return (
        layer_out,
        grad_tokens,
        g_q,
        g_k,
        g_v,
        out_mine,
        up_out,
        down_mine,
        g_small[0],
        g_small[1],
        g_small[2],
        small_sum[8 * rows :],
        g_small[3],
        g_small[4],
        g_small[5],
        g_small[6],
        g_small[7],
    )


def solution(mesh):
    dp_count, ctx_count = mesh.shape["dp"], mesh.shape["ctx"]

    def run(*args):
        per_dp = args[0].shape[0] // dp_count
        if ctx_count == 4 and per_dp == 2 and dp_count == 8:
            devices = mesh.devices.reshape(dp_count // 2, 2, ctx_count // 2, 2)
            used = Mesh(devices, ("z", "x", "y", "core"))
            body, dp, ctx = chip_step, ("z", "x"), ("y", "core")
        else:
            used, body, dp, ctx = mesh, on_device, ("dp",), ("ctx",)
        tokens, matrix, bias = P(dp, ctx, None), P(dp + ctx, None), P(dp + ctx)
        return jax.shard_map(
            body,
            mesh=used,
            in_specs=(tokens,) * 2 + (matrix,) * 6 + (bias,) * 9,
            out_specs=(tokens,) * 2 + (matrix,) * 6 + (bias,) * 9,
            check_vma=False,
        )(*args)

    return run
```

```python
import jax
import jax.numpy as jnp
from jax import lax
from jax.experimental import pallas as pl
from jax.experimental.pallas import tpu as pltpu
from jax.sharding import Mesh
from jax.sharding import PartitionSpec as P

HEADS = 12
DH = 64
MICRO = 2


def shifted(value, axis, by):
    peers = lax.axis_size(axis)
    return lax.ppermute(value, axis, [(i, (i + by) % peers) for i in range(peers)])


def as_sent(value):
    return jax.tree.map(lambda a: a.astype(jnp.bfloat16) if a.dtype == jnp.float32 else a, value)


def layer_norm(values, norm_gain, norm_shift):
    centre = values - jnp.mean(values, axis=-1, keepdims=True)
    spread = jnp.mean(centre * centre, axis=-1, keepdims=True)
    return centre * lax.rsqrt(spread + 1e-05) * norm_gain + norm_shift


def gelu_tanh(values):
    return (
        0.5
        * values
        * (1.0 + jnp.tanh(0.7978845608028654 * (values + 0.044715 * values * values * values)))
    )


def project(left, right):
    return jnp.einsum("scd,de->sce", left, right, preferred_element_type=jnp.float32)


def project_back(left, right):
    return jnp.einsum("sce,de->scd", left, right, preferred_element_type=jnp.float32)


def weight_grad(left, right):
    return jnp.einsum("scd,sce->de", left, right, preferred_element_type=jnp.float32)


def column_sum(values):
    return jnp.sum(values.astype(jnp.float32), axis=(0, 1))


def masked_scores(query_heads, key_full, first_pos):
    seq_count, key_len = (key_full.shape[0], key_full.shape[1])
    key_heads = key_full.reshape(seq_count, key_len, HEADS, DH)
    scores = jnp.einsum(
        "sqhd,skhd->shqk", query_heads, key_heads, preferred_element_type=jnp.float32
    )
    row_pos = first_pos + jnp.arange(query_heads.shape[1], dtype=jnp.int32)
    col_pos = jnp.arange(key_len, dtype=jnp.int32)
    allowed = row_pos[:, None] >= col_pos[None, :]
    return (jnp.where(allowed, scores, -1e30), key_heads)


def micro_step(tokens, cotangent, shards, forward_weights):
    (
        w_query,
        w_key,
        w_value,
        w_out,
        w_up,
        w_down,
        b_query,
        b_value,
        b_out,
        b_up,
        b_down,
        gain_one,
        shift_one,
        gain_two,
        shift_two,
    ) = forward_weights
    seq_count, block_rows, width = tokens.shape
    query_scale = DH ** (-0.5)
    first_pos = lax.axis_index("ctx") * block_rows
    gain_one32, shift_one32 = (gain_one.astype(jnp.float32), shift_one.astype(jnp.float32))
    gain_two32, shift_two32 = (gain_two.astype(jnp.float32), shift_two.astype(jnp.float32))
    tokens32 = tokens.astype(jnp.float32)
    normed = layer_norm(tokens32, gain_one32, shift_one32).astype(jnp.bfloat16)
    queries = ((project(normed, w_query) + b_query.astype(jnp.float32)) * query_scale).astype(
        jnp.bfloat16
    )
    keys_local = project(normed, w_key).astype(jnp.bfloat16)
    values_local = (project(normed, w_value) + b_value.astype(jnp.float32)).astype(jnp.bfloat16)
    key_full, value_full = (
        lax.all_gather(keys_local, "ctx", axis=1, tiled=True),
        lax.all_gather(values_local, "ctx", axis=1, tiled=True),
    )
    query_heads = queries.reshape(seq_count, block_rows, HEADS, DH)
    scores, key_heads = masked_scores(query_heads, key_full, first_pos)
    row_max = jnp.max(scores, axis=-1, keepdims=True)
    exp_scores = jnp.exp(scores - row_max)
    row_total = jnp.sum(exp_scores, axis=-1, keepdims=True)
    probs_low = (exp_scores / row_total).astype(jnp.bfloat16)
    value_heads = value_full.reshape(seq_count, value_full.shape[1], HEADS, DH)
    mixed_heads = jnp.einsum(
        "shqk,skhd->sqhd", probs_low, value_heads, preferred_element_type=jnp.float32
    ).reshape(seq_count, block_rows, width)
    mixed_heads = mixed_heads.astype(jnp.bfloat16)
    residual = tokens32 + project(mixed_heads, w_out) + b_out.astype(jnp.float32)
    normed_two = layer_norm(residual, gain_two32, shift_two32).astype(jnp.bfloat16)
    hidden_pre = project(normed_two, w_up) + b_up.astype(jnp.float32)
    active = gelu_tanh(hidden_pre).astype(jnp.bfloat16)
    output = (residual + project(active, w_down) + b_down.astype(jnp.float32)).astype(jnp.bfloat16)
    back_weights = (
        lax.all_gather(shards[0], ("dp", "ctx"), axis=0, tiled=True),
        lax.all_gather(shards[1], ("dp", "ctx"), axis=0, tiled=True),
        lax.all_gather(shards[2], ("dp", "ctx"), axis=0, tiled=True),
        lax.all_gather(shards[3], ("dp", "ctx"), axis=0, tiled=True),
        lax.all_gather(shards[4], ("dp", "ctx"), axis=0, tiled=True),
        lax.all_gather(shards[5], ("dp", "ctx"), axis=0, tiled=True),
        lax.all_gather(shards[6], ("dp", "ctx"), axis=0, tiled=True),
        lax.all_gather(shards[7], ("dp", "ctx"), axis=0, tiled=True),
        lax.all_gather(shards[8], ("dp", "ctx"), axis=0, tiled=True),
        lax.all_gather(shards[9], ("dp", "ctx"), axis=0, tiled=True),
        lax.all_gather(shards[10], ("dp", "ctx"), axis=0, tiled=True),
        lax.all_gather(shards[11], ("dp", "ctx"), axis=0, tiled=True),
        lax.all_gather(shards[12], ("dp", "ctx"), axis=0, tiled=True),
        lax.all_gather(shards[13], ("dp", "ctx"), axis=0, tiled=True),
        lax.all_gather(shards[14], ("dp", "ctx"), axis=0, tiled=True),
    )
    w_query, w_key, w_value, w_out, w_up, w_down = back_weights[:6]
    grad_active = project_back(cotangent, w_down)
    _, gelu_pull = jax.vjp(gelu_tanh, hidden_pre)
    grad_pre = gelu_pull(grad_active)[0].astype(jnp.bfloat16)
    grad_normed_two = project_back(grad_pre, w_up)
    _, norm_pull_two = jax.vjp(layer_norm, residual, gain_two32, shift_two32)
    grad_res_part, grad_gain_two, grad_shift_two = norm_pull_two(grad_normed_two)
    grad_residual = cotangent.astype(jnp.float32) + grad_res_part
    grad_branch = grad_residual.astype(jnp.bfloat16)
    grad_mixed = project_back(grad_branch, w_out).astype(jnp.bfloat16)
    key_full, value_full = (
        lax.all_gather(keys_local, "ctx", axis=1, tiled=True),
        lax.all_gather(values_local, "ctx", axis=1, tiled=True),
    )
    value_heads = value_full.reshape(seq_count, value_full.shape[1], HEADS, DH)
    scores, key_heads = masked_scores(query_heads, key_full, first_pos)
    probs = jnp.exp(scores - row_max) / row_total
    probs_low = probs.astype(jnp.bfloat16)
    grad_heads = grad_mixed.reshape(seq_count, block_rows, HEADS, DH)
    grad_probs = jnp.einsum(
        "sqhd,skhd->shqk", grad_heads, value_heads, preferred_element_type=jnp.float32
    )
    inner_rows = jnp.sum(probs * grad_probs, axis=-1, keepdims=True)
    grad_scores = (probs * (grad_probs - inner_rows)).astype(jnp.bfloat16)
    grad_queries = jnp.einsum(
        "shqk,skhd->sqhd", grad_scores, key_heads, preferred_element_type=jnp.float32
    )
    grad_queries = grad_queries.reshape(seq_count, block_rows, width).astype(jnp.bfloat16)
    query_grad = grad_queries * query_scale

    def key_terms(first_row, row_count):
        score_part = lax.dynamic_slice_in_dim(grad_scores, first_row, row_count, 3)
        prob_part = lax.dynamic_slice_in_dim(probs_low, first_row, row_count, 3)
        key_part = jnp.einsum(
            "shqk,sqhd->kshd", score_part, query_heads, preferred_element_type=jnp.float32
        )
        value_part = jnp.einsum(
            "shqk,sqhd->kshd", prob_part, grad_heads, preferred_element_type=jnp.float32
        )
        return jnp.concatenate(
            (
                key_part.reshape(row_count, seq_count, width),
                value_part.reshape(row_count, seq_count, width),
            ),
            axis=2,
        )

    cycle_size = lax.axis_size("ctx")
    own_index = lax.axis_index("ctx")

    def carry_step(step, carried):
        holder = (own_index - step) % cycle_size
        carried = carried + key_terms(holder * block_rows, block_rows)
        return shifted(carried.astype(jnp.bfloat16), "ctx", 1).astype(carried.dtype)

    start_sums = jnp.zeros((block_rows, seq_count, 2 * width), jnp.float32)
    key_sums = lax.fori_loop(0, cycle_size, carry_step, start_sums)
    key_sums = jnp.transpose(key_sums, (1, 0, 2))
    grad_keys = key_sums[:, :, :width].astype(jnp.bfloat16)
    grad_values = key_sums[:, :, width:].astype(jnp.bfloat16)
    grad_normed = (
        project_back(query_grad, w_query)
        + project_back(grad_keys, w_key)
        + project_back(grad_values, w_value)
    )
    _, norm_pull_one = jax.vjp(layer_norm, tokens32, gain_one32, shift_one32)
    grad_tok_part, grad_gain_one, grad_shift_one = norm_pull_one(grad_normed)
    grad_tokens = grad_residual + grad_tok_part
    small_grads = (grad_gain_one, grad_shift_one, grad_gain_two, grad_shift_two)
    operands = (
        normed,
        query_grad,
        grad_keys,
        grad_values,
        mixed_heads,
        grad_branch,
        normed_two,
        grad_pre,
        active,
        cotangent,
    )
    return (output, grad_tokens, small_grads, operands)


def owner_sum(grads):
    dp_count = lax.axis_size("dp")
    ctx_count = lax.axis_size("ctx")
    blocks = tuple((grad_part.reshape(dp_count, ctx_count, -1) for grad_part in grads))
    first_section = jax.tree.map(
        lambda part, own: part.astype(own.dtype),
        lax.all_to_all(as_sent(blocks), "ctx", split_axis=1, concat_axis=1, tiled=True),
        blocks,
    )
    partial_sums = tuple((jnp.sum(piece, axis=1, keepdims=True) for piece in first_section))
    second_section = jax.tree.map(
        lambda part, own: part.astype(own.dtype),
        lax.all_to_all(as_sent(partial_sums), "dp", split_axis=0, concat_axis=0, tiled=True),
        partial_sums,
    )
    owned = []
    for grad_part, piece in zip(grads, second_section):
        summed = jnp.sum(piece, axis=(0, 1))
        row_count = grad_part.shape[0] // (dp_count * ctx_count)
        owned.append(summed.reshape((row_count,) + grad_part.shape[1:]))
    return owned


def on_device(
    tokens_in,
    out_grad,
    w_query,
    w_key,
    w_value,
    w_out,
    w_up,
    w_down,
    b_query,
    b_value,
    b_out,
    b_up,
    b_down,
    norm1_gain,
    norm1_shift,
    norm2_gain,
    norm2_shift,
):
    shards = (
        w_query,
        w_key,
        w_value,
        w_out,
        w_up,
        w_down,
        b_query,
        b_value,
        b_out,
        b_up,
        b_down,
        norm1_gain,
        norm1_shift,
        norm2_gain,
        norm2_shift,
    )
    per_micro = tokens_in.shape[0] // MICRO
    outputs = []
    grads_in = []
    operand_lists = []
    small_total = None
    for micro_index in range(MICRO):
        lower = micro_index * per_micro
        tokens = tokens_in[lower : lower + per_micro]
        cotangent = out_grad[lower : lower + per_micro]
        forward_weights = (
            lax.all_gather(shards[0], ("dp", "ctx"), axis=0, tiled=True),
            lax.all_gather(shards[1], ("dp", "ctx"), axis=0, tiled=True),
            lax.all_gather(shards[2], ("dp", "ctx"), axis=0, tiled=True),
            lax.all_gather(shards[3], ("dp", "ctx"), axis=0, tiled=True),
            lax.all_gather(shards[4], ("dp", "ctx"), axis=0, tiled=True),
            lax.all_gather(shards[5], ("dp", "ctx"), axis=0, tiled=True),
            lax.all_gather(shards[6], ("dp", "ctx"), axis=0, tiled=True),
            lax.all_gather(shards[7], ("dp", "ctx"), axis=0, tiled=True),
            lax.all_gather(shards[8], ("dp", "ctx"), axis=0, tiled=True),
            lax.all_gather(shards[9], ("dp", "ctx"), axis=0, tiled=True),
            lax.all_gather(shards[10], ("dp", "ctx"), axis=0, tiled=True),
            lax.all_gather(shards[11], ("dp", "ctx"), axis=0, tiled=True),
            lax.all_gather(shards[12], ("dp", "ctx"), axis=0, tiled=True),
            lax.all_gather(shards[13], ("dp", "ctx"), axis=0, tiled=True),
            lax.all_gather(shards[14], ("dp", "ctx"), axis=0, tiled=True),
        )
        output, grad_tokens, small_grads, operands = micro_step(
            tokens, cotangent, shards, forward_weights
        )
        outputs.append(output)
        grads_in.append(grad_tokens)
        operand_lists.append(operands)
        if small_total is None:
            small_total = small_grads
        else:
            small_total = tuple(
                (total_grad + update for total_grad, update in zip(small_total, small_grads))
            )
    joined = tuple(
        (jnp.concatenate([entry[index] for entry in operand_lists], axis=0) for index in range(10))
    )
    (
        normed,
        query_grad,
        grad_keys,
        grad_values,
        mixed_heads,
        grad_branch,
        normed_two,
        grad_pre,
        active,
        cotangent,
    ) = joined
    grads = (
        weight_grad(normed, query_grad),
        weight_grad(normed, grad_keys),
        weight_grad(normed, grad_values),
        weight_grad(mixed_heads, grad_branch),
        weight_grad(normed_two, grad_pre),
        weight_grad(active, cotangent),
        column_sum(query_grad),
        column_sum(grad_values),
        column_sum(grad_branch),
        column_sum(grad_pre),
        column_sum(cotangent),
        small_total[0],
        small_total[1],
        small_total[2],
        small_total[3],
    )
    owned = owner_sum(grads)
    layer_out = jnp.concatenate(outputs, axis=0)
    grad_tokens_all = jnp.concatenate(grads_in, axis=0)
    return (
        layer_out,
        grad_tokens_all,
        owned[0],
        owned[1],
        owned[2],
        owned[3],
        owned[4],
        owned[5],
        owned[6],
        owned[7],
        owned[8],
        owned[9],
        owned[10],
        owned[11],
        owned[12],
        owned[13],
        owned[14],
    )


BF = jnp.bfloat16
F32 = jnp.float32
SMALL = 8


def other_core(value):
    return lax.ppermute(value, "core", [(0, 1), (1, 0)])


def other_x(value):
    return lax.ppermute(value, "x", [(0, 1), (1, 0)])


def other_y(value):
    return lax.ppermute(value, "y", [(0, 1), (1, 0)])


def other_z(value, by):
    return lax.ppermute(value, "z", [(i, i ^ by) for i in range(lax.axis_size("z"))])


def pair(bit, own, received):
    return jnp.stack((jnp.where(bit == 0, own, received), jnp.where(bit == 0, received, own)))


def pick(value, index, axis):
    return lax.dynamic_index_in_dim(value, index, axis, keepdims=False)


def in_order(index, pieces):
    level = list(pieces)
    bit = 0
    ordered = [p[None] for p in level]
    while len(ordered) > 1:
        flag = (index >> bit) & 1
        ordered = [
            jnp.concatenate(
                (jnp.where(flag == 0, a, b), jnp.where(flag == 0, b, a)), axis=0
            )
            for a, b in zip(ordered[::2], ordered[1::2])
        ]
        bit += 1
    return ordered[0]


def gather_plane(along_z, x, y):
    half = along_z.shape[0] // 2
    first, second = along_z[:half], along_z[half:]
    first = pair(x, first, other_x(first))
    second = pair(y, second, other_y(second))
    first = pair(y, first, other_y(first))
    second = pair(x, second, other_x(second))
    return jnp.concatenate((jnp.moveaxis(first, 2, 0).swapaxes(1, 2), jnp.moveaxis(second, 2, 0)))


def plus(kept, received):
    return kept.astype(F32) + received.astype(F32)


VMEM_LIMIT = 56 * 1024 * 1024
QUERY_BLOCK = 256


def lane_masks(dtype):
    lane = lax.broadcasted_iota(jnp.int32, (1, 2 * DH), 1)
    return [(lane < DH).astype(dtype), (lane >= DH).astype(dtype)]


def visible(key_count, query_block):
    key_pos = lax.broadcasted_iota(jnp.int32, (query_block, query_block), 0)
    query_pos = lax.broadcasted_iota(jnp.int32, (query_block, query_block), 1)
    return key_pos <= query_pos


def masked_tail(scores, allowed):
    key_count, query_block = scores.shape
    tail = jnp.where(allowed, scores[key_count - query_block :], -1e30)
    if key_count == query_block:
        return tail
    return jnp.concatenate((scores[: key_count - query_block], tail), axis=0)


def nt(left, right):
    return lax.dot_general(left, right, (((1,), (1,)), ((), ())), preferred_element_type=F32)


def nn(left, right):
    return lax.dot_general(left, right, (((1,), (0,)), ((), ())), preferred_element_type=F32)


def attend_kernel(q_ref, k_ref, v_ref, mixed_ref, lse_ref):
    length = q_ref.shape[0]
    masks = lane_masks(BF)
    allowed = visible(QUERY_BLOCK, QUERY_BLOCK)
    keys = k_ref[...]
    masked_keys = [keys * m for m in masks]
    v_t = v_ref[...].T
    row = lax.broadcasted_iota(jnp.int32, (2 * DH, 1), 0)
    values_t = [jnp.where(row < DH, v_t, jnp.zeros((), BF)), jnp.where(row >= DH, v_t, jnp.zeros((), BF))]
    for start in range(0, length, QUERY_BLOCK):
        stop = start + QUERY_BLOCK
        q = q_ref[start:stop, :]
        mixed_t = None
        for head in range(2):
            scores = masked_tail(nt(masked_keys[head][:stop], q), allowed)
            top = jnp.max(scores, axis=0, keepdims=True)
            powers = jnp.exp(scores - top)
            total = jnp.sum(powers, axis=0, keepdims=True)
            low = (powers * (1.0 / total)).astype(BF)
            part = nn(values_t[head][:, :stop], low)
            mixed_t = part if mixed_t is None else mixed_t + part
            lse_ref[0, head : head + 1, start:stop] = top + jnp.log(total)
        mixed_ref[start:stop, :] = mixed_t.T.astype(BF)


def attend_back_kernel(q_ref, k_ref, v_ref, g_ref, mixed_ref, lse_ref, gq_ref, gk_ref, gv_ref, ka, va):
    length = q_ref.shape[0]
    masks = lane_masks(BF)
    allowed = visible(QUERY_BLOCK, QUERY_BLOCK)
    keys, values = k_ref[...], v_ref[...]
    masked_keys = [keys * m for m in masks]
    masked_values = [values * m for m in masks]
    keys_t = [m.T for m in masked_keys]
    for start in range(length - QUERY_BLOCK, -1, -QUERY_BLOCK):
        stop = start + QUERY_BLOCK
        q, g = q_ref[start:stop, :], g_ref[start:stop, :]
        products = (g.astype(F32) * mixed_ref[start:stop, :].astype(F32)).T
        grad_q_t = None
        grad_k = grad_v = None
        for head in range(2):
            inner = jnp.sum(products[head * DH : (head + 1) * DH], axis=0, keepdims=True)
            scores = masked_tail(nt(masked_keys[head][:stop], q), allowed)
            probs = jnp.exp(scores - lse_ref[0, head : head + 1, start:stop])
            grad_probs = nt(masked_values[head][:stop], g)
            grad_scores = (probs * (grad_probs - inner)).astype(BF)
            part_v = nn(probs.astype(BF), g * masks[head])
            part_k = nn(grad_scores, q * masks[head])
            part_q = nn(keys_t[head][:, :stop], grad_scores)
            grad_v = part_v if head == 0 else grad_v + part_v
            grad_k = part_k if head == 0 else grad_k + part_k
            grad_q_t = part_q if head == 0 else grad_q_t + part_q
        gq_ref[start:stop, :] = grad_q_t.T.astype(BF)
        if stop == length:
            ka[...] = grad_k
            va[...] = grad_v
        else:
            ka[:stop, :] += grad_k
            va[:stop, :] += grad_v
    gk_ref[...] = ka[...].astype(BF)
    gv_ref[...] = va[...].astype(BF)


def attend(queries, keys, values):
    length, width = queries.shape
    pairs = width // (2 * DH)
    block = pl.BlockSpec((length, 2 * DH), lambda i: (0, i))
    return pl.pallas_call(
        attend_kernel,
        grid=(pairs,),
        in_specs=[block] * 3,
        out_specs=[block, pl.BlockSpec((1, 2, length), lambda i: (i, 0, 0))],
        out_shape=[
            jax.ShapeDtypeStruct((length, width), BF),
            jax.ShapeDtypeStruct((pairs, 2, length), F32),
        ],
        compiler_params=pltpu.CompilerParams(vmem_limit_bytes=VMEM_LIMIT),
        cost_estimate=pl.CostEstimate(
            flops=4 * length * length * width, bytes_accessed=8 * length * width,
            transcendentals=length * length * width // DH,
        ),
        name="attend",
    )(queries, keys, values)


def attend_back(queries, keys, values, mixed, lse, grad_mixed, pair_index, pairs):
    length = queries.shape[0]
    block = pl.BlockSpec((length, 2 * DH), lambda i: (0, i + pair_index))
    out_block = pl.BlockSpec((length, 2 * DH), lambda i: (0, i))
    width = pairs * 2 * DH
    return pl.pallas_call(
        attend_back_kernel,
        grid=(pairs,),
        in_specs=[block] * 5 + [pl.BlockSpec((1, 2, length), lambda i: (i + pair_index, 0, 0))],
        out_specs=[out_block] * 3,
        out_shape=[jax.ShapeDtypeStruct((length, width), BF)] * 3,
        scratch_shapes=[pltpu.VMEM((length, 2 * DH), F32)] * 2,
        compiler_params=pltpu.CompilerParams(vmem_limit_bytes=VMEM_LIMIT),
        cost_estimate=pl.CostEstimate(
            flops=10 * length * length * width, bytes_accessed=16 * length * width,
            transcendentals=length * length * width // DH,
        ),
        name="attend_back",
    )(queries, keys, values, grad_mixed, mixed, lse)


def position_blocks(core, block):
    return [
        (b, own, pl.multiple_of(b * 2 * block + (core if own else 1 - core) * block, block))
        for b in range(2)
        for own in (True, False)
    ]


def normalise(values):
    centre = values - jnp.mean(values, axis=-1, keepdims=True)
    spread = jnp.mean(centre * centre, axis=-1, keepdims=True)
    rate = lax.rsqrt(spread + 1e-05)
    return centre * rate, rate


def normalise_back(unit, rate, gain, grad):
    scaled = grad * gain
    return rate * (
        scaled
        - jnp.mean(scaled, axis=-1, keepdims=True)
        - unit * jnp.mean(scaled * unit, axis=-1, keepdims=True)
    )


CORE, X, Y = range(3)
B_QUERY, B_VALUE, B_OUT, B_DOWN, GAIN1, SHIFT1, GAIN2, SHIFT2 = range(8)


def enter_kernel(core_ref, mine_ref, other_ref, vec_ref, half_ref, w_ref, n_ref, q_ref, k_ref, v_ref):
    core = core_ref[0]
    block = mine_ref.shape[0] // 2
    for b, own, row in position_blocks(core, block):
        tokens = (mine_ref if own else other_ref)[b * block : (b + 1) * block, :].astype(F32)
        unit, _ = normalise(tokens)
        normed = (unit * vec_ref[GAIN1 : GAIN1 + 1, :] + vec_ref[SHIFT1 : SHIFT1 + 1, :]).astype(BF)
        rows = pl.ds(row, block)
        n_ref[rows, :] = normed
        q = (nn(normed, w_ref[0]) + half_ref[B_QUERY : B_QUERY + 1, :]) * DH ** (-0.5)
        q_ref[rows, :] = q.astype(BF)
        k_ref[rows, :] = nn(normed, w_ref[1]).astype(BF)
        v_ref[rows, :] = (nn(normed, w_ref[2]) + half_ref[B_VALUE : B_VALUE + 1, :]).astype(BF)


def out_kernel(core_ref, mixed_ref, w_ref, mine_ref, other_ref):
    block = mine_ref.shape[0] // 2
    for b, own, row in position_blocks(core_ref[0], block):
        part = nn(mixed_ref[pl.ds(row, block), :], w_ref[...])
        ref = mine_ref if own else other_ref
        ref[b * block : (b + 1) * block, :] = part.astype(ref.dtype)


def middle_kernel(tokens_ref, part_ref, received_ref, vec_ref, residual_ref, n_ref):
    residual = (
        tokens_ref[...].astype(F32)
        + part_ref[...]
        + received_ref[...].astype(F32)
        + vec_ref[B_OUT : B_OUT + 1, :]
    )
    unit, _ = normalise(residual)
    residual_ref[...] = residual
    n_ref[...] = (unit * vec_ref[GAIN2 : GAIN2 + 1, :] + vec_ref[SHIFT2 : SHIFT2 + 1, :]).astype(BF)


def middle_back_kernel(residual_ref, gn_ref, gn_received_ref, g_ref, vec_ref, gr_ref, branch_ref, sums_ref):
    unit, rate = normalise(residual_ref[...])
    grad_normed = gn_ref[...] + gn_received_ref[...].astype(F32)
    cotangent = g_ref[...].astype(F32)
    grad = cotangent + normalise_back(unit, rate, vec_ref[GAIN2 : GAIN2 + 1, :], grad_normed)
    gr_ref[...] = grad
    branch = grad.astype(BF)
    branch_ref[...] = branch
    for i, value in enumerate((branch.astype(F32), cotangent, grad_normed * unit, grad_normed)):
        sums_ref[0, i : i + 1, :] = jnp.sum(value, axis=0, keepdims=True)


def mixed_back_kernel(core_ref, mixed_ref, mine_ref, other_ref, w_ref, gm_ref, gw_ref):
    block = mine_ref.shape[0] // 2
    total = None
    for b, own, row in position_blocks(core_ref[0], block):
        branch = (mine_ref if own else other_ref)[b * block : (b + 1) * block, :]
        rows = pl.ds(row, block)
        gm_ref[rows, :] = nt(branch, w_ref[...]).astype(BF)
        part = nn(mixed_ref[rows, :].T, branch)
        total = part if total is None else total + part
    gw_ref[...] = total.astype(BF)


def weight_back_kernel(
    place_ref, n_ref, q_ref, k_ref, v_ref, left_keep, left_send, right_keep, right_send, sums_ref, by_y, by_x
):
    x, y = place_ref[X], place_ref[Y]
    n_t = n_ref[...].T
    rows = by_y.shape[2]
    grads = [q_ref[...] * jnp.asarray(DH ** (-0.5), BF), k_ref[...], v_ref[...]]
    for i in range(2):
        by_y[...] = nn(n_t, grads[i]).astype(BF).reshape(by_y.shape)
        part = slice(i * rows, (i + 1) * rows)
        left_keep[:, part, :] = by_y[:, pl.ds(y, 1)].reshape(-1, rows, by_y.shape[3])
        left_send[:, part, :] = by_y[:, pl.ds(1 - y, 1)].reshape(-1, rows, by_y.shape[3])
    by_x[...] = nn(n_t, grads[2]).astype(BF).reshape(by_x.shape)
    right_keep[...] = by_x[:, pl.ds(x, 1)].reshape(right_keep.shape)
    right_send[...] = by_x[:, pl.ds(1 - x, 1)].reshape(right_send.shape)
    sums_ref[0:1, :] = jnp.sum(grads[0].astype(F32), axis=0, keepdims=True)
    sums_ref[1:2, :] = jnp.sum(grads[2].astype(F32), axis=0, keepdims=True)


def enter_back_kernel(place_ref, q_ref, k_ref, v_ref, w_ref, mine_ref, other_ref):
    block = mine_ref.shape[0] // 2
    for b, own, row in position_blocks(place_ref[CORE], block):
        rows = pl.ds(row, block)
        part = (
            nt(q_ref[rows, :] * jnp.asarray(DH ** (-0.5), BF), w_ref[0])
            + nt(k_ref[rows, :], w_ref[1])
            + nt(v_ref[rows, :], w_ref[2])
        )
        ref = mine_ref if own else other_ref
        ref[b * block : (b + 1) * block, :] = part.astype(ref.dtype)


def leave_kernel(tokens_ref, gn_ref, gn_received_ref, gr_ref, vec_ref, gt_ref, sums_ref):
    unit, rate = normalise(tokens_ref[...].astype(F32))
    grad_normed = gn_ref[...] + gn_received_ref[...].astype(F32)
    gt_ref[...] = gr_ref[...] + normalise_back(unit, rate, vec_ref[GAIN1 : GAIN1 + 1, :], grad_normed)
    for i, value in enumerate((grad_normed * unit, grad_normed)):
        sums_ref[0, i : i + 1, :] = jnp.sum(value, axis=0, keepdims=True)


def shape(dims, dtype):
    return jax.ShapeDtypeStruct(dims, dtype)


def whole_call(kernel, outs, *args, flops=0, scalars=0, scratch=()):
    in_specs = [
        pl.BlockSpec(memory_space=pltpu.SMEM if i < scalars else pltpu.VMEM)
        for i in range(len(args))
    ]
    moved = sum(a.size * a.dtype.itemsize for a in list(args) + outs)
    return pl.pallas_call(
        kernel,
        in_specs=in_specs,
        out_specs=[pl.BlockSpec(memory_space=pltpu.VMEM)] * len(outs),
        out_shape=outs,
        scratch_shapes=list(scratch),
        compiler_params=pltpu.CompilerParams(vmem_limit_bytes=VMEM_LIMIT),
        cost_estimate=pl.CostEstimate(flops=flops, bytes_accessed=moved, transcendentals=0),
        name=kernel.__name__,
    )(*args)


def row_call(kernel, outs, sums, *args):
    length, width = args[0].shape
    block = length // 2
    rows = pl.BlockSpec((block, width), lambda i: (i, 0))
    out_shape = [shape((length, width), dtype) for dtype in outs]
    out_specs = [rows] * len(outs)
    if sums:
        out_shape.append(shape((2, sums, width), F32))
        out_specs.append(pl.BlockSpec((1, sums, width), lambda i: (i, 0, 0)))
    moved = sum(a.size * a.dtype.itemsize for a in list(args) + out_shape)
    return pl.pallas_call(
        kernel,
        grid=(2,),
        in_specs=[rows] * (len(args) - 1) + [pl.BlockSpec(args[-1].shape, lambda i: (0, 0))],
        out_specs=out_specs,
        out_shape=out_shape,
        compiler_params=pltpu.CompilerParams(vmem_limit_bytes=VMEM_LIMIT),
        cost_estimate=pl.CostEstimate(flops=0, bytes_accessed=moved, transcendentals=0),
        name=kernel.__name__,
    )(*args)


def hidden_kernel(
    place_ref, n_mine, n_other, g_mine, g_other, up_ref, down_ref, bias_ref,
    y_mine, y_other, gn_mine, gn_other, up_keep, up_send, down_keep, down_send, gb_ref,
    n_t, y_sum, gn_sum, up_all, down_all,
):
    step = pl.program_id(0)
    length = n_mine.shape[0]

    @pl.when(step == 0)
    def _():
        n_t[:, :length] = n_mine[...].T
        n_t[:, length:] = n_other[...].T
        for ref in (y_mine, gn_mine, y_sum, gn_sum):
            ref[...] = jnp.zeros(ref.shape, F32)

    up = up_ref[...].reshape(-1, up_ref.shape[2])
    down = down_ref[...].reshape(-1, down_ref.shape[2])
    grad_up = grad_down = bias_sum = None
    for part, (n_ref, g_ref, y_ref, gn_ref) in enumerate(
        ((n_mine, g_mine, y_mine, gn_mine), (n_other, g_other, y_sum, gn_sum))
    ):
        n, g = n_ref[...], g_ref[...]
        pre = nn(n, up) + bias_ref[0]
        square = pre * pre
        bent = jnp.tanh(0.7978845608028654 * (pre + 0.044715 * square * pre))
        half = 0.5 * (1.0 + bent)
        active = (pre * half).astype(BF)
        slope = half + 0.5 * pre * (1.0 - bent * bent) * (
            0.7978845608028654 * (1.0 + 3 * 0.044715 * square)
        )
        grad_pre = (nt(g, down) * slope).astype(BF)
        y_ref[...] += nn(active, down)
        gn_ref[...] += nt(grad_pre, up)
        part_up = nn(n_t[:, part * length : (part + 1) * length], grad_pre)
        part_down = lax.dot_general(active, g, (((0,), (0,)), ((), ())), preferred_element_type=F32)
        part_bias = jnp.sum(grad_pre.astype(F32), axis=0, keepdims=True)
        grad_up = part_up if part == 0 else grad_up + part_up
        grad_down = part_down if part == 0 else grad_down + part_down
        bias_sum = part_bias if part == 0 else bias_sum + part_bias
    x, y = place_ref[X], place_ref[Y]
    up_all[...] = grad_up.astype(BF).reshape(up_all.shape)
    up_keep[...] = up_all[:, pl.ds(y, 1)].reshape(up_keep.shape)
    up_send[...] = up_all[:, pl.ds(1 - y, 1)].reshape(up_send.shape)
    down_all[...] = grad_down.astype(BF).reshape(down_all.shape)
    down_keep[...] = down_all[pl.ds(x, 1)].reshape(down_keep.shape)
    down_send[...] = down_all[pl.ds(1 - x, 1)].reshape(down_send.shape)
    gb_ref[0] = bias_sum

    @pl.when(step == pl.num_programs(0) - 1)
    def _():
        y_other[...] = y_sum[...].astype(BF)
        gn_other[...] = gn_sum[...].astype(BF)


def feed_forward(place, n_mine, n_other, g_mine, g_other, late, bias, hidden_rows):
    length, width = n_mine.shape
    chips = late.shape[0]
    steps = chips // 4
    tile = chips * hidden_rows // steps
    up_rows = width // chips
    per_half = steps // 2
    down_chips = chips // steps
    full = pl.BlockSpec((length, width), lambda i: (0, 0))
    hidden = tile * steps
    return pl.pallas_call(
        hidden_kernel,
        grid=(steps,),
        in_specs=[pl.BlockSpec(memory_space=pltpu.SMEM)] + [full] * 4
        + [
            pl.BlockSpec((chips, up_rows, tile), lambda i: (0, i // per_half, i % per_half)),
            pl.BlockSpec((down_chips, hidden_rows, width), lambda i: (i, 1, 0)),
            pl.BlockSpec((1, 1, tile), lambda i: (i, 0, 0)),
        ],
        out_specs=[full] * 4
        + [
            pl.BlockSpec((chips // 2, up_rows, tile), lambda i: (0, 0, i)),
            pl.BlockSpec((chips // 2, up_rows, tile), lambda i: (0, 0, i)),
            pl.BlockSpec((1, 2, hidden_rows, width), lambda i: (i, 0, 0, 0)),
            pl.BlockSpec((1, 2, hidden_rows, width), lambda i: (i, 0, 0, 0)),
            pl.BlockSpec((1, 1, tile), lambda i: (i, 0, 0)),
        ],
        out_shape=[
            shape((length, width), F32),
            shape((length, width), BF),
            shape((length, width), F32),
            shape((length, width), BF),
            shape((chips // 2, up_rows, hidden), BF),
            shape((chips // 2, up_rows, hidden), BF),
            shape((steps, 2, hidden_rows, width), BF),
            shape((steps, 2, hidden_rows, width), BF),
            shape((steps, 1, tile), F32),
        ],
        scratch_shapes=[
            pltpu.VMEM((width, 2 * length), BF),
            pltpu.VMEM((length, width), F32),
            pltpu.VMEM((length, width), F32),
            pltpu.VMEM((chips // 2, 2, up_rows, tile), BF),
            pltpu.VMEM((2, 2, hidden_rows, width), BF),
        ],
        compiler_params=pltpu.CompilerParams(vmem_limit_bytes=VMEM_LIMIT),
        cost_estimate=pl.CostEstimate(
            flops=24 * length * width * hidden, bytes_accessed=48 * length * width,
            transcendentals=2 * length * hidden,
        ),
        name="feed_forward",
    )(place, n_mine, n_other, g_mine, g_other, late, late, bias.reshape(steps, 1, tile))


def chip_step(
    tokens_in,
    out_grad,
    w_query,
    w_key,
    w_value,
    w_out,
    w_up,
    w_down,
    b_query,
    b_value,
    b_out,
    b_up,
    b_down,
    norm1_gain,
    norm1_shift,
    norm2_gain,
    norm2_shift,
):
    z, x, y, core = (lax.axis_index(name) for name in ("z", "x", "y", "core"))
    z_count = lax.axis_size("z")
    chips = z_count * 4
    half_chips = chips // 2
    _, block, width = tokens_in.shape
    half = width // 2
    rows = w_query.shape[0]
    hidden_rows = w_down.shape[0]
    hidden = hidden_rows * chips

    def own_positions(value):
        return pair(y, pick(value, y, 0), other_y(pick(value, 1 - y, 0))).reshape(2 * block, width)

    three = jnp.stack((w_query, w_key, w_value)).reshape(3, rows, 2, half)
    vectors = (
        b_query, b_value, b_out, b_down, norm1_gain, norm1_shift, norm2_gain, norm2_shift, b_up
    )
    small = jnp.concatenate(vectors)
    unit_rows = 3 * rows + SMALL
    small_rows = jnp.zeros((SMALL, half), BF).at[0, : small.shape[0]].set(small)
    unit = pair(
        core,
        jnp.concatenate((pick(three, core, 2).reshape(3 * rows, half), small_rows)),
        other_core(
            jnp.concatenate((pick(three, 1 - core, 2).reshape(3 * rows, half), small_rows))
        ),
    )
    up_parts = w_up.reshape(rows, chips, 2, hidden_rows)
    up_unit = pair(
        core,
        pick(up_parts, core, 2).reshape(rows, hidden),
        other_core(pick(up_parts, 1 - core, 2).reshape(rows, hidden)),
    )
    up_unit = up_unit.reshape(2 * rows, 2, width)
    late = jnp.concatenate((up_unit[:, 0], up_unit[:, 1], w_down))
    late = lax.all_gather(late, ("z", "x", "y"), axis=0, tiled=False)
    unit = jnp.concatenate(
        (unit.reshape(2 * unit_rows, half), w_out[:, :half], w_out[:, half:])
    )
    pieces = [unit] + [other_z(unit, k) for k in range(1, z_count)]
    both = jnp.stack((pick(tokens_in, y, 0), pick(out_grad, y, 0)))
    both_from = other_y(jnp.stack((pick(tokens_in, 1 - y, 0), pick(out_grad, 1 - y, 0))))
    pieces, both_from = lax.optimization_barrier((pieces, both_from))
    both = pair(y, both, both_from).swapaxes(0, 1).reshape(2, 2 * block, width)
    mine, grad_mine = both[0], both[1]
    other, grad_other = other_core(mine), other_core(grad_mine)
    place = jnp.stack((core, x, y)).astype(jnp.int32)
    gathered = gather_plane(in_order(z, pieces), x, y)
    first = gathered[..., : 2 * unit_rows, :].reshape(z_count, 2, 2, 2, unit_rows, half)
    out_parts = jnp.concatenate(
        (gathered[..., 2 * unit_rows : 2 * unit_rows + rows, :], gathered[..., 2 * unit_rows + rows :, :]),
        axis=-1,
    ).reshape(2, half_chips, rows, width)
    out_c = (
        pair(core, pick(out_parts, core, 0), other_core(pick(out_parts, 1 - core, 0)))
        .swapaxes(0, 1)
        .reshape(half, width)
    )
    three_c = first[..., : 3 * rows, :].reshape(chips * 2, 3, rows, half)
    three_c = three_c.swapaxes(0, 1).reshape(3, width, half)
    small_all = first[..., 3 * rows, : small.shape[0]].reshape(chips * 2, -1)
    vectors = small_all[:, : 8 * rows].reshape(chips * 2, 8, rows).swapaxes(0, 1)
    vectors = vectors.reshape(8, width).astype(F32)
    halves = pick(vectors.reshape(8, 2, half), core, 1)
    bias_u = pick(small_all[:, 8 * rows :].reshape(chips, 2, hidden_rows), core, 1)
    bias_u = bias_u.reshape(hidden).astype(F32)

    length = 4 * block
    heads_shape = shape((length, half), BF)
    normed, queries, keys, values = whole_call(
        enter_kernel,
        [shape((length, width), BF)] + [heads_shape] * 3,
        place, mine, other, vectors, halves, three_c,
        flops=6 * length * width * half, scalars=1,
    )
    mixed, lse = attend(queries, keys, values)
    mine_shape = shape((2 * block, width), F32)
    sent_shape = shape((2 * block, width), BF)
    part, to_other = whole_call(
        out_kernel, [mine_shape, sent_shape], place, mixed, out_c,
        flops=2 * length * width * half, scalars=1,
    )
    residual, normed2 = row_call(middle_kernel, (F32, BF), 0, mine, part, other_core(to_other), vectors)
    late, normed2 = lax.optimization_barrier((late, normed2))
    y_mine, y_other, gn_mine, gn_other, up_keep, up_send, down_keep, down_send, up_sums = feed_forward(
        place, normed2, other_core(normed2), grad_mine, grad_other, late, bias_u, hidden_rows
    )

    up_from, down_from = other_y(up_send), other_x(down_send)
    grad_residual, branch, sums2 = row_call(
        middle_back_kernel, (F32, BF), 4, residual, gn_mine, other_core(gn_other), grad_mine, vectors
    )
    grad_mixed, grad_out = whole_call(
        mixed_back_kernel, [heads_shape, shape((half, width), BF)],
        place, mixed, branch, other_core(branch), out_c,
        flops=4 * length * width * half, scalars=1,
    )
    grad_out = grad_out.reshape(half_chips, 2, rows, width)
    grad_out = pair(
        core,
        pick(grad_out, core, 1),
        other_core(pick(grad_out, 1 - core, 1)),
    ).reshape(z_count, 2, 2, rows, width)
    up_from, down_from, grad_mixed = lax.optimization_barrier((up_from, down_from, grad_mixed))
    ups = plus(up_keep, up_from).reshape(z_count, 2, 2 * rows, hidden)
    downs = plus(down_keep, down_from)
    up_send, down_send = pick(ups, 1 - x, 1).astype(BF), pick(downs, 1 - y, 1).astype(BF)
    up_send, down_send, grad_mixed = lax.optimization_barrier((up_send, down_send, grad_mixed))
    up_from, down_from, out_from = other_x(up_send), other_y(down_send), other_x(pick(grad_out, 1 - x, 1))
    grads = attend_back(
        queries, keys, values, mixed, lse, grad_mixed, 0, half // (2 * DH)
    )
    left_shape = shape((2 * z_count, 4 * rows, half), BF)
    right_shape = shape((z_count, 2, 2 * rows, half), BF)
    left_keep, left_send, right_keep, right_send, sums_heads = whole_call(
        weight_back_kernel,
        [left_shape] * 2 + [right_shape] * 2 + [shape((2, half), F32)],
        place, normed, *grads,
        flops=6 * length * width * half, scalars=1,
        scratch=(
            pltpu.VMEM((2 * z_count, 2, 2 * rows, half), BF),
            pltpu.VMEM((z_count, 2, 2, 2 * rows, half), BF),
        ),
    )
    left_from, right_from = other_y(left_send), other_x(right_send)
    gn_mine, gn_other = whole_call(
        enter_back_kernel,
        [mine_shape, sent_shape],
        place, *grads, three_c,
        flops=6 * length * width * half, scalars=1,
    )
    up_from, down_from, out_from, gn_mine, gn_other, y_mine, y_other = lax.optimization_barrier(
        (up_from, down_from, out_from, gn_mine, gn_other, y_mine, y_other)
    )

    def along_z(value):
        kept = pick(value, z, 0)
        for k in range(1, z_count):
            kept = kept + other_z(pick(value, z ^ k, 0).astype(BF), k).astype(F32)
        return kept

    gn_from = other_core(gn_other)
    ups = plus(pick(ups, x, 1), up_from)
    downs = plus(pick(downs, y, 1), down_from)
    outs = plus(pick(grad_out, x, 1), out_from)
    forward_sum = along_z(jnp.concatenate((ups[..., :width], ups[..., width:], downs), axis=1))
    grad_tokens, sums1 = row_call(
        leave_kernel, (F32,), 2, mine, gn_mine, gn_from, grad_residual, vectors
    )
    output = residual + y_mine + other_core(y_other).astype(F32) + vectors[B_DOWN]
    output = output.astype(BF).reshape(2, block, width)
    grad_tokens = grad_tokens.reshape(2, block, width)

    placed = jnp.where((jnp.arange(2) == core)[None, :, None], sums_heads[:, None], 0.0)
    small_grads = jnp.concatenate(
        (placed.reshape(2, width), sums2[0, :2] + sums2[1, :2], sums1[0] + sums1[1], sums2[0, 2:] + sums2[1, 2:])
    )
    small_grads = small_grads.reshape(8, chips * 2, rows).swapaxes(0, 1).reshape(chips, 2, 8 * rows)
    up_sums = jnp.where(
        (jnp.arange(2) == core)[None, :, None], up_sums.reshape(chips, 1, hidden_rows), 0.0
    )
    small_grads = jnp.concatenate((small_grads, up_sums), axis=2)
    small_grads = small_grads.reshape(z_count, 2, 2, 2, -1)
    small_grads = plus(pick(small_grads, y, 2), other_y(pick(small_grads, 1 - y, 2).astype(BF)))
    to_y = jnp.concatenate((pick(output, 1 - y, 0), pick(grad_tokens, 1 - y, 0).astype(BF)))
    lefts = plus(left_keep, left_from).reshape(z_count, 2, 4 * rows, half)
    rights = plus(right_keep, right_from)
    rights = jnp.concatenate((rights, outs[..., :half], outs[..., half:]), axis=2)
    left_from = other_x(pick(lefts, 1 - x, 1).astype(BF))
    right_from = other_y(pick(rights, 1 - y, 1).astype(BF))
    small_grads = plus(pick(small_grads, x, 1), other_x(pick(small_grads, 1 - x, 1).astype(BF)))
    small_grads = jnp.pad(small_grads, ((0, 0), (0, SMALL - 2), (0, half - small_grads.shape[2])))
    left_from, right_from, to_y = lax.optimization_barrier((left_from, right_from, to_y))
    lefts = plus(pick(lefts, x, 1), left_from)
    rights = plus(pick(rights, y, 1), right_from)
    last = along_z(jnp.concatenate((lefts, rights, small_grads), axis=1))
    from_y = other_y(to_y)
    layer_out = pair(y, pick(output, y, 0), from_y[:block])
    grad_tokens = pair(y, pick(grad_tokens, y, 0), from_y[block:].astype(F32))

    up_mine = forward_sum[: 4 * rows].reshape(2, 2, rows, width)
    down_mine = forward_sum[4 * rows :]
    three_mine = last[: 6 * rows].reshape(3, 2, rows, half)
    out_mine = jnp.concatenate((last[6 * rows : 7 * rows], last[7 * rows : 8 * rows]), axis=1)
    small_mine = last[8 * rows : 8 * rows + 2, : small.shape[0]]
    up_from = other_core(pick(up_mine, 1 - core, 1))
    small_from = jnp.pad(pick(small_mine, 1 - core, 0)[None], ((0, 7), (0, half - small.shape[0])))
    three_from = other_core(
        jnp.concatenate((pick(three_mine, 1 - core, 1).reshape(3 * rows, half), small_from))
    )
    small_sum = pick(small_mine, core, 0) + three_from[3 * rows, : small.shape[0]]
    three_out = pair(core, pick(three_mine, core, 1), three_from[: 3 * rows].reshape(3, rows, half))
    up_out = pair(core, pick(up_mine, core, 1), up_from)
    up_out = up_out.reshape(2, 2, rows, half_chips, hidden_rows)
    up_out = jnp.transpose(up_out, (2, 1, 3, 0, 4)).reshape(rows, 2 * hidden)
    g_q, g_k, g_v = (jnp.concatenate((three_out[0, i], three_out[1, i]), axis=1) for i in range(3))
    g_small = [small_sum[i * rows : (i + 1) * rows] for i in range(8)]
    return (
        layer_out,
        grad_tokens,
        g_q,
        g_k,
        g_v,
        out_mine,
        up_out,
        down_mine,
        g_small[0],
        g_small[1],
        g_small[2],
        small_sum[8 * rows :],
        g_small[3],
        g_small[4],
        g_small[5],
        g_small[6],
        g_small[7],
    )


def solution(mesh):
    dp_count, ctx_count = mesh.shape["dp"], mesh.shape["ctx"]

    def run(*args):
        per_dp = args[0].shape[0] // dp_count
        if ctx_count == 4 and per_dp == 2 and dp_count == 8:
            devices = mesh.devices.reshape(dp_count // 2, 2, ctx_count // 2, 2)
            used = Mesh(devices, ("z", "x", "y", "core"))
            body, dp, ctx = chip_step, ("z", "x"), ("y", "core")
        else:
            used, body, dp, ctx = mesh, on_device, ("dp",), ("ctx",)
        tokens, matrix, bias = P(dp, ctx, None), P(dp + ctx, None), P(dp + ctx)
        return jax.shard_map(
            body,
            mesh=used,
            in_specs=(tokens,) * 2 + (matrix,) * 6 + (bias,) * 9,
            out_specs=(tokens,) * 2 + (matrix,) * 6 + (bias,) * 9,
            check_vma=False,
        )(*args)

    return run
```

```python
import jax
import jax.numpy as jnp
from jax import lax
from jax.experimental import pallas as pl
from jax.experimental.pallas import tpu as pltpu
from jax.sharding import Mesh
from jax.sharding import PartitionSpec as P

HEADS = 12
DH = 64
MICRO = 2


def shifted(value, axis, by):
    peers = lax.axis_size(axis)
    return lax.ppermute(value, axis, [(i, (i + by) % peers) for i in range(peers)])


def as_sent(value):
    return jax.tree.map(lambda a: a.astype(jnp.bfloat16) if a.dtype == jnp.float32 else a, value)


def layer_norm(values, norm_gain, norm_shift):
    centre = values - jnp.mean(values, axis=-1, keepdims=True)
    spread = jnp.mean(centre * centre, axis=-1, keepdims=True)
    return centre * lax.rsqrt(spread + 1e-05) * norm_gain + norm_shift


def gelu_tanh(values):
    return (
        0.5
        * values
        * (1.0 + jnp.tanh(0.7978845608028654 * (values + 0.044715 * values * values * values)))
    )


def project(left, right):
    return jnp.einsum("scd,de->sce", left, right, preferred_element_type=jnp.float32)


def project_back(left, right):
    return jnp.einsum("sce,de->scd", left, right, preferred_element_type=jnp.float32)


def weight_grad(left, right):
    return jnp.einsum("scd,sce->de", left, right, preferred_element_type=jnp.float32)


def column_sum(values):
    return jnp.sum(values.astype(jnp.float32), axis=(0, 1))


def masked_scores(query_heads, key_full, first_pos):
    seq_count, key_len = (key_full.shape[0], key_full.shape[1])
    key_heads = key_full.reshape(seq_count, key_len, HEADS, DH)
    scores = jnp.einsum(
        "sqhd,skhd->shqk", query_heads, key_heads, preferred_element_type=jnp.float32
    )
    row_pos = first_pos + jnp.arange(query_heads.shape[1], dtype=jnp.int32)
    col_pos = jnp.arange(key_len, dtype=jnp.int32)
    allowed = row_pos[:, None] >= col_pos[None, :]
    return (jnp.where(allowed, scores, -1e30), key_heads)


def micro_step(tokens, cotangent, shards, forward_weights):
    (
        w_query,
        w_key,
        w_value,
        w_out,
        w_up,
        w_down,
        b_query,
        b_value,
        b_out,
        b_up,
        b_down,
        gain_one,
        shift_one,
        gain_two,
        shift_two,
    ) = forward_weights
    seq_count, block_rows, width = tokens.shape
    query_scale = DH ** (-0.5)
    first_pos = lax.axis_index("ctx") * block_rows
    gain_one32, shift_one32 = (gain_one.astype(jnp.float32), shift_one.astype(jnp.float32))
    gain_two32, shift_two32 = (gain_two.astype(jnp.float32), shift_two.astype(jnp.float32))
    tokens32 = tokens.astype(jnp.float32)
    normed = layer_norm(tokens32, gain_one32, shift_one32).astype(jnp.bfloat16)
    queries = ((project(normed, w_query) + b_query.astype(jnp.float32)) * query_scale).astype(
        jnp.bfloat16
    )
    keys_local = project(normed, w_key).astype(jnp.bfloat16)
    values_local = (project(normed, w_value) + b_value.astype(jnp.float32)).astype(jnp.bfloat16)
    key_full, value_full = (
        lax.all_gather(keys_local, "ctx", axis=1, tiled=True),
        lax.all_gather(values_local, "ctx", axis=1, tiled=True),
    )
    query_heads = queries.reshape(seq_count, block_rows, HEADS, DH)
    scores, key_heads = masked_scores(query_heads, key_full, first_pos)
    row_max = jnp.max(scores, axis=-1, keepdims=True)
    exp_scores = jnp.exp(scores - row_max)
    row_total = jnp.sum(exp_scores, axis=-1, keepdims=True)
    probs_low = (exp_scores / row_total).astype(jnp.bfloat16)
    value_heads = value_full.reshape(seq_count, value_full.shape[1], HEADS, DH)
    mixed_heads = jnp.einsum(
        "shqk,skhd->sqhd", probs_low, value_heads, preferred_element_type=jnp.float32
    ).reshape(seq_count, block_rows, width)
    mixed_heads = mixed_heads.astype(jnp.bfloat16)
    residual = tokens32 + project(mixed_heads, w_out) + b_out.astype(jnp.float32)
    normed_two = layer_norm(residual, gain_two32, shift_two32).astype(jnp.bfloat16)
    hidden_pre = project(normed_two, w_up) + b_up.astype(jnp.float32)
    active = gelu_tanh(hidden_pre).astype(jnp.bfloat16)
    output = (residual + project(active, w_down) + b_down.astype(jnp.float32)).astype(jnp.bfloat16)
    back_weights = (
        lax.all_gather(shards[0], ("dp", "ctx"), axis=0, tiled=True),
        lax.all_gather(shards[1], ("dp", "ctx"), axis=0, tiled=True),
        lax.all_gather(shards[2], ("dp", "ctx"), axis=0, tiled=True),
        lax.all_gather(shards[3], ("dp", "ctx"), axis=0, tiled=True),
        lax.all_gather(shards[4], ("dp", "ctx"), axis=0, tiled=True),
        lax.all_gather(shards[5], ("dp", "ctx"), axis=0, tiled=True),
        lax.all_gather(shards[6], ("dp", "ctx"), axis=0, tiled=True),
        lax.all_gather(shards[7], ("dp", "ctx"), axis=0, tiled=True),
        lax.all_gather(shards[8], ("dp", "ctx"), axis=0, tiled=True),
        lax.all_gather(shards[9], ("dp", "ctx"), axis=0, tiled=True),
        lax.all_gather(shards[10], ("dp", "ctx"), axis=0, tiled=True),
        lax.all_gather(shards[11], ("dp", "ctx"), axis=0, tiled=True),
        lax.all_gather(shards[12], ("dp", "ctx"), axis=0, tiled=True),
        lax.all_gather(shards[13], ("dp", "ctx"), axis=0, tiled=True),
        lax.all_gather(shards[14], ("dp", "ctx"), axis=0, tiled=True),
    )
    w_query, w_key, w_value, w_out, w_up, w_down = back_weights[:6]
    grad_active = project_back(cotangent, w_down)
    _, gelu_pull = jax.vjp(gelu_tanh, hidden_pre)
    grad_pre = gelu_pull(grad_active)[0].astype(jnp.bfloat16)
    grad_normed_two = project_back(grad_pre, w_up)
    _, norm_pull_two = jax.vjp(layer_norm, residual, gain_two32, shift_two32)
    grad_res_part, grad_gain_two, grad_shift_two = norm_pull_two(grad_normed_two)
    grad_residual = cotangent.astype(jnp.float32) + grad_res_part
    grad_branch = grad_residual.astype(jnp.bfloat16)
    grad_mixed = project_back(grad_branch, w_out).astype(jnp.bfloat16)
    key_full, value_full = (
        lax.all_gather(keys_local, "ctx", axis=1, tiled=True),
        lax.all_gather(values_local, "ctx", axis=1, tiled=True),
    )
    value_heads = value_full.reshape(seq_count, value_full.shape[1], HEADS, DH)
    scores, key_heads = masked_scores(query_heads, key_full, first_pos)
    probs = jnp.exp(scores - row_max) / row_total
    probs_low = probs.astype(jnp.bfloat16)
    grad_heads = grad_mixed.reshape(seq_count, block_rows, HEADS, DH)
    grad_probs = jnp.einsum(
        "sqhd,skhd->shqk", grad_heads, value_heads, preferred_element_type=jnp.float32
    )
    inner_rows = jnp.sum(probs * grad_probs, axis=-1, keepdims=True)
    grad_scores = (probs * (grad_probs - inner_rows)).astype(jnp.bfloat16)
    grad_queries = jnp.einsum(
        "shqk,skhd->sqhd", grad_scores, key_heads, preferred_element_type=jnp.float32
    )
    grad_queries = grad_queries.reshape(seq_count, block_rows, width).astype(jnp.bfloat16)
    query_grad = grad_queries * query_scale

    def key_terms(first_row, row_count):
        score_part = lax.dynamic_slice_in_dim(grad_scores, first_row, row_count, 3)
        prob_part = lax.dynamic_slice_in_dim(probs_low, first_row, row_count, 3)
        key_part = jnp.einsum(
            "shqk,sqhd->kshd", score_part, query_heads, preferred_element_type=jnp.float32
        )
        value_part = jnp.einsum(
            "shqk,sqhd->kshd", prob_part, grad_heads, preferred_element_type=jnp.float32
        )
        return jnp.concatenate(
            (
                key_part.reshape(row_count, seq_count, width),
                value_part.reshape(row_count, seq_count, width),
            ),
            axis=2,
        )

    cycle_size = lax.axis_size("ctx")
    own_index = lax.axis_index("ctx")

    def carry_step(step, carried):
        holder = (own_index - step) % cycle_size
        carried = carried + key_terms(holder * block_rows, block_rows)
        return shifted(carried.astype(jnp.bfloat16), "ctx", 1).astype(carried.dtype)

    start_sums = jnp.zeros((block_rows, seq_count, 2 * width), jnp.float32)
    key_sums = lax.fori_loop(0, cycle_size, carry_step, start_sums)
    key_sums = jnp.transpose(key_sums, (1, 0, 2))
    grad_keys = key_sums[:, :, :width].astype(jnp.bfloat16)
    grad_values = key_sums[:, :, width:].astype(jnp.bfloat16)
    grad_normed = (
        project_back(query_grad, w_query)
        + project_back(grad_keys, w_key)
        + project_back(grad_values, w_value)
    )
    _, norm_pull_one = jax.vjp(layer_norm, tokens32, gain_one32, shift_one32)
    grad_tok_part, grad_gain_one, grad_shift_one = norm_pull_one(grad_normed)
    grad_tokens = grad_residual + grad_tok_part
    small_grads = (grad_gain_one, grad_shift_one, grad_gain_two, grad_shift_two)
    operands = (
        normed,
        query_grad,
        grad_keys,
        grad_values,
        mixed_heads,
        grad_branch,
        normed_two,
        grad_pre,
        active,
        cotangent,
    )
    return (output, grad_tokens, small_grads, operands)


def owner_sum(grads):
    dp_count = lax.axis_size("dp")
    ctx_count = lax.axis_size("ctx")
    blocks = tuple((grad_part.reshape(dp_count, ctx_count, -1) for grad_part in grads))
    first_section = jax.tree.map(
        lambda part, own: part.astype(own.dtype),
        lax.all_to_all(as_sent(blocks), "ctx", split_axis=1, concat_axis=1, tiled=True),
        blocks,
    )
    partial_sums = tuple((jnp.sum(piece, axis=1, keepdims=True) for piece in first_section))
    second_section = jax.tree.map(
        lambda part, own: part.astype(own.dtype),
        lax.all_to_all(as_sent(partial_sums), "dp", split_axis=0, concat_axis=0, tiled=True),
        partial_sums,
    )
    owned = []
    for grad_part, piece in zip(grads, second_section):
        summed = jnp.sum(piece, axis=(0, 1))
        row_count = grad_part.shape[0] // (dp_count * ctx_count)
        owned.append(summed.reshape((row_count,) + grad_part.shape[1:]))
    return owned


def on_device(
    tokens_in,
    out_grad,
    w_query,
    w_key,
    w_value,
    w_out,
    w_up,
    w_down,
    b_query,
    b_value,
    b_out,
    b_up,
    b_down,
    norm1_gain,
    norm1_shift,
    norm2_gain,
    norm2_shift,
):
    shards = (
        w_query,
        w_key,
        w_value,
        w_out,
        w_up,
        w_down,
        b_query,
        b_value,
        b_out,
        b_up,
        b_down,
        norm1_gain,
        norm1_shift,
        norm2_gain,
        norm2_shift,
    )
    per_micro = tokens_in.shape[0] // MICRO
    outputs = []
    grads_in = []
    operand_lists = []
    small_total = None
    for micro_index in range(MICRO):
        lower = micro_index * per_micro
        tokens = tokens_in[lower : lower + per_micro]
        cotangent = out_grad[lower : lower + per_micro]
        forward_weights = (
            lax.all_gather(shards[0], ("dp", "ctx"), axis=0, tiled=True),
            lax.all_gather(shards[1], ("dp", "ctx"), axis=0, tiled=True),
            lax.all_gather(shards[2], ("dp", "ctx"), axis=0, tiled=True),
            lax.all_gather(shards[3], ("dp", "ctx"), axis=0, tiled=True),
            lax.all_gather(shards[4], ("dp", "ctx"), axis=0, tiled=True),
            lax.all_gather(shards[5], ("dp", "ctx"), axis=0, tiled=True),
            lax.all_gather(shards[6], ("dp", "ctx"), axis=0, tiled=True),
            lax.all_gather(shards[7], ("dp", "ctx"), axis=0, tiled=True),
            lax.all_gather(shards[8], ("dp", "ctx"), axis=0, tiled=True),
            lax.all_gather(shards[9], ("dp", "ctx"), axis=0, tiled=True),
            lax.all_gather(shards[10], ("dp", "ctx"), axis=0, tiled=True),
            lax.all_gather(shards[11], ("dp", "ctx"), axis=0, tiled=True),
            lax.all_gather(shards[12], ("dp", "ctx"), axis=0, tiled=True),
            lax.all_gather(shards[13], ("dp", "ctx"), axis=0, tiled=True),
            lax.all_gather(shards[14], ("dp", "ctx"), axis=0, tiled=True),
        )
        output, grad_tokens, small_grads, operands = micro_step(
            tokens, cotangent, shards, forward_weights
        )
        outputs.append(output)
        grads_in.append(grad_tokens)
        operand_lists.append(operands)
        if small_total is None:
            small_total = small_grads
        else:
            small_total = tuple(
                (total_grad + update for total_grad, update in zip(small_total, small_grads))
            )
    joined = tuple(
        (jnp.concatenate([entry[index] for entry in operand_lists], axis=0) for index in range(10))
    )
    (
        normed,
        query_grad,
        grad_keys,
        grad_values,
        mixed_heads,
        grad_branch,
        normed_two,
        grad_pre,
        active,
        cotangent,
    ) = joined
    grads = (
        weight_grad(normed, query_grad),
        weight_grad(normed, grad_keys),
        weight_grad(normed, grad_values),
        weight_grad(mixed_heads, grad_branch),
        weight_grad(normed_two, grad_pre),
        weight_grad(active, cotangent),
        column_sum(query_grad),
        column_sum(grad_values),
        column_sum(grad_branch),
        column_sum(grad_pre),
        column_sum(cotangent),
        small_total[0],
        small_total[1],
        small_total[2],
        small_total[3],
    )
    owned = owner_sum(grads)
    layer_out = jnp.concatenate(outputs, axis=0)
    grad_tokens_all = jnp.concatenate(grads_in, axis=0)
    return (
        layer_out,
        grad_tokens_all,
        owned[0],
        owned[1],
        owned[2],
        owned[3],
        owned[4],
        owned[5],
        owned[6],
        owned[7],
        owned[8],
        owned[9],
        owned[10],
        owned[11],
        owned[12],
        owned[13],
        owned[14],
    )


BF = jnp.bfloat16
F32 = jnp.float32
SMALL = 8


def other_core(value):
    return lax.ppermute(value, "core", [(0, 1), (1, 0)])


def other_x(value):
    return lax.ppermute(value, "x", [(0, 1), (1, 0)])


def other_y(value):
    return lax.ppermute(value, "y", [(0, 1), (1, 0)])


def other_z(value, by):
    return lax.ppermute(value, "z", [(i, i ^ by) for i in range(lax.axis_size("z"))])


def pair(bit, own, received):
    return jnp.stack((jnp.where(bit == 0, own, received), jnp.where(bit == 0, received, own)))


def pick(value, index, axis):
    return lax.dynamic_index_in_dim(value, index, axis, keepdims=False)


def in_order(index, pieces):
    level = list(pieces)
    bit = 0
    ordered = [p[None] for p in level]
    while len(ordered) > 1:
        flag = (index >> bit) & 1
        ordered = [
            jnp.concatenate(
                (jnp.where(flag == 0, a, b), jnp.where(flag == 0, b, a)), axis=0
            )
            for a, b in zip(ordered[::2], ordered[1::2])
        ]
        bit += 1
    return ordered[0]


def gather_plane(along_z, x, y):
    half = along_z.shape[0] // 2
    first, second = along_z[:half], along_z[half:]
    first = pair(x, first, other_x(first))
    second = pair(y, second, other_y(second))
    first = pair(y, first, other_y(first))
    second = pair(x, second, other_x(second))
    return jnp.concatenate((jnp.moveaxis(first, 2, 0).swapaxes(1, 2), jnp.moveaxis(second, 2, 0)))


def plus(kept, received):
    return kept.astype(F32) + received.astype(F32)


VMEM_LIMIT = 56 * 1024 * 1024
QUERY_BLOCK = 256


def lane_masks(dtype):
    lane = lax.broadcasted_iota(jnp.int32, (1, 2 * DH), 1)
    return [(lane < DH).astype(dtype), (lane >= DH).astype(dtype)]


def visible(key_count, query_block):
    key_pos = lax.broadcasted_iota(jnp.int32, (query_block, query_block), 0)
    query_pos = lax.broadcasted_iota(jnp.int32, (query_block, query_block), 1)
    return key_pos <= query_pos


def masked_tail(scores, allowed):
    key_count, query_block = scores.shape
    tail = jnp.where(allowed, scores[key_count - query_block :], -1e30)
    if key_count == query_block:
        return tail
    return jnp.concatenate((scores[: key_count - query_block], tail), axis=0)


def nt(left, right):
    return lax.dot_general(left, right, (((1,), (1,)), ((), ())), preferred_element_type=F32)


def nn(left, right):
    return lax.dot_general(left, right, (((1,), (0,)), ((), ())), preferred_element_type=F32)


def attend_kernel(q_ref, k_ref, v_ref, mixed_ref, lse_ref):
    length = q_ref.shape[0]
    masks = lane_masks(BF)
    allowed = visible(QUERY_BLOCK, QUERY_BLOCK)
    keys = k_ref[...]
    masked_keys = [keys * m for m in masks]
    v_t = v_ref[...].T
    row = lax.broadcasted_iota(jnp.int32, (2 * DH, 1), 0)
    values_t = [jnp.where(row < DH, v_t, jnp.zeros((), BF)), jnp.where(row >= DH, v_t, jnp.zeros((), BF))]
    for start in range(0, length, QUERY_BLOCK):
        stop = start + QUERY_BLOCK
        q = q_ref[start:stop, :]
        mixed_t = None
        for head in range(2):
            scores = masked_tail(nt(masked_keys[head][:stop], q), allowed)
            top = jnp.max(scores, axis=0, keepdims=True)
            powers = jnp.exp(scores - top)
            total = jnp.sum(powers, axis=0, keepdims=True)
            low = (powers * (1.0 / total)).astype(BF)
            part = nn(values_t[head][:, :stop], low)
            mixed_t = part if mixed_t is None else mixed_t + part
            lse_ref[0, head : head + 1, start:stop] = top + jnp.log(total)
        mixed_ref[start:stop, :] = mixed_t.T.astype(BF)


def attend_back_kernel(q_ref, k_ref, v_ref, g_ref, mixed_ref, lse_ref, gq_ref, gk_ref, gv_ref, ka, va):
    length = q_ref.shape[0]
    masks = lane_masks(BF)
    allowed = visible(QUERY_BLOCK, QUERY_BLOCK)
    keys, values = k_ref[...], v_ref[...]
    masked_keys = [keys * m for m in masks]
    masked_values = [values * m for m in masks]
    keys_t = [m.T for m in masked_keys]
    for start in range(length - QUERY_BLOCK, -1, -QUERY_BLOCK):
        stop = start + QUERY_BLOCK
        q, g = q_ref[start:stop, :], g_ref[start:stop, :]
        products = (g.astype(F32) * mixed_ref[start:stop, :].astype(F32)).T
        grad_q_t = None
        grad_k = grad_v = None
        for head in range(2):
            inner = jnp.sum(products[head * DH : (head + 1) * DH], axis=0, keepdims=True)
            scores = masked_tail(nt(masked_keys[head][:stop], q), allowed)
            probs = jnp.exp(scores - lse_ref[0, head : head + 1, start:stop])
            grad_probs = nt(masked_values[head][:stop], g)
            grad_scores = (probs * (grad_probs - inner)).astype(BF)
            part_v = nn(probs.astype(BF), g * masks[head])
            part_k = nn(grad_scores, q * masks[head])
            part_q = nn(keys_t[head][:, :stop], grad_scores)
            grad_v = part_v if head == 0 else grad_v + part_v
            grad_k = part_k if head == 0 else grad_k + part_k
            grad_q_t = part_q if head == 0 else grad_q_t + part_q
        gq_ref[start:stop, :] = grad_q_t.T.astype(BF)
        if stop == length:
            ka[...] = grad_k
            va[...] = grad_v
        else:
            ka[:stop, :] += grad_k
            va[:stop, :] += grad_v
    gk_ref[...] = ka[...].astype(BF)
    gv_ref[...] = va[...].astype(BF)


def attend(queries, keys, values):
    length, width = queries.shape
    pairs = width // (2 * DH)
    block = pl.BlockSpec((length, 2 * DH), lambda i: (0, i))
    return pl.pallas_call(
        attend_kernel,
        grid=(pairs,),
        in_specs=[block] * 3,
        out_specs=[block, pl.BlockSpec((1, 2, length), lambda i: (i, 0, 0))],
        out_shape=[
            jax.ShapeDtypeStruct((length, width), BF),
            jax.ShapeDtypeStruct((pairs, 2, length), F32),
        ],
        compiler_params=pltpu.CompilerParams(vmem_limit_bytes=VMEM_LIMIT),
        cost_estimate=pl.CostEstimate(
            flops=4 * length * length * width, bytes_accessed=8 * length * width,
            transcendentals=length * length * width // DH,
        ),
        name="attend",
    )(queries, keys, values)


def attend_back(queries, keys, values, mixed, lse, grad_mixed, pair_index, pairs):
    length = queries.shape[0]
    block = pl.BlockSpec((length, 2 * DH), lambda i: (0, i + pair_index))
    out_block = pl.BlockSpec((length, 2 * DH), lambda i: (0, i))
    width = pairs * 2 * DH
    return pl.pallas_call(
        attend_back_kernel,
        grid=(pairs,),
        in_specs=[block] * 5 + [pl.BlockSpec((1, 2, length), lambda i: (i + pair_index, 0, 0))],
        out_specs=[out_block] * 3,
        out_shape=[jax.ShapeDtypeStruct((length, width), BF)] * 3,
        scratch_shapes=[pltpu.VMEM((length, 2 * DH), F32)] * 2,
        compiler_params=pltpu.CompilerParams(vmem_limit_bytes=VMEM_LIMIT),
        cost_estimate=pl.CostEstimate(
            flops=10 * length * length * width, bytes_accessed=16 * length * width,
            transcendentals=length * length * width // DH,
        ),
        name="attend_back",
    )(queries, keys, values, grad_mixed, mixed, lse)


def position_blocks(core, block):
    return [
        (b, own, pl.multiple_of(b * 2 * block + (core if own else 1 - core) * block, block))
        for b in range(2)
        for own in (True, False)
    ]


def normalise(values):
    centre = values - jnp.mean(values, axis=-1, keepdims=True)
    spread = jnp.mean(centre * centre, axis=-1, keepdims=True)
    rate = lax.rsqrt(spread + 1e-05)
    return centre * rate, rate


def normalise_back(unit, rate, gain, grad):
    scaled = grad * gain
    return rate * (
        scaled
        - jnp.mean(scaled, axis=-1, keepdims=True)
        - unit * jnp.mean(scaled * unit, axis=-1, keepdims=True)
    )


CORE, X, Y = range(3)
B_QUERY, B_VALUE, B_OUT, B_DOWN, GAIN1, SHIFT1, GAIN2, SHIFT2 = range(8)


def weight(ref, i):
    chips, _, width = ref.shape
    rows = width * 2 // chips
    return ref[:, i * rows : (i + 1) * rows, :].reshape(chips * rows, width)


def enter_kernel(core_ref, mine_ref, other_ref, vec_ref, half_ref, w_ref, n_ref, q_ref, k_ref, v_ref):
    core = core_ref[0]
    block = mine_ref.shape[0] // 2
    for b, own, row in position_blocks(core, block):
        tokens = (mine_ref if own else other_ref)[b * block : (b + 1) * block, :].astype(F32)
        unit, _ = normalise(tokens)
        normed = (unit * vec_ref[GAIN1 : GAIN1 + 1, :] + vec_ref[SHIFT1 : SHIFT1 + 1, :]).astype(BF)
        rows = pl.ds(row, block)
        n_ref[rows, :] = normed
        q = (nn(normed, weight(w_ref, 0)) + half_ref[B_QUERY : B_QUERY + 1, :]) * DH ** (-0.5)
        q_ref[rows, :] = q.astype(BF)
        k_ref[rows, :] = nn(normed, weight(w_ref, 1)).astype(BF)
        v_ref[rows, :] = (nn(normed, weight(w_ref, 2)) + half_ref[B_VALUE : B_VALUE + 1, :]).astype(BF)


def out_kernel(core_ref, mixed_ref, w_ref, mine_ref, other_ref):
    block = mine_ref.shape[0] // 2
    for b, own, row in position_blocks(core_ref[0], block):
        part = nn(mixed_ref[pl.ds(row, block), :], w_ref[...])
        ref = mine_ref if own else other_ref
        ref[b * block : (b + 1) * block, :] = part.astype(ref.dtype)


def middle_kernel(tokens_ref, part_ref, received_ref, vec_ref, residual_ref, n_ref):
    residual = (
        tokens_ref[...].astype(F32)
        + part_ref[...]
        + received_ref[...].astype(F32)
        + vec_ref[B_OUT : B_OUT + 1, :]
    )
    unit, _ = normalise(residual)
    residual_ref[...] = residual
    n_ref[...] = (unit * vec_ref[GAIN2 : GAIN2 + 1, :] + vec_ref[SHIFT2 : SHIFT2 + 1, :]).astype(BF)


def middle_back_kernel(residual_ref, gn_ref, gn_received_ref, g_ref, vec_ref, gr_ref, branch_ref, sums_ref):
    unit, rate = normalise(residual_ref[...])
    grad_normed = gn_ref[...] + gn_received_ref[...].astype(F32)
    cotangent = g_ref[...].astype(F32)
    grad = cotangent + normalise_back(unit, rate, vec_ref[GAIN2 : GAIN2 + 1, :], grad_normed)
    gr_ref[...] = grad
    branch = grad.astype(BF)
    branch_ref[...] = branch
    for i, value in enumerate((branch.astype(F32), cotangent, grad_normed * unit, grad_normed)):
        sums_ref[0, i : i + 1, :] = jnp.sum(value, axis=0, keepdims=True)


def mixed_back_kernel(core_ref, mixed_ref, mine_ref, other_ref, w_ref, gm_ref, gw_ref):
    block = mine_ref.shape[0] // 2
    total = None
    for b, own, row in position_blocks(core_ref[0], block):
        branch = (mine_ref if own else other_ref)[b * block : (b + 1) * block, :]
        rows = pl.ds(row, block)
        gm_ref[rows, :] = nt(branch, w_ref[...]).astype(BF)
        part = nn(mixed_ref[rows, :].T, branch)
        total = part if total is None else total + part
    gw_ref[...] = total.astype(BF)


def weight_back_kernel(
    place_ref, n_ref, q_ref, k_ref, v_ref, left_keep, left_send, right_keep, right_send, sums_ref, by_y, by_x
):
    x, y = place_ref[X], place_ref[Y]
    n_t = n_ref[...].T
    rows = by_y.shape[2]
    grads = [q_ref[...] * jnp.asarray(DH ** (-0.5), BF), k_ref[...], v_ref[...]]
    for i in range(2):
        by_y[...] = nn(n_t, grads[i]).astype(BF).reshape(by_y.shape)
        part = slice(i * rows, (i + 1) * rows)
        left_keep[:, part, :] = by_y[:, pl.ds(y, 1)].reshape(-1, rows, by_y.shape[3])
        left_send[:, part, :] = by_y[:, pl.ds(1 - y, 1)].reshape(-1, rows, by_y.shape[3])
    by_x[...] = nn(n_t, grads[2]).astype(BF).reshape(by_x.shape)
    right_keep[...] = by_x[:, pl.ds(x, 1)].reshape(right_keep.shape)
    right_send[...] = by_x[:, pl.ds(1 - x, 1)].reshape(right_send.shape)
    sums_ref[0:1, :] = jnp.sum(grads[0].astype(F32), axis=0, keepdims=True)
    sums_ref[1:2, :] = jnp.sum(grads[2].astype(F32), axis=0, keepdims=True)


def enter_back_kernel(place_ref, q_ref, k_ref, v_ref, w_ref, mine_ref, other_ref):
    block = mine_ref.shape[0] // 2
    for b, own, row in position_blocks(place_ref[CORE], block):
        rows = pl.ds(row, block)
        part = (
            nt(q_ref[rows, :] * jnp.asarray(DH ** (-0.5), BF), weight(w_ref, 0))
            + nt(k_ref[rows, :], weight(w_ref, 1))
            + nt(v_ref[rows, :], weight(w_ref, 2))
        )
        ref = mine_ref if own else other_ref
        ref[b * block : (b + 1) * block, :] = part.astype(ref.dtype)


def leave_kernel(tokens_ref, gn_ref, gn_received_ref, gr_ref, vec_ref, gt_ref, sums_ref):
    unit, rate = normalise(tokens_ref[...].astype(F32))
    grad_normed = gn_ref[...] + gn_received_ref[...].astype(F32)
    gt_ref[...] = gr_ref[...] + normalise_back(unit, rate, vec_ref[GAIN1 : GAIN1 + 1, :], grad_normed)
    for i, value in enumerate((grad_normed * unit, grad_normed)):
        sums_ref[0, i : i + 1, :] = jnp.sum(value, axis=0, keepdims=True)


def shape(dims, dtype):
    return jax.ShapeDtypeStruct(dims, dtype)


def whole_call(kernel, outs, *args, flops=0, scalars=0, scratch=()):
    in_specs = [
        pl.BlockSpec(memory_space=pltpu.SMEM if i < scalars else pltpu.VMEM)
        for i in range(len(args))
    ]
    moved = sum(a.size * a.dtype.itemsize for a in list(args) + outs)
    return pl.pallas_call(
        kernel,
        in_specs=in_specs,
        out_specs=[pl.BlockSpec(memory_space=pltpu.VMEM)] * len(outs),
        out_shape=outs,
        scratch_shapes=list(scratch),
        compiler_params=pltpu.CompilerParams(vmem_limit_bytes=VMEM_LIMIT),
        cost_estimate=pl.CostEstimate(flops=flops, bytes_accessed=moved, transcendentals=0),
        name=kernel.__name__,
    )(*args)


def row_call(kernel, outs, sums, *args):
    length, width = args[0].shape
    block = length // 2
    rows = pl.BlockSpec((block, width), lambda i: (i, 0))
    out_shape = [shape((length, width), dtype) for dtype in outs]
    out_specs = [rows] * len(outs)
    if sums:
        out_shape.append(shape((2, sums, width), F32))
        out_specs.append(pl.BlockSpec((1, sums, width), lambda i: (i, 0, 0)))
    moved = sum(a.size * a.dtype.itemsize for a in list(args) + out_shape)
    return pl.pallas_call(
        kernel,
        grid=(2,),
        in_specs=[rows] * (len(args) - 1) + [pl.BlockSpec(args[-1].shape, lambda i: (0, 0))],
        out_specs=out_specs,
        out_shape=out_shape,
        compiler_params=pltpu.CompilerParams(vmem_limit_bytes=VMEM_LIMIT),
        cost_estimate=pl.CostEstimate(flops=0, bytes_accessed=moved, transcendentals=0),
        name=kernel.__name__,
    )(*args)


def hidden_kernel(
    place_ref, n_mine, n_other, g_mine, g_other, up_ref, down_ref, bias_ref,
    y_mine, y_other, gn_mine, gn_other, up_keep, up_send, down_keep, down_send, gb_ref,
    n_t, y_sum, gn_sum, up_all, down_all,
):
    step = pl.program_id(0)
    length = n_mine.shape[0]

    @pl.when(step == 0)
    def _():
        n_t[:, :length] = n_mine[...].T
        n_t[:, length:] = n_other[...].T
        for ref in (y_mine, gn_mine, y_sum, gn_sum):
            ref[...] = jnp.zeros(ref.shape, F32)

    up = up_ref[...].reshape(-1, up_ref.shape[2])
    down = down_ref[...].reshape(-1, down_ref.shape[2])
    grad_up = grad_down = bias_sum = None
    for part, (n_ref, g_ref, y_ref, gn_ref) in enumerate(
        ((n_mine, g_mine, y_mine, gn_mine), (n_other, g_other, y_sum, gn_sum))
    ):
        n, g = n_ref[...], g_ref[...]
        pre = nn(n, up) + bias_ref[0]
        square = pre * pre
        bent = jnp.tanh(0.7978845608028654 * (pre + 0.044715 * square * pre))
        half = 0.5 * (1.0 + bent)
        active = (pre * half).astype(BF)
        slope = half + 0.5 * pre * (1.0 - bent * bent) * (
            0.7978845608028654 * (1.0 + 3 * 0.044715 * square)
        )
        grad_pre = (nt(g, down) * slope).astype(BF)
        y_ref[...] += nn(active, down)
        gn_ref[...] += nt(grad_pre, up)
        part_up = nn(n_t[:, part * length : (part + 1) * length], grad_pre)
        part_down = lax.dot_general(active, g, (((0,), (0,)), ((), ())), preferred_element_type=F32)
        part_bias = jnp.sum(grad_pre.astype(F32), axis=0, keepdims=True)
        grad_up = part_up if part == 0 else grad_up + part_up
        grad_down = part_down if part == 0 else grad_down + part_down
        bias_sum = part_bias if part == 0 else bias_sum + part_bias
    x, y = place_ref[X], place_ref[Y]
    up_all[...] = grad_up.astype(BF).reshape(up_all.shape)
    up_keep[...] = up_all[:, pl.ds(y, 1)].reshape(up_keep.shape)
    up_send[...] = up_all[:, pl.ds(1 - y, 1)].reshape(up_send.shape)
    down_all[...] = grad_down.astype(BF).reshape(down_all.shape)
    down_keep[...] = down_all[pl.ds(x, 1)].reshape(down_keep.shape)
    down_send[...] = down_all[pl.ds(1 - x, 1)].reshape(down_send.shape)
    gb_ref[0] = bias_sum

    @pl.when(step == pl.num_programs(0) - 1)
    def _():
        y_other[...] = y_sum[...].astype(BF)
        gn_other[...] = gn_sum[...].astype(BF)


def feed_forward(place, n_mine, n_other, g_mine, g_other, late, bias, hidden_rows):
    length, width = n_mine.shape
    chips = late.shape[0]
    steps = chips // 4
    tile = chips * hidden_rows // steps
    up_rows = width // chips
    per_half = steps // 2
    down_chips = chips // steps
    full = pl.BlockSpec((length, width), lambda i: (0, 0))
    hidden = tile * steps
    return pl.pallas_call(
        hidden_kernel,
        grid=(steps,),
        in_specs=[pl.BlockSpec(memory_space=pltpu.SMEM)] + [full] * 4
        + [
            pl.BlockSpec((chips, up_rows, tile), lambda i: (0, i // per_half, i % per_half)),
            pl.BlockSpec((down_chips, hidden_rows, width), lambda i: (i, 1, 0)),
            pl.BlockSpec((1, 1, tile), lambda i: (i, 0, 0)),
        ],
        out_specs=[full] * 4
        + [
            pl.BlockSpec((chips // 2, up_rows, tile), lambda i: (0, 0, i)),
            pl.BlockSpec((chips // 2, up_rows, tile), lambda i: (0, 0, i)),
            pl.BlockSpec((1, 2, hidden_rows, width), lambda i: (i, 0, 0, 0)),
            pl.BlockSpec((1, 2, hidden_rows, width), lambda i: (i, 0, 0, 0)),
            pl.BlockSpec((1, 1, tile), lambda i: (i, 0, 0)),
        ],
        out_shape=[
            shape((length, width), F32),
            shape((length, width), BF),
            shape((length, width), F32),
            shape((length, width), BF),
            shape((chips // 2, up_rows, hidden), BF),
            shape((chips // 2, up_rows, hidden), BF),
            shape((steps, 2, hidden_rows, width), BF),
            shape((steps, 2, hidden_rows, width), BF),
            shape((steps, 1, tile), F32),
        ],
        scratch_shapes=[
            pltpu.VMEM((width, 2 * length), BF),
            pltpu.VMEM((length, width), F32),
            pltpu.VMEM((length, width), F32),
            pltpu.VMEM((chips // 2, 2, up_rows, tile), BF),
            pltpu.VMEM((2, 2, hidden_rows, width), BF),
        ],
        compiler_params=pltpu.CompilerParams(vmem_limit_bytes=VMEM_LIMIT),
        cost_estimate=pl.CostEstimate(
            flops=24 * length * width * hidden, bytes_accessed=48 * length * width,
            transcendentals=2 * length * hidden,
        ),
        name="feed_forward",
    )(place, n_mine, n_other, g_mine, g_other, late, late, bias.reshape(steps, 1, tile))


def chip_step(
    tokens_in,
    out_grad,
    w_query,
    w_key,
    w_value,
    w_out,
    w_up,
    w_down,
    b_query,
    b_value,
    b_out,
    b_up,
    b_down,
    norm1_gain,
    norm1_shift,
    norm2_gain,
    norm2_shift,
):
    z, x, y, core = (lax.axis_index(name) for name in ("z", "x", "y", "core"))
    z_count = lax.axis_size("z")
    chips = z_count * 4
    half_chips = chips // 2
    _, block, width = tokens_in.shape
    half = width // 2
    rows = w_query.shape[0]
    hidden_rows = w_down.shape[0]
    hidden = hidden_rows * chips

    def own_positions(value):
        return pair(y, pick(value, y, 0), other_y(pick(value, 1 - y, 0))).reshape(2 * block, width)

    three = jnp.stack((w_query, w_key, w_value)).reshape(3, rows, 2, half)
    vectors = (
        b_query, b_value, b_out, b_down, norm1_gain, norm1_shift, norm2_gain, norm2_shift, b_up
    )
    small = jnp.concatenate(vectors)
    unit_rows = 3 * rows + SMALL
    small_rows = jnp.zeros((SMALL, half), BF).at[0, : small.shape[0]].set(small)
    own = jnp.concatenate((pick(three, core, 2).reshape(3 * rows, half), small_rows))
    unit = pair(
        core,
        own,
        other_core(
            jnp.concatenate((pick(three, 1 - core, 2).reshape(3 * rows, half), small_rows))
        ),
    )
    up_parts = w_up.reshape(rows, chips, 2, hidden_rows)
    up_unit = pair(
        core,
        pick(up_parts, core, 2).reshape(rows, hidden),
        other_core(pick(up_parts, 1 - core, 2).reshape(rows, hidden)),
    )
    up_unit = up_unit.reshape(2 * rows, 2, width)
    late = jnp.concatenate((up_unit[:, 0], up_unit[:, 1], w_down))
    late = lax.all_gather(late, ("z", "x", "y"), axis=0, tiled=False)
    threes = unit[:, : 3 * rows].reshape(2, 3, rows, half).swapaxes(0, 1).reshape(6 * rows, half)
    unit = jnp.concatenate(
        (threes, unit[:, 3 * rows :].reshape(2 * SMALL, half), w_out[:, :half], w_out[:, half:])
    )
    pieces = [unit] + [other_z(unit, k) for k in range(1, z_count)]
    both = jnp.stack((pick(tokens_in, y, 0), pick(out_grad, y, 0)))
    both_from = other_y(jnp.stack((pick(tokens_in, 1 - y, 0), pick(out_grad, 1 - y, 0))))
    pieces, both_from = lax.optimization_barrier((pieces, both_from))
    both = pair(y, both, both_from).swapaxes(0, 1).reshape(2, 2 * block, width)
    mine, grad_mine = both[0], both[1]
    other, grad_other = other_core(mine), other_core(grad_mine)
    place = jnp.stack((core, x, y)).astype(jnp.int32)
    gathered = gather_plane(in_order(z, pieces), x, y)
    out_parts = jnp.concatenate(
        (gathered[..., 2 * unit_rows : 2 * unit_rows + rows, :], gathered[..., 2 * unit_rows + rows :, :]),
        axis=-1,
    ).reshape(2, half_chips, rows, width)
    out_c = (
        pair(core, pick(out_parts, core, 0), other_core(pick(out_parts, 1 - core, 0)))
        .swapaxes(0, 1)
        .reshape(half, width)
    )
    gathered = gathered.reshape(chips, -1, half)
    small_all = gathered[:, 6 * rows : 6 * rows + 2 * SMALL].reshape(chips * 2, SMALL, half)
    small_all = small_all[:, 0, : small.shape[0]]
    vectors = small_all[:, : 8 * rows].reshape(chips * 2, 8, rows).swapaxes(0, 1)
    vectors = vectors.reshape(8, width).astype(F32)
    halves = pick(vectors.reshape(8, 2, half), core, 1)
    bias_u = pick(small_all[:, 8 * rows :].reshape(chips, 2, hidden_rows), core, 1)
    bias_u = bias_u.reshape(hidden).astype(F32)

    length = 4 * block
    heads_shape = shape((length, half), BF)
    normed, queries, keys, values = whole_call(
        enter_kernel,
        [shape((length, width), BF)] + [heads_shape] * 3,
        place, mine, other, vectors, halves, gathered,
        flops=6 * length * width * half, scalars=1,
    )
    mixed, lse = attend(queries, keys, values)
    mine_shape = shape((2 * block, width), F32)
    sent_shape = shape((2 * block, width), BF)
    part, to_other = whole_call(
        out_kernel, [mine_shape, sent_shape], place, mixed, out_c,
        flops=2 * length * width * half, scalars=1,
    )
    residual, normed2 = row_call(middle_kernel, (F32, BF), 0, mine, part, other_core(to_other), vectors)
    late, normed2 = lax.optimization_barrier((late, normed2))
    y_mine, y_other, gn_mine, gn_other, up_keep, up_send, down_keep, down_send, up_sums = feed_forward(
        place, normed2, other_core(normed2), grad_mine, grad_other, late, bias_u, hidden_rows
    )

    up_from, down_from = other_y(up_send), other_x(down_send)
    grad_residual, branch, sums2 = row_call(
        middle_back_kernel, (F32, BF), 4, residual, gn_mine, other_core(gn_other), grad_mine, vectors
    )
    grad_mixed, grad_out = whole_call(
        mixed_back_kernel, [heads_shape, shape((half, width), BF)],
        place, mixed, branch, other_core(branch), out_c,
        flops=4 * length * width * half, scalars=1,
    )
    grad_out = grad_out.reshape(half_chips, 2, rows, width)
    grad_out = pair(
        core,
        pick(grad_out, core, 1),
        other_core(pick(grad_out, 1 - core, 1)),
    ).reshape(z_count, 2, 2, rows, width)
    up_from, down_from, grad_mixed = lax.optimization_barrier((up_from, down_from, grad_mixed))
    ups = plus(up_keep, up_from).reshape(z_count, 2, 2 * rows, hidden)
    downs = plus(down_keep, down_from)
    up_send, down_send = pick(ups, 1 - x, 1).astype(BF), pick(downs, 1 - y, 1).astype(BF)
    up_send, down_send, grad_mixed = lax.optimization_barrier((up_send, down_send, grad_mixed))
    up_from, down_from, out_from = other_x(up_send), other_y(down_send), other_x(pick(grad_out, 1 - x, 1))
    grads = attend_back(
        queries, keys, values, mixed, lse, grad_mixed, 0, half // (2 * DH)
    )
    up_from, down_from, out_from, grads = lax.optimization_barrier(
        (up_from, down_from, out_from, grads)
    )
    left_shape = shape((2 * z_count, 4 * rows, half), BF)
    right_shape = shape((z_count, 2, 2 * rows, half), BF)
    left_keep, left_send, right_keep, right_send, sums_heads = whole_call(
        weight_back_kernel,
        [left_shape] * 2 + [right_shape] * 2 + [shape((2, half), F32)],
        place, normed, *grads,
        flops=6 * length * width * half, scalars=1,
        scratch=(
            pltpu.VMEM((2 * z_count, 2, 2 * rows, half), BF),
            pltpu.VMEM((z_count, 2, 2, 2 * rows, half), BF),
        ),
    )
    left_send, right_send, grads, y_mine, y_other = lax.optimization_barrier(
        (left_send, right_send, grads, y_mine, y_other)
    )
    left_from, right_from = other_y(left_send), other_x(right_send)
    gn_mine, gn_other = whole_call(
        enter_back_kernel,
        [mine_shape, sent_shape],
        place, *grads, gathered,
        flops=6 * length * width * half, scalars=1,
    )
    def along_z(value):
        received = [other_z(pick(value, z ^ k, 0).astype(BF), k) for k in range(1, z_count)]
        return pick(value, z, 0), received

    gn_from = other_core(gn_other)
    ups = plus(pick(ups, x, 1), up_from)
    downs = plus(pick(downs, y, 1), down_from)
    outs = plus(pick(grad_out, x, 1), out_from)
    forward_kept, forward_from = along_z(jnp.concatenate((ups[..., :width], ups[..., width:], downs), axis=1))
    grad_tokens, sums1 = row_call(
        leave_kernel, (F32,), 2, mine, gn_mine, gn_from, grad_residual, vectors
    )
    left_from, right_from, grad_tokens = lax.optimization_barrier((left_from, right_from, grad_tokens))
    output = residual + y_mine + other_core(y_other).astype(F32) + vectors[B_DOWN]
    output = output.astype(BF).reshape(2, block, width)
    grad_tokens = grad_tokens.reshape(2, block, width)

    placed = jnp.where((jnp.arange(2) == core)[None, :, None], sums_heads[:, None], 0.0)
    small_grads = jnp.concatenate(
        (placed.reshape(2, width), sums2[0, :2] + sums2[1, :2], sums1[0] + sums1[1], sums2[0, 2:] + sums2[1, 2:])
    )
    small_grads = small_grads.reshape(8, chips * 2, rows).swapaxes(0, 1).reshape(chips, 2, 8 * rows)
    up_sums = jnp.where(
        (jnp.arange(2) == core)[None, :, None], up_sums.reshape(chips, 1, hidden_rows), 0.0
    )
    small_grads = jnp.concatenate((small_grads, up_sums), axis=2)
    small_grads = small_grads.reshape(z_count, 2, 2, 2, -1)
    small_grads = plus(pick(small_grads, y, 2), other_y(pick(small_grads, 1 - y, 2).astype(BF)))
    to_y = jnp.concatenate((pick(output, 1 - y, 0), pick(grad_tokens, 1 - y, 0).astype(BF)))
    lefts = plus(left_keep, left_from).reshape(z_count, 2, 4 * rows, half)
    rights = plus(right_keep, right_from)
    rights = jnp.concatenate((rights, outs[..., :half], outs[..., half:]), axis=2)
    left_from = other_x(pick(lefts, 1 - x, 1).astype(BF))
    right_from = other_y(pick(rights, 1 - y, 1).astype(BF))
    small_from = other_x(pick(small_grads, 1 - x, 1).astype(BF))
    left_from, right_from, to_y, forward_from, small_from = lax.optimization_barrier(
        (left_from, right_from, to_y, forward_from, small_from)
    )
    small_grads = plus(pick(small_grads, x, 1), small_from)
    small_grads = jnp.pad(small_grads, ((0, 0), (0, SMALL - 2), (0, half - small_grads.shape[2])))
    forward_sum = forward_kept
    for part in forward_from:
        forward_sum = plus(forward_sum, part)
    lefts = plus(pick(lefts, x, 1), left_from)
    rights = plus(pick(rights, y, 1), right_from)
    last, last_from = along_z(jnp.concatenate((lefts, rights, small_grads), axis=1))
    for part in last_from:
        last = plus(last, part)
    from_y = other_y(to_y)
    layer_out = pair(y, pick(output, y, 0), from_y[:block])
    grad_tokens = pair(y, pick(grad_tokens, y, 0), from_y[block:].astype(F32))

    up_mine = forward_sum[: 4 * rows].reshape(2, 2, rows, width)
    down_mine = forward_sum[4 * rows :]
    three_mine = last[: 6 * rows].reshape(3, 2, rows, half)
    out_mine = jnp.concatenate((last[6 * rows : 7 * rows], last[7 * rows : 8 * rows]), axis=1)
    small_mine = last[8 * rows : 8 * rows + 2, : small.shape[0]]
    up_from = other_core(pick(up_mine, 1 - core, 1))
    small_from = jnp.pad(pick(small_mine, 1 - core, 0)[None], ((0, 7), (0, half - small.shape[0])))
    three_from = other_core(
        jnp.concatenate((pick(three_mine, 1 - core, 1).reshape(3 * rows, half), small_from))
    )
    small_sum = pick(small_mine, core, 0) + three_from[3 * rows, : small.shape[0]]
    three_out = pair(core, pick(three_mine, core, 1), three_from[: 3 * rows].reshape(3, rows, half))
    up_out = pair(core, pick(up_mine, core, 1), up_from)
    up_out = up_out.reshape(2, 2, rows, half_chips, hidden_rows)
    up_out = jnp.transpose(up_out, (2, 1, 3, 0, 4)).reshape(rows, 2 * hidden)
    g_q, g_k, g_v = (jnp.concatenate((three_out[0, i], three_out[1, i]), axis=1) for i in range(3))
    g_small = [small_sum[i * rows : (i + 1) * rows] for i in range(8)]
    return (
        layer_out,
        grad_tokens,
        g_q,
        g_k,
        g_v,
        out_mine,
        up_out,
        down_mine,
        g_small[0],
        g_small[1],
        g_small[2],
        small_sum[8 * rows :],
        g_small[3],
        g_small[4],
        g_small[5],
        g_small[6],
        g_small[7],
    )


def solution(mesh):
    dp_count, ctx_count = mesh.shape["dp"], mesh.shape["ctx"]

    def run(*args):
        per_dp = args[0].shape[0] // dp_count
        if ctx_count == 4 and per_dp == 2 and dp_count == 8:
            devices = mesh.devices.reshape(dp_count // 2, 2, ctx_count // 2, 2)
            used = Mesh(devices, ("z", "x", "y", "core"))
            body, dp, ctx = chip_step, ("z", "x"), ("y", "core")
        else:
            used, body, dp, ctx = mesh, on_device, ("dp",), ("ctx",)
        tokens, matrix, bias = P(dp, ctx, None), P(dp + ctx, None), P(dp + ctx)
        return jax.shard_map(
            body,
            mesh=used,
            in_specs=(tokens,) * 2 + (matrix,) * 6 + (bias,) * 9,
            out_specs=(tokens,) * 2 + (matrix,) * 6 + (bias,) * 9,
            check_vma=False,
        )(*args)

    return run
```

```python
import jax
import jax.numpy as jnp
from jax import lax
from jax.experimental import pallas as pl
from jax.experimental.pallas import tpu as pltpu
from jax.sharding import Mesh
from jax.sharding import PartitionSpec as P

HEADS = 12
DH = 64
MICRO = 2


def shifted(value, axis, by):
    peers = lax.axis_size(axis)
    return lax.ppermute(value, axis, [(i, (i + by) % peers) for i in range(peers)])


def as_sent(value):
    return jax.tree.map(lambda a: a.astype(jnp.bfloat16) if a.dtype == jnp.float32 else a, value)


def layer_norm(values, norm_gain, norm_shift):
    centre = values - jnp.mean(values, axis=-1, keepdims=True)
    spread = jnp.mean(centre * centre, axis=-1, keepdims=True)
    return centre * lax.rsqrt(spread + 1e-05) * norm_gain + norm_shift


def gelu_tanh(values):
    return (
        0.5
        * values
        * (1.0 + jnp.tanh(0.7978845608028654 * (values + 0.044715 * values * values * values)))
    )


def project(left, right):
    return jnp.einsum("scd,de->sce", left, right, preferred_element_type=jnp.float32)


def project_back(left, right):
    return jnp.einsum("sce,de->scd", left, right, preferred_element_type=jnp.float32)


def weight_grad(left, right):
    return jnp.einsum("scd,sce->de", left, right, preferred_element_type=jnp.float32)


def column_sum(values):
    return jnp.sum(values.astype(jnp.float32), axis=(0, 1))


def masked_scores(query_heads, key_full, first_pos):
    seq_count, key_len = (key_full.shape[0], key_full.shape[1])
    key_heads = key_full.reshape(seq_count, key_len, HEADS, DH)
    scores = jnp.einsum(
        "sqhd,skhd->shqk", query_heads, key_heads, preferred_element_type=jnp.float32
    )
    row_pos = first_pos + jnp.arange(query_heads.shape[1], dtype=jnp.int32)
    col_pos = jnp.arange(key_len, dtype=jnp.int32)
    allowed = row_pos[:, None] >= col_pos[None, :]
    return (jnp.where(allowed, scores, -1e30), key_heads)


def micro_step(tokens, cotangent, shards, forward_weights):
    (
        w_query,
        w_key,
        w_value,
        w_out,
        w_up,
        w_down,
        b_query,
        b_value,
        b_out,
        b_up,
        b_down,
        gain_one,
        shift_one,
        gain_two,
        shift_two,
    ) = forward_weights
    seq_count, block_rows, width = tokens.shape
    query_scale = DH ** (-0.5)
    first_pos = lax.axis_index("ctx") * block_rows
    gain_one32, shift_one32 = (gain_one.astype(jnp.float32), shift_one.astype(jnp.float32))
    gain_two32, shift_two32 = (gain_two.astype(jnp.float32), shift_two.astype(jnp.float32))
    tokens32 = tokens.astype(jnp.float32)
    normed = layer_norm(tokens32, gain_one32, shift_one32).astype(jnp.bfloat16)
    queries = ((project(normed, w_query) + b_query.astype(jnp.float32)) * query_scale).astype(
        jnp.bfloat16
    )
    keys_local = project(normed, w_key).astype(jnp.bfloat16)
    values_local = (project(normed, w_value) + b_value.astype(jnp.float32)).astype(jnp.bfloat16)
    key_full, value_full = (
        lax.all_gather(keys_local, "ctx", axis=1, tiled=True),
        lax.all_gather(values_local, "ctx", axis=1, tiled=True),
    )
    query_heads = queries.reshape(seq_count, block_rows, HEADS, DH)
    scores, key_heads = masked_scores(query_heads, key_full, first_pos)
    row_max = jnp.max(scores, axis=-1, keepdims=True)
    exp_scores = jnp.exp(scores - row_max)
    row_total = jnp.sum(exp_scores, axis=-1, keepdims=True)
    probs_low = (exp_scores / row_total).astype(jnp.bfloat16)
    value_heads = value_full.reshape(seq_count, value_full.shape[1], HEADS, DH)
    mixed_heads = jnp.einsum(
        "shqk,skhd->sqhd", probs_low, value_heads, preferred_element_type=jnp.float32
    ).reshape(seq_count, block_rows, width)
    mixed_heads = mixed_heads.astype(jnp.bfloat16)
    residual = tokens32 + project(mixed_heads, w_out) + b_out.astype(jnp.float32)
    normed_two = layer_norm(residual, gain_two32, shift_two32).astype(jnp.bfloat16)
    hidden_pre = project(normed_two, w_up) + b_up.astype(jnp.float32)
    active = gelu_tanh(hidden_pre).astype(jnp.bfloat16)
    output = (residual + project(active, w_down) + b_down.astype(jnp.float32)).astype(jnp.bfloat16)
    back_weights = (
        lax.all_gather(shards[0], ("dp", "ctx"), axis=0, tiled=True),
        lax.all_gather(shards[1], ("dp", "ctx"), axis=0, tiled=True),
        lax.all_gather(shards[2], ("dp", "ctx"), axis=0, tiled=True),
        lax.all_gather(shards[3], ("dp", "ctx"), axis=0, tiled=True),
        lax.all_gather(shards[4], ("dp", "ctx"), axis=0, tiled=True),
        lax.all_gather(shards[5], ("dp", "ctx"), axis=0, tiled=True),
        lax.all_gather(shards[6], ("dp", "ctx"), axis=0, tiled=True),
        lax.all_gather(shards[7], ("dp", "ctx"), axis=0, tiled=True),
        lax.all_gather(shards[8], ("dp", "ctx"), axis=0, tiled=True),
        lax.all_gather(shards[9], ("dp", "ctx"), axis=0, tiled=True),
        lax.all_gather(shards[10], ("dp", "ctx"), axis=0, tiled=True),
        lax.all_gather(shards[11], ("dp", "ctx"), axis=0, tiled=True),
        lax.all_gather(shards[12], ("dp", "ctx"), axis=0, tiled=True),
        lax.all_gather(shards[13], ("dp", "ctx"), axis=0, tiled=True),
        lax.all_gather(shards[14], ("dp", "ctx"), axis=0, tiled=True),
    )
    w_query, w_key, w_value, w_out, w_up, w_down = back_weights[:6]
    grad_active = project_back(cotangent, w_down)
    _, gelu_pull = jax.vjp(gelu_tanh, hidden_pre)
    grad_pre = gelu_pull(grad_active)[0].astype(jnp.bfloat16)
    grad_normed_two = project_back(grad_pre, w_up)
    _, norm_pull_two = jax.vjp(layer_norm, residual, gain_two32, shift_two32)
    grad_res_part, grad_gain_two, grad_shift_two = norm_pull_two(grad_normed_two)
    grad_residual = cotangent.astype(jnp.float32) + grad_res_part
    grad_branch = grad_residual.astype(jnp.bfloat16)
    grad_mixed = project_back(grad_branch, w_out).astype(jnp.bfloat16)
    key_full, value_full = (
        lax.all_gather(keys_local, "ctx", axis=1, tiled=True),
        lax.all_gather(values_local, "ctx", axis=1, tiled=True),
    )
    value_heads = value_full.reshape(seq_count, value_full.shape[1], HEADS, DH)
    scores, key_heads = masked_scores(query_heads, key_full, first_pos)
    probs = jnp.exp(scores - row_max) / row_total
    probs_low = probs.astype(jnp.bfloat16)
    grad_heads = grad_mixed.reshape(seq_count, block_rows, HEADS, DH)
    grad_probs = jnp.einsum(
        "sqhd,skhd->shqk", grad_heads, value_heads, preferred_element_type=jnp.float32
    )
    inner_rows = jnp.sum(probs * grad_probs, axis=-1, keepdims=True)
    grad_scores = (probs * (grad_probs - inner_rows)).astype(jnp.bfloat16)
    grad_queries = jnp.einsum(
        "shqk,skhd->sqhd", grad_scores, key_heads, preferred_element_type=jnp.float32
    )
    grad_queries = grad_queries.reshape(seq_count, block_rows, width).astype(jnp.bfloat16)
    query_grad = grad_queries * query_scale

    def key_terms(first_row, row_count):
        score_part = lax.dynamic_slice_in_dim(grad_scores, first_row, row_count, 3)
        prob_part = lax.dynamic_slice_in_dim(probs_low, first_row, row_count, 3)
        key_part = jnp.einsum(
            "shqk,sqhd->kshd", score_part, query_heads, preferred_element_type=jnp.float32
        )
        value_part = jnp.einsum(
            "shqk,sqhd->kshd", prob_part, grad_heads, preferred_element_type=jnp.float32
        )
        return jnp.concatenate(
            (
                key_part.reshape(row_count, seq_count, width),
                value_part.reshape(row_count, seq_count, width),
            ),
            axis=2,
        )

    cycle_size = lax.axis_size("ctx")
    own_index = lax.axis_index("ctx")

    def carry_step(step, carried):
        holder = (own_index - step) % cycle_size
        carried = carried + key_terms(holder * block_rows, block_rows)
        return shifted(carried.astype(jnp.bfloat16), "ctx", 1).astype(carried.dtype)

    start_sums = jnp.zeros((block_rows, seq_count, 2 * width), jnp.float32)
    key_sums = lax.fori_loop(0, cycle_size, carry_step, start_sums)
    key_sums = jnp.transpose(key_sums, (1, 0, 2))
    grad_keys = key_sums[:, :, :width].astype(jnp.bfloat16)
    grad_values = key_sums[:, :, width:].astype(jnp.bfloat16)
    grad_normed = (
        project_back(query_grad, w_query)
        + project_back(grad_keys, w_key)
        + project_back(grad_values, w_value)
    )
    _, norm_pull_one = jax.vjp(layer_norm, tokens32, gain_one32, shift_one32)
    grad_tok_part, grad_gain_one, grad_shift_one = norm_pull_one(grad_normed)
    grad_tokens = grad_residual + grad_tok_part
    small_grads = (grad_gain_one, grad_shift_one, grad_gain_two, grad_shift_two)
    operands = (
        normed,
        query_grad,
        grad_keys,
        grad_values,
        mixed_heads,
        grad_branch,
        normed_two,
        grad_pre,
        active,
        cotangent,
    )
    return (output, grad_tokens, small_grads, operands)


def owner_sum(grads):
    dp_count = lax.axis_size("dp")
    ctx_count = lax.axis_size("ctx")
    blocks = tuple((grad_part.reshape(dp_count, ctx_count, -1) for grad_part in grads))
    first_section = jax.tree.map(
        lambda part, own: part.astype(own.dtype),
        lax.all_to_all(as_sent(blocks), "ctx", split_axis=1, concat_axis=1, tiled=True),
        blocks,
    )
    partial_sums = tuple((jnp.sum(piece, axis=1, keepdims=True) for piece in first_section))
    second_section = jax.tree.map(
        lambda part, own: part.astype(own.dtype),
        lax.all_to_all(as_sent(partial_sums), "dp", split_axis=0, concat_axis=0, tiled=True),
        partial_sums,
    )
    owned = []
    for grad_part, piece in zip(grads, second_section):
        summed = jnp.sum(piece, axis=(0, 1))
        row_count = grad_part.shape[0] // (dp_count * ctx_count)
        owned.append(summed.reshape((row_count,) + grad_part.shape[1:]))
    return owned


def on_device(
    tokens_in,
    out_grad,
    w_query,
    w_key,
    w_value,
    w_out,
    w_up,
    w_down,
    b_query,
    b_value,
    b_out,
    b_up,
    b_down,
    norm1_gain,
    norm1_shift,
    norm2_gain,
    norm2_shift,
):
    shards = (
        w_query,
        w_key,
        w_value,
        w_out,
        w_up,
        w_down,
        b_query,
        b_value,
        b_out,
        b_up,
        b_down,
        norm1_gain,
        norm1_shift,
        norm2_gain,
        norm2_shift,
    )
    per_micro = tokens_in.shape[0] // MICRO
    outputs = []
    grads_in = []
    operand_lists = []
    small_total = None
    for micro_index in range(MICRO):
        lower = micro_index * per_micro
        tokens = tokens_in[lower : lower + per_micro]
        cotangent = out_grad[lower : lower + per_micro]
        forward_weights = (
            lax.all_gather(shards[0], ("dp", "ctx"), axis=0, tiled=True),
            lax.all_gather(shards[1], ("dp", "ctx"), axis=0, tiled=True),
            lax.all_gather(shards[2], ("dp", "ctx"), axis=0, tiled=True),
            lax.all_gather(shards[3], ("dp", "ctx"), axis=0, tiled=True),
            lax.all_gather(shards[4], ("dp", "ctx"), axis=0, tiled=True),
            lax.all_gather(shards[5], ("dp", "ctx"), axis=0, tiled=True),
            lax.all_gather(shards[6], ("dp", "ctx"), axis=0, tiled=True),
            lax.all_gather(shards[7], ("dp", "ctx"), axis=0, tiled=True),
            lax.all_gather(shards[8], ("dp", "ctx"), axis=0, tiled=True),
            lax.all_gather(shards[9], ("dp", "ctx"), axis=0, tiled=True),
            lax.all_gather(shards[10], ("dp", "ctx"), axis=0, tiled=True),
            lax.all_gather(shards[11], ("dp", "ctx"), axis=0, tiled=True),
            lax.all_gather(shards[12], ("dp", "ctx"), axis=0, tiled=True),
            lax.all_gather(shards[13], ("dp", "ctx"), axis=0, tiled=True),
            lax.all_gather(shards[14], ("dp", "ctx"), axis=0, tiled=True),
        )
        output, grad_tokens, small_grads, operands = micro_step(
            tokens, cotangent, shards, forward_weights
        )
        outputs.append(output)
        grads_in.append(grad_tokens)
        operand_lists.append(operands)
        if small_total is None:
            small_total = small_grads
        else:
            small_total = tuple(
                (total_grad + update for total_grad, update in zip(small_total, small_grads))
            )
    joined = tuple(
        (jnp.concatenate([entry[index] for entry in operand_lists], axis=0) for index in range(10))
    )
    (
        normed,
        query_grad,
        grad_keys,
        grad_values,
        mixed_heads,
        grad_branch,
        normed_two,
        grad_pre,
        active,
        cotangent,
    ) = joined
    grads = (
        weight_grad(normed, query_grad),
        weight_grad(normed, grad_keys),
        weight_grad(normed, grad_values),
        weight_grad(mixed_heads, grad_branch),
        weight_grad(normed_two, grad_pre),
        weight_grad(active, cotangent),
        column_sum(query_grad),
        column_sum(grad_values),
        column_sum(grad_branch),
        column_sum(grad_pre),
        column_sum(cotangent),
        small_total[0],
        small_total[1],
        small_total[2],
        small_total[3],
    )
    owned = owner_sum(grads)
    layer_out = jnp.concatenate(outputs, axis=0)
    grad_tokens_all = jnp.concatenate(grads_in, axis=0)
    return (
        layer_out,
        grad_tokens_all,
        owned[0],
        owned[1],
        owned[2],
        owned[3],
        owned[4],
        owned[5],
        owned[6],
        owned[7],
        owned[8],
        owned[9],
        owned[10],
        owned[11],
        owned[12],
        owned[13],
        owned[14],
    )


BF = jnp.bfloat16
F32 = jnp.float32
SMALL = 8


def other_core(value):
    return lax.ppermute(value, "core", [(0, 1), (1, 0)])


def other_x(value):
    return lax.ppermute(value, "x", [(0, 1), (1, 0)])


def other_y(value):
    return lax.ppermute(value, "y", [(0, 1), (1, 0)])


def other_z(value, by):
    return lax.ppermute(value, "z", [(i, i ^ by) for i in range(lax.axis_size("z"))])


def pair(bit, own, received):
    return jnp.stack((jnp.where(bit == 0, own, received), jnp.where(bit == 0, received, own)))


def pick(value, index, axis):
    return lax.dynamic_index_in_dim(value, index, axis, keepdims=False)


def in_order(index, pieces):
    level = list(pieces)
    bit = 0
    ordered = [p[None] for p in level]
    while len(ordered) > 1:
        flag = (index >> bit) & 1
        ordered = [
            jnp.concatenate(
                (jnp.where(flag == 0, a, b), jnp.where(flag == 0, b, a)), axis=0
            )
            for a, b in zip(ordered[::2], ordered[1::2])
        ]
        bit += 1
    return ordered[0]


def gather_plane(along_z, x, y):
    half = along_z.shape[0] // 2
    first, second = along_z[:half], along_z[half:]
    first = pair(x, first, other_x(first))
    second = pair(y, second, other_y(second))
    first = pair(y, first, other_y(first))
    second = pair(x, second, other_x(second))
    return jnp.concatenate((jnp.moveaxis(first, 2, 0).swapaxes(1, 2), jnp.moveaxis(second, 2, 0)))


def plus(kept, received):
    return kept.astype(F32) + received.astype(F32)


LIGHT = pl.CostEstimate(flops=0, bytes_accessed=1, transcendentals=0)
VMEM_LIMIT = 56 * 1024 * 1024
QUERY_BLOCK = 256


def lane_masks(dtype):
    lane = lax.broadcasted_iota(jnp.int32, (1, 2 * DH), 1)
    return [(lane < DH).astype(dtype), (lane >= DH).astype(dtype)]


def visible(key_count, query_block):
    key_pos = lax.broadcasted_iota(jnp.int32, (query_block, query_block), 0)
    query_pos = lax.broadcasted_iota(jnp.int32, (query_block, query_block), 1)
    return key_pos <= query_pos


def masked_tail(scores, allowed):
    key_count, query_block = scores.shape
    tail = jnp.where(allowed, scores[key_count - query_block :], -1e30)
    if key_count == query_block:
        return tail
    return jnp.concatenate((scores[: key_count - query_block], tail), axis=0)


def nt(left, right):
    return lax.dot_general(left, right, (((1,), (1,)), ((), ())), preferred_element_type=F32)


def nn(left, right):
    return lax.dot_general(left, right, (((1,), (0,)), ((), ())), preferred_element_type=F32)


def attend_kernel(q_ref, k_ref, v_ref, mixed_ref, lse_ref):
    length = q_ref.shape[0]
    masks = lane_masks(BF)
    allowed = visible(QUERY_BLOCK, QUERY_BLOCK)
    keys = k_ref[...]
    masked_keys = [keys * m for m in masks]
    v_t = v_ref[...].T
    row = lax.broadcasted_iota(jnp.int32, (2 * DH, 1), 0)
    values_t = [jnp.where(row < DH, v_t, jnp.zeros((), BF)), jnp.where(row >= DH, v_t, jnp.zeros((), BF))]
    for start in range(0, length, QUERY_BLOCK):
        stop = start + QUERY_BLOCK
        q = q_ref[start:stop, :]
        mixed_t = None
        for head in range(2):
            scores = masked_tail(nt(masked_keys[head][:stop], q), allowed)
            top = jnp.max(scores, axis=0, keepdims=True)
            powers = jnp.exp(scores - top)
            total = jnp.sum(powers, axis=0, keepdims=True)
            low = (powers * (1.0 / total)).astype(BF)
            part = nn(values_t[head][:, :stop], low)
            mixed_t = part if mixed_t is None else mixed_t + part
            lse_ref[0, head : head + 1, start:stop] = top + jnp.log(total)
        mixed_ref[start:stop, :] = mixed_t.T.astype(BF)


def attend_back_kernel(q_ref, k_ref, v_ref, g_ref, mixed_ref, lse_ref, gq_ref, gk_ref, gv_ref, ka, va):
    length = q_ref.shape[0]
    masks = lane_masks(BF)
    allowed = visible(QUERY_BLOCK, QUERY_BLOCK)
    keys, values = k_ref[...], v_ref[...]
    masked_keys = [keys * m for m in masks]
    masked_values = [values * m for m in masks]
    keys_t = [m.T for m in masked_keys]
    for start in range(length - QUERY_BLOCK, -1, -QUERY_BLOCK):
        stop = start + QUERY_BLOCK
        q, g = q_ref[start:stop, :], g_ref[start:stop, :]
        products = (g.astype(F32) * mixed_ref[start:stop, :].astype(F32)).T
        grad_q_t = None
        grad_k = grad_v = None
        for head in range(2):
            inner = jnp.sum(products[head * DH : (head + 1) * DH], axis=0, keepdims=True)
            scores = masked_tail(nt(masked_keys[head][:stop], q), allowed)
            probs = jnp.exp(scores - lse_ref[0, head : head + 1, start:stop])
            grad_probs = nt(masked_values[head][:stop], g)
            grad_scores = (probs * (grad_probs - inner)).astype(BF)
            part_v = nn(probs.astype(BF), g * masks[head])
            part_k = nn(grad_scores, q * masks[head])
            part_q = nn(keys_t[head][:, :stop], grad_scores)
            grad_v = part_v if head == 0 else grad_v + part_v
            grad_k = part_k if head == 0 else grad_k + part_k
            grad_q_t = part_q if head == 0 else grad_q_t + part_q
        gq_ref[start:stop, :] = grad_q_t.T.astype(BF)
        if stop == length:
            ka[...] = grad_k
            va[...] = grad_v
        else:
            ka[:stop, :] += grad_k
            va[:stop, :] += grad_v
    gk_ref[...] = ka[...].astype(BF)
    gv_ref[...] = va[...].astype(BF)


def attend(queries, keys, values):
    length, width = queries.shape
    pairs = width // (2 * DH)
    block = pl.BlockSpec((length, 2 * DH), lambda i: (0, i))
    return pl.pallas_call(
        attend_kernel,
        grid=(pairs,),
        in_specs=[block] * 3,
        out_specs=[block, pl.BlockSpec((1, 2, length), lambda i: (i, 0, 0))],
        out_shape=[
            jax.ShapeDtypeStruct((length, width), BF),
            jax.ShapeDtypeStruct((pairs, 2, length), F32),
        ],
        compiler_params=pltpu.CompilerParams(vmem_limit_bytes=VMEM_LIMIT),
        cost_estimate=LIGHT,
        name="attend",
    )(queries, keys, values)


def attend_back(queries, keys, values, mixed, lse, grad_mixed, pair_index, pairs):
    length = queries.shape[0]
    block = pl.BlockSpec((length, 2 * DH), lambda i: (0, i + pair_index))
    out_block = pl.BlockSpec((length, 2 * DH), lambda i: (0, i))
    width = pairs * 2 * DH
    return pl.pallas_call(
        attend_back_kernel,
        grid=(pairs,),
        in_specs=[block] * 5 + [pl.BlockSpec((1, 2, length), lambda i: (i + pair_index, 0, 0))],
        out_specs=[out_block] * 3,
        out_shape=[jax.ShapeDtypeStruct((length, width), BF)] * 3,
        scratch_shapes=[pltpu.VMEM((length, 2 * DH), F32)] * 2,
        compiler_params=pltpu.CompilerParams(vmem_limit_bytes=VMEM_LIMIT),
        cost_estimate=LIGHT,
        name="attend_back",
    )(queries, keys, values, grad_mixed, mixed, lse)


def position_blocks(core, block):
    return [
        (b, own, pl.multiple_of(b * 2 * block + (core if own else 1 - core) * block, block))
        for b in range(2)
        for own in (True, False)
    ]


def normalise(values):
    centre = values - jnp.mean(values, axis=-1, keepdims=True)
    spread = jnp.mean(centre * centre, axis=-1, keepdims=True)
    rate = lax.rsqrt(spread + 1e-05)
    return centre * rate, rate


def normalise_back(unit, rate, gain, grad):
    scaled = grad * gain
    return rate * (
        scaled
        - jnp.mean(scaled, axis=-1, keepdims=True)
        - unit * jnp.mean(scaled * unit, axis=-1, keepdims=True)
    )


CORE, X, Y = range(3)
B_QUERY, B_VALUE, B_OUT, B_DOWN, GAIN1, SHIFT1, GAIN2, SHIFT2 = range(8)


def weight(ref, i):
    chips, _, width = ref.shape
    rows = width * 2 // chips
    return ref[:, i * rows : (i + 1) * rows, :].reshape(chips * rows, width)


def enter_kernel(core_ref, mine_ref, other_ref, vec_ref, half_ref, w_ref, n_ref, q_ref, k_ref, v_ref):
    core = core_ref[0]
    block = mine_ref.shape[0] // 2
    for b, own, row in position_blocks(core, block):
        tokens = (mine_ref if own else other_ref)[b * block : (b + 1) * block, :].astype(F32)
        unit, _ = normalise(tokens)
        normed = (unit * vec_ref[GAIN1 : GAIN1 + 1, :] + vec_ref[SHIFT1 : SHIFT1 + 1, :]).astype(BF)
        rows = pl.ds(row, block)
        n_ref[rows, :] = normed
        q = (nn(normed, weight(w_ref, 0)) + half_ref[B_QUERY : B_QUERY + 1, :]) * DH ** (-0.5)
        q_ref[rows, :] = q.astype(BF)
        k_ref[rows, :] = nn(normed, weight(w_ref, 1)).astype(BF)
        v_ref[rows, :] = (nn(normed, weight(w_ref, 2)) + half_ref[B_VALUE : B_VALUE + 1, :]).astype(BF)


def out_kernel(core_ref, mixed_ref, w_ref, mine_ref, other_ref):
    block = mine_ref.shape[0] // 2
    for b, own, row in position_blocks(core_ref[0], block):
        part = nn(mixed_ref[pl.ds(row, block), :], w_ref[...])
        ref = mine_ref if own else other_ref
        ref[b * block : (b + 1) * block, :] = part.astype(ref.dtype)


def middle_kernel(tokens_ref, part_ref, received_ref, vec_ref, residual_ref, n_ref):
    residual = (
        tokens_ref[...].astype(F32)
        + part_ref[...]
        + received_ref[...].astype(F32)
        + vec_ref[B_OUT : B_OUT + 1, :]
    )
    unit, _ = normalise(residual)
    residual_ref[...] = residual
    n_ref[...] = (unit * vec_ref[GAIN2 : GAIN2 + 1, :] + vec_ref[SHIFT2 : SHIFT2 + 1, :]).astype(BF)


def middle_back_kernel(residual_ref, gn_ref, gn_received_ref, g_ref, vec_ref, gr_ref, branch_ref, sums_ref):
    unit, rate = normalise(residual_ref[...])
    grad_normed = gn_ref[...] + gn_received_ref[...].astype(F32)
    cotangent = g_ref[...].astype(F32)
    grad = cotangent + normalise_back(unit, rate, vec_ref[GAIN2 : GAIN2 + 1, :], grad_normed)
    gr_ref[...] = grad
    branch = grad.astype(BF)
    branch_ref[...] = branch
    for i, value in enumerate((branch.astype(F32), cotangent, grad_normed * unit, grad_normed)):
        sums_ref[0, i : i + 1, :] = jnp.sum(value, axis=0, keepdims=True)


def mixed_back_kernel(core_ref, mixed_ref, mine_ref, other_ref, w_ref, gm_ref, gw_ref):
    block = mine_ref.shape[0] // 2
    total = None
    for b, own, row in position_blocks(core_ref[0], block):
        branch = (mine_ref if own else other_ref)[b * block : (b + 1) * block, :]
        rows = pl.ds(row, block)
        gm_ref[rows, :] = nt(branch, w_ref[...]).astype(BF)
        part = nn(mixed_ref[rows, :].T, branch)
        total = part if total is None else total + part
    gw_ref[...] = total.astype(BF)


def weight_back_kernel(
    place_ref, n_ref, q_ref, k_ref, v_ref, left_keep, left_send, right_keep, right_send, sums_ref, by_y, by_x
):
    x, y = place_ref[X], place_ref[Y]
    n_t = n_ref[...].T
    rows = by_y.shape[2]
    grads = [q_ref[...] * jnp.asarray(DH ** (-0.5), BF), k_ref[...], v_ref[...]]
    for i in range(2):
        by_y[...] = nn(n_t, grads[i]).astype(BF).reshape(by_y.shape)
        part = slice(i * rows, (i + 1) * rows)
        left_keep[:, part, :] = by_y[:, pl.ds(y, 1)].reshape(-1, rows, by_y.shape[3])
        left_send[:, part, :] = by_y[:, pl.ds(1 - y, 1)].reshape(-1, rows, by_y.shape[3])
    by_x[...] = nn(n_t, grads[2]).astype(BF).reshape(by_x.shape)
    right_keep[...] = by_x[:, pl.ds(x, 1)].reshape(right_keep.shape)
    right_send[...] = by_x[:, pl.ds(1 - x, 1)].reshape(right_send.shape)
    sums_ref[0:1, :] = jnp.sum(grads[0].astype(F32), axis=0, keepdims=True)
    sums_ref[1:2, :] = jnp.sum(grads[2].astype(F32), axis=0, keepdims=True)


def enter_back_kernel(place_ref, q_ref, k_ref, v_ref, w_ref, mine_ref, other_ref):
    block = mine_ref.shape[0] // 2
    for b, own, row in position_blocks(place_ref[CORE], block):
        rows = pl.ds(row, block)
        part = (
            nt(q_ref[rows, :] * jnp.asarray(DH ** (-0.5), BF), weight(w_ref, 0))
            + nt(k_ref[rows, :], weight(w_ref, 1))
            + nt(v_ref[rows, :], weight(w_ref, 2))
        )
        ref = mine_ref if own else other_ref
        ref[b * block : (b + 1) * block, :] = part.astype(ref.dtype)


def leave_kernel(tokens_ref, gn_ref, gn_received_ref, gr_ref, vec_ref, gt_ref, sums_ref):
    unit, rate = normalise(tokens_ref[...].astype(F32))
    grad_normed = gn_ref[...] + gn_received_ref[...].astype(F32)
    gt_ref[...] = gr_ref[...] + normalise_back(unit, rate, vec_ref[GAIN1 : GAIN1 + 1, :], grad_normed)
    for i, value in enumerate((grad_normed * unit, grad_normed)):
        sums_ref[0, i : i + 1, :] = jnp.sum(value, axis=0, keepdims=True)


def shape(dims, dtype):
    return jax.ShapeDtypeStruct(dims, dtype)


def whole_call(kernel, outs, *args, flops=0, scalars=0, scratch=()):
    in_specs = [
        pl.BlockSpec(memory_space=pltpu.SMEM if i < scalars else pltpu.VMEM)
        for i in range(len(args))
    ]
    moved = sum(a.size * a.dtype.itemsize for a in list(args) + outs)
    return pl.pallas_call(
        kernel,
        in_specs=in_specs,
        out_specs=[pl.BlockSpec(memory_space=pltpu.VMEM)] * len(outs),
        out_shape=outs,
        scratch_shapes=list(scratch),
        compiler_params=pltpu.CompilerParams(vmem_limit_bytes=VMEM_LIMIT),
        cost_estimate=LIGHT,
        name=kernel.__name__,
    )(*args)


def row_call(kernel, outs, sums, *args):
    length, width = args[0].shape
    block = length // 2
    rows = pl.BlockSpec((block, width), lambda i: (i, 0))
    out_shape = [shape((length, width), dtype) for dtype in outs]
    out_specs = [rows] * len(outs)
    if sums:
        out_shape.append(shape((2, sums, width), F32))
        out_specs.append(pl.BlockSpec((1, sums, width), lambda i: (i, 0, 0)))
    moved = sum(a.size * a.dtype.itemsize for a in list(args) + out_shape)
    return pl.pallas_call(
        kernel,
        grid=(2,),
        in_specs=[rows] * (len(args) - 1) + [pl.BlockSpec(args[-1].shape, lambda i: (0, 0))],
        out_specs=out_specs,
        out_shape=out_shape,
        compiler_params=pltpu.CompilerParams(vmem_limit_bytes=VMEM_LIMIT),
        cost_estimate=LIGHT,
        name=kernel.__name__,
    )(*args)


def hidden_kernel(
    place_ref, n_mine, n_other, g_mine, g_other, up_ref, down_ref, bias_ref,
    y_mine, y_other, gn_mine, gn_other, up_keep, up_send, down_keep, down_send, gb_ref,
    n_t, y_sum, gn_sum, up_all, down_all,
):
    step = pl.program_id(0)
    length = n_mine.shape[0]

    @pl.when(step == 0)
    def _():
        n_t[:, :length] = n_mine[...].T
        n_t[:, length:] = n_other[...].T
        for ref in (y_mine, gn_mine, y_sum, gn_sum):
            ref[...] = jnp.zeros(ref.shape, F32)

    up = up_ref[...].reshape(-1, up_ref.shape[2])
    down = down_ref[...].reshape(-1, down_ref.shape[2])
    grad_up = grad_down = bias_sum = None
    for part, (n_ref, g_ref, y_ref, gn_ref) in enumerate(
        ((n_mine, g_mine, y_mine, gn_mine), (n_other, g_other, y_sum, gn_sum))
    ):
        n, g = n_ref[...], g_ref[...]
        pre = nn(n, up) + bias_ref[0]
        square = pre * pre
        bent = jnp.tanh(pre * (0.7978845608028654 + 0.7978845608028654 * 0.044715 * square))
        half = 0.5 + 0.5 * bent
        active = (pre * half).astype(BF)
        rise = pre * (2 * 0.7978845608028654 + 6 * 0.7978845608028654 * 0.044715 * square)
        slope = half * (1.0 + (1.0 - half) * rise)
        grad_pre = (nt(g, down) * slope).astype(BF)
        y_ref[...] += nn(active, down)
        gn_ref[...] += nt(grad_pre, up)
        part_up = nn(n_t[:, part * length : (part + 1) * length], grad_pre)
        part_down = lax.dot_general(active, g, (((0,), (0,)), ((), ())), preferred_element_type=F32)
        part_bias = jnp.sum(grad_pre.astype(F32), axis=0, keepdims=True)
        grad_up = part_up if part == 0 else grad_up + part_up
        grad_down = part_down if part == 0 else grad_down + part_down
        bias_sum = part_bias if part == 0 else bias_sum + part_bias
    x, y = place_ref[X], place_ref[Y]
    up_all[...] = grad_up.astype(BF).reshape(up_all.shape)
    up_keep[...] = up_all[:, pl.ds(y, 1)].reshape(up_keep.shape)
    up_send[...] = up_all[:, pl.ds(1 - y, 1)].reshape(up_send.shape)
    down_all[...] = grad_down.astype(BF).reshape(down_all.shape)
    down_keep[...] = down_all[:, pl.ds(x, 1)].reshape(down_keep.shape)
    down_send[...] = down_all[:, pl.ds(1 - x, 1)].reshape(down_send.shape)
    gb_ref[0] = bias_sum

    @pl.when(step == pl.num_programs(0) - 1)
    def _():
        y_other[...] = y_sum[...].astype(BF)
        gn_other[...] = gn_sum[...].astype(BF)


def feed_forward(place, n_mine, n_other, g_mine, g_other, late, bias, hidden_rows):
    length, width = n_mine.shape
    chips = late.shape[0]
    steps = 2
    z_count = chips // 4
    z_step = z_count // steps
    tile = chips * hidden_rows // steps
    up_rows = width // chips
    per_half = steps // 2
    down_chips = chips // steps
    full = pl.BlockSpec((length, width), lambda i: (0, 0))
    hidden = tile * steps
    return pl.pallas_call(
        hidden_kernel,
        grid=(steps,),
        in_specs=[pl.BlockSpec(memory_space=pltpu.SMEM)] + [full] * 4
        + [
            pl.BlockSpec((chips, up_rows, tile), lambda i: (0, i // per_half, i % per_half)),
            pl.BlockSpec((down_chips, hidden_rows, width), lambda i: (i, 1, 0)),
            pl.BlockSpec((1, 1, tile), lambda i: (i, 0, 0)),
        ],
        out_specs=[full] * 4
        + [
            pl.BlockSpec((chips // 2, up_rows, tile), lambda i: (0, 0, i)),
            pl.BlockSpec((chips // 2, up_rows, tile), lambda i: (0, 0, i)),
            pl.BlockSpec((z_step, 2, hidden_rows, width), lambda i: (i, 0, 0, 0)),
            pl.BlockSpec((z_step, 2, hidden_rows, width), lambda i: (i, 0, 0, 0)),
            pl.BlockSpec((1, 1, tile), lambda i: (i, 0, 0)),
        ],
        out_shape=[
            shape((length, width), F32),
            shape((length, width), BF),
            shape((length, width), F32),
            shape((length, width), BF),
            shape((chips // 2, up_rows, hidden), BF),
            shape((chips // 2, up_rows, hidden), BF),
            shape((z_count, 2, hidden_rows, width), BF),
            shape((z_count, 2, hidden_rows, width), BF),
            shape((steps, 1, tile), F32),
        ],
        scratch_shapes=[
            pltpu.VMEM((width, 2 * length), BF),
            pltpu.VMEM((length, width), F32),
            pltpu.VMEM((length, width), F32),
            pltpu.VMEM((chips // 2, 2, up_rows, tile), BF),
            pltpu.VMEM((z_step, 2, 2, hidden_rows, width), BF),
        ],
        compiler_params=pltpu.CompilerParams(vmem_limit_bytes=VMEM_LIMIT),
        cost_estimate=LIGHT,
        name="feed_forward",
    )(place, n_mine, n_other, g_mine, g_other, late, late, bias.reshape(steps, 1, tile))


def chip_step(
    tokens_in,
    out_grad,
    w_query,
    w_key,
    w_value,
    w_out,
    w_up,
    w_down,
    b_query,
    b_value,
    b_out,
    b_up,
    b_down,
    norm1_gain,
    norm1_shift,
    norm2_gain,
    norm2_shift,
):
    z, x, y, core = (lax.axis_index(name) for name in ("z", "x", "y", "core"))
    z_count = lax.axis_size("z")
    chips = z_count * 4
    half_chips = chips // 2
    _, block, width = tokens_in.shape
    half = width // 2
    rows = w_query.shape[0]
    hidden_rows = w_down.shape[0]
    hidden = hidden_rows * chips

    def own_positions(value):
        return pair(y, pick(value, y, 0), other_y(pick(value, 1 - y, 0))).reshape(2 * block, width)

    three = jnp.stack((w_query, w_key, w_value)).reshape(3, rows, 2, half)
    vectors = (
        b_query, b_value, b_out, b_down, norm1_gain, norm1_shift, norm2_gain, norm2_shift, b_up
    )
    small = jnp.concatenate(vectors)
    unit_rows = 3 * rows + SMALL
    small_rows = jnp.zeros((SMALL, half), BF).at[0, : small.shape[0]].set(small)
    own = jnp.concatenate((pick(three, core, 2).reshape(3 * rows, half), small_rows))
    unit = pair(
        core,
        own,
        other_core(
            jnp.concatenate((pick(three, 1 - core, 2).reshape(3 * rows, half), small_rows))
        ),
    )
    up_parts = w_up.reshape(rows, chips, 2, hidden_rows)
    up_unit = pair(
        core,
        pick(up_parts, core, 2).reshape(rows, hidden),
        other_core(pick(up_parts, 1 - core, 2).reshape(rows, hidden)),
    )
    up_unit = up_unit.reshape(2 * rows, 2, width)
    late = jnp.concatenate((up_unit[:, 0], up_unit[:, 1], w_down))
    late = lax.all_gather(late, ("z", "x", "y"), axis=0, tiled=False)
    threes = unit[:, : 3 * rows].reshape(2, 3, rows, half).swapaxes(0, 1).reshape(6 * rows, half)
    unit = jnp.concatenate(
        (threes, unit[:, 3 * rows :].reshape(2 * SMALL, half), w_out[:, :half], w_out[:, half:])
    )
    pieces = [unit] + [other_z(unit, k) for k in range(1, z_count)]
    both = jnp.stack((pick(tokens_in, y, 0), pick(out_grad, y, 0)))
    both_from = other_y(jnp.stack((pick(tokens_in, 1 - y, 0), pick(out_grad, 1 - y, 0))))
    pieces, both_from = lax.optimization_barrier((pieces, both_from))
    both = pair(y, both, both_from).swapaxes(0, 1).reshape(2, 2 * block, width)
    mine, grad_mine = both[0], both[1]
    other, grad_other = other_core(mine), other_core(grad_mine)
    place = jnp.stack((core, x, y)).astype(jnp.int32)
    gathered = gather_plane(in_order(z, pieces), x, y)
    out_parts = jnp.concatenate(
        (gathered[..., 2 * unit_rows : 2 * unit_rows + rows, :], gathered[..., 2 * unit_rows + rows :, :]),
        axis=-1,
    ).reshape(2, half_chips, rows, width)
    out_c = (
        pair(core, pick(out_parts, core, 0), other_core(pick(out_parts, 1 - core, 0)))
        .swapaxes(0, 1)
        .reshape(half, width)
    )
    gathered = gathered.reshape(chips, -1, half)
    small_all = gathered[:, 6 * rows : 6 * rows + 2 * SMALL].reshape(chips * 2, SMALL, half)
    small_all = small_all[:, 0, : small.shape[0]]
    vectors = small_all[:, : 8 * rows].reshape(chips * 2, 8, rows).swapaxes(0, 1)
    vectors = vectors.reshape(8, width).astype(F32)
    halves = pick(vectors.reshape(8, 2, half), core, 1)
    bias_u = pick(small_all[:, 8 * rows :].reshape(chips, 2, hidden_rows), core, 1)
    bias_u = bias_u.reshape(hidden).astype(F32)

    length = 4 * block
    heads_shape = shape((length, half), BF)
    normed, queries, keys, values = whole_call(
        enter_kernel,
        [shape((length, width), BF)] + [heads_shape] * 3,
        place, mine, other, vectors, halves, gathered,
        flops=6 * length * width * half, scalars=1,
    )
    mixed, lse = attend(queries, keys, values)
    mine_shape = shape((2 * block, width), F32)
    sent_shape = shape((2 * block, width), BF)
    part, to_other = whole_call(
        out_kernel, [mine_shape, sent_shape], place, mixed, out_c,
        flops=2 * length * width * half, scalars=1,
    )
    residual, normed2 = row_call(middle_kernel, (F32, BF), 0, mine, part, other_core(to_other), vectors)
    late, normed2 = lax.optimization_barrier((late, normed2))
    y_mine, y_other, gn_mine, gn_other, up_keep, up_send, down_keep, down_send, up_sums = feed_forward(
        place, normed2, other_core(normed2), grad_mine, grad_other, late, bias_u, hidden_rows
    )

    up_from, down_from = other_y(up_send), other_x(down_send)
    grad_residual, branch, sums2 = row_call(
        middle_back_kernel, (F32, BF), 4, residual, gn_mine, other_core(gn_other), grad_mine, vectors
    )
    grad_mixed, grad_out = whole_call(
        mixed_back_kernel, [heads_shape, shape((half, width), BF)],
        place, mixed, branch, other_core(branch), out_c,
        flops=4 * length * width * half, scalars=1,
    )
    grad_out = grad_out.reshape(half_chips, 2, rows, width)
    grad_out = pair(
        core,
        pick(grad_out, core, 1),
        other_core(pick(grad_out, 1 - core, 1)),
    ).reshape(z_count, 2, 2, rows, width)
    grads = attend_back(
        queries, keys, values, mixed, lse, grad_mixed, 0, half // (2 * DH)
    )
    up_from, down_from, grads = lax.optimization_barrier((up_from, down_from, grads))
    ups = plus(up_keep, up_from).reshape(z_count, 2, 2 * rows, hidden)
    downs = plus(down_keep, down_from)
    up_send, down_send = pick(ups, 1 - x, 1).astype(BF), pick(downs, 1 - y, 1).astype(BF)
    up_send, down_send, grads = lax.optimization_barrier((up_send, down_send, grads))
    up_from, down_from, out_from = other_x(up_send), other_y(down_send), other_x(pick(grad_out, 1 - x, 1))
    left_shape = shape((2 * z_count, 4 * rows, half), BF)
    right_shape = shape((z_count, 2, 2 * rows, half), BF)
    left_keep, left_send, right_keep, right_send, sums_heads = whole_call(
        weight_back_kernel,
        [left_shape] * 2 + [right_shape] * 2 + [shape((2, half), F32)],
        place, normed, *grads,
        flops=6 * length * width * half, scalars=1,
        scratch=(
            pltpu.VMEM((2 * z_count, 2, 2 * rows, half), BF),
            pltpu.VMEM((z_count, 2, 2, 2 * rows, half), BF),
        ),
    )
    left_send, right_send, grads, y_mine, y_other = lax.optimization_barrier(
        (left_send, right_send, grads, y_mine, y_other)
    )
    left_from, right_from = other_y(left_send), other_x(right_send)
    gn_mine, gn_other = whole_call(
        enter_back_kernel,
        [mine_shape, sent_shape],
        place, *grads, gathered,
        flops=6 * length * width * half, scalars=1,
    )
    up_from, down_from, out_from, gn_mine, gn_other = lax.optimization_barrier(
        (up_from, down_from, out_from, gn_mine, gn_other)
    )
    low, high = z & 1, z >> 1

    def first_z(value):
        value = value.reshape((z_count // 2, 2) + value.shape[1:])
        return pick(value, low, 1), other_z(pick(value, 1 - low, 1).astype(BF), 1)

    def second_z(value):
        return pick(value, high, 0), other_z(pick(value, 1 - high, 0).astype(BF), 2)

    gn_from = other_core(gn_other)
    ups = plus(pick(ups, x, 1), up_from)
    downs = plus(pick(downs, y, 1), down_from)
    outs = plus(pick(grad_out, x, 1), out_from)
    forward_kept, forward_from = first_z(
        jnp.concatenate((ups[..., :width], ups[..., width:], downs), axis=1)
    )
    grad_tokens, sums1 = row_call(
        leave_kernel, (F32,), 2, mine, gn_mine, gn_from, grad_residual, vectors
    )
    left_from, right_from, grad_tokens = lax.optimization_barrier((left_from, right_from, grad_tokens))
    output = residual + y_mine + other_core(y_other).astype(F32) + vectors[B_DOWN]
    output = output.astype(BF).reshape(2, block, width)
    grad_tokens = grad_tokens.reshape(2, block, width)
    lefts = plus(left_keep, left_from).reshape(z_count, 2, 4 * rows, half)
    rights = plus(right_keep, right_from)
    rights = jnp.concatenate((rights, outs[..., :half], outs[..., half:]), axis=2)
    left_send, right_send = pick(lefts, 1 - x, 1).astype(BF), pick(rights, 1 - y, 1).astype(BF)
    left_send, right_send, forward_from = lax.optimization_barrier((left_send, right_send, forward_from))
    left_from, right_from = other_x(left_send), other_y(right_send)
    forward_kept, forward_from = second_z(plus(forward_kept, forward_from))
    to_y = jnp.concatenate((pick(output, 1 - y, 0), pick(grad_tokens, 1 - y, 0).astype(BF)))

    placed = jnp.where((jnp.arange(2) == core)[None, :, None], sums_heads[:, None], 0.0)
    small_grads = jnp.concatenate(
        (placed.reshape(2, width), sums2[0, :2] + sums2[1, :2], sums1[0] + sums1[1], sums2[0, 2:] + sums2[1, 2:])
    )
    small_grads = small_grads.reshape(8, chips * 2, rows).swapaxes(0, 1).reshape(chips, 2, 8 * rows)
    up_sums = jnp.where(
        (jnp.arange(2) == core)[None, :, None], up_sums.reshape(chips, 1, hidden_rows), 0.0
    )
    small_grads = jnp.concatenate((small_grads, up_sums), axis=2)
    small_grads = small_grads.reshape(z_count, 2, 2, 2, -1)
    small_grads = plus(pick(small_grads, y, 2), other_y(pick(small_grads, 1 - y, 2).astype(BF)))
    small_from = other_x(pick(small_grads, 1 - x, 1).astype(BF))
    left_from, right_from, to_y = lax.optimization_barrier((left_from, right_from, to_y))
    lefts = plus(pick(lefts, x, 1), left_from)
    rights = plus(pick(rights, y, 1), right_from)
    last, last_from = first_z(jnp.concatenate((lefts, rights), axis=1))
    from_y = other_y(to_y)
    small_grads = plus(*first_z(plus(pick(small_grads, x, 1), small_from)))
    small_mine = plus(*second_z(small_grads))
    last_from, forward_from = lax.optimization_barrier((last_from, forward_from))
    last, last_from = second_z(plus(last, last_from))
    forward_sum = plus(forward_kept, forward_from)
    last = plus(last, last_from)
    layer_out = pair(y, pick(output, y, 0), from_y[:block])
    grad_tokens = pair(y, pick(grad_tokens, y, 0), from_y[block:].astype(F32))

    up_mine = forward_sum[: 4 * rows].reshape(2, 2, rows, width)
    down_mine = forward_sum[4 * rows :]
    three_mine = last[: 6 * rows].reshape(3, 2, rows, half)
    out_mine = jnp.concatenate((last[6 * rows : 7 * rows], last[7 * rows : 8 * rows]), axis=1)
    up_from = other_core(pick(up_mine, 1 - core, 1))
    small_sum = pick(small_mine, core, 0) + other_core(pick(small_mine, 1 - core, 0))
    three_from = other_core(pick(three_mine, 1 - core, 1))
    three_out = pair(core, pick(three_mine, core, 1), three_from)
    up_out = pair(core, pick(up_mine, core, 1), up_from)
    up_out = up_out.reshape(2, 2, rows, half_chips, hidden_rows)
    up_out = jnp.transpose(up_out, (2, 1, 3, 0, 4)).reshape(rows, 2 * hidden)
    g_q, g_k, g_v = (jnp.concatenate((three_out[0, i], three_out[1, i]), axis=1) for i in range(3))
    g_small = [small_sum[i * rows : (i + 1) * rows] for i in range(8)]
    return (
        layer_out,
        grad_tokens,
        g_q,
        g_k,
        g_v,
        out_mine,
        up_out,
        down_mine,
        g_small[0],
        g_small[1],
        g_small[2],
        small_sum[8 * rows :],
        g_small[3],
        g_small[4],
        g_small[5],
        g_small[6],
        g_small[7],
    )


def solution(mesh):
    dp_count, ctx_count = mesh.shape["dp"], mesh.shape["ctx"]

    def run(*args):
        per_dp = args[0].shape[0] // dp_count
        if ctx_count == 4 and per_dp == 2 and dp_count == 8:
            devices = mesh.devices.reshape(dp_count // 2, 2, ctx_count // 2, 2)
            used = Mesh(devices, ("z", "x", "y", "core"))
            body, dp, ctx = chip_step, ("z", "x"), ("y", "core")
        else:
            used, body, dp, ctx = mesh, on_device, ("dp",), ("ctx",)
        tokens, matrix, bias = P(dp, ctx, None), P(dp + ctx, None), P(dp + ctx)
        return jax.shard_map(
            body,
            mesh=used,
            in_specs=(tokens,) * 2 + (matrix,) * 6 + (bias,) * 9,
            out_specs=(tokens,) * 2 + (matrix,) * 6 + (bias,) * 9,
            check_vma=False,
        )(*args)

    return run
```

```python
import jax
import jax.numpy as jnp
from jax import lax
from jax.experimental import pallas as pl
from jax.experimental.pallas import tpu as pltpu
from jax.sharding import Mesh
from jax.sharding import PartitionSpec as P

HEADS = 12
DH = 64
MICRO = 2


def shifted(value, axis, by):
    peers = lax.axis_size(axis)
    return lax.ppermute(value, axis, [(i, (i + by) % peers) for i in range(peers)])


def as_sent(value):
    return jax.tree.map(lambda a: a.astype(jnp.bfloat16) if a.dtype == jnp.float32 else a, value)


def layer_norm(values, norm_gain, norm_shift):
    centre = values - jnp.mean(values, axis=-1, keepdims=True)
    spread = jnp.mean(centre * centre, axis=-1, keepdims=True)
    return centre * lax.rsqrt(spread + 1e-05) * norm_gain + norm_shift


def gelu_tanh(values):
    return (
        0.5
        * values
        * (1.0 + jnp.tanh(0.7978845608028654 * (values + 0.044715 * values * values * values)))
    )


def project(left, right):
    return jnp.einsum("scd,de->sce", left, right, preferred_element_type=jnp.float32)


def project_back(left, right):
    return jnp.einsum("sce,de->scd", left, right, preferred_element_type=jnp.float32)


def weight_grad(left, right):
    return jnp.einsum("scd,sce->de", left, right, preferred_element_type=jnp.float32)


def column_sum(values):
    return jnp.sum(values.astype(jnp.float32), axis=(0, 1))


def masked_scores(query_heads, key_full, first_pos):
    seq_count, key_len = (key_full.shape[0], key_full.shape[1])
    key_heads = key_full.reshape(seq_count, key_len, HEADS, DH)
    scores = jnp.einsum(
        "sqhd,skhd->shqk", query_heads, key_heads, preferred_element_type=jnp.float32
    )
    row_pos = first_pos + jnp.arange(query_heads.shape[1], dtype=jnp.int32)
    col_pos = jnp.arange(key_len, dtype=jnp.int32)
    allowed = row_pos[:, None] >= col_pos[None, :]
    return (jnp.where(allowed, scores, -1e30), key_heads)


def micro_step(tokens, cotangent, shards, forward_weights):
    (
        w_query,
        w_key,
        w_value,
        w_out,
        w_up,
        w_down,
        b_query,
        b_value,
        b_out,
        b_up,
        b_down,
        gain_one,
        shift_one,
        gain_two,
        shift_two,
    ) = forward_weights
    seq_count, block_rows, width = tokens.shape
    query_scale = DH ** (-0.5)
    first_pos = lax.axis_index("ctx") * block_rows
    gain_one32, shift_one32 = (gain_one.astype(jnp.float32), shift_one.astype(jnp.float32))
    gain_two32, shift_two32 = (gain_two.astype(jnp.float32), shift_two.astype(jnp.float32))
    tokens32 = tokens.astype(jnp.float32)
    normed = layer_norm(tokens32, gain_one32, shift_one32).astype(jnp.bfloat16)
    queries = ((project(normed, w_query) + b_query.astype(jnp.float32)) * query_scale).astype(
        jnp.bfloat16
    )
    keys_local = project(normed, w_key).astype(jnp.bfloat16)
    values_local = (project(normed, w_value) + b_value.astype(jnp.float32)).astype(jnp.bfloat16)
    key_full, value_full = (
        lax.all_gather(keys_local, "ctx", axis=1, tiled=True),
        lax.all_gather(values_local, "ctx", axis=1, tiled=True),
    )
    query_heads = queries.reshape(seq_count, block_rows, HEADS, DH)
    scores, key_heads = masked_scores(query_heads, key_full, first_pos)
    row_max = jnp.max(scores, axis=-1, keepdims=True)
    exp_scores = jnp.exp(scores - row_max)
    row_total = jnp.sum(exp_scores, axis=-1, keepdims=True)
    probs_low = (exp_scores / row_total).astype(jnp.bfloat16)
    value_heads = value_full.reshape(seq_count, value_full.shape[1], HEADS, DH)
    mixed_heads = jnp.einsum(
        "shqk,skhd->sqhd", probs_low, value_heads, preferred_element_type=jnp.float32
    ).reshape(seq_count, block_rows, width)
    mixed_heads = mixed_heads.astype(jnp.bfloat16)
    residual = tokens32 + project(mixed_heads, w_out) + b_out.astype(jnp.float32)
    normed_two = layer_norm(residual, gain_two32, shift_two32).astype(jnp.bfloat16)
    hidden_pre = project(normed_two, w_up) + b_up.astype(jnp.float32)
    active = gelu_tanh(hidden_pre).astype(jnp.bfloat16)
    output = (residual + project(active, w_down) + b_down.astype(jnp.float32)).astype(jnp.bfloat16)
    back_weights = (
        lax.all_gather(shards[0], ("dp", "ctx"), axis=0, tiled=True),
        lax.all_gather(shards[1], ("dp", "ctx"), axis=0, tiled=True),
        lax.all_gather(shards[2], ("dp", "ctx"), axis=0, tiled=True),
        lax.all_gather(shards[3], ("dp", "ctx"), axis=0, tiled=True),
        lax.all_gather(shards[4], ("dp", "ctx"), axis=0, tiled=True),
        lax.all_gather(shards[5], ("dp", "ctx"), axis=0, tiled=True),
        lax.all_gather(shards[6], ("dp", "ctx"), axis=0, tiled=True),
        lax.all_gather(shards[7], ("dp", "ctx"), axis=0, tiled=True),
        lax.all_gather(shards[8], ("dp", "ctx"), axis=0, tiled=True),
        lax.all_gather(shards[9], ("dp", "ctx"), axis=0, tiled=True),
        lax.all_gather(shards[10], ("dp", "ctx"), axis=0, tiled=True),
        lax.all_gather(shards[11], ("dp", "ctx"), axis=0, tiled=True),
        lax.all_gather(shards[12], ("dp", "ctx"), axis=0, tiled=True),
        lax.all_gather(shards[13], ("dp", "ctx"), axis=0, tiled=True),
        lax.all_gather(shards[14], ("dp", "ctx"), axis=0, tiled=True),
    )
    w_query, w_key, w_value, w_out, w_up, w_down = back_weights[:6]
    grad_active = project_back(cotangent, w_down)
    _, gelu_pull = jax.vjp(gelu_tanh, hidden_pre)
    grad_pre = gelu_pull(grad_active)[0].astype(jnp.bfloat16)
    grad_normed_two = project_back(grad_pre, w_up)
    _, norm_pull_two = jax.vjp(layer_norm, residual, gain_two32, shift_two32)
    grad_res_part, grad_gain_two, grad_shift_two = norm_pull_two(grad_normed_two)
    grad_residual = cotangent.astype(jnp.float32) + grad_res_part
    grad_branch = grad_residual.astype(jnp.bfloat16)
    grad_mixed = project_back(grad_branch, w_out).astype(jnp.bfloat16)
    key_full, value_full = (
        lax.all_gather(keys_local, "ctx", axis=1, tiled=True),
        lax.all_gather(values_local, "ctx", axis=1, tiled=True),
    )
    value_heads = value_full.reshape(seq_count, value_full.shape[1], HEADS, DH)
    scores, key_heads = masked_scores(query_heads, key_full, first_pos)
    probs = jnp.exp(scores - row_max) / row_total
    probs_low = probs.astype(jnp.bfloat16)
    grad_heads = grad_mixed.reshape(seq_count, block_rows, HEADS, DH)
    grad_probs = jnp.einsum(
        "sqhd,skhd->shqk", grad_heads, value_heads, preferred_element_type=jnp.float32
    )
    inner_rows = jnp.sum(probs * grad_probs, axis=-1, keepdims=True)
    grad_scores = (probs * (grad_probs - inner_rows)).astype(jnp.bfloat16)
    grad_queries = jnp.einsum(
        "shqk,skhd->sqhd", grad_scores, key_heads, preferred_element_type=jnp.float32
    )
    grad_queries = grad_queries.reshape(seq_count, block_rows, width).astype(jnp.bfloat16)
    query_grad = grad_queries * query_scale

    def key_terms(first_row, row_count):
        score_part = lax.dynamic_slice_in_dim(grad_scores, first_row, row_count, 3)
        prob_part = lax.dynamic_slice_in_dim(probs_low, first_row, row_count, 3)
        key_part = jnp.einsum(
            "shqk,sqhd->kshd", score_part, query_heads, preferred_element_type=jnp.float32
        )
        value_part = jnp.einsum(
            "shqk,sqhd->kshd", prob_part, grad_heads, preferred_element_type=jnp.float32
        )
        return jnp.concatenate(
            (
                key_part.reshape(row_count, seq_count, width),
                value_part.reshape(row_count, seq_count, width),
            ),
            axis=2,
        )

    cycle_size = lax.axis_size("ctx")
    own_index = lax.axis_index("ctx")

    def carry_step(step, carried):
        holder = (own_index - step) % cycle_size
        carried = carried + key_terms(holder * block_rows, block_rows)
        return shifted(carried.astype(jnp.bfloat16), "ctx", 1).astype(carried.dtype)

    start_sums = jnp.zeros((block_rows, seq_count, 2 * width), jnp.float32)
    key_sums = lax.fori_loop(0, cycle_size, carry_step, start_sums)
    key_sums = jnp.transpose(key_sums, (1, 0, 2))
    grad_keys = key_sums[:, :, :width].astype(jnp.bfloat16)
    grad_values = key_sums[:, :, width:].astype(jnp.bfloat16)
    grad_normed = (
        project_back(query_grad, w_query)
        + project_back(grad_keys, w_key)
        + project_back(grad_values, w_value)
    )
    _, norm_pull_one = jax.vjp(layer_norm, tokens32, gain_one32, shift_one32)
    grad_tok_part, grad_gain_one, grad_shift_one = norm_pull_one(grad_normed)
    grad_tokens = grad_residual + grad_tok_part
    small_grads = (grad_gain_one, grad_shift_one, grad_gain_two, grad_shift_two)
    operands = (
        normed,
        query_grad,
        grad_keys,
        grad_values,
        mixed_heads,
        grad_branch,
        normed_two,
        grad_pre,
        active,
        cotangent,
    )
    return (output, grad_tokens, small_grads, operands)


def owner_sum(grads):
    dp_count = lax.axis_size("dp")
    ctx_count = lax.axis_size("ctx")
    blocks = tuple((grad_part.reshape(dp_count, ctx_count, -1) for grad_part in grads))
    first_section = jax.tree.map(
        lambda part, own: part.astype(own.dtype),
        lax.all_to_all(as_sent(blocks), "ctx", split_axis=1, concat_axis=1, tiled=True),
        blocks,
    )
    partial_sums = tuple((jnp.sum(piece, axis=1, keepdims=True) for piece in first_section))
    second_section = jax.tree.map(
        lambda part, own: part.astype(own.dtype),
        lax.all_to_all(as_sent(partial_sums), "dp", split_axis=0, concat_axis=0, tiled=True),
        partial_sums,
    )
    owned = []
    for grad_part, piece in zip(grads, second_section):
        summed = jnp.sum(piece, axis=(0, 1))
        row_count = grad_part.shape[0] // (dp_count * ctx_count)
        owned.append(summed.reshape((row_count,) + grad_part.shape[1:]))
    return owned


def on_device(
    tokens_in,
    out_grad,
    w_query,
    w_key,
    w_value,
    w_out,
    w_up,
    w_down,
    b_query,
    b_value,
    b_out,
    b_up,
    b_down,
    norm1_gain,
    norm1_shift,
    norm2_gain,
    norm2_shift,
):
    shards = (
        w_query,
        w_key,
        w_value,
        w_out,
        w_up,
        w_down,
        b_query,
        b_value,
        b_out,
        b_up,
        b_down,
        norm1_gain,
        norm1_shift,
        norm2_gain,
        norm2_shift,
    )
    per_micro = tokens_in.shape[0] // MICRO
    outputs = []
    grads_in = []
    operand_lists = []
    small_total = None
    for micro_index in range(MICRO):
        lower = micro_index * per_micro
        tokens = tokens_in[lower : lower + per_micro]
        cotangent = out_grad[lower : lower + per_micro]
        forward_weights = (
            lax.all_gather(shards[0], ("dp", "ctx"), axis=0, tiled=True),
            lax.all_gather(shards[1], ("dp", "ctx"), axis=0, tiled=True),
            lax.all_gather(shards[2], ("dp", "ctx"), axis=0, tiled=True),
            lax.all_gather(shards[3], ("dp", "ctx"), axis=0, tiled=True),
            lax.all_gather(shards[4], ("dp", "ctx"), axis=0, tiled=True),
            lax.all_gather(shards[5], ("dp", "ctx"), axis=0, tiled=True),
            lax.all_gather(shards[6], ("dp", "ctx"), axis=0, tiled=True),
            lax.all_gather(shards[7], ("dp", "ctx"), axis=0, tiled=True),
            lax.all_gather(shards[8], ("dp", "ctx"), axis=0, tiled=True),
            lax.all_gather(shards[9], ("dp", "ctx"), axis=0, tiled=True),
            lax.all_gather(shards[10], ("dp", "ctx"), axis=0, tiled=True),
            lax.all_gather(shards[11], ("dp", "ctx"), axis=0, tiled=True),
            lax.all_gather(shards[12], ("dp", "ctx"), axis=0, tiled=True),
            lax.all_gather(shards[13], ("dp", "ctx"), axis=0, tiled=True),
            lax.all_gather(shards[14], ("dp", "ctx"), axis=0, tiled=True),
        )
        output, grad_tokens, small_grads, operands = micro_step(
            tokens, cotangent, shards, forward_weights
        )
        outputs.append(output)
        grads_in.append(grad_tokens)
        operand_lists.append(operands)
        if small_total is None:
            small_total = small_grads
        else:
            small_total = tuple(
                (total_grad + update for total_grad, update in zip(small_total, small_grads))
            )
    joined = tuple(
        (jnp.concatenate([entry[index] for entry in operand_lists], axis=0) for index in range(10))
    )
    (
        normed,
        query_grad,
        grad_keys,
        grad_values,
        mixed_heads,
        grad_branch,
        normed_two,
        grad_pre,
        active,
        cotangent,
    ) = joined
    grads = (
        weight_grad(normed, query_grad),
        weight_grad(normed, grad_keys),
        weight_grad(normed, grad_values),
        weight_grad(mixed_heads, grad_branch),
        weight_grad(normed_two, grad_pre),
        weight_grad(active, cotangent),
        column_sum(query_grad),
        column_sum(grad_values),
        column_sum(grad_branch),
        column_sum(grad_pre),
        column_sum(cotangent),
        small_total[0],
        small_total[1],
        small_total[2],
        small_total[3],
    )
    owned = owner_sum(grads)
    layer_out = jnp.concatenate(outputs, axis=0)
    grad_tokens_all = jnp.concatenate(grads_in, axis=0)
    return (
        layer_out,
        grad_tokens_all,
        owned[0],
        owned[1],
        owned[2],
        owned[3],
        owned[4],
        owned[5],
        owned[6],
        owned[7],
        owned[8],
        owned[9],
        owned[10],
        owned[11],
        owned[12],
        owned[13],
        owned[14],
    )


BF = jnp.bfloat16
F32 = jnp.float32
SMALL = 8


def other_core(value):
    return lax.ppermute(value, "core", [(0, 1), (1, 0)])


def other_x(value):
    return lax.ppermute(value, "x", [(0, 1), (1, 0)])


def other_y(value):
    return lax.ppermute(value, "y", [(0, 1), (1, 0)])


def other_z(value, by):
    return lax.ppermute(value, "z", [(i, i ^ by) for i in range(lax.axis_size("z"))])


def pair(bit, own, received):
    return jnp.stack((jnp.where(bit == 0, own, received), jnp.where(bit == 0, received, own)))


def pick(value, index, axis):
    return lax.dynamic_index_in_dim(value, index, axis, keepdims=False)


def in_order(index, pieces):
    level = list(pieces)
    bit = 0
    ordered = [p[None] for p in level]
    while len(ordered) > 1:
        flag = (index >> bit) & 1
        ordered = [
            jnp.concatenate(
                (jnp.where(flag == 0, a, b), jnp.where(flag == 0, b, a)), axis=0
            )
            for a, b in zip(ordered[::2], ordered[1::2])
        ]
        bit += 1
    return ordered[0]


def gather_plane(along_z, x, y):
    half = along_z.shape[0] // 2
    first, second = along_z[:half], along_z[half:]
    first = pair(x, first, other_x(first))
    second = pair(y, second, other_y(second))
    first = pair(y, first, other_y(first))
    second = pair(x, second, other_x(second))
    return jnp.concatenate((jnp.moveaxis(first, 2, 0).swapaxes(1, 2), jnp.moveaxis(second, 2, 0)))


def plus(kept, received):
    return kept.astype(F32) + received.astype(F32)


LIGHT = pl.CostEstimate(flops=0, bytes_accessed=1, transcendentals=0)
VMEM_LIMIT = 56 * 1024 * 1024
QUERY_BLOCK = 256


def lane_masks(dtype):
    lane = lax.broadcasted_iota(jnp.int32, (1, 2 * DH), 1)
    return [(lane < DH).astype(dtype), (lane >= DH).astype(dtype)]


def visible(key_count, query_block):
    key_pos = lax.broadcasted_iota(jnp.int32, (query_block, query_block), 0)
    query_pos = lax.broadcasted_iota(jnp.int32, (query_block, query_block), 1)
    return key_pos <= query_pos


def masked_tail(scores, allowed):
    key_count, query_block = scores.shape
    tail = jnp.where(allowed, scores[key_count - query_block :], -1e30)
    if key_count == query_block:
        return tail
    return jnp.concatenate((scores[: key_count - query_block], tail), axis=0)


def nt(left, right):
    return lax.dot_general(left, right, (((1,), (1,)), ((), ())), preferred_element_type=F32)


def nn(left, right):
    return lax.dot_general(left, right, (((1,), (0,)), ((), ())), preferred_element_type=F32)


def attend_kernel(q_ref, k_ref, v_ref, mixed_ref, lse_ref):
    length = q_ref.shape[0]
    masks = lane_masks(BF)
    allowed = visible(QUERY_BLOCK, QUERY_BLOCK)
    keys = k_ref[...]
    masked_keys = [keys * m for m in masks]
    v_t = v_ref[...].T
    row = lax.broadcasted_iota(jnp.int32, (2 * DH, 1), 0)
    values_t = [jnp.where(row < DH, v_t, jnp.zeros((), BF)), jnp.where(row >= DH, v_t, jnp.zeros((), BF))]
    for start in range(0, length, QUERY_BLOCK):
        stop = start + QUERY_BLOCK
        q = q_ref[start:stop, :]
        mixed_t = None
        for head in range(2):
            scores = masked_tail(nt(masked_keys[head][:stop], q), allowed)
            top = jnp.max(scores, axis=0, keepdims=True)
            powers = jnp.exp(scores - top)
            total = jnp.sum(powers, axis=0, keepdims=True)
            low = (powers * (1.0 / total)).astype(BF)
            part = nn(values_t[head][:, :stop], low)
            mixed_t = part if mixed_t is None else mixed_t + part
            lse_ref[0, head : head + 1, start:stop] = top + jnp.log(total)
        mixed_ref[start:stop, :] = mixed_t.T.astype(BF)


def attend_back_kernel(q_ref, k_ref, v_ref, g_ref, mixed_ref, lse_ref, gq_ref, gk_ref, gv_ref, ka, va):
    length = q_ref.shape[0]
    masks = lane_masks(BF)
    allowed = visible(QUERY_BLOCK, QUERY_BLOCK)
    keys, values = k_ref[...], v_ref[...]
    masked_keys = [keys * m for m in masks]
    masked_values = [values * m for m in masks]
    keys_t = [m.T for m in masked_keys]
    for start in range(length - QUERY_BLOCK, -1, -QUERY_BLOCK):
        stop = start + QUERY_BLOCK
        q, g = q_ref[start:stop, :], g_ref[start:stop, :]
        products = (g.astype(F32) * mixed_ref[start:stop, :].astype(F32)).T
        grad_q_t = None
        grad_k = grad_v = None
        for head in range(2):
            inner = jnp.sum(products[head * DH : (head + 1) * DH], axis=0, keepdims=True)
            scores = masked_tail(nt(masked_keys[head][:stop], q), allowed)
            probs = jnp.exp(scores - lse_ref[0, head : head + 1, start:stop])
            grad_probs = nt(masked_values[head][:stop], g)
            grad_scores = (probs * (grad_probs - inner)).astype(BF)
            part_v = nn(probs.astype(BF), g * masks[head])
            part_k = nn(grad_scores, q * masks[head])
            part_q = nn(keys_t[head][:, :stop], grad_scores)
            grad_v = part_v if head == 0 else grad_v + part_v
            grad_k = part_k if head == 0 else grad_k + part_k
            grad_q_t = part_q if head == 0 else grad_q_t + part_q
        gq_ref[start:stop, :] = grad_q_t.T.astype(BF)
        if stop == length:
            ka[...] = grad_k
            va[...] = grad_v
        else:
            ka[:stop, :] += grad_k
            va[:stop, :] += grad_v
    gk_ref[...] = ka[...].astype(BF)
    gv_ref[...] = va[...].astype(BF)


def attend(queries, keys, values):
    length, width = queries.shape
    pairs = width // (2 * DH)
    block = pl.BlockSpec((length, 2 * DH), lambda i: (0, i))
    return pl.pallas_call(
        attend_kernel,
        grid=(pairs,),
        in_specs=[block] * 3,
        out_specs=[block, pl.BlockSpec((1, 2, length), lambda i: (i, 0, 0))],
        out_shape=[
            jax.ShapeDtypeStruct((length, width), BF),
            jax.ShapeDtypeStruct((pairs, 2, length), F32),
        ],
        compiler_params=pltpu.CompilerParams(vmem_limit_bytes=VMEM_LIMIT),
        cost_estimate=LIGHT,
        name="attend",
    )(queries, keys, values)


def attend_back(queries, keys, values, mixed, lse, grad_mixed, pair_index, pairs):
    length = queries.shape[0]
    block = pl.BlockSpec((length, 2 * DH), lambda i: (0, i + pair_index))
    out_block = pl.BlockSpec((length, 2 * DH), lambda i: (0, i))
    width = pairs * 2 * DH
    return pl.pallas_call(
        attend_back_kernel,
        grid=(pairs,),
        in_specs=[block] * 5 + [pl.BlockSpec((1, 2, length), lambda i: (i + pair_index, 0, 0))],
        out_specs=[out_block] * 3,
        out_shape=[jax.ShapeDtypeStruct((length, width), BF)] * 3,
        scratch_shapes=[pltpu.VMEM((length, 2 * DH), F32)] * 2,
        compiler_params=pltpu.CompilerParams(vmem_limit_bytes=VMEM_LIMIT),
        cost_estimate=LIGHT,
        name="attend_back",
    )(queries, keys, values, grad_mixed, mixed, lse)


def position_blocks(core, block):
    return [
        (b, own, pl.multiple_of(b * 2 * block + (core if own else 1 - core) * block, block))
        for b in range(2)
        for own in (True, False)
    ]


def normalise(values):
    centre = values - jnp.mean(values, axis=-1, keepdims=True)
    spread = jnp.mean(centre * centre, axis=-1, keepdims=True)
    rate = lax.rsqrt(spread + 1e-05)
    return centre * rate, rate


def normalise_back(unit, rate, gain, grad):
    scaled = grad * gain
    return rate * (
        scaled
        - jnp.mean(scaled, axis=-1, keepdims=True)
        - unit * jnp.mean(scaled * unit, axis=-1, keepdims=True)
    )


CORE, X, Y = range(3)
B_QUERY, B_VALUE, B_OUT, B_DOWN, GAIN1, SHIFT1, GAIN2, SHIFT2 = range(8)


def weight(ref, i):
    chips, _, width = ref.shape
    rows = width * 2 // chips
    return ref[:, i * rows : (i + 1) * rows, :].reshape(chips * rows, width)


def add_sums(ref, values):
    @pl.when(pl.program_id(0) == 0)
    def _():
        ref[...] = jnp.zeros(ref.shape, F32)

    for i, value in enumerate(values):
        ref[i : i + 1, :] += jnp.sum(value, axis=0, keepdims=True)


def enter_kernel(core_ref, mine_ref, other_ref, vec_ref, half_ref, w_ref, n_ref, q_ref, k_ref, v_ref):
    core = core_ref[0]
    block = mine_ref.shape[0] // 2
    for b, own, row in position_blocks(core, block):
        tokens = (mine_ref if own else other_ref)[b * block : (b + 1) * block, :].astype(F32)
        unit, _ = normalise(tokens)
        normed = (unit * vec_ref[GAIN1 : GAIN1 + 1, :] + vec_ref[SHIFT1 : SHIFT1 + 1, :]).astype(BF)
        rows = pl.ds(row, block)
        n_ref[rows, :] = normed
        q = (nn(normed, weight(w_ref, 0)) + half_ref[B_QUERY : B_QUERY + 1, :]) * DH ** (-0.5)
        q_ref[rows, :] = q.astype(BF)
        k_ref[rows, :] = nn(normed, weight(w_ref, 1)).astype(BF)
        v_ref[rows, :] = (nn(normed, weight(w_ref, 2)) + half_ref[B_VALUE : B_VALUE + 1, :]).astype(BF)


def out_kernel(core_ref, mixed_ref, w_ref, mine_ref, other_ref):
    block = mine_ref.shape[0] // 2
    for b, own, row in position_blocks(core_ref[0], block):
        part = nn(mixed_ref[pl.ds(row, block), :], w_ref[...])
        ref = mine_ref if own else other_ref
        ref[b * block : (b + 1) * block, :] = part.astype(ref.dtype)


def middle_kernel(tokens_ref, part_ref, received_ref, vec_ref, residual_ref, n_ref):
    residual = (
        tokens_ref[...].astype(F32)
        + part_ref[...]
        + received_ref[...].astype(F32)
        + vec_ref[B_OUT : B_OUT + 1, :]
    )
    unit, _ = normalise(residual)
    residual_ref[...] = residual
    n_ref[...] = (unit * vec_ref[GAIN2 : GAIN2 + 1, :] + vec_ref[SHIFT2 : SHIFT2 + 1, :]).astype(BF)


def middle_back_kernel(residual_ref, gn_ref, gn_received_ref, g_ref, vec_ref, gr_ref, branch_ref, sums_ref):
    unit, rate = normalise(residual_ref[...])
    grad_normed = gn_ref[...] + gn_received_ref[...].astype(F32)
    cotangent = g_ref[...].astype(F32)
    grad = cotangent + normalise_back(unit, rate, vec_ref[GAIN2 : GAIN2 + 1, :], grad_normed)
    gr_ref[...] = grad
    branch = grad.astype(BF)
    branch_ref[...] = branch
    add_sums(sums_ref, (branch.astype(F32), cotangent, grad_normed * unit, grad_normed))


def mixed_back_kernel(core_ref, mixed_ref, mine_ref, other_ref, w_ref, gm_ref, gw_ref):
    block = mine_ref.shape[0] // 2
    total = None
    for b, own, row in position_blocks(core_ref[0], block):
        branch = (mine_ref if own else other_ref)[b * block : (b + 1) * block, :]
        rows = pl.ds(row, block)
        gm_ref[rows, :] = nt(branch, w_ref[...]).astype(BF)
        part = nn(mixed_ref[rows, :].T, branch)
        total = part if total is None else total + part
    gw_ref[...] = total.astype(BF)


def weight_back_kernel(
    place_ref, n_ref, q_ref, k_ref, v_ref, left_keep, left_send, right_keep, right_send, sums_ref, by_y, by_x
):
    x, y = place_ref[X], place_ref[Y]
    n_t = n_ref[...].T
    rows = by_y.shape[2]
    grads = [q_ref[...] * jnp.asarray(DH ** (-0.5), BF), k_ref[...], v_ref[...]]
    for i in range(2):
        by_y[...] = nn(n_t, grads[i]).astype(BF).reshape(by_y.shape)
        part = slice(i * rows, (i + 1) * rows)
        left_keep[:, part, :] = by_y[:, pl.ds(y, 1)].reshape(-1, rows, by_y.shape[3])
        left_send[:, part, :] = by_y[:, pl.ds(1 - y, 1)].reshape(-1, rows, by_y.shape[3])
    by_x[...] = nn(n_t, grads[2]).astype(BF).reshape(by_x.shape)
    right_keep[...] = by_x[:, pl.ds(x, 1)].reshape(right_keep.shape)
    right_send[...] = by_x[:, pl.ds(1 - x, 1)].reshape(right_send.shape)
    half = q_ref.shape[1]
    side = lax.broadcasted_iota(jnp.int32, (1, 2 * half), 1) >= half
    for i, grad in enumerate((grads[0], grads[2])):
        total = jnp.sum(grad.astype(F32), axis=0, keepdims=True)
        total = jnp.concatenate((total, total), axis=1)
        sums_ref[i : i + 1, :] = jnp.where(side == (place_ref[CORE] == 1), total, 0.0)


def enter_back_kernel(place_ref, q_ref, k_ref, v_ref, w_ref, mine_ref, other_ref):
    block = mine_ref.shape[0] // 2
    for b, own, row in position_blocks(place_ref[CORE], block):
        rows = pl.ds(row, block)
        part = (
            nt(q_ref[rows, :] * jnp.asarray(DH ** (-0.5), BF), weight(w_ref, 0))
            + nt(k_ref[rows, :], weight(w_ref, 1))
            + nt(v_ref[rows, :], weight(w_ref, 2))
        )
        ref = mine_ref if own else other_ref
        ref[b * block : (b + 1) * block, :] = part.astype(ref.dtype)


def leave_kernel(tokens_ref, gn_ref, gn_received_ref, gr_ref, vec_ref, gt_ref, sums_ref):
    unit, rate = normalise(tokens_ref[...].astype(F32))
    grad_normed = gn_ref[...] + gn_received_ref[...].astype(F32)
    gt_ref[...] = gr_ref[...] + normalise_back(unit, rate, vec_ref[GAIN1 : GAIN1 + 1, :], grad_normed)
    add_sums(sums_ref, (grad_normed * unit, grad_normed))


def shape(dims, dtype):
    return jax.ShapeDtypeStruct(dims, dtype)


def whole_call(kernel, outs, *args, flops=0, scalars=0, scratch=()):
    in_specs = [
        pl.BlockSpec(memory_space=pltpu.SMEM if i < scalars else pltpu.VMEM)
        for i in range(len(args))
    ]
    moved = sum(a.size * a.dtype.itemsize for a in list(args) + outs)
    return pl.pallas_call(
        kernel,
        in_specs=in_specs,
        out_specs=[pl.BlockSpec(memory_space=pltpu.VMEM)] * len(outs),
        out_shape=outs,
        scratch_shapes=list(scratch),
        compiler_params=pltpu.CompilerParams(vmem_limit_bytes=VMEM_LIMIT),
        cost_estimate=LIGHT,
        name=kernel.__name__,
    )(*args)


def row_call(kernel, outs, sums, *args):
    length, width = args[0].shape
    block = length // 2
    rows = pl.BlockSpec((block, width), lambda i: (i, 0))
    out_shape = [shape((length, width), dtype) for dtype in outs]
    out_specs = [rows] * len(outs)
    if sums:
        out_shape.append(shape((sums, width), F32))
        out_specs.append(pl.BlockSpec((sums, width), lambda i: (0, 0)))
    moved = sum(a.size * a.dtype.itemsize for a in list(args) + out_shape)
    return pl.pallas_call(
        kernel,
        grid=(2,),
        in_specs=[rows] * (len(args) - 1) + [pl.BlockSpec(args[-1].shape, lambda i: (0, 0))],
        out_specs=out_specs,
        out_shape=out_shape,
        compiler_params=pltpu.CompilerParams(vmem_limit_bytes=VMEM_LIMIT),
        cost_estimate=LIGHT,
        name=kernel.__name__,
    )(*args)


def hidden_kernel(
    place_ref, n_mine, n_other, g_mine, g_other, up_ref, down_ref, bias_ref,
    y_mine, y_other, gn_mine, gn_other, up_keep, up_send, down_keep, down_send, gb_ref,
    n_t, y_sum, gn_sum, up_all, down_all,
):
    step = pl.program_id(0)
    length = n_mine.shape[0]

    @pl.when(step == 0)
    def _():
        n_t[:, :length] = n_mine[...].T
        n_t[:, length:] = n_other[...].T
        for ref in (y_mine, gn_mine, y_sum, gn_sum):
            ref[...] = jnp.zeros(ref.shape, F32)

    up = up_ref[...].reshape(-1, up_ref.shape[2])
    down = down_ref[...].reshape(-1, down_ref.shape[2])
    grad_up = grad_down = bias_sum = None
    for part, (n_ref, g_ref, y_ref, gn_ref) in enumerate(
        ((n_mine, g_mine, y_mine, gn_mine), (n_other, g_other, y_sum, gn_sum))
    ):
        n, g = n_ref[...], g_ref[...]
        pre = nn(n, up) + bias_ref[0]
        square = pre * pre
        bent = jnp.tanh(pre * (0.7978845608028654 + 0.7978845608028654 * 0.044715 * square))
        half = 0.5 + 0.5 * bent
        active = (pre * half).astype(BF)
        rise = pre * (2 * 0.7978845608028654 + 6 * 0.7978845608028654 * 0.044715 * square)
        slope = half * (1.0 + (1.0 - half) * rise)
        grad_pre = (nt(g, down) * slope).astype(BF)
        y_ref[...] += nn(active, down)
        gn_ref[...] += nt(grad_pre, up)
        part_up = nn(n_t[:, part * length : (part + 1) * length], grad_pre)
        part_down = lax.dot_general(active, g, (((0,), (0,)), ((), ())), preferred_element_type=F32)
        part_bias = jnp.sum(grad_pre.astype(F32), axis=0, keepdims=True)
        grad_up = part_up if part == 0 else grad_up + part_up
        grad_down = part_down if part == 0 else grad_down + part_down
        bias_sum = part_bias if part == 0 else bias_sum + part_bias
    x, y = place_ref[X], place_ref[Y]
    up_all[...] = grad_up.astype(BF).reshape(up_all.shape)
    up_keep[...] = up_all[:, pl.ds(y, 1)].reshape(up_keep.shape)
    up_send[...] = up_all[:, pl.ds(1 - y, 1)].reshape(up_send.shape)
    down_all[...] = grad_down.astype(BF).reshape(down_all.shape)
    down_keep[...] = down_all[:, pl.ds(x, 1)].reshape(down_keep.shape)
    down_send[...] = down_all[:, pl.ds(1 - x, 1)].reshape(down_send.shape)
    gb_ref[0] = bias_sum

    @pl.when(step == pl.num_programs(0) - 1)
    def _():
        y_other[...] = y_sum[...].astype(BF)
        gn_other[...] = gn_sum[...].astype(BF)


def feed_forward(place, n_mine, n_other, g_mine, g_other, late, bias, hidden_rows):
    length, width = n_mine.shape
    chips = late.shape[0]
    steps = 2
    z_count = chips // 4
    z_step = z_count // steps
    tile = chips * hidden_rows // steps
    up_rows = width // chips
    per_half = steps // 2
    down_chips = chips // steps
    full = pl.BlockSpec((length, width), lambda i: (0, 0))
    hidden = tile * steps
    return pl.pallas_call(
        hidden_kernel,
        grid=(steps,),
        in_specs=[pl.BlockSpec(memory_space=pltpu.SMEM)] + [full] * 4
        + [
            pl.BlockSpec((chips, up_rows, tile), lambda i: (0, i // per_half, i % per_half)),
            pl.BlockSpec((down_chips, hidden_rows, width), lambda i: (i, 1, 0)),
            pl.BlockSpec((1, 1, tile), lambda i: (i, 0, 0)),
        ],
        out_specs=[full] * 4
        + [
            pl.BlockSpec((chips // 2, up_rows, tile), lambda i: (0, 0, i)),
            pl.BlockSpec((chips // 2, up_rows, tile), lambda i: (0, 0, i)),
            pl.BlockSpec((z_step, 2, hidden_rows, width), lambda i: (i, 0, 0, 0)),
            pl.BlockSpec((z_step, 2, hidden_rows, width), lambda i: (i, 0, 0, 0)),
            pl.BlockSpec((1, 1, tile), lambda i: (i, 0, 0)),
        ],
        out_shape=[
            shape((length, width), F32),
            shape((length, width), BF),
            shape((length, width), F32),
            shape((length, width), BF),
            shape((chips // 2, up_rows, hidden), BF),
            shape((chips // 2, up_rows, hidden), BF),
            shape((z_count, 2, hidden_rows, width), BF),
            shape((z_count, 2, hidden_rows, width), BF),
            shape((steps, 1, tile), F32),
        ],
        scratch_shapes=[
            pltpu.VMEM((width, 2 * length), BF),
            pltpu.VMEM((length, width), F32),
            pltpu.VMEM((length, width), F32),
            pltpu.VMEM((chips // 2, 2, up_rows, tile), BF),
            pltpu.VMEM((z_step, 2, 2, hidden_rows, width), BF),
        ],
        compiler_params=pltpu.CompilerParams(vmem_limit_bytes=VMEM_LIMIT),
        cost_estimate=LIGHT,
        name="feed_forward",
    )(place, n_mine, n_other, g_mine, g_other, late, late, bias.reshape(steps, 1, tile))


def chip_step(
    tokens_in,
    out_grad,
    w_query,
    w_key,
    w_value,
    w_out,
    w_up,
    w_down,
    b_query,
    b_value,
    b_out,
    b_up,
    b_down,
    norm1_gain,
    norm1_shift,
    norm2_gain,
    norm2_shift,
):
    z, x, y, core = (lax.axis_index(name) for name in ("z", "x", "y", "core"))
    z_count = lax.axis_size("z")
    chips = z_count * 4
    half_chips = chips // 2
    _, block, width = tokens_in.shape
    half = width // 2
    rows = w_query.shape[0]
    hidden_rows = w_down.shape[0]
    hidden = hidden_rows * chips

    def own_positions(value):
        return pair(y, pick(value, y, 0), other_y(pick(value, 1 - y, 0))).reshape(2 * block, width)

    three = jnp.stack((w_query, w_key, w_value)).reshape(3, rows, 2, half)
    vectors = (
        b_query, b_value, b_out, b_down, norm1_gain, norm1_shift, norm2_gain, norm2_shift, b_up
    )
    small = jnp.concatenate(vectors)
    unit_rows = 3 * rows + SMALL
    small_rows = jnp.zeros((SMALL, half), BF).at[0, : small.shape[0]].set(small)
    own = jnp.concatenate((pick(three, core, 2).reshape(3 * rows, half), small_rows))
    unit = pair(
        core,
        own,
        other_core(
            jnp.concatenate((pick(three, 1 - core, 2).reshape(3 * rows, half), small_rows))
        ),
    )
    up_parts = w_up.reshape(rows, chips, 2, hidden_rows)
    up_unit = pair(
        core,
        pick(up_parts, core, 2).reshape(rows, hidden),
        other_core(pick(up_parts, 1 - core, 2).reshape(rows, hidden)),
    )
    up_unit = up_unit.reshape(2 * rows, 2, width)
    late = jnp.concatenate((up_unit[:, 0], up_unit[:, 1], w_down))
    late = lax.all_gather(late, ("z", "x", "y"), axis=0, tiled=False)
    threes = unit[:, : 3 * rows].reshape(2, 3, rows, half).swapaxes(0, 1).reshape(6 * rows, half)
    unit = jnp.concatenate(
        (threes, unit[:, 3 * rows :].reshape(2 * SMALL, half), w_out[:, :half], w_out[:, half:])
    )
    pieces = [unit] + [other_z(unit, k) for k in range(1, z_count)]
    both = jnp.stack((pick(tokens_in, y, 0), pick(out_grad, y, 0)))
    both_from = other_y(jnp.stack((pick(tokens_in, 1 - y, 0), pick(out_grad, 1 - y, 0))))
    pieces, both_from = lax.optimization_barrier((pieces, both_from))
    both = pair(y, both, both_from).swapaxes(0, 1).reshape(2, 2 * block, width)
    mine, grad_mine = both[0], both[1]
    other, grad_other = other_core(mine), other_core(grad_mine)
    place = jnp.stack((core, x, y)).astype(jnp.int32)
    gathered = gather_plane(in_order(z, pieces), x, y)
    out_parts = jnp.concatenate(
        (gathered[..., 2 * unit_rows : 2 * unit_rows + rows, :], gathered[..., 2 * unit_rows + rows :, :]),
        axis=-1,
    ).reshape(2, half_chips, rows, width)
    out_c = (
        pair(core, pick(out_parts, core, 0), other_core(pick(out_parts, 1 - core, 0)))
        .swapaxes(0, 1)
        .reshape(half, width)
    )
    gathered = gathered.reshape(chips, -1, half)
    small_all = gathered[:, 6 * rows : 6 * rows + 2 * SMALL].reshape(chips * 2, SMALL, half)
    small_all = small_all[:, 0, : small.shape[0]]
    vectors = small_all[:, : 8 * rows].reshape(chips * 2, 8, rows).swapaxes(0, 1)
    vectors = vectors.reshape(8, width).astype(F32)
    halves = pick(vectors.reshape(8, 2, half), core, 1)
    bias_u = pick(small_all[:, 8 * rows :].reshape(chips, 2, hidden_rows), core, 1)
    bias_u = bias_u.reshape(hidden).astype(F32)

    length = 4 * block
    heads_shape = shape((length, half), BF)
    normed, queries, keys, values = whole_call(
        enter_kernel,
        [shape((length, width), BF)] + [heads_shape] * 3,
        place, mine, other, vectors, halves, gathered,
        flops=6 * length * width * half, scalars=1,
    )
    mixed, lse = attend(queries, keys, values)
    mine_shape = shape((2 * block, width), F32)
    sent_shape = shape((2 * block, width), BF)
    part, to_other = whole_call(
        out_kernel, [mine_shape, sent_shape], place, mixed, out_c,
        flops=2 * length * width * half, scalars=1,
    )
    residual, normed2 = row_call(middle_kernel, (F32, BF), 0, mine, part, other_core(to_other), vectors)
    late, normed2 = lax.optimization_barrier((late, normed2))
    y_mine, y_other, gn_mine, gn_other, up_keep, up_send, down_keep, down_send, up_sums = feed_forward(
        place, normed2, other_core(normed2), grad_mine, grad_other, late, bias_u, hidden_rows
    )

    up_from, down_from = other_y(up_send), other_x(down_send)
    grad_residual, branch, sums2 = row_call(
        middle_back_kernel, (F32, BF), 4, residual, gn_mine, other_core(gn_other), grad_mine, vectors
    )
    grad_mixed, grad_out = whole_call(
        mixed_back_kernel, [heads_shape, shape((half, width), BF)],
        place, mixed, branch, other_core(branch), out_c,
        flops=4 * length * width * half, scalars=1,
    )
    grad_out = grad_out.reshape(half_chips, 2, rows, width)
    grad_out = pair(
        core,
        pick(grad_out, core, 1),
        other_core(pick(grad_out, 1 - core, 1)),
    ).reshape(z_count, 2, 2, rows, width)
    grads = attend_back(
        queries, keys, values, mixed, lse, grad_mixed, 0, half // (2 * DH)
    )
    up_from, down_from, grads = lax.optimization_barrier((up_from, down_from, grads))
    ups = plus(up_keep, up_from).reshape(z_count, 2, 2 * rows, hidden)
    downs = plus(down_keep, down_from)
    up_send, down_send = pick(ups, 1 - x, 1).astype(BF), pick(downs, 1 - y, 1).astype(BF)
    up_send, down_send, grads = lax.optimization_barrier((up_send, down_send, grads))
    up_from, down_from, out_from = other_x(up_send), other_y(down_send), other_x(pick(grad_out, 1 - x, 1))
    left_shape = shape((2 * z_count, 4 * rows, half), BF)
    right_shape = shape((z_count, 2, 2 * rows, half), BF)
    left_keep, left_send, right_keep, right_send, sums_heads = whole_call(
        weight_back_kernel,
        [left_shape] * 2 + [right_shape] * 2 + [shape((2, width), F32)],
        place, normed, *grads,
        flops=6 * length * width * half, scalars=1,
        scratch=(
            pltpu.VMEM((2 * z_count, 2, 2 * rows, half), BF),
            pltpu.VMEM((z_count, 2, 2, 2 * rows, half), BF),
        ),
    )
    left_send, right_send, grads, y_mine, y_other = lax.optimization_barrier(
        (left_send, right_send, grads, y_mine, y_other)
    )
    left_from, right_from = other_y(left_send), other_x(right_send)
    gn_mine, gn_other = whole_call(
        enter_back_kernel,
        [mine_shape, sent_shape],
        place, *grads, gathered,
        flops=6 * length * width * half, scalars=1,
    )
    up_from, down_from, out_from, gn_mine, gn_other = lax.optimization_barrier(
        (up_from, down_from, out_from, gn_mine, gn_other)
    )
    low, high = z & 1, z >> 1

    def first_z(value):
        value = value.reshape((z_count // 2, 2) + value.shape[1:])
        return pick(value, low, 1), other_z(pick(value, 1 - low, 1).astype(BF), 1)

    def second_z(value):
        return pick(value, high, 0), other_z(pick(value, 1 - high, 0).astype(BF), 2)

    gn_from = other_core(gn_other)
    ups = plus(pick(ups, x, 1), up_from)
    downs = plus(pick(downs, y, 1), down_from)
    outs = plus(pick(grad_out, x, 1), out_from)
    forward_kept, forward_from = first_z(
        jnp.concatenate((ups[..., :width], ups[..., width:], downs), axis=1)
    )
    left_from, right_from, gn_from = lax.optimization_barrier((left_from, right_from, gn_from))
    lefts = plus(left_keep, left_from).reshape(z_count, 2, 4 * rows, half)
    rights = plus(right_keep, right_from)
    rights = jnp.concatenate((rights, outs[..., :half], outs[..., half:]), axis=2)
    left_send, right_send = pick(lefts, 1 - x, 1).astype(BF), pick(rights, 1 - y, 1).astype(BF)
    left_send, right_send, gn_from = lax.optimization_barrier((left_send, right_send, gn_from))
    left_from, right_from = other_x(left_send), other_y(right_send)
    grad_tokens, sums1 = row_call(
        leave_kernel, (F32,), 2, mine, gn_mine, gn_from, grad_residual, vectors
    )
    output = residual + y_mine + other_core(y_other).astype(F32) + vectors[B_DOWN]
    output = output.astype(BF).reshape(2, block, width)
    grad_tokens = grad_tokens.reshape(2, block, width)
    to_y = jnp.concatenate((pick(output, 1 - y, 0), pick(grad_tokens, 1 - y, 0).astype(BF)))
    forward_from, to_y = lax.optimization_barrier((forward_from, to_y))
    from_y = other_y(to_y)
    forward_kept, forward_from = second_z(plus(forward_kept, forward_from))

    left_from, right_from, sums1 = lax.optimization_barrier((left_from, right_from, sums1))
    small_grads = jnp.concatenate((sums_heads, sums2, sums1, up_sums.reshape(2, width)))
    small_grads = small_grads + other_y(small_grads)
    small_grads = small_grads + other_x(small_grads)
    lefts = plus(pick(lefts, x, 1), left_from)
    rights = plus(pick(rights, y, 1), right_from)
    last, last_from = first_z(jnp.concatenate((lefts, rights), axis=1))
    last_from, small_grads = lax.optimization_barrier((last_from, small_grads))
    small_grads = small_grads + other_z(small_grads, 1)
    small_grads = small_grads + other_z(small_grads, 2)
    small_core = small_grads[:8] + other_core(small_grads[:8])
    last_from, forward_from = lax.optimization_barrier((last_from, forward_from))
    last, last_from = second_z(plus(last, last_from))
    forward_sum = plus(forward_kept, forward_from)
    last = plus(last, last_from)
    layer_out = pair(y, pick(output, y, 0), from_y[:block])
    grad_tokens = pair(y, pick(grad_tokens, y, 0), from_y[block:].astype(F32))

    up_mine = forward_sum[: 4 * rows].reshape(2, 2, rows, width)
    down_mine = forward_sum[4 * rows :]
    three_mine = last[: 6 * rows].reshape(3, 2, rows, half)
    out_mine = jnp.concatenate((last[6 * rows : 7 * rows], last[7 * rows : 8 * rows]), axis=1)
    up_from = other_core(pick(up_mine, 1 - core, 1))
    chip = (z * 2 + x) * 2 + y
    small_mine = lax.dynamic_slice_in_dim(small_core, (chip * 2 + core) * rows, rows, 1)
    up_bias = lax.dynamic_slice_in_dim(small_grads[8:].reshape(hidden), chip * hidden_rows, hidden_rows, 0)
    three_from = other_core(pick(three_mine, 1 - core, 1))
    three_out = pair(core, pick(three_mine, core, 1), three_from)
    up_out = pair(core, pick(up_mine, core, 1), up_from)
    up_out = up_out.reshape(2, 2, rows, half_chips, hidden_rows)
    up_out = jnp.transpose(up_out, (2, 1, 3, 0, 4)).reshape(rows, 2 * hidden)
    g_q, g_k, g_v = (jnp.concatenate((three_out[0, i], three_out[1, i]), axis=1) for i in range(3))
    g_small = [small_mine[i] for i in (0, 1, 2, 3, 6, 7, 4, 5)]
    return (
        layer_out,
        grad_tokens,
        g_q,
        g_k,
        g_v,
        out_mine,
        up_out,
        down_mine,
        g_small[0],
        g_small[1],
        g_small[2],
        up_bias,
        g_small[3],
        g_small[4],
        g_small[5],
        g_small[6],
        g_small[7],
    )


def solution(mesh):
    dp_count, ctx_count = mesh.shape["dp"], mesh.shape["ctx"]

    def run(*args):
        per_dp = args[0].shape[0] // dp_count
        if ctx_count == 4 and per_dp == 2 and dp_count == 8:
            devices = mesh.devices.reshape(dp_count // 2, 2, ctx_count // 2, 2)
            used = Mesh(devices, ("z", "x", "y", "core"))
            body, dp, ctx = chip_step, ("z", "x"), ("y", "core")
        else:
            used, body, dp, ctx = mesh, on_device, ("dp",), ("ctx",)
        tokens, matrix, bias = P(dp, ctx, None), P(dp + ctx, None), P(dp + ctx)
        return jax.shard_map(
            body,
            mesh=used,
            in_specs=(tokens,) * 2 + (matrix,) * 6 + (bias,) * 9,
            out_specs=(tokens,) * 2 + (matrix,) * 6 + (bias,) * 9,
            check_vma=False,
        )(*args)

    return run
```

```python
import jax
import jax.numpy as jnp
from jax import lax
from jax.experimental import pallas as pl
from jax.experimental.pallas import tpu as pltpu
from jax.sharding import Mesh
from jax.sharding import PartitionSpec as P

HEADS = 12
DH = 64
MICRO = 2


def shifted(value, axis, by):
    peers = lax.axis_size(axis)
    return lax.ppermute(value, axis, [(i, (i + by) % peers) for i in range(peers)])


def as_sent(value):
    return jax.tree.map(lambda a: a.astype(jnp.bfloat16) if a.dtype == jnp.float32 else a, value)


def layer_norm(values, norm_gain, norm_shift):
    centre = values - jnp.mean(values, axis=-1, keepdims=True)
    spread = jnp.mean(centre * centre, axis=-1, keepdims=True)
    return centre * lax.rsqrt(spread + 1e-05) * norm_gain + norm_shift


def gelu_tanh(values):
    return (
        0.5
        * values
        * (1.0 + jnp.tanh(0.7978845608028654 * (values + 0.044715 * values * values * values)))
    )


def project(left, right):
    return jnp.einsum("scd,de->sce", left, right, preferred_element_type=jnp.float32)


def project_back(left, right):
    return jnp.einsum("sce,de->scd", left, right, preferred_element_type=jnp.float32)


def weight_grad(left, right):
    return jnp.einsum("scd,sce->de", left, right, preferred_element_type=jnp.float32)


def column_sum(values):
    return jnp.sum(values.astype(jnp.float32), axis=(0, 1))


def masked_scores(query_heads, key_full, first_pos):
    seq_count, key_len = (key_full.shape[0], key_full.shape[1])
    key_heads = key_full.reshape(seq_count, key_len, HEADS, DH)
    scores = jnp.einsum(
        "sqhd,skhd->shqk", query_heads, key_heads, preferred_element_type=jnp.float32
    )
    row_pos = first_pos + jnp.arange(query_heads.shape[1], dtype=jnp.int32)
    col_pos = jnp.arange(key_len, dtype=jnp.int32)
    allowed = row_pos[:, None] >= col_pos[None, :]
    return (jnp.where(allowed, scores, -1e30), key_heads)


def micro_step(tokens, cotangent, shards, forward_weights):
    (
        w_query,
        w_key,
        w_value,
        w_out,
        w_up,
        w_down,
        b_query,
        b_value,
        b_out,
        b_up,
        b_down,
        gain_one,
        shift_one,
        gain_two,
        shift_two,
    ) = forward_weights
    seq_count, block_rows, width = tokens.shape
    query_scale = DH ** (-0.5)
    first_pos = lax.axis_index("ctx") * block_rows
    gain_one32, shift_one32 = (gain_one.astype(jnp.float32), shift_one.astype(jnp.float32))
    gain_two32, shift_two32 = (gain_two.astype(jnp.float32), shift_two.astype(jnp.float32))
    tokens32 = tokens.astype(jnp.float32)
    normed = layer_norm(tokens32, gain_one32, shift_one32).astype(jnp.bfloat16)
    queries = ((project(normed, w_query) + b_query.astype(jnp.float32)) * query_scale).astype(
        jnp.bfloat16
    )
    keys_local = project(normed, w_key).astype(jnp.bfloat16)
    values_local = (project(normed, w_value) + b_value.astype(jnp.float32)).astype(jnp.bfloat16)
    key_full, value_full = (
        lax.all_gather(keys_local, "ctx", axis=1, tiled=True),
        lax.all_gather(values_local, "ctx", axis=1, tiled=True),
    )
    query_heads = queries.reshape(seq_count, block_rows, HEADS, DH)
    scores, key_heads = masked_scores(query_heads, key_full, first_pos)
    row_max = jnp.max(scores, axis=-1, keepdims=True)
    exp_scores = jnp.exp(scores - row_max)
    row_total = jnp.sum(exp_scores, axis=-1, keepdims=True)
    probs_low = (exp_scores / row_total).astype(jnp.bfloat16)
    value_heads = value_full.reshape(seq_count, value_full.shape[1], HEADS, DH)
    mixed_heads = jnp.einsum(
        "shqk,skhd->sqhd", probs_low, value_heads, preferred_element_type=jnp.float32
    ).reshape(seq_count, block_rows, width)
    mixed_heads = mixed_heads.astype(jnp.bfloat16)
    residual = tokens32 + project(mixed_heads, w_out) + b_out.astype(jnp.float32)
    normed_two = layer_norm(residual, gain_two32, shift_two32).astype(jnp.bfloat16)
    hidden_pre = project(normed_two, w_up) + b_up.astype(jnp.float32)
    active = gelu_tanh(hidden_pre).astype(jnp.bfloat16)
    output = (residual + project(active, w_down) + b_down.astype(jnp.float32)).astype(jnp.bfloat16)
    back_weights = (
        lax.all_gather(shards[0], ("dp", "ctx"), axis=0, tiled=True),
        lax.all_gather(shards[1], ("dp", "ctx"), axis=0, tiled=True),
        lax.all_gather(shards[2], ("dp", "ctx"), axis=0, tiled=True),
        lax.all_gather(shards[3], ("dp", "ctx"), axis=0, tiled=True),
        lax.all_gather(shards[4], ("dp", "ctx"), axis=0, tiled=True),
        lax.all_gather(shards[5], ("dp", "ctx"), axis=0, tiled=True),
        lax.all_gather(shards[6], ("dp", "ctx"), axis=0, tiled=True),
        lax.all_gather(shards[7], ("dp", "ctx"), axis=0, tiled=True),
        lax.all_gather(shards[8], ("dp", "ctx"), axis=0, tiled=True),
        lax.all_gather(shards[9], ("dp", "ctx"), axis=0, tiled=True),
        lax.all_gather(shards[10], ("dp", "ctx"), axis=0, tiled=True),
        lax.all_gather(shards[11], ("dp", "ctx"), axis=0, tiled=True),
        lax.all_gather(shards[12], ("dp", "ctx"), axis=0, tiled=True),
        lax.all_gather(shards[13], ("dp", "ctx"), axis=0, tiled=True),
        lax.all_gather(shards[14], ("dp", "ctx"), axis=0, tiled=True),
    )
    w_query, w_key, w_value, w_out, w_up, w_down = back_weights[:6]
    grad_active = project_back(cotangent, w_down)
    _, gelu_pull = jax.vjp(gelu_tanh, hidden_pre)
    grad_pre = gelu_pull(grad_active)[0].astype(jnp.bfloat16)
    grad_normed_two = project_back(grad_pre, w_up)
    _, norm_pull_two = jax.vjp(layer_norm, residual, gain_two32, shift_two32)
    grad_res_part, grad_gain_two, grad_shift_two = norm_pull_two(grad_normed_two)
    grad_residual = cotangent.astype(jnp.float32) + grad_res_part
    grad_branch = grad_residual.astype(jnp.bfloat16)
    grad_mixed = project_back(grad_branch, w_out).astype(jnp.bfloat16)
    key_full, value_full = (
        lax.all_gather(keys_local, "ctx", axis=1, tiled=True),
        lax.all_gather(values_local, "ctx", axis=1, tiled=True),
    )
    value_heads = value_full.reshape(seq_count, value_full.shape[1], HEADS, DH)
    scores, key_heads = masked_scores(query_heads, key_full, first_pos)
    probs = jnp.exp(scores - row_max) / row_total
    probs_low = probs.astype(jnp.bfloat16)
    grad_heads = grad_mixed.reshape(seq_count, block_rows, HEADS, DH)
    grad_probs = jnp.einsum(
        "sqhd,skhd->shqk", grad_heads, value_heads, preferred_element_type=jnp.float32
    )
    inner_rows = jnp.sum(probs * grad_probs, axis=-1, keepdims=True)
    grad_scores = (probs * (grad_probs - inner_rows)).astype(jnp.bfloat16)
    grad_queries = jnp.einsum(
        "shqk,skhd->sqhd", grad_scores, key_heads, preferred_element_type=jnp.float32
    )
    grad_queries = grad_queries.reshape(seq_count, block_rows, width).astype(jnp.bfloat16)
    query_grad = grad_queries * query_scale

    def key_terms(first_row, row_count):
        score_part = lax.dynamic_slice_in_dim(grad_scores, first_row, row_count, 3)
        prob_part = lax.dynamic_slice_in_dim(probs_low, first_row, row_count, 3)
        key_part = jnp.einsum(
            "shqk,sqhd->kshd", score_part, query_heads, preferred_element_type=jnp.float32
        )
        value_part = jnp.einsum(
            "shqk,sqhd->kshd", prob_part, grad_heads, preferred_element_type=jnp.float32
        )
        return jnp.concatenate(
            (
                key_part.reshape(row_count, seq_count, width),
                value_part.reshape(row_count, seq_count, width),
            ),
            axis=2,
        )

    cycle_size = lax.axis_size("ctx")
    own_index = lax.axis_index("ctx")

    def carry_step(step, carried):
        holder = (own_index - step) % cycle_size
        carried = carried + key_terms(holder * block_rows, block_rows)
        return shifted(carried.astype(jnp.bfloat16), "ctx", 1).astype(carried.dtype)

    start_sums = jnp.zeros((block_rows, seq_count, 2 * width), jnp.float32)
    key_sums = lax.fori_loop(0, cycle_size, carry_step, start_sums)
    key_sums = jnp.transpose(key_sums, (1, 0, 2))
    grad_keys = key_sums[:, :, :width].astype(jnp.bfloat16)
    grad_values = key_sums[:, :, width:].astype(jnp.bfloat16)
    grad_normed = (
        project_back(query_grad, w_query)
        + project_back(grad_keys, w_key)
        + project_back(grad_values, w_value)
    )
    _, norm_pull_one = jax.vjp(layer_norm, tokens32, gain_one32, shift_one32)
    grad_tok_part, grad_gain_one, grad_shift_one = norm_pull_one(grad_normed)
    grad_tokens = grad_residual + grad_tok_part
    small_grads = (grad_gain_one, grad_shift_one, grad_gain_two, grad_shift_two)
    operands = (
        normed,
        query_grad,
        grad_keys,
        grad_values,
        mixed_heads,
        grad_branch,
        normed_two,
        grad_pre,
        active,
        cotangent,
    )
    return (output, grad_tokens, small_grads, operands)


def owner_sum(grads):
    dp_count = lax.axis_size("dp")
    ctx_count = lax.axis_size("ctx")
    blocks = tuple((grad_part.reshape(dp_count, ctx_count, -1) for grad_part in grads))
    first_section = jax.tree.map(
        lambda part, own: part.astype(own.dtype),
        lax.all_to_all(as_sent(blocks), "ctx", split_axis=1, concat_axis=1, tiled=True),
        blocks,
    )
    partial_sums = tuple((jnp.sum(piece, axis=1, keepdims=True) for piece in first_section))
    second_section = jax.tree.map(
        lambda part, own: part.astype(own.dtype),
        lax.all_to_all(as_sent(partial_sums), "dp", split_axis=0, concat_axis=0, tiled=True),
        partial_sums,
    )
    owned = []
    for grad_part, piece in zip(grads, second_section):
        summed = jnp.sum(piece, axis=(0, 1))
        row_count = grad_part.shape[0] // (dp_count * ctx_count)
        owned.append(summed.reshape((row_count,) + grad_part.shape[1:]))
    return owned


def on_device(
    tokens_in,
    out_grad,
    w_query,
    w_key,
    w_value,
    w_out,
    w_up,
    w_down,
    b_query,
    b_value,
    b_out,
    b_up,
    b_down,
    norm1_gain,
    norm1_shift,
    norm2_gain,
    norm2_shift,
):
    shards = (
        w_query,
        w_key,
        w_value,
        w_out,
        w_up,
        w_down,
        b_query,
        b_value,
        b_out,
        b_up,
        b_down,
        norm1_gain,
        norm1_shift,
        norm2_gain,
        norm2_shift,
    )
    per_micro = tokens_in.shape[0] // MICRO
    outputs = []
    grads_in = []
    operand_lists = []
    small_total = None
    for micro_index in range(MICRO):
        lower = micro_index * per_micro
        tokens = tokens_in[lower : lower + per_micro]
        cotangent = out_grad[lower : lower + per_micro]
        forward_weights = (
            lax.all_gather(shards[0], ("dp", "ctx"), axis=0, tiled=True),
            lax.all_gather(shards[1], ("dp", "ctx"), axis=0, tiled=True),
            lax.all_gather(shards[2], ("dp", "ctx"), axis=0, tiled=True),
            lax.all_gather(shards[3], ("dp", "ctx"), axis=0, tiled=True),
            lax.all_gather(shards[4], ("dp", "ctx"), axis=0, tiled=True),
            lax.all_gather(shards[5], ("dp", "ctx"), axis=0, tiled=True),
            lax.all_gather(shards[6], ("dp", "ctx"), axis=0, tiled=True),
            lax.all_gather(shards[7], ("dp", "ctx"), axis=0, tiled=True),
            lax.all_gather(shards[8], ("dp", "ctx"), axis=0, tiled=True),
            lax.all_gather(shards[9], ("dp", "ctx"), axis=0, tiled=True),
            lax.all_gather(shards[10], ("dp", "ctx"), axis=0, tiled=True),
            lax.all_gather(shards[11], ("dp", "ctx"), axis=0, tiled=True),
            lax.all_gather(shards[12], ("dp", "ctx"), axis=0, tiled=True),
            lax.all_gather(shards[13], ("dp", "ctx"), axis=0, tiled=True),
            lax.all_gather(shards[14], ("dp", "ctx"), axis=0, tiled=True),
        )
        output, grad_tokens, small_grads, operands = micro_step(
            tokens, cotangent, shards, forward_weights
        )
        outputs.append(output)
        grads_in.append(grad_tokens)
        operand_lists.append(operands)
        if small_total is None:
            small_total = small_grads
        else:
            small_total = tuple(
                (total_grad + update for total_grad, update in zip(small_total, small_grads))
            )
    joined = tuple(
        (jnp.concatenate([entry[index] for entry in operand_lists], axis=0) for index in range(10))
    )
    (
        normed,
        query_grad,
        grad_keys,
        grad_values,
        mixed_heads,
        grad_branch,
        normed_two,
        grad_pre,
        active,
        cotangent,
    ) = joined
    grads = (
        weight_grad(normed, query_grad),
        weight_grad(normed, grad_keys),
        weight_grad(normed, grad_values),
        weight_grad(mixed_heads, grad_branch),
        weight_grad(normed_two, grad_pre),
        weight_grad(active, cotangent),
        column_sum(query_grad),
        column_sum(grad_values),
        column_sum(grad_branch),
        column_sum(grad_pre),
        column_sum(cotangent),
        small_total[0],
        small_total[1],
        small_total[2],
        small_total[3],
    )
    owned = owner_sum(grads)
    layer_out = jnp.concatenate(outputs, axis=0)
    grad_tokens_all = jnp.concatenate(grads_in, axis=0)
    return (
        layer_out,
        grad_tokens_all,
        owned[0],
        owned[1],
        owned[2],
        owned[3],
        owned[4],
        owned[5],
        owned[6],
        owned[7],
        owned[8],
        owned[9],
        owned[10],
        owned[11],
        owned[12],
        owned[13],
        owned[14],
    )


BF = jnp.bfloat16
F32 = jnp.float32
SMALL = 8


def other_core(value):
    return lax.ppermute(value, "core", [(0, 1), (1, 0)])


def other_x(value):
    return lax.ppermute(value, "x", [(0, 1), (1, 0)])


def other_y(value):
    return lax.ppermute(value, "y", [(0, 1), (1, 0)])


def other_z(value, by):
    return lax.ppermute(value, "z", [(i, i ^ by) for i in range(lax.axis_size("z"))])


def pair(bit, own, received):
    return jnp.stack((jnp.where(bit == 0, own, received), jnp.where(bit == 0, received, own)))


def pick(value, index, axis):
    return lax.dynamic_index_in_dim(value, index, axis, keepdims=False)


def in_order(index, pieces):
    level = list(pieces)
    bit = 0
    ordered = [p[None] for p in level]
    while len(ordered) > 1:
        flag = (index >> bit) & 1
        ordered = [
            jnp.concatenate(
                (jnp.where(flag == 0, a, b), jnp.where(flag == 0, b, a)), axis=0
            )
            for a, b in zip(ordered[::2], ordered[1::2])
        ]
        bit += 1
    return ordered[0]


def gather_plane(along_z, x, y):
    half = along_z.shape[0] // 2
    first, second = along_z[:half], along_z[half:]
    first = pair(x, first, other_x(first))
    second = pair(y, second, other_y(second))
    first = pair(y, first, other_y(first))
    second = pair(x, second, other_x(second))
    return jnp.concatenate((jnp.moveaxis(first, 2, 0).swapaxes(1, 2), jnp.moveaxis(second, 2, 0)))


def plus(kept, received):
    return kept.astype(F32) + received.astype(F32)


LIGHT = pl.CostEstimate(flops=0, bytes_accessed=1, transcendentals=0)
VMEM_LIMIT = 56 * 1024 * 1024
QUERY_BLOCK = 256


def lane_masks(dtype):
    lane = lax.broadcasted_iota(jnp.int32, (1, 2 * DH), 1)
    return [(lane < DH).astype(dtype), (lane >= DH).astype(dtype)]


def visible(key_count, query_block):
    key_pos = lax.broadcasted_iota(jnp.int32, (query_block, query_block), 0)
    query_pos = lax.broadcasted_iota(jnp.int32, (query_block, query_block), 1)
    return key_pos <= query_pos


def masked_tail(scores, allowed):
    key_count, query_block = scores.shape
    tail = jnp.where(allowed, scores[key_count - query_block :], -1e30)
    if key_count == query_block:
        return tail
    return jnp.concatenate((scores[: key_count - query_block], tail), axis=0)


def nt(left, right):
    return lax.dot_general(left, right, (((1,), (1,)), ((), ())), preferred_element_type=F32)


def nn(left, right):
    return lax.dot_general(left, right, (((1,), (0,)), ((), ())), preferred_element_type=F32)


def attend_kernel(q_ref, k_ref, v_ref, mixed_ref, lse_ref):
    length = q_ref.shape[0]
    masks = lane_masks(BF)
    allowed = visible(QUERY_BLOCK, QUERY_BLOCK)
    keys = k_ref[...]
    masked_keys = [keys * m for m in masks]
    v_t = v_ref[...].T
    row = lax.broadcasted_iota(jnp.int32, (2 * DH, 1), 0)
    values_t = [jnp.where(row < DH, v_t, jnp.zeros((), BF)), jnp.where(row >= DH, v_t, jnp.zeros((), BF))]
    for start in range(0, length, QUERY_BLOCK):
        stop = start + QUERY_BLOCK
        q = q_ref[start:stop, :]
        mixed_t = None
        for head in range(2):
            scores = masked_tail(nt(masked_keys[head][:stop], q), allowed)
            top = jnp.max(scores, axis=0, keepdims=True)
            powers = jnp.exp(scores - top)
            total = jnp.sum(powers, axis=0, keepdims=True)
            low = (powers * (1.0 / total)).astype(BF)
            part = nn(values_t[head][:, :stop], low)
            mixed_t = part if mixed_t is None else mixed_t + part
            lse_ref[0, head : head + 1, start:stop] = top + jnp.log(total)
        mixed_ref[start:stop, :] = mixed_t.T.astype(BF)


def attend_back_kernel(q_ref, k_ref, v_ref, g_ref, mixed_ref, lse_ref, gq_ref, gk_ref, gv_ref, ka, va):
    length = q_ref.shape[0]
    masks = lane_masks(BF)
    allowed = visible(QUERY_BLOCK, QUERY_BLOCK)
    keys, values = k_ref[...], v_ref[...]
    masked_keys = [keys * m for m in masks]
    masked_values = [values * m for m in masks]
    keys_t = [m.T for m in masked_keys]
    for start in range(length - QUERY_BLOCK, -1, -QUERY_BLOCK):
        stop = start + QUERY_BLOCK
        q, g = q_ref[start:stop, :], g_ref[start:stop, :]
        products = (g.astype(F32) * mixed_ref[start:stop, :].astype(F32)).T
        grad_q_t = None
        grad_k = grad_v = None
        for head in range(2):
            inner = jnp.sum(products[head * DH : (head + 1) * DH], axis=0, keepdims=True)
            scores = masked_tail(nt(masked_keys[head][:stop], q), allowed)
            probs = jnp.exp(scores - lse_ref[0, head : head + 1, start:stop])
            grad_probs = nt(masked_values[head][:stop], g)
            grad_scores = (probs * (grad_probs - inner)).astype(BF)
            part_v = nn(probs.astype(BF), g * masks[head])
            part_k = nn(grad_scores, q * masks[head])
            part_q = nn(keys_t[head][:, :stop], grad_scores)
            grad_v = part_v if head == 0 else grad_v + part_v
            grad_k = part_k if head == 0 else grad_k + part_k
            grad_q_t = part_q if head == 0 else grad_q_t + part_q
        gq_ref[start:stop, :] = grad_q_t.T.astype(BF)
        if stop == length:
            ka[...] = grad_k
            va[...] = grad_v
        else:
            ka[:stop, :] += grad_k
            va[:stop, :] += grad_v
    gk_ref[...] = ka[...].astype(BF)
    gv_ref[...] = va[...].astype(BF)


def attend(queries, keys, values):
    length, width = queries.shape
    pairs = width // (2 * DH)
    block = pl.BlockSpec((length, 2 * DH), lambda i: (0, i))
    return pl.pallas_call(
        attend_kernel,
        grid=(pairs,),
        in_specs=[block] * 3,
        out_specs=[block, pl.BlockSpec((1, 2, length), lambda i: (i, 0, 0))],
        out_shape=[
            jax.ShapeDtypeStruct((length, width), BF),
            jax.ShapeDtypeStruct((pairs, 2, length), F32),
        ],
        compiler_params=pltpu.CompilerParams(vmem_limit_bytes=VMEM_LIMIT),
        cost_estimate=LIGHT,
        name="attend",
    )(queries, keys, values)


def attend_back(queries, keys, values, mixed, lse, grad_mixed, pair_index, pairs):
    length = queries.shape[0]
    block = pl.BlockSpec((length, 2 * DH), lambda i: (0, i + pair_index))
    out_block = pl.BlockSpec((length, 2 * DH), lambda i: (0, i))
    width = pairs * 2 * DH
    return pl.pallas_call(
        attend_back_kernel,
        grid=(pairs,),
        in_specs=[block] * 5 + [pl.BlockSpec((1, 2, length), lambda i: (i + pair_index, 0, 0))],
        out_specs=[out_block] * 3,
        out_shape=[jax.ShapeDtypeStruct((length, width), BF)] * 3,
        scratch_shapes=[pltpu.VMEM((length, 2 * DH), F32)] * 2,
        compiler_params=pltpu.CompilerParams(vmem_limit_bytes=VMEM_LIMIT),
        cost_estimate=LIGHT,
        name="attend_back",
    )(queries, keys, values, grad_mixed, mixed, lse)


def position_blocks(core, block):
    return [
        (b, own, pl.multiple_of(b * 2 * block + (core if own else 1 - core) * block, block))
        for b in range(2)
        for own in (True, False)
    ]


def normalise(values):
    centre = values - jnp.mean(values, axis=-1, keepdims=True)
    spread = jnp.mean(centre * centre, axis=-1, keepdims=True)
    rate = lax.rsqrt(spread + 1e-05)
    return centre * rate, rate


def normalise_back(unit, rate, gain, grad):
    scaled = grad * gain
    return rate * (
        scaled
        - jnp.mean(scaled, axis=-1, keepdims=True)
        - unit * jnp.mean(scaled * unit, axis=-1, keepdims=True)
    )


CORE, X, Y = range(3)
B_QUERY, B_VALUE, B_OUT, B_DOWN, GAIN1, SHIFT1, GAIN2, SHIFT2 = range(8)


def weight(ref, i):
    chips, _, width = ref.shape
    rows = width * 2 // chips
    return ref[:, i * rows : (i + 1) * rows, :].reshape(chips * rows, width)


def add_sums(ref, values):
    @pl.when(pl.program_id(0) == 0)
    def _():
        ref[...] = jnp.zeros(ref.shape, F32)

    for i, value in enumerate(values):
        ref[i : i + 1, :] += jnp.sum(value, axis=0, keepdims=True)


def enter_kernel(core_ref, mine_ref, other_ref, vec_ref, half_ref, w_ref, n_ref, q_ref, k_ref, v_ref):
    core = core_ref[0]
    block = mine_ref.shape[0] // 2
    for b, own, row in position_blocks(core, block):
        tokens = (mine_ref if own else other_ref)[b * block : (b + 1) * block, :].astype(F32)
        unit, _ = normalise(tokens)
        normed = (unit * vec_ref[GAIN1 : GAIN1 + 1, :] + vec_ref[SHIFT1 : SHIFT1 + 1, :]).astype(BF)
        rows = pl.ds(row, block)
        n_ref[rows, :] = normed
        q = (nn(normed, weight(w_ref, 0)) + half_ref[B_QUERY : B_QUERY + 1, :]) * DH ** (-0.5)
        q_ref[rows, :] = q.astype(BF)
        k_ref[rows, :] = nn(normed, weight(w_ref, 1)).astype(BF)
        v_ref[rows, :] = (nn(normed, weight(w_ref, 2)) + half_ref[B_VALUE : B_VALUE + 1, :]).astype(BF)


def out_kernel(core_ref, mixed_ref, w_ref, mine_ref, other_ref):
    block = mine_ref.shape[0] // 2
    for b, own, row in position_blocks(core_ref[0], block):
        part = nn(mixed_ref[pl.ds(row, block), :], w_ref[...])
        ref = mine_ref if own else other_ref
        ref[b * block : (b + 1) * block, :] = part.astype(ref.dtype)


def middle_kernel(tokens_ref, part_ref, received_ref, vec_ref, residual_ref, n_ref):
    residual = (
        tokens_ref[...].astype(F32)
        + part_ref[...]
        + received_ref[...].astype(F32)
        + vec_ref[B_OUT : B_OUT + 1, :]
    )
    unit, _ = normalise(residual)
    residual_ref[...] = residual
    n_ref[...] = (unit * vec_ref[GAIN2 : GAIN2 + 1, :] + vec_ref[SHIFT2 : SHIFT2 + 1, :]).astype(BF)


def middle_back_kernel(residual_ref, gn_ref, gn_received_ref, g_ref, vec_ref, gr_ref, branch_ref, sums_ref):
    unit, rate = normalise(residual_ref[...])
    grad_normed = gn_ref[...] + gn_received_ref[...].astype(F32)
    cotangent = g_ref[...].astype(F32)
    grad = cotangent + normalise_back(unit, rate, vec_ref[GAIN2 : GAIN2 + 1, :], grad_normed)
    gr_ref[...] = grad
    branch = grad.astype(BF)
    branch_ref[...] = branch
    add_sums(sums_ref, (branch.astype(F32), cotangent, grad_normed * unit, grad_normed))


def mixed_back_kernel(core_ref, mixed_ref, mine_ref, other_ref, w_ref, gm_ref, gw_ref):
    block = mine_ref.shape[0] // 2
    total = None
    for b, own, row in position_blocks(core_ref[0], block):
        branch = (mine_ref if own else other_ref)[b * block : (b + 1) * block, :]
        rows = pl.ds(row, block)
        gm_ref[rows, :] = nt(branch, w_ref[...]).astype(BF)
        part = nn(mixed_ref[rows, :].T, branch)
        total = part if total is None else total + part
    gw_ref[...] = total.astype(BF)


def weight_back_kernel(
    place_ref, n_ref, q_ref, k_ref, v_ref, left_keep, left_send, right_keep, right_send, sums_ref, by_y, by_x
):
    x, y = place_ref[X], place_ref[Y]
    n_t = n_ref[...].T
    rows = by_y.shape[2]
    grads = [q_ref[...] * jnp.asarray(DH ** (-0.5), BF), k_ref[...], v_ref[...]]
    for i in range(2):
        by_y[...] = nn(n_t, grads[i]).astype(BF).reshape(by_y.shape)
        part = slice(i * rows, (i + 1) * rows)
        left_keep[:, part, :] = by_y[:, pl.ds(y, 1)].reshape(-1, rows, by_y.shape[3])
        left_send[:, part, :] = by_y[:, pl.ds(1 - y, 1)].reshape(-1, rows, by_y.shape[3])
    by_x[...] = nn(n_t, grads[2]).astype(BF).reshape(by_x.shape)
    right_keep[...] = by_x[:, pl.ds(x, 1)].reshape(right_keep.shape)
    right_send[...] = by_x[:, pl.ds(1 - x, 1)].reshape(right_send.shape)
    half = q_ref.shape[1]
    side = lax.broadcasted_iota(jnp.int32, (1, 2 * half), 1) >= half
    for i, grad in enumerate((grads[0], grads[2])):
        total = jnp.sum(grad.astype(F32), axis=0, keepdims=True)
        total = jnp.concatenate((total, total), axis=1)
        sums_ref[i : i + 1, :] = jnp.where(side == (place_ref[CORE] == 1), total, 0.0)


def enter_back_kernel(place_ref, q_ref, k_ref, v_ref, w_ref, mine_ref, other_ref):
    block = mine_ref.shape[0] // 2
    for b, own, row in position_blocks(place_ref[CORE], block):
        rows = pl.ds(row, block)
        part = (
            nt(q_ref[rows, :] * jnp.asarray(DH ** (-0.5), BF), weight(w_ref, 0))
            + nt(k_ref[rows, :], weight(w_ref, 1))
            + nt(v_ref[rows, :], weight(w_ref, 2))
        )
        ref = mine_ref if own else other_ref
        ref[b * block : (b + 1) * block, :] = part.astype(ref.dtype)


def leave_kernel(tokens_ref, gn_ref, gn_received_ref, gr_ref, vec_ref, gt_ref, sums_ref):
    unit, rate = normalise(tokens_ref[...].astype(F32))
    grad_normed = gn_ref[...] + gn_received_ref[...].astype(F32)
    gt_ref[...] = gr_ref[...] + normalise_back(unit, rate, vec_ref[GAIN1 : GAIN1 + 1, :], grad_normed)
    add_sums(sums_ref, (grad_normed * unit, grad_normed))


def shape(dims, dtype):
    return jax.ShapeDtypeStruct(dims, dtype)


def whole_call(kernel, outs, *args, flops=0, scalars=0, scratch=()):
    in_specs = [
        pl.BlockSpec(memory_space=pltpu.SMEM if i < scalars else pltpu.VMEM)
        for i in range(len(args))
    ]
    moved = sum(a.size * a.dtype.itemsize for a in list(args) + outs)
    return pl.pallas_call(
        kernel,
        in_specs=in_specs,
        out_specs=[pl.BlockSpec(memory_space=pltpu.VMEM)] * len(outs),
        out_shape=outs,
        scratch_shapes=list(scratch),
        compiler_params=pltpu.CompilerParams(vmem_limit_bytes=VMEM_LIMIT),
        cost_estimate=LIGHT,
        name=kernel.__name__,
    )(*args)


def row_call(kernel, outs, sums, *args):
    length, width = args[0].shape
    block = length // 2
    rows = pl.BlockSpec((block, width), lambda i: (i, 0))
    out_shape = [shape((length, width), dtype) for dtype in outs]
    out_specs = [rows] * len(outs)
    if sums:
        out_shape.append(shape((sums, width), F32))
        out_specs.append(pl.BlockSpec((sums, width), lambda i: (0, 0)))
    moved = sum(a.size * a.dtype.itemsize for a in list(args) + out_shape)
    return pl.pallas_call(
        kernel,
        grid=(2,),
        in_specs=[rows] * (len(args) - 1) + [pl.BlockSpec(args[-1].shape, lambda i: (0, 0))],
        out_specs=out_specs,
        out_shape=out_shape,
        compiler_params=pltpu.CompilerParams(vmem_limit_bytes=VMEM_LIMIT),
        cost_estimate=LIGHT,
        name=kernel.__name__,
    )(*args)


def hidden_kernel(
    place_ref, n_mine, n_other, g_mine, g_other, up_ref, down_ref, bias_ref,
    y_mine, y_other, gn_mine, gn_other, up_keep, up_send, down_keep, down_send, gb_ref,
    n_t, y_sum, gn_sum, up_all, down_all,
):
    step = pl.program_id(0)
    length = n_mine.shape[0]

    @pl.when(step == 0)
    def _():
        n_t[:, :length] = n_mine[...].T
        n_t[:, length:] = n_other[...].T
        for ref in (y_mine, gn_mine, y_sum, gn_sum):
            ref[...] = jnp.zeros(ref.shape, F32)

    up = up_ref[...].reshape(-1, up_ref.shape[2])
    down = down_ref[...].reshape(-1, down_ref.shape[2])
    grad_up = grad_down = bias_sum = None
    for part, (n_ref, g_ref, y_ref, gn_ref) in enumerate(
        ((n_mine, g_mine, y_mine, gn_mine), (n_other, g_other, y_sum, gn_sum))
    ):
        n, g = n_ref[...], g_ref[...]
        pre = nn(n, up) + bias_ref[0]
        square = pre * pre
        bent = jnp.tanh(pre * (0.7978845608028654 + 0.7978845608028654 * 0.044715 * square))
        half = 0.5 + 0.5 * bent
        active = (pre * half).astype(BF)
        rise = pre * (2 * 0.7978845608028654 + 6 * 0.7978845608028654 * 0.044715 * square)
        slope = half * (1.0 + (1.0 - half) * rise)
        grad_pre = (nt(g, down) * slope).astype(BF)
        y_ref[...] += nn(active, down)
        gn_ref[...] += nt(grad_pre, up)
        part_up = nn(n_t[:, part * length : (part + 1) * length], grad_pre)
        part_down = lax.dot_general(active, g, (((0,), (0,)), ((), ())), preferred_element_type=F32)
        part_bias = jnp.sum(grad_pre.astype(F32), axis=0, keepdims=True)
        grad_up = part_up if part == 0 else grad_up + part_up
        grad_down = part_down if part == 0 else grad_down + part_down
        bias_sum = part_bias if part == 0 else bias_sum + part_bias
    x, y = place_ref[X], place_ref[Y]
    up_all[...] = grad_up.astype(BF).reshape(up_all.shape)
    up_keep[...] = up_all[:, pl.ds(y, 1)].reshape(up_keep.shape)
    up_send[...] = up_all[:, pl.ds(1 - y, 1)].reshape(up_send.shape)
    down_all[...] = grad_down.astype(BF).reshape(down_all.shape)
    down_keep[...] = down_all[:, pl.ds(x, 1)].reshape(down_keep.shape)
    down_send[...] = down_all[:, pl.ds(1 - x, 1)].reshape(down_send.shape)
    gb_ref[0] = bias_sum

    @pl.when(step == pl.num_programs(0) - 1)
    def _():
        y_other[...] = y_sum[...].astype(BF)
        gn_other[...] = gn_sum[...].astype(BF)


def feed_forward(place, n_mine, n_other, g_mine, g_other, late, bias, hidden_rows):
    length, width = n_mine.shape
    chips = late.shape[0]
    steps = 2
    z_count = chips // 4
    z_step = z_count // steps
    tile = chips * hidden_rows // steps
    up_rows = width // chips
    per_half = steps // 2
    down_chips = chips // steps
    full = pl.BlockSpec((length, width), lambda i: (0, 0))
    hidden = tile * steps
    return pl.pallas_call(
        hidden_kernel,
        grid=(steps,),
        in_specs=[pl.BlockSpec(memory_space=pltpu.SMEM)] + [full] * 4
        + [
            pl.BlockSpec((chips, up_rows, tile), lambda i: (0, i // per_half, i % per_half)),
            pl.BlockSpec((down_chips, hidden_rows, width), lambda i: (i, 1, 0)),
            pl.BlockSpec((1, 1, tile), lambda i: (i, 0, 0)),
        ],
        out_specs=[full] * 4
        + [
            pl.BlockSpec((chips // 2, up_rows, tile), lambda i: (0, 0, i)),
            pl.BlockSpec((chips // 2, up_rows, tile), lambda i: (0, 0, i)),
            pl.BlockSpec((z_step, 2, hidden_rows, width), lambda i: (i, 0, 0, 0)),
            pl.BlockSpec((z_step, 2, hidden_rows, width), lambda i: (i, 0, 0, 0)),
            pl.BlockSpec((1, 1, tile), lambda i: (i, 0, 0)),
        ],
        out_shape=[
            shape((length, width), F32),
            shape((length, width), BF),
            shape((length, width), F32),
            shape((length, width), BF),
            shape((chips // 2, up_rows, hidden), BF),
            shape((chips // 2, up_rows, hidden), BF),
            shape((z_count, 2, hidden_rows, width), BF),
            shape((z_count, 2, hidden_rows, width), BF),
            shape((steps, 1, tile), F32),
        ],
        scratch_shapes=[
            pltpu.VMEM((width, 2 * length), BF),
            pltpu.VMEM((length, width), F32),
            pltpu.VMEM((length, width), F32),
            pltpu.VMEM((chips // 2, 2, up_rows, tile), BF),
            pltpu.VMEM((z_step, 2, 2, hidden_rows, width), BF),
        ],
        compiler_params=pltpu.CompilerParams(vmem_limit_bytes=VMEM_LIMIT),
        cost_estimate=LIGHT,
        name="feed_forward",
    )(place, n_mine, n_other, g_mine, g_other, late, late, bias.reshape(steps, 1, tile))


def chip_step(
    tokens_in,
    out_grad,
    w_query,
    w_key,
    w_value,
    w_out,
    w_up,
    w_down,
    b_query,
    b_value,
    b_out,
    b_up,
    b_down,
    norm1_gain,
    norm1_shift,
    norm2_gain,
    norm2_shift,
):
    z, x, y, core = (lax.axis_index(name) for name in ("z", "x", "y", "core"))
    z_count = lax.axis_size("z")
    chips = z_count * 4
    half_chips = chips // 2
    _, block, width = tokens_in.shape
    half = width // 2
    rows = w_query.shape[0]
    hidden_rows = w_down.shape[0]
    hidden = hidden_rows * chips

    def own_positions(value):
        return pair(y, pick(value, y, 0), other_y(pick(value, 1 - y, 0))).reshape(2 * block, width)

    three = jnp.stack((w_query, w_key, w_value)).reshape(3, rows, 2, half)
    vectors = (
        b_query, b_value, b_out, b_down, norm1_gain, norm1_shift, norm2_gain, norm2_shift, b_up
    )
    small = jnp.concatenate(vectors)
    unit_rows = 3 * rows + SMALL
    small_rows = jnp.zeros((SMALL, half), BF).at[0, : small.shape[0]].set(small)
    own = jnp.concatenate((pick(three, core, 2).reshape(3 * rows, half), small_rows))
    unit = pair(
        core,
        own,
        other_core(
            jnp.concatenate((pick(three, 1 - core, 2).reshape(3 * rows, half), small_rows))
        ),
    )
    up_parts = w_up.reshape(rows, chips, 2, hidden_rows)
    up_unit = pair(
        core,
        pick(up_parts, core, 2).reshape(rows, hidden),
        other_core(pick(up_parts, 1 - core, 2).reshape(rows, hidden)),
    )
    up_unit = up_unit.reshape(2 * rows, 2, width)
    late = jnp.concatenate((up_unit[:, 0], up_unit[:, 1], w_down))
    late = lax.all_gather(late, ("z", "x", "y"), axis=0, tiled=False)
    threes = unit[:, : 3 * rows].reshape(2, 3, rows, half).swapaxes(0, 1).reshape(6 * rows, half)
    unit = jnp.concatenate(
        (threes, unit[:, 3 * rows :].reshape(2 * SMALL, half), w_out[:, :half], w_out[:, half:])
    )
    pieces = [unit] + [other_z(unit, k) for k in range(1, z_count)]
    both = jnp.stack((pick(tokens_in, y, 0), pick(out_grad, y, 0)))
    both_from = other_y(jnp.stack((pick(tokens_in, 1 - y, 0), pick(out_grad, 1 - y, 0))))
    pieces, both_from = lax.optimization_barrier((pieces, both_from))
    both = pair(y, both, both_from).swapaxes(0, 1).reshape(2, 2 * block, width)
    mine, grad_mine = both[0], both[1]
    other, grad_other = other_core(mine), other_core(grad_mine)
    place = jnp.stack((core, x, y)).astype(jnp.int32)
    gathered = gather_plane(in_order(z, pieces), x, y)
    out_parts = jnp.concatenate(
        (gathered[..., 2 * unit_rows : 2 * unit_rows + rows, :], gathered[..., 2 * unit_rows + rows :, :]),
        axis=-1,
    ).reshape(2, half_chips, rows, width)
    out_c = (
        pair(core, pick(out_parts, core, 0), other_core(pick(out_parts, 1 - core, 0)))
        .swapaxes(0, 1)
        .reshape(half, width)
    )
    gathered = gathered.reshape(chips, -1, half)
    small_all = gathered[:, 6 * rows : 6 * rows + 2 * SMALL].reshape(chips * 2, SMALL, half)
    small_all = small_all[:, 0, : small.shape[0]]
    vectors = small_all[:, : 8 * rows].reshape(chips * 2, 8, rows).swapaxes(0, 1)
    vectors = vectors.reshape(8, width).astype(F32)
    halves = pick(vectors.reshape(8, 2, half), core, 1)
    bias_u = pick(small_all[:, 8 * rows :].reshape(chips, 2, hidden_rows), core, 1)
    bias_u = bias_u.reshape(hidden).astype(F32)

    length = 4 * block
    heads_shape = shape((length, half), BF)
    normed, queries, keys, values = whole_call(
        enter_kernel,
        [shape((length, width), BF)] + [heads_shape] * 3,
        place, mine, other, vectors, halves, gathered,
        flops=6 * length * width * half, scalars=1,
    )
    mixed, lse = attend(queries, keys, values)
    mine_shape = shape((2 * block, width), F32)
    sent_shape = shape((2 * block, width), BF)
    part, to_other = whole_call(
        out_kernel, [mine_shape, sent_shape], place, mixed, out_c,
        flops=2 * length * width * half, scalars=1,
    )
    residual, normed2 = row_call(middle_kernel, (F32, BF), 0, mine, part, other_core(to_other), vectors)
    late, normed2 = lax.optimization_barrier((late, normed2))
    y_mine, y_other, gn_mine, gn_other, up_keep, up_send, down_keep, down_send, up_sums = feed_forward(
        place, normed2, other_core(normed2), grad_mine, grad_other, late, bias_u, hidden_rows
    )

    up_from, down_from = other_y(up_send), other_x(down_send)
    grad_residual, branch, sums2 = row_call(
        middle_back_kernel, (F32, BF), 4, residual, gn_mine, other_core(gn_other), grad_mine, vectors
    )
    grad_mixed, grad_out = whole_call(
        mixed_back_kernel, [heads_shape, shape((half, width), BF)],
        place, mixed, branch, other_core(branch), out_c,
        flops=4 * length * width * half, scalars=1,
    )
    grad_out = grad_out.reshape(half_chips, 2, rows, width)
    grad_out = pair(
        core,
        pick(grad_out, core, 1),
        other_core(pick(grad_out, 1 - core, 1)),
    ).reshape(z_count, 2, 2, rows, width)
    grads = attend_back(
        queries, keys, values, mixed, lse, grad_mixed, 0, half // (2 * DH)
    )
    up_from, down_from, grads = lax.optimization_barrier((up_from, down_from, grads))
    ups = plus(up_keep, up_from).reshape(z_count, 2, 2 * rows, hidden)
    downs = plus(down_keep, down_from)
    up_send, down_send = pick(ups, 1 - x, 1).astype(BF), pick(downs, 1 - y, 1).astype(BF)
    up_send, down_send, grads = lax.optimization_barrier((up_send, down_send, grads))
    up_from, down_from, out_from = other_x(up_send), other_y(down_send), other_x(pick(grad_out, 1 - x, 1))
    left_shape = shape((2 * z_count, 4 * rows, half), BF)
    right_shape = shape((z_count, 2, 2 * rows, half), BF)
    left_keep, left_send, right_keep, right_send, sums_heads = whole_call(
        weight_back_kernel,
        [left_shape] * 2 + [right_shape] * 2 + [shape((2, width), F32)],
        place, normed, *grads,
        flops=6 * length * width * half, scalars=1,
        scratch=(
            pltpu.VMEM((2 * z_count, 2, 2 * rows, half), BF),
            pltpu.VMEM((z_count, 2, 2, 2 * rows, half), BF),
        ),
    )
    left_send, right_send, grads, y_mine, y_other = lax.optimization_barrier(
        (left_send, right_send, grads, y_mine, y_other)
    )
    left_from, right_from = other_y(left_send), other_x(right_send)
    gn_mine, gn_other = whole_call(
        enter_back_kernel,
        [mine_shape, sent_shape],
        place, *grads, gathered,
        flops=6 * length * width * half, scalars=1,
    )
    up_from, down_from, out_from, gn_mine, gn_other = lax.optimization_barrier(
        (up_from, down_from, out_from, gn_mine, gn_other)
    )
    low, high = z & 1, z >> 1

    def first_z(value):
        value = value.reshape((z_count // 2, 2) + value.shape[1:])
        return pick(value, low, 1), other_z(pick(value, 1 - low, 1).astype(BF), 1)

    def second_z(value):
        return pick(value, high, 0), other_z(pick(value, 1 - high, 0).astype(BF), 2)

    gn_from = other_core(gn_other)
    ups = plus(pick(ups, x, 1), up_from)
    downs = plus(pick(downs, y, 1), down_from)
    outs = plus(pick(grad_out, x, 1), out_from)
    forward_kept, forward_from = first_z(
        jnp.concatenate((ups[..., :width], ups[..., width:], downs), axis=1)
    )
    left_from, right_from, gn_from = lax.optimization_barrier((left_from, right_from, gn_from))
    lefts = plus(left_keep, left_from).reshape(z_count, 2, 4 * rows, half)
    rights = plus(right_keep, right_from)
    rights = jnp.concatenate((rights, outs[..., :half], outs[..., half:]), axis=2)
    left_send, right_send = pick(lefts, 1 - x, 1).astype(BF), pick(rights, 1 - y, 1).astype(BF)
    left_send, right_send, gn_from = lax.optimization_barrier((left_send, right_send, gn_from))
    left_from, right_from = other_x(left_send), other_y(right_send)
    grad_tokens, sums1 = row_call(
        leave_kernel, (F32,), 2, mine, gn_mine, gn_from, grad_residual, vectors
    )
    output = residual + y_mine + other_core(y_other).astype(F32) + vectors[B_DOWN]
    output = output.astype(BF).reshape(2, block, width)
    grad_tokens = grad_tokens.reshape(2, block, width)
    to_y = jnp.concatenate((pick(output, 1 - y, 0), pick(grad_tokens, 1 - y, 0).astype(BF)))
    forward_from, to_y = lax.optimization_barrier((forward_from, to_y))
    from_y = other_y(to_y)
    forward_kept, forward_from = second_z(plus(forward_kept, forward_from))

    left_from, right_from, sums1 = lax.optimization_barrier((left_from, right_from, sums1))
    small_grads = jnp.concatenate((sums_heads, sums2, sums1, up_sums.reshape(2, width)))
    lefts = plus(pick(lefts, x, 1), left_from)
    rights = plus(pick(rights, y, 1), right_from)
    last = jnp.concatenate((lefts, rights), axis=1)
    last, small_grads = lax.optimization_barrier((last, small_grads))
    last, last_from = first_z(last)
    small_grads = small_grads + other_y(small_grads)
    small_grads = small_grads + other_x(small_grads)
    small_from = other_z(small_grads, 1)
    last_from, small_from, from_y, forward_from = lax.optimization_barrier(
        (last_from, small_from, from_y, forward_from)
    )
    last, last_from = second_z(plus(last, last_from))
    small_grads = small_grads + small_from
    small_from = other_z(small_grads, 2)
    forward_sum = plus(forward_kept, forward_from)
    layer_out = pair(y, pick(output, y, 0), from_y[:block])
    grad_tokens = pair(y, pick(grad_tokens, y, 0), from_y[block:].astype(F32))

    up_mine = forward_sum[: 4 * rows].reshape(2, 2, rows, width)
    down_mine = forward_sum[4 * rows :]
    up_from = other_core(pick(up_mine, 1 - core, 1))
    up_out = pair(core, pick(up_mine, core, 1), up_from)
    up_out = up_out.reshape(2, 2, rows, half_chips, hidden_rows)
    up_out = jnp.transpose(up_out, (2, 1, 3, 0, 4)).reshape(rows, 2 * hidden)
    last_from, small_from, layer_out, grad_tokens, up_out, down_mine = lax.optimization_barrier(
        (last_from, small_from, layer_out, grad_tokens, up_out, down_mine)
    )
    last = plus(last, last_from)
    small_grads = small_grads + small_from
    small_core = small_grads[:8] + other_core(small_grads[:8])
    three_mine = last[: 6 * rows].reshape(3, 2, rows, half)
    three_from = other_core(pick(three_mine, 1 - core, 1))
    out_mine = jnp.concatenate((last[6 * rows : 7 * rows], last[7 * rows : 8 * rows]), axis=1)
    chip = (z * 2 + x) * 2 + y
    small_mine = lax.dynamic_slice_in_dim(small_core, (chip * 2 + core) * rows, rows, 1)
    up_bias = lax.dynamic_slice_in_dim(small_grads[8:].reshape(hidden), chip * hidden_rows, hidden_rows, 0)
    three_out = pair(core, pick(three_mine, core, 1), three_from)
    g_q, g_k, g_v = (jnp.concatenate((three_out[0, i], three_out[1, i]), axis=1) for i in range(3))
    g_small = [small_mine[i] for i in (0, 1, 2, 3, 6, 7, 4, 5)]
    return (
        layer_out,
        grad_tokens,
        g_q,
        g_k,
        g_v,
        out_mine,
        up_out,
        down_mine,
        g_small[0],
        g_small[1],
        g_small[2],
        up_bias,
        g_small[3],
        g_small[4],
        g_small[5],
        g_small[6],
        g_small[7],
    )


def solution(mesh):
    dp_count, ctx_count = mesh.shape["dp"], mesh.shape["ctx"]

    def run(*args):
        per_dp = args[0].shape[0] // dp_count
        if ctx_count == 4 and per_dp == 2 and dp_count == 8:
            devices = mesh.devices.reshape(dp_count // 2, 2, ctx_count // 2, 2)
            used = Mesh(devices, ("z", "x", "y", "core"))
            body, dp, ctx = chip_step, ("z", "x"), ("y", "core")
        else:
            used, body, dp, ctx = mesh, on_device, ("dp",), ("ctx",)
        tokens, matrix, bias = P(dp, ctx, None), P(dp + ctx, None), P(dp + ctx)
        return jax.shard_map(
            body,
            mesh=used,
            in_specs=(tokens,) * 2 + (matrix,) * 6 + (bias,) * 9,
            out_specs=(tokens,) * 2 + (matrix,) * 6 + (bias,) * 9,
            check_vma=False,
        )(*args)

    return run
```

```python
import jax
import jax.numpy as jnp
from jax import lax
from jax.experimental import pallas as pl
from jax.experimental.pallas import tpu as pltpu
from jax.sharding import Mesh
from jax.sharding import PartitionSpec as P

HEADS = 12
DH = 64
MICRO = 2


def shifted(value, axis, by):
    peers = lax.axis_size(axis)
    return lax.ppermute(value, axis, [(i, (i + by) % peers) for i in range(peers)])


def as_sent(value):
    return jax.tree.map(lambda a: a.astype(jnp.bfloat16) if a.dtype == jnp.float32 else a, value)


def layer_norm(values, norm_gain, norm_shift):
    centre = values - jnp.mean(values, axis=-1, keepdims=True)
    spread = jnp.mean(centre * centre, axis=-1, keepdims=True)
    return centre * lax.rsqrt(spread + 1e-05) * norm_gain + norm_shift


def gelu_tanh(values):
    return (
        0.5
        * values
        * (1.0 + jnp.tanh(0.7978845608028654 * (values + 0.044715 * values * values * values)))
    )


def project(left, right):
    return jnp.einsum("scd,de->sce", left, right, preferred_element_type=jnp.float32)


def project_back(left, right):
    return jnp.einsum("sce,de->scd", left, right, preferred_element_type=jnp.float32)


def weight_grad(left, right):
    return jnp.einsum("scd,sce->de", left, right, preferred_element_type=jnp.float32)


def column_sum(values):
    return jnp.sum(values.astype(jnp.float32), axis=(0, 1))


def masked_scores(query_heads, key_full, first_pos):
    seq_count, key_len = (key_full.shape[0], key_full.shape[1])
    key_heads = key_full.reshape(seq_count, key_len, HEADS, DH)
    scores = jnp.einsum(
        "sqhd,skhd->shqk", query_heads, key_heads, preferred_element_type=jnp.float32
    )
    row_pos = first_pos + jnp.arange(query_heads.shape[1], dtype=jnp.int32)
    col_pos = jnp.arange(key_len, dtype=jnp.int32)
    allowed = row_pos[:, None] >= col_pos[None, :]
    return (jnp.where(allowed, scores, -1e30), key_heads)


def micro_step(tokens, cotangent, shards, forward_weights):
    (
        w_query,
        w_key,
        w_value,
        w_out,
        w_up,
        w_down,
        b_query,
        b_value,
        b_out,
        b_up,
        b_down,
        gain_one,
        shift_one,
        gain_two,
        shift_two,
    ) = forward_weights
    seq_count, block_rows, width = tokens.shape
    query_scale = DH ** (-0.5)
    first_pos = lax.axis_index("ctx") * block_rows
    gain_one32, shift_one32 = (gain_one.astype(jnp.float32), shift_one.astype(jnp.float32))
    gain_two32, shift_two32 = (gain_two.astype(jnp.float32), shift_two.astype(jnp.float32))
    tokens32 = tokens.astype(jnp.float32)
    normed = layer_norm(tokens32, gain_one32, shift_one32).astype(jnp.bfloat16)
    queries = ((project(normed, w_query) + b_query.astype(jnp.float32)) * query_scale).astype(
        jnp.bfloat16
    )
    keys_local = project(normed, w_key).astype(jnp.bfloat16)
    values_local = (project(normed, w_value) + b_value.astype(jnp.float32)).astype(jnp.bfloat16)
    key_full, value_full = (
        lax.all_gather(keys_local, "ctx", axis=1, tiled=True),
        lax.all_gather(values_local, "ctx", axis=1, tiled=True),
    )
    query_heads = queries.reshape(seq_count, block_rows, HEADS, DH)
    scores, key_heads = masked_scores(query_heads, key_full, first_pos)
    row_max = jnp.max(scores, axis=-1, keepdims=True)
    exp_scores = jnp.exp(scores - row_max)
    row_total = jnp.sum(exp_scores, axis=-1, keepdims=True)
    probs_low = (exp_scores / row_total).astype(jnp.bfloat16)
    value_heads = value_full.reshape(seq_count, value_full.shape[1], HEADS, DH)
    mixed_heads = jnp.einsum(
        "shqk,skhd->sqhd", probs_low, value_heads, preferred_element_type=jnp.float32
    ).reshape(seq_count, block_rows, width)
    mixed_heads = mixed_heads.astype(jnp.bfloat16)
    residual = tokens32 + project(mixed_heads, w_out) + b_out.astype(jnp.float32)
    normed_two = layer_norm(residual, gain_two32, shift_two32).astype(jnp.bfloat16)
    hidden_pre = project(normed_two, w_up) + b_up.astype(jnp.float32)
    active = gelu_tanh(hidden_pre).astype(jnp.bfloat16)
    output = (residual + project(active, w_down) + b_down.astype(jnp.float32)).astype(jnp.bfloat16)
    back_weights = (
        lax.all_gather(shards[0], ("dp", "ctx"), axis=0, tiled=True),
        lax.all_gather(shards[1], ("dp", "ctx"), axis=0, tiled=True),
        lax.all_gather(shards[2], ("dp", "ctx"), axis=0, tiled=True),
        lax.all_gather(shards[3], ("dp", "ctx"), axis=0, tiled=True),
        lax.all_gather(shards[4], ("dp", "ctx"), axis=0, tiled=True),
        lax.all_gather(shards[5], ("dp", "ctx"), axis=0, tiled=True),
        lax.all_gather(shards[6], ("dp", "ctx"), axis=0, tiled=True),
        lax.all_gather(shards[7], ("dp", "ctx"), axis=0, tiled=True),
        lax.all_gather(shards[8], ("dp", "ctx"), axis=0, tiled=True),
        lax.all_gather(shards[9], ("dp", "ctx"), axis=0, tiled=True),
        lax.all_gather(shards[10], ("dp", "ctx"), axis=0, tiled=True),
        lax.all_gather(shards[11], ("dp", "ctx"), axis=0, tiled=True),
        lax.all_gather(shards[12], ("dp", "ctx"), axis=0, tiled=True),
        lax.all_gather(shards[13], ("dp", "ctx"), axis=0, tiled=True),
        lax.all_gather(shards[14], ("dp", "ctx"), axis=0, tiled=True),
    )
    w_query, w_key, w_value, w_out, w_up, w_down = back_weights[:6]
    grad_active = project_back(cotangent, w_down)
    _, gelu_pull = jax.vjp(gelu_tanh, hidden_pre)
    grad_pre = gelu_pull(grad_active)[0].astype(jnp.bfloat16)
    grad_normed_two = project_back(grad_pre, w_up)
    _, norm_pull_two = jax.vjp(layer_norm, residual, gain_two32, shift_two32)
    grad_res_part, grad_gain_two, grad_shift_two = norm_pull_two(grad_normed_two)
    grad_residual = cotangent.astype(jnp.float32) + grad_res_part
    grad_branch = grad_residual.astype(jnp.bfloat16)
    grad_mixed = project_back(grad_branch, w_out).astype(jnp.bfloat16)
    key_full, value_full = (
        lax.all_gather(keys_local, "ctx", axis=1, tiled=True),
        lax.all_gather(values_local, "ctx", axis=1, tiled=True),
    )
    value_heads = value_full.reshape(seq_count, value_full.shape[1], HEADS, DH)
    scores, key_heads = masked_scores(query_heads, key_full, first_pos)
    probs = jnp.exp(scores - row_max) / row_total
    probs_low = probs.astype(jnp.bfloat16)
    grad_heads = grad_mixed.reshape(seq_count, block_rows, HEADS, DH)
    grad_probs = jnp.einsum(
        "sqhd,skhd->shqk", grad_heads, value_heads, preferred_element_type=jnp.float32
    )
    inner_rows = jnp.sum(probs * grad_probs, axis=-1, keepdims=True)
    grad_scores = (probs * (grad_probs - inner_rows)).astype(jnp.bfloat16)
    grad_queries = jnp.einsum(
        "shqk,skhd->sqhd", grad_scores, key_heads, preferred_element_type=jnp.float32
    )
    grad_queries = grad_queries.reshape(seq_count, block_rows, width).astype(jnp.bfloat16)
    query_grad = grad_queries * query_scale

    def key_terms(first_row, row_count):
        score_part = lax.dynamic_slice_in_dim(grad_scores, first_row, row_count, 3)
        prob_part = lax.dynamic_slice_in_dim(probs_low, first_row, row_count, 3)
        key_part = jnp.einsum(
            "shqk,sqhd->kshd", score_part, query_heads, preferred_element_type=jnp.float32
        )
        value_part = jnp.einsum(
            "shqk,sqhd->kshd", prob_part, grad_heads, preferred_element_type=jnp.float32
        )
        return jnp.concatenate(
            (
                key_part.reshape(row_count, seq_count, width),
                value_part.reshape(row_count, seq_count, width),
            ),
            axis=2,
        )

    cycle_size = lax.axis_size("ctx")
    own_index = lax.axis_index("ctx")

    def carry_step(step, carried):
        holder = (own_index - step) % cycle_size
        carried = carried + key_terms(holder * block_rows, block_rows)
        return shifted(carried.astype(jnp.bfloat16), "ctx", 1).astype(carried.dtype)

    start_sums = jnp.zeros((block_rows, seq_count, 2 * width), jnp.float32)
    key_sums = lax.fori_loop(0, cycle_size, carry_step, start_sums)
    key_sums = jnp.transpose(key_sums, (1, 0, 2))
    grad_keys = key_sums[:, :, :width].astype(jnp.bfloat16)
    grad_values = key_sums[:, :, width:].astype(jnp.bfloat16)
    grad_normed = (
        project_back(query_grad, w_query)
        + project_back(grad_keys, w_key)
        + project_back(grad_values, w_value)
    )
    _, norm_pull_one = jax.vjp(layer_norm, tokens32, gain_one32, shift_one32)
    grad_tok_part, grad_gain_one, grad_shift_one = norm_pull_one(grad_normed)
    grad_tokens = grad_residual + grad_tok_part
    small_grads = (grad_gain_one, grad_shift_one, grad_gain_two, grad_shift_two)
    operands = (
        normed,
        query_grad,
        grad_keys,
        grad_values,
        mixed_heads,
        grad_branch,
        normed_two,
        grad_pre,
        active,
        cotangent,
    )
    return (output, grad_tokens, small_grads, operands)


def owner_sum(grads):
    dp_count = lax.axis_size("dp")
    ctx_count = lax.axis_size("ctx")
    blocks = tuple((grad_part.reshape(dp_count, ctx_count, -1) for grad_part in grads))
    first_section = jax.tree.map(
        lambda part, own: part.astype(own.dtype),
        lax.all_to_all(as_sent(blocks), "ctx", split_axis=1, concat_axis=1, tiled=True),
        blocks,
    )
    partial_sums = tuple((jnp.sum(piece, axis=1, keepdims=True) for piece in first_section))
    second_section = jax.tree.map(
        lambda part, own: part.astype(own.dtype),
        lax.all_to_all(as_sent(partial_sums), "dp", split_axis=0, concat_axis=0, tiled=True),
        partial_sums,
    )
    owned = []
    for grad_part, piece in zip(grads, second_section):
        summed = jnp.sum(piece, axis=(0, 1))
        row_count = grad_part.shape[0] // (dp_count * ctx_count)
        owned.append(summed.reshape((row_count,) + grad_part.shape[1:]))
    return owned


def on_device(
    tokens_in,
    out_grad,
    w_query,
    w_key,
    w_value,
    w_out,
    w_up,
    w_down,
    b_query,
    b_value,
    b_out,
    b_up,
    b_down,
    norm1_gain,
    norm1_shift,
    norm2_gain,
    norm2_shift,
):
    shards = (
        w_query,
        w_key,
        w_value,
        w_out,
        w_up,
        w_down,
        b_query,
        b_value,
        b_out,
        b_up,
        b_down,
        norm1_gain,
        norm1_shift,
        norm2_gain,
        norm2_shift,
    )
    per_micro = tokens_in.shape[0] // MICRO
    outputs = []
    grads_in = []
    operand_lists = []
    small_total = None
    for micro_index in range(MICRO):
        lower = micro_index * per_micro
        tokens = tokens_in[lower : lower + per_micro]
        cotangent = out_grad[lower : lower + per_micro]
        forward_weights = (
            lax.all_gather(shards[0], ("dp", "ctx"), axis=0, tiled=True),
            lax.all_gather(shards[1], ("dp", "ctx"), axis=0, tiled=True),
            lax.all_gather(shards[2], ("dp", "ctx"), axis=0, tiled=True),
            lax.all_gather(shards[3], ("dp", "ctx"), axis=0, tiled=True),
            lax.all_gather(shards[4], ("dp", "ctx"), axis=0, tiled=True),
            lax.all_gather(shards[5], ("dp", "ctx"), axis=0, tiled=True),
            lax.all_gather(shards[6], ("dp", "ctx"), axis=0, tiled=True),
            lax.all_gather(shards[7], ("dp", "ctx"), axis=0, tiled=True),
            lax.all_gather(shards[8], ("dp", "ctx"), axis=0, tiled=True),
            lax.all_gather(shards[9], ("dp", "ctx"), axis=0, tiled=True),
            lax.all_gather(shards[10], ("dp", "ctx"), axis=0, tiled=True),
            lax.all_gather(shards[11], ("dp", "ctx"), axis=0, tiled=True),
            lax.all_gather(shards[12], ("dp", "ctx"), axis=0, tiled=True),
            lax.all_gather(shards[13], ("dp", "ctx"), axis=0, tiled=True),
            lax.all_gather(shards[14], ("dp", "ctx"), axis=0, tiled=True),
        )
        output, grad_tokens, small_grads, operands = micro_step(
            tokens, cotangent, shards, forward_weights
        )
        outputs.append(output)
        grads_in.append(grad_tokens)
        operand_lists.append(operands)
        if small_total is None:
            small_total = small_grads
        else:
            small_total = tuple(
                (total_grad + update for total_grad, update in zip(small_total, small_grads))
            )
    joined = tuple(
        (jnp.concatenate([entry[index] for entry in operand_lists], axis=0) for index in range(10))
    )
    (
        normed,
        query_grad,
        grad_keys,
        grad_values,
        mixed_heads,
        grad_branch,
        normed_two,
        grad_pre,
        active,
        cotangent,
    ) = joined
    grads = (
        weight_grad(normed, query_grad),
        weight_grad(normed, grad_keys),
        weight_grad(normed, grad_values),
        weight_grad(mixed_heads, grad_branch),
        weight_grad(normed_two, grad_pre),
        weight_grad(active, cotangent),
        column_sum(query_grad),
        column_sum(grad_values),
        column_sum(grad_branch),
        column_sum(grad_pre),
        column_sum(cotangent),
        small_total[0],
        small_total[1],
        small_total[2],
        small_total[3],
    )
    owned = owner_sum(grads)
    layer_out = jnp.concatenate(outputs, axis=0)
    grad_tokens_all = jnp.concatenate(grads_in, axis=0)
    return (
        layer_out,
        grad_tokens_all,
        owned[0],
        owned[1],
        owned[2],
        owned[3],
        owned[4],
        owned[5],
        owned[6],
        owned[7],
        owned[8],
        owned[9],
        owned[10],
        owned[11],
        owned[12],
        owned[13],
        owned[14],
    )


BF = jnp.bfloat16
F32 = jnp.float32
SMALL = 8


def other_core(value):
    return lax.ppermute(value, "core", [(0, 1), (1, 0)])


def other_x(value):
    return lax.ppermute(value, "x", [(0, 1), (1, 0)])


def other_y(value):
    return lax.ppermute(value, "y", [(0, 1), (1, 0)])


def other_z(value, by):
    return lax.ppermute(value, "z", [(i, i ^ by) for i in range(lax.axis_size("z"))])


def pair(bit, own, received):
    return jnp.stack((jnp.where(bit == 0, own, received), jnp.where(bit == 0, received, own)))


def pick(value, index, axis):
    return lax.dynamic_index_in_dim(value, index, axis, keepdims=False)


def in_order(index, pieces):
    level = list(pieces)
    bit = 0
    ordered = [p[None] for p in level]
    while len(ordered) > 1:
        flag = (index >> bit) & 1
        ordered = [
            jnp.concatenate(
                (jnp.where(flag == 0, a, b), jnp.where(flag == 0, b, a)), axis=0
            )
            for a, b in zip(ordered[::2], ordered[1::2])
        ]
        bit += 1
    return ordered[0]


def gather_plane(along_z, x, y):
    half = along_z.shape[0] // 2
    first, second = along_z[:half], along_z[half:]
    first = pair(x, first, other_x(first))
    second = pair(y, second, other_y(second))
    first = pair(y, first, other_y(first))
    second = pair(x, second, other_x(second))
    return jnp.concatenate((jnp.moveaxis(first, 2, 0).swapaxes(1, 2), jnp.moveaxis(second, 2, 0)))


def plus(kept, received):
    return kept.astype(F32) + received.astype(F32)


LIGHT = pl.CostEstimate(flops=0, bytes_accessed=1, transcendentals=0)
VMEM_LIMIT = 56 * 1024 * 1024
QUERY_BLOCK = 256


def lane_masks(dtype):
    lane = lax.broadcasted_iota(jnp.int32, (1, 2 * DH), 1)
    return [(lane < DH).astype(dtype), (lane >= DH).astype(dtype)]


def visible(key_count, query_block):
    key_pos = lax.broadcasted_iota(jnp.int32, (query_block, query_block), 0)
    query_pos = lax.broadcasted_iota(jnp.int32, (query_block, query_block), 1)
    return key_pos <= query_pos


def masked_tail(scores, allowed):
    key_count, query_block = scores.shape
    tail = jnp.where(allowed, scores[key_count - query_block :], -1e30)
    if key_count == query_block:
        return tail
    return jnp.concatenate((scores[: key_count - query_block], tail), axis=0)


def nt(left, right):
    return lax.dot_general(left, right, (((1,), (1,)), ((), ())), preferred_element_type=F32)


def nn(left, right):
    return lax.dot_general(left, right, (((1,), (0,)), ((), ())), preferred_element_type=F32)


def attend_kernel(q_ref, k_ref, v_ref, mixed_ref, lse_ref):
    length = q_ref.shape[0]
    masks = lane_masks(BF)
    allowed = visible(QUERY_BLOCK, QUERY_BLOCK)
    keys = k_ref[...]
    masked_keys = [keys * m for m in masks]
    v_t = v_ref[...].T
    row = lax.broadcasted_iota(jnp.int32, (2 * DH, 1), 0)
    values_t = [jnp.where(row < DH, v_t, jnp.zeros((), BF)), jnp.where(row >= DH, v_t, jnp.zeros((), BF))]
    for start in range(0, length, QUERY_BLOCK):
        stop = start + QUERY_BLOCK
        q = q_ref[start:stop, :]
        mixed_t = None
        for head in range(2):
            scores = masked_tail(nt(masked_keys[head][:stop], q), allowed)
            top = jnp.max(scores, axis=0, keepdims=True)
            powers = jnp.exp(scores - top)
            total = jnp.sum(powers, axis=0, keepdims=True)
            low = (powers * (1.0 / total)).astype(BF)
            part = nn(values_t[head][:, :stop], low)
            mixed_t = part if mixed_t is None else mixed_t + part
            lse_ref[0, head : head + 1, start:stop] = top + jnp.log(total)
        mixed_ref[start:stop, :] = mixed_t.T.astype(BF)


def attend_back_kernel(q_ref, k_ref, v_ref, g_ref, mixed_ref, lse_ref, gq_ref, gk_ref, gv_ref, ka, va):
    length = q_ref.shape[0]
    masks = lane_masks(BF)
    allowed = visible(QUERY_BLOCK, QUERY_BLOCK)
    keys, values = k_ref[...], v_ref[...]
    masked_keys = [keys * m for m in masks]
    masked_values = [values * m for m in masks]
    keys_t = [m.T for m in masked_keys]
    for start in range(length - QUERY_BLOCK, -1, -QUERY_BLOCK):
        stop = start + QUERY_BLOCK
        q, g = q_ref[start:stop, :], g_ref[start:stop, :]
        products = (g.astype(F32) * mixed_ref[start:stop, :].astype(F32)).T
        grad_q_t = None
        grad_k = grad_v = None
        for head in range(2):
            inner = jnp.sum(products[head * DH : (head + 1) * DH], axis=0, keepdims=True)
            scores = masked_tail(nt(masked_keys[head][:stop], q), allowed)
            probs = jnp.exp(scores - lse_ref[0, head : head + 1, start:stop])
            grad_probs = nt(masked_values[head][:stop], g)
            grad_scores = (probs * (grad_probs - inner)).astype(BF)
            part_v = nn(probs.astype(BF), g * masks[head])
            part_k = nn(grad_scores, q * masks[head])
            part_q = nn(keys_t[head][:, :stop], grad_scores)
            grad_v = part_v if head == 0 else grad_v + part_v
            grad_k = part_k if head == 0 else grad_k + part_k
            grad_q_t = part_q if head == 0 else grad_q_t + part_q
        gq_ref[start:stop, :] = grad_q_t.T.astype(BF)
        if stop == length:
            ka[...] = grad_k
            va[...] = grad_v
        else:
            ka[:stop, :] += grad_k
            va[:stop, :] += grad_v
    gk_ref[...] = ka[...].astype(BF)
    gv_ref[...] = va[...].astype(BF)


def attend(queries, keys, values):
    length, width = queries.shape
    pairs = width // (2 * DH)
    block = pl.BlockSpec((length, 2 * DH), lambda i: (0, i))
    return pl.pallas_call(
        attend_kernel,
        grid=(pairs,),
        in_specs=[block] * 3,
        out_specs=[block, pl.BlockSpec((1, 2, length), lambda i: (i, 0, 0))],
        out_shape=[
            jax.ShapeDtypeStruct((length, width), BF),
            jax.ShapeDtypeStruct((pairs, 2, length), F32),
        ],
        compiler_params=pltpu.CompilerParams(vmem_limit_bytes=VMEM_LIMIT),
        cost_estimate=LIGHT,
        name="attend",
    )(queries, keys, values)


def attend_back(queries, keys, values, mixed, lse, grad_mixed, pair_index, pairs):
    length = queries.shape[0]
    block = pl.BlockSpec((length, 2 * DH), lambda i: (0, i + pair_index))
    out_block = pl.BlockSpec((length, 2 * DH), lambda i: (0, i))
    width = pairs * 2 * DH
    return pl.pallas_call(
        attend_back_kernel,
        grid=(pairs,),
        in_specs=[block] * 5 + [pl.BlockSpec((1, 2, length), lambda i: (i + pair_index, 0, 0))],
        out_specs=[out_block] * 3,
        out_shape=[jax.ShapeDtypeStruct((length, width), BF)] * 3,
        scratch_shapes=[pltpu.VMEM((length, 2 * DH), F32)] * 2,
        compiler_params=pltpu.CompilerParams(vmem_limit_bytes=VMEM_LIMIT),
        cost_estimate=LIGHT,
        name="attend_back",
    )(queries, keys, values, grad_mixed, mixed, lse)


def position_blocks(core, block):
    return [
        (b, own, pl.multiple_of(b * 2 * block + (core if own else 1 - core) * block, block))
        for b in range(2)
        for own in (True, False)
    ]


def normalise(values):
    centre = values - jnp.mean(values, axis=-1, keepdims=True)
    spread = jnp.mean(centre * centre, axis=-1, keepdims=True)
    rate = lax.rsqrt(spread + 1e-05)
    return centre * rate, rate


def normalise_back(unit, rate, gain, grad):
    scaled = grad * gain
    return rate * (
        scaled
        - jnp.mean(scaled, axis=-1, keepdims=True)
        - unit * jnp.mean(scaled * unit, axis=-1, keepdims=True)
    )


CORE, X, Y = range(3)
B_QUERY, B_VALUE, B_OUT, B_DOWN, GAIN1, SHIFT1, GAIN2, SHIFT2 = range(8)


def weight(ref, i):
    chips, _, width = ref.shape
    rows = width * 2 // chips
    return ref[:, i * rows : (i + 1) * rows, :].reshape(chips * rows, width)


def add_sums(ref, values):
    @pl.when(pl.program_id(0) == 0)
    def _():
        ref[...] = jnp.zeros(ref.shape, F32)

    for i, value in enumerate(values):
        ref[i : i + 1, :] += jnp.sum(value, axis=0, keepdims=True)


def enter_kernel(core_ref, mine_ref, other_ref, vec_ref, half_ref, w_ref, n_ref, q_ref, k_ref, v_ref):
    core = core_ref[0]
    block = mine_ref.shape[0] // 2
    for b, own, row in position_blocks(core, block):
        tokens = (mine_ref if own else other_ref)[b * block : (b + 1) * block, :].astype(F32)
        unit, _ = normalise(tokens)
        normed = (unit * vec_ref[GAIN1 : GAIN1 + 1, :] + vec_ref[SHIFT1 : SHIFT1 + 1, :]).astype(BF)
        rows = pl.ds(row, block)
        n_ref[rows, :] = normed
        q = (nn(normed, weight(w_ref, 0)) + half_ref[B_QUERY : B_QUERY + 1, :]) * DH ** (-0.5)
        q_ref[rows, :] = q.astype(BF)
        k_ref[rows, :] = nn(normed, weight(w_ref, 1)).astype(BF)
        v_ref[rows, :] = (nn(normed, weight(w_ref, 2)) + half_ref[B_VALUE : B_VALUE + 1, :]).astype(BF)


def out_kernel(core_ref, mixed_ref, w_ref, mine_ref, other_ref):
    block = mine_ref.shape[0] // 2
    for b, own, row in position_blocks(core_ref[0], block):
        part = nn(mixed_ref[pl.ds(row, block), :], w_ref[...])
        ref = mine_ref if own else other_ref
        ref[b * block : (b + 1) * block, :] = part.astype(ref.dtype)


def middle_kernel(tokens_ref, part_ref, received_ref, vec_ref, residual_ref, n_ref):
    residual = (
        tokens_ref[...].astype(F32)
        + part_ref[...]
        + received_ref[...].astype(F32)
        + vec_ref[B_OUT : B_OUT + 1, :]
    )
    unit, _ = normalise(residual)
    residual_ref[...] = residual
    n_ref[...] = (unit * vec_ref[GAIN2 : GAIN2 + 1, :] + vec_ref[SHIFT2 : SHIFT2 + 1, :]).astype(BF)


def middle_back_kernel(residual_ref, gn_ref, gn_received_ref, g_ref, vec_ref, gr_ref, branch_ref, sums_ref):
    unit, rate = normalise(residual_ref[...])
    grad_normed = gn_ref[...] + gn_received_ref[...].astype(F32)
    cotangent = g_ref[...].astype(F32)
    grad = cotangent + normalise_back(unit, rate, vec_ref[GAIN2 : GAIN2 + 1, :], grad_normed)
    gr_ref[...] = grad
    branch = grad.astype(BF)
    branch_ref[...] = branch
    add_sums(sums_ref, (branch.astype(F32), cotangent, grad_normed * unit, grad_normed))


def mixed_back_kernel(core_ref, mixed_ref, mine_ref, other_ref, w_ref, gm_ref, gw_ref):
    block = mine_ref.shape[0] // 2
    total = None
    for b, own, row in position_blocks(core_ref[0], block):
        branch = (mine_ref if own else other_ref)[b * block : (b + 1) * block, :]
        rows = pl.ds(row, block)
        gm_ref[rows, :] = nt(branch, w_ref[...]).astype(BF)
        part = nn(mixed_ref[rows, :].T, branch)
        total = part if total is None else total + part
    gw_ref[...] = total.astype(BF)


def weight_back_kernel(
    place_ref, n_ref, q_ref, k_ref, v_ref, left_keep, left_send, right_keep, right_send, sums_ref, by_y, by_x
):
    x, y = place_ref[X], place_ref[Y]
    n_t = n_ref[...].T
    rows = by_y.shape[2]
    grads = [q_ref[...] * jnp.asarray(DH ** (-0.5), BF), k_ref[...], v_ref[...]]
    for i in range(2):
        by_y[...] = nn(n_t, grads[i]).astype(BF).reshape(by_y.shape)
        part = slice(i * rows, (i + 1) * rows)
        left_keep[:, part, :] = by_y[:, pl.ds(y, 1)].reshape(-1, rows, by_y.shape[3])
        left_send[:, part, :] = by_y[:, pl.ds(1 - y, 1)].reshape(-1, rows, by_y.shape[3])
    by_x[...] = nn(n_t, grads[2]).astype(BF).reshape(by_x.shape)
    right_keep[...] = by_x[:, pl.ds(x, 1)].reshape(right_keep.shape)
    right_send[...] = by_x[:, pl.ds(1 - x, 1)].reshape(right_send.shape)
    half = q_ref.shape[1]
    side = lax.broadcasted_iota(jnp.int32, (1, 2 * half), 1) >= half
    for i, grad in enumerate((grads[0], grads[2])):
        total = jnp.sum(grad.astype(F32), axis=0, keepdims=True)
        total = jnp.concatenate((total, total), axis=1)
        sums_ref[i : i + 1, :] = jnp.where(side == (place_ref[CORE] == 1), total, 0.0)


def enter_back_kernel(place_ref, q_ref, k_ref, v_ref, w_ref, mine_ref, other_ref):
    block = mine_ref.shape[0] // 2
    for b, own, row in position_blocks(place_ref[CORE], block):
        rows = pl.ds(row, block)
        part = (
            nt(q_ref[rows, :] * jnp.asarray(DH ** (-0.5), BF), weight(w_ref, 0))
            + nt(k_ref[rows, :], weight(w_ref, 1))
            + nt(v_ref[rows, :], weight(w_ref, 2))
        )
        ref = mine_ref if own else other_ref
        ref[b * block : (b + 1) * block, :] = part.astype(ref.dtype)


def leave_kernel(tokens_ref, gn_ref, gn_received_ref, gr_ref, vec_ref, gt_ref, sums_ref):
    unit, rate = normalise(tokens_ref[...].astype(F32))
    grad_normed = gn_ref[...] + gn_received_ref[...].astype(F32)
    gt_ref[...] = gr_ref[...] + normalise_back(unit, rate, vec_ref[GAIN1 : GAIN1 + 1, :], grad_normed)
    add_sums(sums_ref, (grad_normed * unit, grad_normed))


def shape(dims, dtype):
    return jax.ShapeDtypeStruct(dims, dtype)


def whole_call(kernel, outs, *args, flops=0, scalars=0, scratch=()):
    in_specs = [
        pl.BlockSpec(memory_space=pltpu.SMEM if i < scalars else pltpu.VMEM)
        for i in range(len(args))
    ]
    moved = sum(a.size * a.dtype.itemsize for a in list(args) + outs)
    return pl.pallas_call(
        kernel,
        in_specs=in_specs,
        out_specs=[pl.BlockSpec(memory_space=pltpu.VMEM)] * len(outs),
        out_shape=outs,
        scratch_shapes=list(scratch),
        compiler_params=pltpu.CompilerParams(vmem_limit_bytes=VMEM_LIMIT),
        cost_estimate=LIGHT,
        name=kernel.__name__,
    )(*args)


def row_call(kernel, outs, sums, *args):
    length, width = args[0].shape
    block = length // 2
    rows = pl.BlockSpec((block, width), lambda i: (i, 0))
    out_shape = [shape((length, width), dtype) for dtype in outs]
    out_specs = [rows] * len(outs)
    if sums:
        out_shape.append(shape((sums, width), F32))
        out_specs.append(pl.BlockSpec((sums, width), lambda i: (0, 0)))
    moved = sum(a.size * a.dtype.itemsize for a in list(args) + out_shape)
    return pl.pallas_call(
        kernel,
        grid=(2,),
        in_specs=[rows] * (len(args) - 1) + [pl.BlockSpec(args[-1].shape, lambda i: (0, 0))],
        out_specs=out_specs,
        out_shape=out_shape,
        compiler_params=pltpu.CompilerParams(vmem_limit_bytes=VMEM_LIMIT),
        cost_estimate=LIGHT,
        name=kernel.__name__,
    )(*args)


def hidden_kernel(
    place_ref, n_mine, n_other, g_mine, g_other, up_ref, down_ref, bias_ref,
    y_mine, y_other, gn_mine, gn_other, up_keep, up_send, down_keep, down_send, gb_ref,
    n_t, y_sum, gn_sum, up_all, down_all,
):
    step = pl.program_id(0)
    length = n_mine.shape[0]

    @pl.when(step == 0)
    def _():
        n_t[:, :length] = n_mine[...].T
        n_t[:, length:] = n_other[...].T
        for ref in (y_mine, gn_mine, y_sum, gn_sum):
            ref[...] = jnp.zeros(ref.shape, F32)

    up = up_ref[...].reshape(-1, up_ref.shape[2])
    down = down_ref[...].reshape(-1, down_ref.shape[2])
    grad_up = grad_down = bias_sum = None
    for part, (n_ref, g_ref, y_ref, gn_ref) in enumerate(
        ((n_mine, g_mine, y_mine, gn_mine), (n_other, g_other, y_sum, gn_sum))
    ):
        n, g = n_ref[...], g_ref[...]
        pre = nn(n, up) + bias_ref[0]
        square = pre * pre
        bent = jnp.tanh(pre * (0.7978845608028654 + 0.7978845608028654 * 0.044715 * square))
        half = 0.5 + 0.5 * bent
        active = (pre * half).astype(BF)
        rise = pre * (2 * 0.7978845608028654 + 6 * 0.7978845608028654 * 0.044715 * square)
        slope = half * (1.0 + (1.0 - half) * rise)
        grad_pre = (nt(g, down) * slope).astype(BF)
        y_ref[...] += nn(active, down)
        gn_ref[...] += nt(grad_pre, up)
        part_up = nn(n_t[:, part * length : (part + 1) * length], grad_pre)
        part_down = lax.dot_general(active, g, (((0,), (0,)), ((), ())), preferred_element_type=F32)
        part_bias = jnp.sum(grad_pre.astype(F32), axis=0, keepdims=True)
        grad_up = part_up if part == 0 else grad_up + part_up
        grad_down = part_down if part == 0 else grad_down + part_down
        bias_sum = part_bias if part == 0 else bias_sum + part_bias
    x, y = place_ref[X], place_ref[Y]
    up_all[...] = grad_up.astype(BF).reshape(up_all.shape)
    up_keep[...] = up_all[:, pl.ds(y, 1)].reshape(up_keep.shape)
    up_send[...] = up_all[:, pl.ds(1 - y, 1)].reshape(up_send.shape)
    down_all[...] = grad_down.astype(BF).reshape(down_all.shape)
    down_keep[...] = down_all[:, pl.ds(x, 1)].reshape(down_keep.shape)
    down_send[...] = down_all[:, pl.ds(1 - x, 1)].reshape(down_send.shape)
    gb_ref[0] = bias_sum

    @pl.when(step == pl.num_programs(0) - 1)
    def _():
        y_other[...] = y_sum[...].astype(BF)
        gn_other[...] = gn_sum[...].astype(BF)


def feed_forward(place, n_mine, n_other, g_mine, g_other, late, bias, hidden_rows):
    length, width = n_mine.shape
    chips = late.shape[0]
    steps = 2
    z_count = chips // 4
    z_step = z_count // steps
    tile = chips * hidden_rows // steps
    up_rows = width // chips
    per_half = steps // 2
    down_chips = chips // steps
    full = pl.BlockSpec((length, width), lambda i: (0, 0))
    hidden = tile * steps
    return pl.pallas_call(
        hidden_kernel,
        grid=(steps,),
        in_specs=[pl.BlockSpec(memory_space=pltpu.SMEM)] + [full] * 4
        + [
            pl.BlockSpec((chips, up_rows, tile), lambda i: (0, i // per_half, i % per_half)),
            pl.BlockSpec((down_chips, hidden_rows, width), lambda i: (i, 1, 0)),
            pl.BlockSpec((1, 1, tile), lambda i: (i, 0, 0)),
        ],
        out_specs=[full] * 4
        + [
            pl.BlockSpec((chips // 2, up_rows, tile), lambda i: (0, 0, i)),
            pl.BlockSpec((chips // 2, up_rows, tile), lambda i: (0, 0, i)),
            pl.BlockSpec((z_step, 2, hidden_rows, width), lambda i: (i, 0, 0, 0)),
            pl.BlockSpec((z_step, 2, hidden_rows, width), lambda i: (i, 0, 0, 0)),
            pl.BlockSpec((1, 1, tile), lambda i: (i, 0, 0)),
        ],
        out_shape=[
            shape((length, width), F32),
            shape((length, width), BF),
            shape((length, width), F32),
            shape((length, width), BF),
            shape((chips // 2, up_rows, hidden), BF),
            shape((chips // 2, up_rows, hidden), BF),
            shape((z_count, 2, hidden_rows, width), BF),
            shape((z_count, 2, hidden_rows, width), BF),
            shape((steps, 1, tile), F32),
        ],
        scratch_shapes=[
            pltpu.VMEM((width, 2 * length), BF),
            pltpu.VMEM((length, width), F32),
            pltpu.VMEM((length, width), F32),
            pltpu.VMEM((chips // 2, 2, up_rows, tile), BF),
            pltpu.VMEM((z_step, 2, 2, hidden_rows, width), BF),
        ],
        compiler_params=pltpu.CompilerParams(vmem_limit_bytes=VMEM_LIMIT),
        cost_estimate=LIGHT,
        name="feed_forward",
    )(place, n_mine, n_other, g_mine, g_other, late, late, bias.reshape(steps, 1, tile))


def chip_step(
    tokens_in,
    out_grad,
    w_query,
    w_key,
    w_value,
    w_out,
    w_up,
    w_down,
    b_query,
    b_value,
    b_out,
    b_up,
    b_down,
    norm1_gain,
    norm1_shift,
    norm2_gain,
    norm2_shift,
):
    z, x, y, core = (lax.axis_index(name) for name in ("z", "x", "y", "core"))
    z_count = lax.axis_size("z")
    chips = z_count * 4
    half_chips = chips // 2
    _, block, width = tokens_in.shape
    half = width // 2
    rows = w_query.shape[0]
    hidden_rows = w_down.shape[0]
    hidden = hidden_rows * chips

    def own_positions(value):
        return pair(y, pick(value, y, 0), other_y(pick(value, 1 - y, 0))).reshape(2 * block, width)

    three = jnp.stack((w_query, w_key, w_value)).reshape(3, rows, 2, half)
    vectors = (
        b_query, b_value, b_out, b_down, norm1_gain, norm1_shift, norm2_gain, norm2_shift, b_up
    )
    small = jnp.concatenate(vectors)
    unit_rows = 3 * rows + SMALL
    small_rows = jnp.zeros((SMALL, half), BF).at[0, : small.shape[0]].set(small)
    own = jnp.concatenate((pick(three, core, 2).reshape(3 * rows, half), small_rows))
    unit = pair(
        core,
        own,
        other_core(
            jnp.concatenate((pick(three, 1 - core, 2).reshape(3 * rows, half), small_rows))
        ),
    )
    up_parts = w_up.reshape(rows, chips, 2, hidden_rows)
    up_unit = pair(
        core,
        pick(up_parts, core, 2).reshape(rows, hidden),
        other_core(pick(up_parts, 1 - core, 2).reshape(rows, hidden)),
    )
    up_unit = up_unit.reshape(2 * rows, 2, width)
    late = jnp.concatenate((up_unit[:, 0], up_unit[:, 1], w_down))
    late = lax.all_gather(late, ("z", "x", "y"), axis=0, tiled=False)
    threes = unit[:, : 3 * rows].reshape(2, 3, rows, half).swapaxes(0, 1).reshape(6 * rows, half)
    unit = jnp.concatenate(
        (threes, unit[:, 3 * rows :].reshape(2 * SMALL, half), w_out[:, :half], w_out[:, half:])
    )
    pieces = [unit] + [other_z(unit, k) for k in range(1, z_count)]
    both = jnp.stack((pick(tokens_in, y, 0), pick(out_grad, y, 0)))
    both_from = other_y(jnp.stack((pick(tokens_in, 1 - y, 0), pick(out_grad, 1 - y, 0))))
    pieces, both_from = lax.optimization_barrier((pieces, both_from))
    both = pair(y, both, both_from).swapaxes(0, 1).reshape(2, 2 * block, width)
    mine, grad_mine = both[0], both[1]
    other, grad_other = other_core(mine), other_core(grad_mine)
    place = jnp.stack((core, x, y)).astype(jnp.int32)
    gathered = gather_plane(in_order(z, pieces), x, y)
    out_parts = jnp.concatenate(
        (gathered[..., 2 * unit_rows : 2 * unit_rows + rows, :], gathered[..., 2 * unit_rows + rows :, :]),
        axis=-1,
    ).reshape(2, half_chips, rows, width)
    out_c = (
        pair(core, pick(out_parts, core, 0), other_core(pick(out_parts, 1 - core, 0)))
        .swapaxes(0, 1)
        .reshape(half, width)
    )
    gathered = gathered.reshape(chips, -1, half)
    small_all = gathered[:, 6 * rows : 6 * rows + 2 * SMALL].reshape(chips * 2, SMALL, half)
    small_all = small_all[:, 0, : small.shape[0]]
    vectors = small_all[:, : 8 * rows].reshape(chips * 2, 8, rows).swapaxes(0, 1)
    vectors = vectors.reshape(8, width).astype(F32)
    halves = pick(vectors.reshape(8, 2, half), core, 1)
    bias_u = pick(small_all[:, 8 * rows :].reshape(chips, 2, hidden_rows), core, 1)
    bias_u = bias_u.reshape(hidden).astype(F32)

    length = 4 * block
    heads_shape = shape((length, half), BF)
    normed, queries, keys, values = whole_call(
        enter_kernel,
        [shape((length, width), BF)] + [heads_shape] * 3,
        place, mine, other, vectors, halves, gathered,
        flops=6 * length * width * half, scalars=1,
    )
    mixed, lse = attend(queries, keys, values)
    mine_shape = shape((2 * block, width), F32)
    sent_shape = shape((2 * block, width), BF)
    part, to_other = whole_call(
        out_kernel, [mine_shape, sent_shape], place, mixed, out_c,
        flops=2 * length * width * half, scalars=1,
    )
    residual, normed2 = row_call(middle_kernel, (F32, BF), 0, mine, part, other_core(to_other), vectors)
    late, normed2 = lax.optimization_barrier((late, normed2))
    y_mine, y_other, gn_mine, gn_other, up_keep, up_send, down_keep, down_send, up_sums = feed_forward(
        place, normed2, other_core(normed2), grad_mine, grad_other, late, bias_u, hidden_rows
    )

    up_from, down_from = other_y(up_send), other_x(down_send)
    grad_residual, branch, sums2 = row_call(
        middle_back_kernel, (F32, BF), 4, residual, gn_mine, other_core(gn_other), grad_mine, vectors
    )
    grad_mixed, grad_out = whole_call(
        mixed_back_kernel, [heads_shape, shape((half, width), BF)],
        place, mixed, branch, other_core(branch), out_c,
        flops=4 * length * width * half, scalars=1,
    )
    grad_out = grad_out.reshape(half_chips, 2, rows, width)
    grad_out = pair(
        core,
        pick(grad_out, core, 1),
        other_core(pick(grad_out, 1 - core, 1)),
    ).reshape(z_count, 2, 2, rows, width)
    grads = attend_back(
        queries, keys, values, mixed, lse, grad_mixed, 0, half // (2 * DH)
    )
    up_from, down_from, grads = lax.optimization_barrier((up_from, down_from, grads))
    ups = plus(up_keep, up_from).reshape(z_count, 2, 2 * rows, hidden)
    downs = plus(down_keep, down_from)
    up_send, down_send = pick(ups, 1 - x, 1).astype(BF), pick(downs, 1 - y, 1).astype(BF)
    up_send, down_send, grads = lax.optimization_barrier((up_send, down_send, grads))
    up_from, down_from, out_from = other_x(up_send), other_y(down_send), other_x(pick(grad_out, 1 - x, 1))
    left_shape = shape((2 * z_count, 4 * rows, half), BF)
    right_shape = shape((z_count, 2, 2 * rows, half), BF)
    left_keep, left_send, right_keep, right_send, sums_heads = whole_call(
        weight_back_kernel,
        [left_shape] * 2 + [right_shape] * 2 + [shape((2, width), F32)],
        place, normed, *grads,
        flops=6 * length * width * half, scalars=1,
        scratch=(
            pltpu.VMEM((2 * z_count, 2, 2 * rows, half), BF),
            pltpu.VMEM((z_count, 2, 2, 2 * rows, half), BF),
        ),
    )
    left_send, right_send, grads, y_mine, y_other = lax.optimization_barrier(
        (left_send, right_send, grads, y_mine, y_other)
    )
    left_from, right_from = other_y(left_send), other_x(right_send)
    gn_mine, gn_other = whole_call(
        enter_back_kernel,
        [mine_shape, sent_shape],
        place, *grads, gathered,
        flops=6 * length * width * half, scalars=1,
    )
    up_from, down_from, out_from, gn_mine, gn_other = lax.optimization_barrier(
        (up_from, down_from, out_from, gn_mine, gn_other)
    )
    low, high = z & 1, z >> 1

    def first_z(value):
        value = value.reshape((z_count // 2, 2) + value.shape[1:])
        return pick(value, low, 1), other_z(pick(value, 1 - low, 1).astype(BF), 1)

    def second_z(value):
        return pick(value, high, 0), other_z(pick(value, 1 - high, 0).astype(BF), 2)

    gn_from = other_core(gn_other)
    ups = plus(pick(ups, x, 1), up_from)
    downs = plus(pick(downs, y, 1), down_from)
    outs = plus(pick(grad_out, x, 1), out_from)
    forward_kept, forward_from = first_z(
        jnp.concatenate((ups[..., :width], ups[..., width:], downs), axis=1)
    )
    left_from, right_from, gn_from = lax.optimization_barrier((left_from, right_from, gn_from))
    lefts = plus(left_keep, left_from).reshape(z_count, 2, 4 * rows, half)
    rights = plus(right_keep, right_from)
    rights = jnp.concatenate((rights, outs[..., :half], outs[..., half:]), axis=2)
    left_send, right_send = pick(lefts, 1 - x, 1).astype(BF), pick(rights, 1 - y, 1).astype(BF)
    left_send, right_send, gn_from = lax.optimization_barrier((left_send, right_send, gn_from))
    left_from, right_from = other_x(left_send), other_y(right_send)
    grad_tokens, sums1 = row_call(
        leave_kernel, (F32,), 2, mine, gn_mine, gn_from, grad_residual, vectors
    )
    output = residual + y_mine + other_core(y_other).astype(F32) + vectors[B_DOWN]
    output = output.astype(BF).reshape(2, block, width)
    grad_tokens = grad_tokens.reshape(2, block, width)
    to_y = jnp.concatenate((pick(output, 1 - y, 0), pick(grad_tokens, 1 - y, 0).astype(BF)))
    forward_kept, forward_from = second_z(plus(forward_kept, forward_from))

    left_from, right_from, sums1 = lax.optimization_barrier((left_from, right_from, sums1))
    small_grads = jnp.concatenate((sums_heads, sums2, sums1, up_sums.reshape(2, width)))
    lefts = plus(pick(lefts, x, 1), left_from)
    rights = plus(pick(rights, y, 1), right_from)
    last = jnp.concatenate((lefts, rights), axis=1)
    last, small_grads = lax.optimization_barrier((last, small_grads))
    last, last_from = first_z(last)
    small_grads = small_grads + other_y(small_grads)
    small_grads, to_y = lax.optimization_barrier((small_grads, to_y))
    from_y = other_y(to_y)
    small_grads = small_grads + other_x(small_grads)
    small_from = other_z(small_grads, 1)
    last_from, small_from, forward_from = lax.optimization_barrier((last_from, small_from, forward_from))
    last, last_from = second_z(plus(last, last_from))
    small_grads = small_grads + small_from
    small_from = other_z(small_grads, 2)
    forward_sum = plus(forward_kept, forward_from)
    layer_out = pair(y, pick(output, y, 0), from_y[:block])
    grad_tokens = pair(y, pick(grad_tokens, y, 0), from_y[block:].astype(F32))

    up_mine = forward_sum[: 4 * rows].reshape(2, 2, rows, width)
    down_mine = forward_sum[4 * rows :]
    up_from = other_core(pick(up_mine, 1 - core, 1))
    up_out = pair(core, pick(up_mine, core, 1), up_from)
    up_out = up_out.reshape(2, 2, rows, half_chips, hidden_rows)
    up_out = jnp.transpose(up_out, (2, 1, 3, 0, 4)).reshape(rows, 2 * hidden)
    last_from, small_from, layer_out, grad_tokens, up_out, down_mine = lax.optimization_barrier(
        (last_from, small_from, layer_out, grad_tokens, up_out, down_mine)
    )
    last = plus(last, last_from)
    small_grads = small_grads + small_from
    small_core = small_grads[:8] + other_core(small_grads[:8])
    three_mine = last[: 6 * rows].reshape(3, 2, rows, half)
    three_from = other_core(pick(three_mine, 1 - core, 1))
    out_mine = jnp.concatenate((last[6 * rows : 7 * rows], last[7 * rows : 8 * rows]), axis=1)
    chip = (z * 2 + x) * 2 + y
    small_mine = lax.dynamic_slice_in_dim(small_core, (chip * 2 + core) * rows, rows, 1)
    up_bias = lax.dynamic_slice_in_dim(small_grads[8:].reshape(hidden), chip * hidden_rows, hidden_rows, 0)
    three_out = pair(core, pick(three_mine, core, 1), three_from)
    g_q, g_k, g_v = (jnp.concatenate((three_out[0, i], three_out[1, i]), axis=1) for i in range(3))
    g_small = [small_mine[i] for i in (0, 1, 2, 3, 6, 7, 4, 5)]
    return (
        layer_out,
        grad_tokens,
        g_q,
        g_k,
        g_v,
        out_mine,
        up_out,
        down_mine,
        g_small[0],
        g_small[1],
        g_small[2],
        up_bias,
        g_small[3],
        g_small[4],
        g_small[5],
        g_small[6],
        g_small[7],
    )


def solution(mesh):
    dp_count, ctx_count = mesh.shape["dp"], mesh.shape["ctx"]

    def run(*args):
        per_dp = args[0].shape[0] // dp_count
        if ctx_count == 4 and per_dp == 2 and dp_count == 8:
            devices = mesh.devices.reshape(dp_count // 2, 2, ctx_count // 2, 2)
            used = Mesh(devices, ("z", "x", "y", "core"))
            body, dp, ctx = chip_step, ("z", "x"), ("y", "core")
        else:
            used, body, dp, ctx = mesh, on_device, ("dp",), ("ctx",)
        tokens, matrix, bias = P(dp, ctx, None), P(dp + ctx, None), P(dp + ctx)
        return jax.shard_map(
            body,
            mesh=used,
            in_specs=(tokens,) * 2 + (matrix,) * 6 + (bias,) * 9,
            out_specs=(tokens,) * 2 + (matrix,) * 6 + (bias,) * 9,
            check_vma=False,
        )(*args)

    return run
```
